32 devices in a mesh: exp: 2 (over core), row: 4 (over y, x), col: 4 (over z).
Axes of the slice: x: 2, y: 2, z: 4, core: 2. Of those that a mesh axis runs over, the one named last changes fastest.
Arguments:
- inputs: bfloat16 [4096, 2560], P(('exp', 'row'), 'col'), may hold values from -30 to 30
- routes: int32 [4096, 6], P(('exp', 'row')), may hold values from 0 to 15, all different within a row; in each aligned block of 512 rows (0 to 511, 512 to 1023, ...) at most 256 rows name the same one
- w_query: bfloat16 [2560, 2560], P('col', 'row'), may hold values from -0.15625 to 0.15625
- w_key: bfloat16 [2560, 512], P('col', 'row'), may hold values from -0.15625 to 0.15625
- w_value: bfloat16 [2560, 512], P('col', 'row'), may hold values from -0.125 to 0.125
- w_output: bfloat16 [2560, 2560], P('row', 'col'), may hold values from -0.625 to 0.625
- gain_attn: float32 [2560], P('col'), may hold values from 0.5 to 1.5
- gain_moe: float32 [2560], P('col'), may hold values from 0.5 to 1.5
- w_router: float32 [2560, 16], P('col'), may hold values from -0.0625 to 0.0625
- shared_gate: bfloat16 [2560, 3072], P('col', 'row'), may hold values from -0.125 to 0.125
- shared_up: bfloat16 [2560, 3072], P('col', 'row'), may hold values from -0.125 to 0.125
- shared_down: bfloat16 [3072, 2560], P('row', 'col'), may hold values from -0.21875 to 0.21875
- expert_gate: bfloat16 [16, 2560, 1536], P(('exp', 'row'), None, 'col'), may hold values from -0.125 to 0.125
- expert_up: bfloat16 [16, 2560, 1536], P(('exp', 'row'), None, 'col'), may hold values from -0.125 to 0.125
- expert_down: bfloat16 [16, 1536, 2560], P(('exp', 'row'), 'col'), may hold values from -0.3125 to 0.3125
- out_grad: bfloat16 [4096, 2560], P(('exp', 'row'), 'col'), may hold values from -6 to 6
Outputs:
- output: bfloat16 [4096, 2560], P(('exp', 'row'), 'col')
- grad_inputs: bfloat16 [4096, 2560], P(('exp', 'row'), 'col')
- grad_query: float32 [2560, 2560], P('col', 'row')
- grad_key: float32 [2560, 512], P('col', 'row')
- grad_value: float32 [2560, 512], P('col', 'row')
- grad_output: float32 [2560, 2560], P('row', 'col')
- grad_gain_attn: float32 [2560], P('col')
- grad_gain_moe: float32 [2560], P('col')
- grad_router: float32 [2560, 16], P('col')
- grad_shared_gate: float32 [2560, 3072], P('col', 'row')
- grad_shared_up: float32 [2560, 3072], P('col', 'row')
- grad_shared_down: float32 [3072, 2560], P('row', 'col')
- grad_expert_gate: float32 [16, 2560, 1536], P(('exp', 'row'), None, 'col')
- grad_expert_up: float32 [16, 2560, 1536], P(('exp', 'row'), None, 'col')
- grad_expert_down: float32 [16, 1536, 2560], P(('exp', 'row'), 'col')
The draws below stay inside these ranges and needn't reach their ends.
Inputs may be any that keep to these rules, and one draw needn't show every extreme that they name: `routes`: in each aligned block of 512 rows no expert is named by more than 256 rows, a bound that some block reaches.
All inputs are finite; a program needn't handle non-finite values.
Results may differ from the reference program's by a relative error of at most 0.02.
Values may be sent and summed in bfloat16 or wider, within the bound.
No kernel may reach another device: no remote copies, remote signals or barrier semaphores. Data moves between devices by JAX's collectives and lax.ppermute only.
A program may use at most 448 MiB of HBM per device.

```python
import math
import jax
import jax.numpy as jnp
import numpy as np
from jax import lax

D = 2560
HEADS = 20
KV_HEADS = 4
HEAD_DIM = 128
FFE = 1536
FFS = 3072
TOPK = 6
EXPERTS = 16
SEQ = 2048
BLOCK = 512
TOKENS = 4096
CAP = 256
N_COL = 4


def draw_inputs(key, part):
    key = jax.random.fold_in(key, 11)
    base_key, row_key = jax.random.split(key, 2)
    row_scale = jnp.exp(jax.random.uniform(row_key, (TOKENS, 1), jnp.float32, jnp.log(0.3), jnp.log(3.0)))
    feature_scale = 0.5 * 3.0 ** (jnp.arange(D, dtype=jnp.float32) / D)
    base = jnp.clip(jax.random.normal(base_key, (TOKENS, D), jnp.float32), -6.0, 6.0)
    return (base * row_scale * feature_scale[None, :]).astype(jnp.bfloat16)


def shard_levels(own_key, dims, cuts, low, top_value):
    loudness, own = 1.0, jax.random.fold_in(own_key, 6)
    for axis_at, parts in cuts:
        draws = jnp.exp(jax.random.uniform(jax.random.fold_in(own, axis_at), (parts,), jnp.float32, low / len(cuts), top_value / len(cuts)))
        loudness = loudness * jnp.repeat(draws, dims[axis_at] // parts).reshape([-1 if axis == axis_at else 1 for axis in range(len(dims))])
    return loudness


def assign_block(key, own, number, rows, amount, top, most, slope):
    sequence = jax.random.permutation(key, amount)
    crowded, usual = shares(amount, rows * top, most, slope, True), shares(amount, rows * top, most, slope, False)
    places = jnp.arange(amount)

    def named(lengths, offset_by):
        used = int((lengths > 0).sum())
        fixed = max(1, used // 4)
        moved = fixed + (places - fixed + offset_by * (used - fixed)) % max(1, amount - fixed)
        return jnp.zeros((amount,), jnp.int32).at[sequence[jnp.where(places < fixed, places, moved)]].set(jnp.asarray(lengths, jnp.int32))

    lengths = jnp.where(number % 4 == 0, named(crowded, number // 4), named(usual, number - number // 4 - 1))
    mixed = jax.random.permutation(jax.random.fold_in(own, 3), amount)
    giver, taker = mixed[0:amount // 2 * 2:2], mixed[1:amount // 2 * 2:2]
    margin = jnp.minimum(lengths[giver] - 1, most - lengths[taker]) // 2
    margin = jnp.where((giver == sequence[0]) | (taker == sequence[0]) | (lengths[taker] == 0), 0, jnp.maximum(margin, 0))
    moved = jax.random.randint(jax.random.fold_in(own, 4), (amount // 2,), 0, 1 << 20) % (margin + 1)
    lengths = lengths.at[giver].add(-moved).at[taker].add(moved)
    members = jnp.searchsorted(jnp.cumsum(lengths), jnp.arange(rows * top), side="right").astype(jnp.int32)
    listing = members.reshape(top, rows).T
    listing = listing[jax.random.permutation(jax.random.fold_in(own, 1), rows)]
    offset_by = jax.random.randint(jax.random.fold_in(own, 2), (rows, 1), 0, top)
    return jnp.take_along_axis(listing, (jnp.arange(top)[None, :] + offset_by) % top, axis=1)


def shares(amount, total, most, lean, full):
    portions = [(1 << 20) // math.isqrt(standing ** lean) + 1 for standing in range(1, amount + 1)]
    largest = most if full else min(most, max(-(-total // amount), total * portions[0] // sum(portions)))
    least = 1 if total - largest >= amount - 1 else 0
    counts, spare = [largest] + [least] * (amount - 1), total - largest - least * (amount - 1)
    while spare > 0:
        candidates = [i for i in range(1, amount) if counts[i] < largest] or [i for i in range(1, amount) if counts[i] < most]
        pool, budget = sum([portions[i] for i in candidates]), spare
        for i in candidates:
            addition = min(most - counts[i], max(1, budget * portions[i] // pool), spare)
            counts[i] = counts[i] + addition
            spare = spare - addition
    return np.array(counts)


def bell_draw(rng, extent, width, limit, shards=(), kind=jnp.bfloat16):
    factor_of = shard_levels(rng, extent, shards, -0.22, 0.18) if shards else 1.0
    entries = jax.random.normal(rng, extent, jnp.float32) * width * factor_of
    return jnp.minimum(jnp.maximum(entries, -limit), limit).astype(kind)


def setup_inputs(seed: int = 0) -> dict:
    seeds = jax.random.split(jax.random.key(seed), 17)
    inputs = draw_inputs(jax.random.fold_in(seeds[16], 71), 0)
    routes_keys = jax.random.split(jax.random.fold_in(seeds[1], 1), TOKENS // BLOCK)
    routes_turns = jax.random.permutation(jax.random.fold_in(seeds[1], 3), TOKENS // BLOCK)
    routes = jax.vmap(lambda own, number: assign_block(jax.random.fold_in(seeds[1], 2), own, number, BLOCK, EXPERTS, TOPK, CAP, 1))(routes_keys, routes_turns).reshape((TOKENS, TOPK))
    w_query = bell_draw(seeds[2], (D, HEADS * HEAD_DIM), (D // 2) ** -0.5, 0.15625, ((0, 4), (1, 4)))
    w_key = bell_draw(seeds[3], (D, KV_HEADS * HEAD_DIM), (D // 2) ** -0.5, 0.15625, ((0, 4), (1, 4)))
    w_value = bell_draw(seeds[4], (D, KV_HEADS * HEAD_DIM), D ** -0.5, 0.125, ((0, 4), (1, 4)))
    w_output = bell_draw(seeds[5], (HEADS * HEAD_DIM, D), (HEADS * HEAD_DIM // 32) ** -0.5, 0.625, ((0, 4), (1, 4)))
    gain_attn = jnp.clip(1.0 + 0.1 * jax.random.normal(seeds[6], (D,), jnp.float32), 0.5, 1.5)
    gain_moe = jnp.clip(1.0 + 0.1 * jax.random.normal(seeds[7], (D,), jnp.float32), 0.5, 1.5)
    w_router = bell_draw(seeds[8], (D, EXPERTS), (4 * D) ** -0.5, 0.0625, ((0, 4),), jnp.float32)
    shared_gate = bell_draw(seeds[9], (D, FFS), D ** -0.5, 0.125, ((0, 4), (1, 4)))
    shared_up = bell_draw(seeds[10], (D, FFS), D ** -0.5, 0.125, ((0, 4), (1, 4)))
    shared_down = bell_draw(seeds[11], (FFS, D), (FFS // 4) ** -0.5, 0.21875, ((0, 4), (1, 4)))
    expert_gate = bell_draw(seeds[12], (EXPERTS, D, FFE), D ** -0.5, 0.125, ((0, 8), (2, 4)))
    expert_up = bell_draw(seeds[13], (EXPERTS, D, FFE), D ** -0.5, 0.125, ((0, 8), (2, 4)))
    expert_down = bell_draw(seeds[14], (EXPERTS, FFE, D), (FFE // 4) ** -0.5, 0.3125, ((0, 8), (1, 4)))
    out_grad = bell_draw(seeds[15], (TOKENS, D), 1.0, 6.0, ((0, 8), (1, 4)))
    return dict(inputs=inputs, routes=routes, w_query=w_query, w_key=w_key, w_value=w_value, w_output=w_output, gain_attn=gain_attn, gain_moe=gain_moe, w_router=w_router, shared_gate=shared_gate, shared_up=shared_up, shared_down=shared_down, expert_gate=expert_gate, expert_up=expert_up, expert_down=expert_down, out_grad=out_grad)


eps = 1e-05
theta = 500000.0
highest = lax.Precision.HIGHEST
masked_value = -1e+30

@jax.custom_vjp
def low(v):
    return lax.optimization_barrier(v.astype(jnp.bfloat16)).astype(jnp.float32)

@jax.custom_vjp
def low_back(v):
    return v

def low_keep(v):
    return (low(v), None)

def low_pass(kept, grad):
    return (grad,)

def back_keep(v):
    return (v, None)

def back_low(kept, grad):
    return (low(grad),)
low.defvjp(low_keep, low_pass)
low_back.defvjp(back_keep, back_low)

def product(left, right):
    return jnp.dot(left, right, precision=highest)

def rms_norm(values, gain):
    return values * lax.rsqrt(lax.optimization_barrier(jnp.mean(values * values, axis=-1, keepdims=True)) + eps) * gain

def rope_tables(positions, head_width):
    half_width = head_width // 2
    frequency = theta ** (-2.0 * jnp.arange(half_width, dtype=jnp.float32) / head_width)
    angles = positions.astype(jnp.float32)[:, None] * frequency[None, :]
    return (jnp.cos(angles), jnp.sin(angles))

def rotate(source, cosines, sine_part):
    half_width = source.shape[-1] // 2
    first_half = source[..., :half_width]
    second_half = source[..., half_width:]
    cos_view = cosines[:, None, :]
    sin_view = sine_part[:, None, :]
    return jnp.concatenate([first_half * cos_view - second_half * sin_view, first_half * sin_view + second_half * cos_view], axis=-1)

def attend_sequence(queries, key_rows, value_rows):
    length = queries.shape[0]
    block_size = min(512, length)
    block_count = length // block_size
    key_pos = jnp.arange(length).astype(jnp.int32)

    def one_block(packed):
        query_part, first_row = packed
        scores = jnp.einsum('qkgd,skd->kgqs', query_part, key_rows, precision=highest)
        scores = low_back(scores)
        query_pos = first_row + jnp.arange(block_size).astype(jnp.int32)
        allowed = key_pos[None, :] <= query_pos[:, None]
        scores = jnp.where(allowed[None, None], scores, masked_value)
        peak_score = lax.optimization_barrier(jnp.max(scores, axis=-1, keepdims=True))
        weights = jnp.exp(scores - peak_score)
        prob_vals = weights / lax.optimization_barrier(jnp.sum(weights, axis=-1, keepdims=True))
        return jnp.einsum('kgqs,skd->qkgd', low(prob_vals), value_rows, precision=highest)
    starts = (jnp.arange(block_count) * block_size).astype(jnp.int32)
    blocks = queries.reshape((block_count, block_size) + queries.shape[1:])
    attended = lax.map(jax.checkpoint(one_block), (blocks, starts))
    return attended.reshape(queries.shape)

def expert_mix(normed, mix, expert_gate, expert_up, expert_down):
    part_count = N_COL
    part_width = expert_gate.shape[2] // part_count

    def one_expert(totals, packed):
        gate_weight, up_weight, down_weight, mix_column = packed
        expert_sum = jnp.zeros_like(normed)
        for part_index in range(part_count):
            lower = part_index * part_width
            upper = lower + part_width
            part_rows = low_back(normed)
            gate_pre = low_back(product(part_rows, gate_weight[:, lower:upper]))
            up_pre = low_back(product(part_rows, up_weight[:, lower:upper]))
            hidden = low(jax.nn.silu(gate_pre) * up_pre)
            expert_sum = expert_sum + low(product(hidden, down_weight[lower:upper, :]))
        expert_sum = low_back(expert_sum)
        return (totals + mix_column[:, None] * expert_sum, None)
    return lax.scan(jax.checkpoint(one_expert), jnp.zeros_like(normed), (expert_gate, expert_up, expert_down, mix.T))[0]

def layer(params, routes):
    inputs, w_query, w_key, w_value, w_output, gain_attn, gain_moe, w_router, shared_gate, shared_up, shared_down, expert_gate, expert_up, expert_down = params
    tokens = inputs.shape[0]
    normed_one = low(rms_norm(inputs, gain_attn))
    raw_query = low_back(product(normed_one, w_query))
    raw_key = low_back(product(normed_one, w_key))
    raw_value = low_back(product(normed_one, w_value))
    positions = jnp.arange(tokens).astype(jnp.int32) % SEQ
    cosines, sine_part = rope_tables(positions, HEAD_DIM)
    queries = low(rotate(raw_query.reshape(tokens, HEADS, HEAD_DIM), cosines, sine_part) * HEAD_DIM ** (-0.5))
    key_rows = low(rotate(raw_key.reshape(tokens, KV_HEADS, HEAD_DIM), cosines, sine_part))
    value_rows = low(raw_value.reshape(tokens, KV_HEADS, HEAD_DIM))
    group_heads = HEADS // KV_HEADS
    seq_count = tokens // SEQ
    attended = lax.map(lambda packed: attend_sequence(packed[0], packed[1], packed[2]), (queries.reshape(seq_count, SEQ, KV_HEADS, group_heads, HEAD_DIM), key_rows.reshape(seq_count, SEQ, KV_HEADS, HEAD_DIM), value_rows.reshape(seq_count, SEQ, KV_HEADS, HEAD_DIM)))
    attended = low_back(low(attended.reshape(tokens, HEADS * HEAD_DIM)))
    attn_out = low_back(product(attended, w_output))
    hidden_state = inputs + attn_out
    normed_two = low(rms_norm(hidden_state, gain_moe))
    shared_gate_pre = low_back(product(normed_two, shared_gate))
    shared_up_pre = low_back(product(normed_two, shared_up))
    shared_hidden = low(jax.nn.silu(shared_gate_pre) * shared_up_pre)
    shared_out = low_back(product(shared_hidden, shared_down))
    logits = product(normed_two, w_router)
    router_probs = jax.nn.softmax(logits, axis=-1)
    chosen = jnp.take_along_axis(router_probs, routes, axis=1)
    gate_vals = chosen / lax.optimization_barrier(jnp.sum(chosen, axis=1, keepdims=True))
    expert_count = w_router.shape[1]
    expert_ids = jnp.arange(expert_count).astype(jnp.int32)
    mix = lax.optimization_barrier(jnp.sum((routes[:, :, None] == expert_ids[None, None, :]).astype(gate_vals.dtype) * gate_vals[:, :, None], axis=1))
    moe_out = expert_mix(normed_two, mix, expert_gate, expert_up, expert_down)
    return hidden_state + moe_out + shared_out

def reference(inputs, routes, w_query, w_key, w_value, w_output, gain_attn, gain_moe, w_router, shared_gate, shared_up, shared_down, expert_gate, expert_up, expert_down, out_grad):
    params = tuple((member.astype(jnp.float32) for member in (inputs, w_query, w_key, w_value, w_output, gain_attn, gain_moe, w_router, shared_gate, shared_up, shared_down, expert_gate, expert_up, expert_down)))
    result, pullback = jax.vjp(lambda packed: layer(packed, routes), params)
    grads = pullback(out_grad.astype(jnp.float32))[0]
    return (result.astype(jnp.bfloat16), grads[0].astype(jnp.bfloat16), grads[1], grads[2], grads[3], grads[4], grads[5], grads[6], grads[7], grads[8], grads[9], grads[10], grads[11], grads[12], grads[13])
```

```python
import functools

import jax
import jax.numpy as jnp
from jax import lax
from jax.experimental import pallas as pl
from jax.experimental.pallas import tpu as pltpu
from jax.sharding import PartitionSpec as P

HEAD_DIM = 128

eps = 1e-05
theta = 500000.0
highest = lax.Precision.HIGHEST
masked_value = -1e30
f32 = jnp.float32
bf16 = jnp.bfloat16
vmem_limit = 56 * 2**20
cheap = 2**14


def swap(x, axis, step):
    return lax.ppermute(x, axis, [(i, i ^ step) for i in range(lax.axis_size(axis))])


def exchange(x, axis):
    return [x] + [swap(x, axis, step) for step in range(1, lax.axis_size(axis))]


def reduce_parts(parts, axis):
    total = parts[0].astype(f32)
    for step in range(1, len(parts)):
        total = total + swap(parts[step], axis, step).astype(f32)
    return total


def all_sum(x, axis):
    step = 1
    while step < lax.axis_size(axis):
        x = x + swap(x, axis, step)
        step *= 2
    return x


def zero_of(*arrays):
    found = jnp.int32(0)
    for x in arrays:
        first = x[(slice(0, 1),) * x.ndim].reshape(())
        found = found + (first != first).astype(jnp.int32)
    return found


def after(x, earlier):
    place = pl.BlockSpec(memory_space=pl.ANY)
    return pl.pallas_call(
        lambda *refs: None,
        out_shape=jax.ShapeDtypeStruct(x.shape, x.dtype),
        in_specs=[place, place],
        out_specs=place,
        input_output_aliases={0: 0},
    )(x, earlier)


def ring_order(n):
    return [0] + list(range(1, n, 2)) + [i for i in range(n - 1, 0, -1) if i % 2 == 0]


def ring_pairs(n, back=False):
    order = ring_order(n)
    pairs = [(order[i], order[(i + 1) % n]) for i in range(n)]
    return [(b, a) for a, b in pairs] if back else pairs


def ring_sources(axis):
    n = lax.axis_size(axis)
    order = ring_order(n)
    place = jnp.array([order.index(i) for i in range(n)])[lax.axis_index(axis)]
    return jnp.array(order)[(place - jnp.arange(n)) % n]


def ring_gather(x, axis):
    parts, n = [x], lax.axis_size(axis)
    for _ in range(n - 1):
        parts.append(lax.ppermute(parts[-1], axis, ring_pairs(n)))
    return parts


def ring_reduce(parts, axis):
    n = len(parts)
    order = ring_order(n)
    total = parts[0].astype(f32)
    for k in range(1, n):
        pairs = [(order[i], order[(i - k) % n]) for i in range(n)]
        total = total + lax.ppermute(parts[k], axis, pairs).astype(f32)
    return total


def row_gather(x):
    if lax.axis_size("row") != 4:
        return exchange(x, "row")
    x_near, y_near = swap(x, "row", 1), swap(x, "row", 2)
    middle = x.shape[0] // 2
    return [x, x_near, y_near, swap(y_near[:middle], "row", 1), swap(x_near[middle:], "row", 2)]


def add(left, right):
    return left.astype(f32) + right.astype(f32)


def row_reduce(blocks):
    if len(blocks) != 4:
        return reduce_parts(blocks, "row")
    own, x_near, y_near, far = blocks
    middle = own.shape[0] // 2
    far_x, far_y = swap(far[:middle], "row", 1), swap(far[middle:], "row", 2)
    y_first = add(y_near[:middle], far_x).astype(bf16)
    x_second = add(x_near[middle:], far_y).astype(bf16)
    y_sum = swap(jnp.concatenate([y_first, y_near[middle:]], axis=0), "row", 2)
    x_sum = swap(jnp.concatenate([x_near[:middle], x_second], axis=0), "row", 1)
    return add(own, x_sum) + y_sum.astype(f32)


def tokens_home(x, wait):
    c, n = lax.axis_index("col"), lax.axis_size("col")
    rows, width = x.shape[0] // n, x.shape[1]
    whole = jnp.zeros((rows, n * width), x.dtype)
    for s in range(n):
        piece = lax.dynamic_slice_in_dim(x, (c ^ s) * rows + wait, rows, 0)
        piece = swap(piece, "col", s) if s else piece
        whole = lax.dynamic_update_slice(whole, piece, (0, (c ^ s) * width))
    return whole


def tokens_back(x):
    c, n = lax.axis_index("col"), lax.axis_size("col")
    rows, width = x.shape[0], x.shape[1] // n
    whole = jnp.zeros((n * rows, width), x.dtype)
    for s in range(n):
        piece = lax.dynamic_slice_in_dim(x, (c ^ s) * width, width, 1)
        piece = swap(piece, "col", s) if s else piece
        whole = lax.dynamic_update_slice(whole, piece, ((c ^ s) * rows, 0))
    return whole


def own_share(weight, wait=0):
    share = weight.shape[0] // lax.axis_size("exp")
    return lax.dynamic_slice_in_dim(weight, lax.axis_index("exp") * share + wait, share, 0)


def all_shares(total):
    e = lax.axis_index("exp")
    shares = lax.axis_size("exp")
    whole = jnp.zeros((shares,) + total.shape, total.dtype)
    for t, piece in enumerate(exchange(total, "exp")):
        whole = lax.dynamic_update_index_in_dim(whole, piece, e ^ t, 0)
    return whole.reshape((shares * total.shape[0],) + total.shape[1:])


def reduce_weight(grad):
    total = lax.psum_scatter(grad, ("col", "exp"), scatter_dimension=0, tiled=True)
    return all_shares(total).astype(f32)


def rope_tables(positions, head_width):
    half_width = head_width // 2
    frequency = theta ** (-2.0 * jnp.arange(half_width, dtype=f32) / head_width)
    angles = positions.astype(f32)[:, None] * frequency[None, :]
    return (jnp.cos(angles), jnp.sin(angles))


def rotate(source, cosines, sines):
    half_width = source.shape[-1] // 2
    first, second = source[..., :half_width], source[..., half_width:]
    cos_view, sin_view = cosines[:, None, :], sines[:, None, :]
    return jnp.concatenate(
        [first * cos_view - second * sin_view, first * sin_view + second * cos_view], axis=-1
    )


def dot(left, right, contract=(1, 0)):
    return lax.dot_general(
        left, right, (((contract[0],), (contract[1],)), ((), ())), preferred_element_type=f32
    )


def batch_dot(spec, left, right):
    return jnp.einsum(spec, left, right, preferred_element_type=f32)


def rms_inverse(values):
    return lax.rsqrt(jnp.mean(values * values, axis=1, keepdims=True) + eps)


def rms_backward(values, inv_rms, gain, grad_norm):
    scaled_grad = grad_norm * gain[None, :]
    inner = jnp.mean(scaled_grad * values, axis=1, keepdims=True)
    grad_values = inv_rms * (scaled_grad - values * (inv_rms * inv_rms * inner))
    return grad_values, jnp.sum(grad_norm * values * inv_rms, axis=0)


def place_keys(place, kv_refs, key_buf, value_buf, chunk):
    row, blocks, width = place[0], kv_refs[0].shape[0] // chunk, key_buf.shape[1]
    for k, ref in enumerate(kv_refs):
        for s in range(blocks):
            at = pl.multiple_of(((row ^ s) * len(kv_refs) + place[2 + k]) * chunk, chunk)
            key_buf[pl.ds(at, chunk), :] = ref[s * chunk : (s + 1) * chunk, :width]
            value_buf[pl.ds(at, chunk), :] = ref[s * chunk : (s + 1) * chunk, width:]


def head_rows(ref, rows, width):
    block = ref[rows, :]
    return jnp.concatenate(
        [block[:, h * width : (h + 1) * width] for h in range(block.shape[1] // width)], axis=0
    )


def scores_tile(place, key_tile, queries, block, tile, chunk):
    scores = dot(key_tile, queries, (1, 1))
    key_at = tile * key_tile.shape[0] + lax.broadcasted_iota(jnp.int32, scores.shape, 0)
    lane = lax.broadcasted_iota(jnp.int32, scores.shape, 1)
    query_at = block * key_tile.shape[0] + place[1] * chunk + lane % chunk
    return jnp.where(key_at <= query_at, scores, masked_value)


def attention_kernel(chunk, place, q_ref, *refs):
    kv_refs, (out_ref, total_ref, lse_ref, key_buf, value_buf) = refs[:-5], refs[-5:]
    width = key_buf.shape[1]
    blocks = q_ref.shape[0] // chunk
    tile_rows = key_buf.shape[0] // blocks
    place_keys(place, kv_refs, key_buf, value_buf, chunk)

    @pl.loop(0, blocks)
    def _(block):
        rows = pl.ds(pl.multiple_of((place[0] ^ block) * chunk, chunk), chunk)
        queries = head_rows(q_ref, rows, width)
        count = queries.shape[0]

        def step(tile, carry):
            peak, total, out = carry
            at = pl.ds(pl.multiple_of(tile * tile_rows, tile_rows), tile_rows)
            scores = scores_tile(place, key_buf[at, :], queries, block, tile, chunk)
            new_peak = jnp.maximum(peak, jnp.max(scores, axis=0, keepdims=True))
            weights = jnp.exp(scores - new_peak)
            shrink = jnp.exp(peak - new_peak)
            total = total * shrink + jnp.sum(weights, axis=0, keepdims=True)
            part = dot(value_buf[at, :], weights.astype(bf16), (0, 0))
            return new_peak, total, out * shrink + part

        start = (
            jnp.full((1, count), masked_value, f32),
            jnp.zeros((1, count), f32),
            jnp.zeros((width, count), f32),
        )
        peak, total, out = lax.fori_loop(0, block + 1, step, start)
        out = out / total
        total_ref[pl.ds(block, 1)] = out[None]
        lse_ref[pl.ds(block, 1)] = (peak + jnp.log(total))[None]
        for h in range(count // chunk):
            head = out[:, h * chunk : (h + 1) * chunk]
            out_ref[rows, h * width : (h + 1) * width] = head.T.astype(bf16)


def attention_back_kernel(chunk, place, q_ref, grad_ref, total_ref, lse_ref, *refs):
    kv_refs = refs[:-6]
    dq_ref, dkv_ref, key_buf, value_buf, dk_buf, dv_buf = refs[-6:]
    width = key_buf.shape[1]
    blocks = q_ref.shape[0] // chunk
    tile_rows = key_buf.shape[0] // blocks
    place_keys(place, kv_refs, key_buf, value_buf, chunk)
    dk_buf[...] = jnp.zeros_like(dk_buf)
    dv_buf[...] = jnp.zeros_like(dv_buf)

    @pl.loop(0, blocks)
    def _(block):
        rows = pl.ds(pl.multiple_of((place[0] ^ block) * chunk, chunk), chunk)
        queries = head_rows(q_ref, rows, width)
        grads = head_rows(grad_ref, rows, width)
        count = queries.shape[0]
        out = total_ref[pl.ds(block, 1)][0]
        lse = lse_ref[pl.ds(block, 1)][0]
        grads_t = jnp.concatenate(
            [grads[h * chunk : (h + 1) * chunk].astype(f32).T for h in range(count // chunk)], axis=1
        )
        inner = jnp.sum(out * grads_t, axis=0, keepdims=True)

        def step(tile, d_queries):
            at = pl.ds(pl.multiple_of(tile * tile_rows, tile_rows), tile_rows)
            keys = key_buf[at, :]
            scores = scores_tile(place, keys, queries, block, tile, chunk)
            probs = jnp.exp(scores - lse)
            d_probs = dot(value_buf[at, :], grads, (1, 1))
            d_scores = (probs * (d_probs - inner)).astype(bf16)
            dk_buf[at, :] += dot(d_scores, queries)
            dv_buf[at, :] += dot(probs.astype(bf16), grads)
            return d_queries + dot(keys, d_scores, (0, 0))

        d_queries = lax.fori_loop(0, block + 1, step, jnp.zeros((width, count), f32))
        for h in range(count // chunk):
            head = d_queries[:, h * chunk : (h + 1) * chunk]
            dq_ref[rows, h * width : (h + 1) * width] = head.T

    for k in range(len(kv_refs)):
        for s in range(blocks):
            at = pl.ds(pl.multiple_of(((place[0] ^ s) * len(kv_refs) + place[2 + k]) * chunk, chunk), chunk)
            dkv_ref[k, s * chunk : (s + 1) * chunk, :width] = dk_buf[at, :].astype(bf16)
            dkv_ref[k, s * chunk : (s + 1) * chunk, width:] = dv_buf[at, :].astype(bf16)


def whole_spec(shape):
    return pl.BlockSpec(shape, lambda *_: (0,) * len(shape))


def side_by_side(left, right, wait):
    count, rows, width = left.shape
    tile = 512

    def kernel(wait_ref, left_ref, right_ref, both_ref):
        both_ref[:, :width] = left_ref[...]
        both_ref[:, width:] = right_ref[...]

    spec = pl.BlockSpec((None, tile, width), lambda i, j, _: (i, j, 0))
    return pl.pallas_call(
        kernel,
        out_shape=jax.ShapeDtypeStruct((count, rows, 2 * width), left.dtype),
        grid_spec=pltpu.PrefetchScalarGridSpec(
            num_scalar_prefetch=1,
            grid=(count, rows // tile),
            in_specs=[spec, spec],
            out_specs=pl.BlockSpec((None, tile, 2 * width), lambda i, j, _: (i, j, 0)),
        ),
        cost_estimate=pl.CostEstimate(flops=0, bytes_accessed=4 * left.nbytes, transcendentals=0),
    )(wait.reshape(1), left, right)


def attention_call(kernel, place, operands, outs, scratch, work):
    return pl.pallas_call(
        kernel,
        out_shape=outs,
        grid_spec=pltpu.PrefetchScalarGridSpec(
            num_scalar_prefetch=1,
            grid=(1,),
            in_specs=[whole_spec(x.shape) for x in operands],
            out_specs=[whole_spec(x.shape) for x in outs],
            scratch_shapes=scratch,
        ),
        compiler_params=pltpu.CompilerParams(vmem_limit_bytes=vmem_limit),
        cost_estimate=pl.CostEstimate(
            flops=work // cheap, bytes_accessed=2**10, transcendentals=0
        ),
    )(place, *operands)


def attention_forward(place, queries, kv_parts, chunk):
    rows, total_width = queries.shape
    width = kv_parts[0].shape[1] // 2
    heads, blocks, keys = total_width // width, rows // chunk, rows * len(kv_parts)
    return attention_call(
        functools.partial(attention_kernel, chunk),
        place,
        (queries, *kv_parts),
        (
            jax.ShapeDtypeStruct((rows, total_width), bf16),
            jax.ShapeDtypeStruct((blocks, width, heads * chunk), f32),
            jax.ShapeDtypeStruct((blocks, 1, heads * chunk), f32),
        ),
        [pltpu.VMEM((keys, width), bf16)] * 2,
        4 * rows * heads * keys * width,
    )


def attention_backward(place, queries, grads, out, lse, kv_parts, chunk):
    rows, total_width = queries.shape
    width = kv_parts[0].shape[1] // 2
    keys = rows * len(kv_parts)
    return attention_call(
        functools.partial(attention_back_kernel, chunk),
        place,
        (queries, grads, out, lse, *kv_parts),
        (
            jax.ShapeDtypeStruct((rows, total_width), f32),
            jax.ShapeDtypeStruct((len(kv_parts), rows, 2 * width), bf16),
        ),
        [pltpu.VMEM((keys, width), bf16)] * 2 + [pltpu.VMEM((keys, width), f32)] * 2,
        10 * rows * total_width * keys,
    )


def silu_back(gate_pre, up_pre, grad_hidden):
    sigmoid_vals = jax.nn.sigmoid(gate_pre)
    silu = gate_pre * sigmoid_vals
    grad_gate = grad_hidden * up_pre * sigmoid_vals * (1.0 + gate_pre * (1.0 - sigmoid_vals))
    return silu * up_pre, grad_gate.astype(bf16), (grad_hidden * silu).astype(bf16)


def experts_kernel(counts, held, local, tiles, chunks, info, *refs):
    groups = len(counts)
    x_refs, refs = refs[: sum(counts)], refs[sum(counts) :]
    mix_refs, refs = refs[: sum(counts)], refs[sum(counts) :]
    g_refs, refs = refs[:groups], refs[groups:]
    refs = refs[:6] + refs[6 + held :]
    (
        slot_ref, slot_t_ref, w_in, w_down, s_in, s_down,
        xs_ref, gs_ref, hidden_ref, pre_ref, own_x_ref, own_g_ref, s_hidden_ref, s_pre_ref,
    ), refs = refs[:14], refs[14:]
    out_refs, refs = refs[:groups], refs[groups:]
    norm_refs, refs = refs[:groups], refs[groups:]
    pick, put, acc_in, acc_down, s_acc_in, s_acc_down, term_buf = refs
    step = pl.program_id(0)
    capacity, tokens = pick.shape[1], pick.shape[2]
    width, s_width = w_down.shape[1], s_down.shape[0]

    @pl.when(step == 0)
    def _():
        for at in range(groups * local):
            slots = lax.broadcasted_iota(jnp.int32, (capacity, tokens), 0)
            pick[at] = jnp.where(slots == slot_ref[at : at + 1, :], 1.0, 0.0).astype(bf16)
            slots = lax.broadcasted_iota(jnp.int32, (tokens, capacity), 1)
            put[at // local, :, (at % local) * capacity : (at % local + 1) * capacity] = jnp.where(
                slots == slot_t_ref[:, at : at + 1], 1.0, 0.0
            ).astype(bf16)
        acc_in[...] = jnp.zeros_like(acc_in)
        acc_down[...] = jnp.zeros_like(acc_down)
        s_acc_in[...] = jnp.zeros_like(s_acc_in)
        s_acc_down[...] = jnp.zeros_like(s_acc_down)

    @pl.when(step < tiles)
    def _():
        for t in range(groups):
            parts = slice(sum(counts[:t]), sum(counts[: t + 1]))
            x = jnp.concatenate([ref[...] for ref in x_refs[parts]], axis=0)
            chunk = tokens // chunks
            g = jnp.concatenate(
                [
                    g_refs[t][pl.ds(pl.multiple_of(info[groups + k] * chunk, chunk), chunk), :]
                    for k in range(chunks)
                ],
                axis=0,
            )
            for l in range(local):
                rows = slice(t * capacity, (t + 1) * capacity)
                xs_ref[l, rows, :] = dot(pick[t * local + l], x).astype(bf16)
                gs_ref[l, rows, :] = dot(pick[t * local + l], g).astype(bf16)
            if t == 0:
                own_x_ref[...] = x
                own_g_ref[...] = g
                s_acc_in[...] += dot(x, s_in[...])
                s_acc_down[...] += dot(g, s_down[...], (1, 1))
        for l in range(local):
            acc_in[l] += dot(xs_ref[l], w_in[l])
            acc_down[l] += dot(gs_ref[l], w_down[l], (1, 1))

    @pl.when(step == tiles - 1)
    def _():
        mixes = [
            jnp.concatenate([ref[...] for ref in mix_refs[sum(counts[:t]) : sum(counts[: t + 1])]], axis=0)
            for t in range(groups)
        ]
        lanes = mixes[0].shape[1]
        lane = lax.broadcasted_iota(jnp.int32, (1, lanes), 1)
        spread = []
        for l in range(local):
            expert = info[groups + chunks] + l
            weights = jnp.concatenate([dot(pick[t * local + l], mixes[t]) for t in range(groups)], axis=0)
            weights = jnp.sum(
                jnp.where(lane % (lanes // 2) == expert, weights, 0.0), axis=1, keepdims=True
            )
            grad = acc_down[l]
            hidden, d_gate, d_up = silu_back(acc_in[l, :, :width], acc_in[l, :, width:], grad * weights)
            terms = jnp.sum(hidden * grad, axis=1, keepdims=True)
            hidden_ref[l] = (hidden * weights).astype(bf16)
            pre_ref[l, :, :width] = d_gate
            pre_ref[l, :, width:] = d_up
            spread.append(jnp.where(lane == expert, terms, 0.0).astype(bf16))
        for t in range(groups):
            rows = slice(t * capacity, (t + 1) * capacity)
            term_buf[t] = dot(
                put[t], jnp.concatenate([terms[rows] for terms in spread], axis=0)
            ).astype(bf16)
        hidden, d_gate, d_up = silu_back(s_acc_in[:, :s_width], s_acc_in[:, s_width:], s_acc_down[...])
        s_hidden_ref[...] = hidden.astype(bf16)
        s_pre_ref[:, :s_width] = d_gate
        s_pre_ref[:, s_width:] = d_up

    @pl.when((step >= tiles) & (step < 2 * tiles))
    def _():
        pieces = [dot(hidden_ref[l], w_down[l]).astype(bf16) for l in range(local)]
        d_pieces = [dot(pre_ref[l], w_in[l], (1, 1)).astype(bf16) for l in range(local)]
        for t in range(groups):
            rows = slice(t * capacity, (t + 1) * capacity)
            out = dot(put[t], jnp.concatenate([piece[rows] for piece in pieces], axis=0))
            norm = dot(put[t], jnp.concatenate([piece[rows] for piece in d_pieces], axis=0))
            if t == 0:
                out = out + dot(s_hidden_ref[...], s_down[...])
                norm = norm + dot(s_pre_ref[...], s_in[...], (1, 1))
            out_refs[t][...] = out.astype(bf16)
            norm_refs[t][...] = norm.astype(bf16)

    @pl.when(step == 2 * tiles)
    def _():
        for t in range(groups):
            norm_refs[t][:, : term_buf.shape[2]] = term_buf[t]


def experts_call(at, blocks, held, x_parts, g_all, info, slots, w_in, w_down, s_in, s_down, capacity):
    counts = [len(parts) for parts in x_parts]
    x_parts = [x for parts in x_parts for x in parts]
    groups, local = len(counts), w_in.shape[0]
    chunks = info.shape[0] - groups - 2
    model, whole_width = g_all.shape[1], x_parts[0].shape[1]
    lanes = whole_width - model
    tokens = sum(x.shape[0] for x in x_parts[: counts[0]])
    tile = 512 if groups <= 2 else 256
    tiles = model // tile
    width, s_width = w_down.shape[1], s_down.shape[0]
    rows = groups * capacity

    def tokens_in(i, info):
        return (0, jnp.minimum(i, tiles - 1))

    def grads_in(t):
        return pl.BlockSpec((tokens, tile), lambda i, info: (info[t], jnp.minimum(i, tiles - 1)))

    def picked(i, info):
        return (0, at, jnp.minimum(i, tiles - 1))

    def own(i, info):
        return (at, jnp.minimum(i, tiles - 1))

    def summed(i, info):
        return (info[groups + chunks + 1], jnp.clip(i - tiles, 0, tiles - 1))

    def summed_norm(i, info):
        return (0, jnp.maximum(i - tiles, 0))

    in_specs = [
        *(pl.BlockSpec((x.shape[0], tile), tokens_in) for x in x_parts),
        *(pl.BlockSpec((x.shape[0], lanes), lambda i, info: (0, model // lanes)) for x in x_parts),
        *(grads_in(t) for t in range(groups)),
        whole_spec(slots.shape),
        whole_spec(slots.shape[::-1]),
        pl.BlockSpec((local, tile, 2 * width), lambda i, info: (0, i % tiles, 0)),
        pl.BlockSpec((local, width, tile), lambda i, info: (0, 0, i % tiles)),
        pl.BlockSpec((tile, 2 * s_width), lambda i, info: (i % tiles, 0)),
        pl.BlockSpec((s_width, tile), lambda i, info: (0, i % tiles)),
        *[pl.BlockSpec(memory_space=pl.ANY)] * len(held),
    ]
    kept = (
        jax.ShapeDtypeStruct((local, blocks * rows, model), bf16),
        jax.ShapeDtypeStruct((local, blocks * rows, model), bf16),
        jax.ShapeDtypeStruct((local, blocks * rows, width), bf16),
        jax.ShapeDtypeStruct((local, blocks * rows, 2 * width), bf16),
        jax.ShapeDtypeStruct((blocks * tokens, model), bf16),
        jax.ShapeDtypeStruct((blocks * tokens, model), bf16),
        jax.ShapeDtypeStruct((blocks * tokens, s_width), bf16),
        jax.ShapeDtypeStruct((blocks * tokens, 2 * s_width), bf16),
        *[jax.ShapeDtypeStruct((blocks * tokens, model), bf16)] * groups,
    )
    norms = (jax.ShapeDtypeStruct((tokens, whole_width), bf16),) * groups
    out_specs = [
        pl.BlockSpec((local, rows, tile), picked),
        pl.BlockSpec((local, rows, tile), picked),
        pl.BlockSpec((local, rows, width), lambda i, info: (0, at, 0)),
        pl.BlockSpec((local, rows, 2 * width), lambda i, info: (0, at, 0)),
        pl.BlockSpec((tokens, tile), own),
        pl.BlockSpec((tokens, tile), own),
        pl.BlockSpec((tokens, s_width), lambda i, info: (at, 0)),
        pl.BlockSpec((tokens, 2 * s_width), lambda i, info: (at, 0)),
        *[pl.BlockSpec((tokens, tile), summed)] * groups,
        *[pl.BlockSpec((tokens, tile), summed_norm)] * groups,
    ]
    work = 2 * model * (
        4 * groups * local * capacity * tokens + 6 * local * rows * width + 6 * tokens * s_width
    )
    first = 1 + len(in_specs) - len(held)
    results = pl.pallas_call(
        functools.partial(experts_kernel, counts, len(held), local, tiles, chunks),
        out_shape=(*kept, *norms),
        grid_spec=pltpu.PrefetchScalarGridSpec(
            num_scalar_prefetch=1,
            grid=(2 * tiles + 1,),
            in_specs=in_specs,
            out_specs=out_specs,
            scratch_shapes=[
                pltpu.VMEM((groups * local, capacity, tokens), bf16),
                pltpu.VMEM((groups, tokens, local * capacity), bf16),
                pltpu.VMEM((local, rows, 2 * width), f32),
                pltpu.VMEM((local, rows, width), f32),
                pltpu.VMEM((tokens, 2 * s_width), f32),
                pltpu.VMEM((tokens, s_width), f32),
                pltpu.VMEM((groups, tokens, lanes), bf16),
            ],
        ),
        input_output_aliases={first + i: i for i in range(len(held))},
        compiler_params=pltpu.CompilerParams(vmem_limit_bytes=vmem_limit),
        cost_estimate=pl.CostEstimate(flops=work // cheap, bytes_accessed=2**10, transcendentals=0),
    )(info, *x_parts, *x_parts, *[g_all] * groups, slots, slots.T, w_in, w_down, s_in, s_down, *held)
    return list(results[: len(kept)]), list(results[len(kept) :])


def shards(
    inputs,
    routes,
    w_query,
    w_key,
    w_value,
    w_output,
    gain_attn,
    gain_moe,
    w_router,
    shared_gate,
    shared_up,
    shared_down,
    expert_gate,
    expert_up,
    expert_down,
    out_grad,
):
    e, r, c = lax.axis_index("exp"), lax.axis_index("row"), lax.axis_index("col")
    E, R, C = lax.axis_size("exp"), lax.axis_size("row"), lax.axis_size("col")
    local_count, model_width, _ = expert_gate.shape
    n_experts = local_count * E * R
    block_rows, top_count = routes.shape
    capacity = 4 * block_rows * top_count // (3 * n_experts)
    home_rows = block_rows // C
    head_width = HEAD_DIM
    query_width, key_width = w_query.shape[1], w_key.shape[1]
    group_heads = query_width // key_width
    attn_scale = head_width ** (-0.5)
    sources = ring_sources("col")

    x = tokens_home(inputs, 0).astype(f32)
    small = jnp.concatenate([w_router.T, gain_attn[None], gain_moe[None]], axis=0)
    small_all = jnp.zeros((small.shape[0], model_width), f32)
    for s, part in enumerate(exchange(small, "col")):
        small_all = lax.dynamic_update_slice(small_all, part, (0, (c ^ s) * small.shape[1]))
    router_t, gain_one, gain_two = (
        small_all[:n_experts],
        small_all[n_experts],
        small_all[n_experts + 1],
    )
    inv_one = rms_inverse(x)
    norm_one = (x * inv_one * gain_one[None, :]).astype(bf16)
    norm_one_all = jnp.concatenate(row_gather(norm_one), axis=0)

    own_weights = own_share(jnp.concatenate([w_key, w_value, w_query, w_output], axis=1))
    weights = lax.all_gather(own_weights, ("col", "exp"), tiled=True)
    in_width = query_width + 2 * key_width
    weight_in = weights[:, :in_width]
    weight_out = weights[:, in_width:].reshape(C, query_width, -1)
    weight_out = weight_out.transpose(1, 0, 2).reshape(query_width, model_width)
    raw = dot(norm_one_all, weight_in)
    wait = zero_of(raw)
    g = tokens_home(out_grad, zero_of(x, small_all))
    g_all = lax.all_gather(g, ("exp", "row", "col"), tiled=True)

    s_width = shared_gate.shape[1] // C
    s_padded = -(-s_width // 128) * 128
    pad = ((0, 0), (0, s_padded - s_width))
    own_gate, own_up = own_share(shared_gate, wait), own_share(shared_up, wait)
    in_rows = own_gate.shape[0]
    down_share, feature_width = s_width // E, shared_down.shape[1]

    def col_swap(x):
        return lax.all_to_all(x, "col", split_axis=0, concat_axis=0, tiled=True)

    to_in = jnp.concatenate([own_gate, own_up], axis=1).reshape(in_rows, 2, C, s_width)
    to_in = to_in.transpose(2, 0, 1, 3).reshape(C, in_rows, 2 * s_width)
    to_down = shared_down.reshape(C, E, down_share, feature_width)
    to_down = lax.dynamic_index_in_dim(to_down, e + wait, 1, keepdims=False)
    sh_in = all_shares(col_swap(to_in)[None]).transpose(1, 0, 2, 3).reshape(model_width, 2, s_width)
    sh_in = jnp.pad(sh_in, ((0, 0), *pad)).reshape(model_width, 2 * s_padded)
    sh_down = all_shares(col_swap(to_down)[None]).transpose(0, 2, 1, 3).reshape(s_width, model_width)
    sh_down = jnp.pad(sh_down, ((0, s_padded - s_width), (0, 0)))
    expert_in = side_by_side(expert_gate, expert_up, wait)

    own_routes = lax.dynamic_slice_in_dim(routes, c * home_rows, home_rows, 0)
    routes_here = routes.reshape(C, home_rows, top_count)[sources].reshape(block_rows, top_count)
    expert_ids = jnp.arange(n_experts)
    first_expert = (e * R + r) * local_count
    own_ids = first_expert + jnp.arange(local_count)
    earlier = (jnp.arange(block_rows)[:, None] < jnp.arange(block_rows)[None, :]).astype(bf16)
    routes_t = routes_here.T
    routes_t = routes_t + wait
    named = jnp.stack(
        [
            (block[None] == own_ids[:, None, None]).any(axis=1)
            for of_row in exchange(routes_t, "row")
            for block in exchange(of_row, "exp")
        ]
    ).reshape(R, E * local_count, block_rows)
    rank = dot(named.reshape(-1, block_rows).astype(bf16), earlier).astype(jnp.int32)
    slots = jnp.where(named, rank.reshape(named.shape), -1)

    positions = (
        ((r ^ jnp.arange(R)) * block_rows + c * home_rows)[:, None]
        + jnp.arange(home_rows)[None, :]
    ).reshape(-1)
    cosines, sines = rope_tables(positions, head_width)
    own_rows = R * home_rows
    keys = rotate(raw[:, :key_width].reshape(own_rows, 1, head_width), cosines, sines)
    kv = jnp.concatenate([keys.reshape(own_rows, key_width), raw[:, key_width : 2 * key_width]], axis=1)
    kv_parts = exchange(kv.astype(bf16), "col")
    queries = rotate(
        raw[:, 2 * key_width :].reshape(own_rows, group_heads, head_width), cosines, sines
    )
    queries = (queries * attn_scale).astype(bf16).reshape(own_rows, query_width)
    place = jnp.concatenate([jnp.stack([r, c]), c ^ jnp.arange(C)]).astype(jnp.int32)
    attended, att_total, lse = attention_forward(place, queries, kv_parts, home_rows)
    attn_part = dot(attended, weight_out).astype(bf16)
    hidden_state = x + row_reduce(jnp.split(attn_part, R, axis=0))
    inv_two = rms_inverse(hidden_state) + zero_of(sh_in, sh_down).astype(f32)
    norm_two = (hidden_state * inv_two * gain_two[None, :]).astype(bf16)

    norm_float = norm_two.astype(f32)
    logits = lax.dot_general(
        norm_float, router_t, (((1,), (1,)), ((), ())), precision=highest
    )
    router_probs = jax.nn.softmax(logits, axis=-1)
    routed = (own_routes[:, :, None] == expert_ids[None, None, :]).any(axis=1)
    chosen = jnp.where(routed, router_probs, 0.0)
    chosen_sum = jnp.sum(chosen, axis=1, keepdims=True)
    mix = chosen / chosen_sum

    mix_lanes = -(-n_experts // 64) * 64
    mix_first = lax.reduce_precision(mix, 8, 7)
    mix_pad = ((0, 0), (0, mix_lanes - n_experts))
    payload = jnp.concatenate(
        [
            norm_two,
            jnp.pad(mix_first.astype(bf16), mix_pad),
            jnp.pad((mix - mix_first).astype(bf16), mix_pad),
        ],
        axis=1,
    )
    payload_rows = exchange(jnp.concatenate(ring_gather(payload, "col"), axis=0), "row")
    kept, norms, moved = [], [], []
    for s in range(R):
        x_block = payload_rows[s]
        if E > 2 and kept:
            x_block = after(x_block, kept[-1])
        waits = [payload_rows[2]] if s == 1 else [payload_rows[3]] if s == 2 else []
        if s:
            waits.append(norms[s - 1])
        if s >= 3:
            waits.append(moved[s - 3])
        info = jnp.concatenate(
            [(e ^ jnp.arange(E)) * R + (r ^ s), sources, jnp.stack([first_expert, r ^ s])]
        ).astype(jnp.int32)
        kept, norm = experts_call(
            s, R, kept, [[block] for block in exchange(x_block, "exp")], g_all, info,
            slots[s] + zero_of(*waits), expert_in, expert_down, sh_in, sh_down, capacity,
        )
        if s == R - 1:
            norm = [norm[0], *(after(x, moved[-1]) for x in norm[1:])]
        norms.append(reduce_parts(norm, "exp").astype(bf16))
        if s:
            moved.append(swap(norms[s], "row", s))
    kept, outs = kept[:8], kept[8:]
    norm_block = norms[0].astype(f32)
    for x_sum in moved:
        norm_block = norm_block + x_sum.astype(f32)
    chunks = jnp.split(norm_block.astype(bf16), C, axis=0)
    home = ring_reduce(chunks, "col")
    d_norm, gate_terms = home[:, :model_width], home[:, model_width : model_width + n_experts]
    outs = [outs[0], *(after(x, norms[-1]) for x in outs[1:])]
    out_sum = after(reduce_parts(outs, "exp").astype(bf16), moved[-1])
    out_rows = lax.psum_scatter(out_sum, "row", scatter_dimension=0, tiled=True)

    rows_x, rows_g, hidden, pre, own_x, own_g, s_hidden, s_pre = kept
    expert_width = expert_gate.shape[2]
    pre = after(pre, moved[-1])
    grad_expert_gate = batch_dot("lrd,lrf->ldf", rows_x, pre[:, :, :expert_width])
    grad_expert_up = batch_dot("lrd,lrf->ldf", rows_x, pre[:, :, expert_width:])
    inner = jnp.sum(mix * gate_terms, axis=1, keepdims=True)
    d_probs = jnp.where(routed, (gate_terms - inner) / chosen_sum, 0.0)
    d_logits = router_probs * (
        d_probs - jnp.sum(router_probs * d_probs, axis=1, keepdims=True)
    )
    d_norm = d_norm + jnp.dot(d_logits, router_t, precision=highest)
    d_norm = d_norm + zero_of(grad_expert_gate, grad_expert_up).astype(f32)
    router_part = lax.dot_general(
        d_logits, norm_float, (((0,), (0,)), ((), ())), precision=highest
    )
    d_v, gain_two_part = rms_backward(hidden_state, inv_two, gain_two, d_norm)
    d_hidden = g.astype(f32) + d_v
    d_attn = d_hidden.astype(bf16)
    d_attn_all = jnp.concatenate(row_gather(d_attn), axis=0)

    grad_expert_down = batch_dot("lrf,lrd->lfd", after(hidden, d_attn), rows_g)

    d_attended = dot(d_attn_all, weight_out, (1, 1)).astype(bf16)
    d_queries, d_kv_parts = attention_backward(
        place + zero_of(grad_expert_down), queries, d_attended, att_total, lse, kv_parts, home_rows
    )
    d_kv = reduce_parts([d_kv_parts[k] for k in range(C)], "col")
    d_query_raw = rotate(
        d_queries.reshape(own_rows, group_heads, head_width), cosines, -sines
    ) * (attn_scale + zero_of(out_rows).astype(f32))
    d_key_raw = rotate(d_kv[:, :key_width].reshape(own_rows, 1, head_width), cosines, -sines)
    d_raw = jnp.concatenate(
        [
            d_key_raw.reshape(own_rows, key_width),
            d_kv[:, key_width:],
            d_query_raw.reshape(own_rows, query_width),
        ],
        axis=1,
    ).astype(bf16)
    norm_one_part = dot(d_raw, weight_in, (1, 1)).astype(bf16)
    d_norm_one = row_reduce(jnp.split(norm_one_part, R, axis=0))
    out_rows = after(out_rows, norm_one_part)
    moe_out = ring_reduce(jnp.split(out_rows, C, axis=0), "col")
    d_x, gain_one_part = rms_backward(
        x, inv_one, gain_one + zero_of(moe_out).astype(f32), d_norm_one
    )
    grad_inputs = tokens_back((d_hidden + d_x).astype(bf16))

    output = tokens_back((hidden_state + moe_out).astype(bf16))
    grad_output = reduce_weight(
        batch_dot("sf,scd->cfd", attended, d_attn_all.reshape(own_rows, C, -1))
        .astype(bf16)
        .reshape(C * query_width, -1)
    )
    grad_in_all = reduce_weight(dot(norm_one_all, d_raw, (0, 0)).astype(bf16))

    small_part = jnp.concatenate([router_part, gain_one_part[None], gain_two_part[None]], axis=0)
    width = small.shape[1]
    mine = [
        lax.dynamic_slice_in_dim(small_part, (c ^ s) * width, width, 1) for s in range(C)
    ]
    small_sum = all_sum(all_sum(reduce_parts(mine, "col"), "row"), "exp")

    s_pre, s_hidden = after(s_pre, d_attn), after(s_hidden, d_attn)
    d_in = dot(own_x, s_pre, (0, 0)).reshape(C, E, in_rows, 2, s_padded)[..., :s_width]
    d_in = d_in.astype(bf16).reshape(C, E, in_rows, 2 * s_width)
    d_down = dot(s_hidden, own_g, (0, 0)).astype(bf16)[:s_width]
    d_down = d_down.reshape(E, down_share, C, feature_width).transpose(2, 0, 1, 3)

    def shared_back(grad):
        mine = [lax.dynamic_index_in_dim(grad, e ^ t, 1, keepdims=False) for t in range(E)]
        return all_shares(col_swap(reduce_parts(mine, "exp").astype(bf16))[None])

    grad_shared_in = shared_back(d_in).reshape(E, C, in_rows, 2, s_width)
    grad_shared_in = grad_shared_in.transpose(3, 0, 2, 1, 4).reshape(2, E * in_rows, C * s_width)
    grad_shared_gate, grad_shared_up = grad_shared_in.astype(f32)
    grad_shared_down = shared_back(d_down).transpose(1, 0, 2, 3).astype(f32)
    return (
        output,
        grad_inputs,
        grad_in_all[:, 2 * key_width :],
        grad_in_all[:, :key_width],
        grad_in_all[:, key_width : 2 * key_width],
        grad_output,
        small_sum[n_experts],
        small_sum[n_experts + 1],
        small_sum[:n_experts].T,
        grad_shared_gate,
        grad_shared_up,
        grad_shared_down.reshape(C * s_width, model_width // C),
        grad_expert_gate,
        grad_expert_up,
        grad_expert_down,
    )


def solution(mesh):
    tokens, weight, experts = P(("exp", "row"), "col"), P("col", "row"), P(("exp", "row"), None, "col")
    expert_down, feature = P(("exp", "row"), "col", None), P("col")
    placed = (
        tokens,
        P(("exp", "row"), None),
        weight,
        weight,
        weight,
        P("row", "col"),
        feature,
        feature,
        P("col", None),
        weight,
        weight,
        P("row", "col"),
        experts,
        experts,
        expert_down,
        tokens,
    )
    return jax.shard_map(
        shards,
        mesh=mesh,
        in_specs=placed,
        out_specs=(
            tokens,
            tokens,
            weight,
            weight,
            weight,
            P("row", "col"),
            feature,
            feature,
            P("col", None),
            weight,
            weight,
            P("row", "col"),
            experts,
            experts,
            expert_down,
        ),
        check_vma=False,
    )
```

```python
import functools

import jax
import jax.numpy as jnp
from jax import lax
from jax.experimental import pallas as pl
from jax.experimental.pallas import tpu as pltpu
from jax.sharding import PartitionSpec as P

HEAD_DIM = 128

eps = 1e-05
theta = 500000.0
highest = lax.Precision.HIGHEST
masked_value = -1e30
f32 = jnp.float32
bf16 = jnp.bfloat16
vmem_limit = 56 * 2**20


def swap(x, axis, step):
    return lax.ppermute(x, axis, [(i, i ^ step) for i in range(lax.axis_size(axis))])


def exchange(x, axis):
    return [x] + [swap(x, axis, step) for step in range(1, lax.axis_size(axis))]


def reduce_parts(parts, axis):
    total = parts[0].astype(f32)
    for step in range(1, len(parts)):
        total = total + swap(parts[step], axis, step).astype(f32)
    return total


def all_sum(x, axis):
    step = 1
    while step < lax.axis_size(axis):
        x = x + swap(x, axis, step)
        step *= 2
    return x


def zero_of(*arrays):
    found = jnp.int32(0)
    for x in arrays:
        first = x[(slice(0, 1),) * x.ndim].reshape(())
        found = found + (first != first).astype(jnp.int32)
    return found


def after(x, *earlier):
    place = pl.BlockSpec(memory_space=pl.ANY)
    return pl.pallas_call(
        lambda *refs: None,
        out_shape=jax.ShapeDtypeStruct(x.shape, x.dtype),
        in_specs=[place] * (1 + len(earlier)),
        out_specs=place,
        input_output_aliases={0: 0},
    )(x, *earlier)


def ring_order(n):
    return [0] + list(range(1, n, 2)) + [i for i in range(n - 1, 0, -1) if i % 2 == 0]


def ring_pairs(n, back=False):
    order = ring_order(n)
    pairs = [(order[i], order[(i + 1) % n]) for i in range(n)]
    return [(b, a) for a, b in pairs] if back else pairs


def ring_sources(axis):
    n = lax.axis_size(axis)
    order = ring_order(n)
    place = jnp.array([order.index(i) for i in range(n)])[lax.axis_index(axis)]
    return jnp.array(order)[(place - jnp.arange(n)) % n]


def ring_gather(x, axis):
    parts, n = [x], lax.axis_size(axis)
    for _ in range(n - 1):
        parts.append(lax.ppermute(parts[-1], axis, ring_pairs(n)))
    return parts


def ring_send(x, axis, k):
    order = ring_order(lax.axis_size(axis))
    n = len(order)
    return lax.ppermute(x, axis, [(order[i], order[(i - k) % n]) for i in range(n)])


def ring_reduce(parts, axis):
    total = parts[0].astype(f32)
    for k in range(1, len(parts)):
        total = total + ring_send(parts[k], axis, k).astype(f32)
    return total


def row_gather(x):
    if lax.axis_size("row") != 4:
        return exchange(x, "row")
    x_near, y_near = swap(x, "row", 1), swap(x, "row", 2)
    middle = x.shape[0] // 2
    return [x, x_near, y_near, swap(y_near[:middle], "row", 1), swap(x_near[middle:], "row", 2)]


def add(left, right):
    return left.astype(f32) + right.astype(f32)


def row_reduce(blocks):
    if len(blocks) != 4:
        return reduce_parts(blocks, "row"), blocks[:1]
    own, x_near, y_near, far = blocks
    middle = own.shape[0] // 2
    far_x, far_y = swap(far[:middle], "row", 1), swap(far[middle:], "row", 2)
    y_first = add(y_near[:middle], far_x).astype(bf16)
    x_second = add(x_near[middle:], far_y).astype(bf16)
    y_sum = swap(jnp.concatenate([y_first, y_near[middle:]], axis=0), "row", 2)
    x_sum = swap(jnp.concatenate([x_near[:middle], x_second], axis=0), "row", 1)
    return add(own, x_sum) + y_sum.astype(f32), [far_x, far_y]


def tokens_home(x, wait):
    c, n = lax.axis_index("col"), lax.axis_size("col")
    rows, width = x.shape[0] // n, x.shape[1]
    whole = jnp.zeros((rows, n * width), x.dtype)
    for s in range(n):
        piece = lax.dynamic_slice_in_dim(x, (c ^ s) * rows + wait, rows, 0)
        piece = swap(piece, "col", s) if s else piece
        whole = lax.dynamic_update_slice(whole, piece, (0, (c ^ s) * width))
    return whole


def tokens_back(x):
    c, n = lax.axis_index("col"), lax.axis_size("col")
    rows, width = x.shape[0], x.shape[1] // n
    whole = jnp.zeros((n * rows, width), x.dtype)
    for s in range(n):
        piece = lax.dynamic_slice_in_dim(x, (c ^ s) * width, width, 1)
        piece = swap(piece, "col", s) if s else piece
        whole = lax.dynamic_update_slice(whole, piece, ((c ^ s) * rows, 0))
    return whole


def own_share(weight, wait=0):
    share = weight.shape[0] // lax.axis_size("exp")
    return lax.dynamic_slice_in_dim(weight, lax.axis_index("exp") * share + wait, share, 0)


def all_shares(total):
    e = lax.axis_index("exp")
    shares = lax.axis_size("exp")
    whole = jnp.zeros((shares,) + total.shape, total.dtype)
    for t, piece in enumerate(exchange(total, "exp")):
        whole = lax.dynamic_update_index_in_dim(whole, piece, e ^ t, 0)
    return whole.reshape((shares * total.shape[0],) + total.shape[1:])


def reduce_weight(grad, late):
    total = lax.psum_scatter(grad, ("col", "exp"), scatter_dimension=0, tiled=True)
    return all_shares(after(total, late)).astype(f32)


def rope_tables(positions, head_width):
    half_width = head_width // 2
    frequency = theta ** (-2.0 * jnp.arange(half_width, dtype=f32) / head_width)
    angles = positions.astype(f32)[:, None] * frequency[None, :]
    return (jnp.cos(angles), jnp.sin(angles))


def rotate(source, cosines, sines):
    half_width = source.shape[-1] // 2
    first, second = source[..., :half_width], source[..., half_width:]
    cos_view, sin_view = cosines[:, None, :], sines[:, None, :]
    return jnp.concatenate(
        [first * cos_view - second * sin_view, first * sin_view + second * cos_view], axis=-1
    )


def dot(left, right, contract=(1, 0)):
    return lax.dot_general(
        left, right, (((contract[0],), (contract[1],)), ((), ())), preferred_element_type=f32
    )


def batch_dot(spec, left, right):
    return jnp.einsum(spec, left, right, preferred_element_type=f32)


def rms_inverse(values):
    return lax.rsqrt(jnp.mean(values * values, axis=1, keepdims=True) + eps)


def rms_backward(values, inv_rms, gain, grad_norm):
    scaled_grad = grad_norm * gain[None, :]
    inner = jnp.mean(scaled_grad * values, axis=1, keepdims=True)
    grad_values = inv_rms * (scaled_grad - values * (inv_rms * inv_rms * inner))
    return grad_values, jnp.sum(grad_norm * values * inv_rms, axis=0)


def place_keys(place, kv_refs, key_buf, value_buf, chunk):
    row, blocks, width = place[0], kv_refs[0].shape[0] // chunk, key_buf.shape[1]
    for k, ref in enumerate(kv_refs):
        for s in range(blocks):
            at = pl.multiple_of(((row ^ s) * len(kv_refs) + place[2 + k]) * chunk, chunk)
            key_buf[pl.ds(at, chunk), :] = ref[s * chunk : (s + 1) * chunk, :width]
            value_buf[pl.ds(at, chunk), :] = ref[s * chunk : (s + 1) * chunk, width:]


def head_rows(ref, rows, width):
    block = ref[rows, :]
    return jnp.concatenate(
        [block[:, h * width : (h + 1) * width] for h in range(block.shape[1] // width)], axis=0
    )


def scores_tile(place, key_tile, queries, block, tile, chunk):
    scores = dot(key_tile, queries, (1, 1))
    key_at = tile * key_tile.shape[0] + lax.broadcasted_iota(jnp.int32, scores.shape, 0)
    lane = lax.broadcasted_iota(jnp.int32, scores.shape, 1)
    query_at = block * key_tile.shape[0] + place[1] * chunk + lane % chunk
    return jnp.where(key_at <= query_at, scores, masked_value)


def attention_kernel(chunk, place, q_ref, *refs):
    kv_refs, (out_ref, total_ref, lse_ref, key_buf, value_buf) = refs[:-5], refs[-5:]
    width = key_buf.shape[1]
    blocks = q_ref.shape[0] // chunk
    tile_rows = key_buf.shape[0] // blocks
    place_keys(place, kv_refs, key_buf, value_buf, chunk)

    @pl.loop(0, blocks)
    def _(block):
        rows = pl.ds(pl.multiple_of((place[0] ^ block) * chunk, chunk), chunk)
        queries = head_rows(q_ref, rows, width)
        count = queries.shape[0]

        def step(tile, carry):
            peak, total, out = carry
            at = pl.ds(pl.multiple_of(tile * tile_rows, tile_rows), tile_rows)
            scores = scores_tile(place, key_buf[at, :], queries, block, tile, chunk)
            new_peak = jnp.maximum(peak, jnp.max(scores, axis=0, keepdims=True))
            weights = jnp.exp(scores - new_peak)
            shrink = jnp.exp(peak - new_peak)
            total = total * shrink + jnp.sum(weights, axis=0, keepdims=True)
            part = dot(value_buf[at, :], weights.astype(bf16), (0, 0))
            return new_peak, total, out * shrink + part

        start = (
            jnp.full((1, count), masked_value, f32),
            jnp.zeros((1, count), f32),
            jnp.zeros((width, count), f32),
        )
        peak, total, out = lax.fori_loop(0, block + 1, step, start)
        out = out / total
        total_ref[pl.ds(block, 1)] = out[None]
        lse_ref[pl.ds(block, 1)] = (peak + jnp.log(total))[None]
        for h in range(count // chunk):
            head = out[:, h * chunk : (h + 1) * chunk]
            out_ref[rows, h * width : (h + 1) * width] = head.T.astype(bf16)


def attention_back_kernel(chunk, place, q_ref, grad_ref, total_ref, lse_ref, *refs):
    kv_refs = refs[:-6]
    dq_ref, dkv_ref, key_buf, value_buf, dk_buf, dv_buf = refs[-6:]
    width = key_buf.shape[1]
    blocks = q_ref.shape[0] // chunk
    tile_rows = key_buf.shape[0] // blocks
    place_keys(place, kv_refs, key_buf, value_buf, chunk)
    dk_buf[...] = jnp.zeros_like(dk_buf)
    dv_buf[...] = jnp.zeros_like(dv_buf)

    @pl.loop(0, blocks)
    def _(block):
        rows = pl.ds(pl.multiple_of((place[0] ^ block) * chunk, chunk), chunk)
        queries = head_rows(q_ref, rows, width)
        grads = head_rows(grad_ref, rows, width)
        count = queries.shape[0]
        out = total_ref[pl.ds(block, 1)][0]
        lse = lse_ref[pl.ds(block, 1)][0]
        grads_t = jnp.concatenate(
            [grads[h * chunk : (h + 1) * chunk].astype(f32).T for h in range(count // chunk)], axis=1
        )
        inner = jnp.sum(out * grads_t, axis=0, keepdims=True)

        def step(tile, d_queries):
            at = pl.ds(pl.multiple_of(tile * tile_rows, tile_rows), tile_rows)
            keys = key_buf[at, :]
            scores = scores_tile(place, keys, queries, block, tile, chunk)
            probs = jnp.exp(scores - lse)
            d_probs = dot(value_buf[at, :], grads, (1, 1))
            d_scores = (probs * (d_probs - inner)).astype(bf16)
            dk_buf[at, :] += dot(d_scores, queries)
            dv_buf[at, :] += dot(probs.astype(bf16), grads)
            return d_queries + dot(keys, d_scores, (0, 0))

        d_queries = lax.fori_loop(0, block + 1, step, jnp.zeros((width, count), f32))
        for h in range(count // chunk):
            head = d_queries[:, h * chunk : (h + 1) * chunk]
            dq_ref[rows, h * width : (h + 1) * width] = head.T

    for k in range(len(kv_refs)):
        for s in range(blocks):
            at = pl.ds(pl.multiple_of(((place[0] ^ s) * len(kv_refs) + place[2 + k]) * chunk, chunk), chunk)
            dkv_ref[k, s * chunk : (s + 1) * chunk, :width] = dk_buf[at, :].astype(bf16)
            dkv_ref[k, s * chunk : (s + 1) * chunk, width:] = dv_buf[at, :].astype(bf16)


in_place = pl.BlockSpec(memory_space=pl.ANY)


def whole_spec(shape):
    return pl.BlockSpec(shape, lambda *_: (0,) * len(shape))


def side_by_side(left, right, wait):
    count, rows, width = left.shape
    tile = 512

    def kernel(left_ref, right_ref, _, both_ref):
        both_ref[:, :width] = left_ref[...]
        both_ref[:, width:] = right_ref[...]

    spec = pl.BlockSpec((None, tile, width), lambda i, j: (i, j, 0))
    return pl.pallas_call(
        kernel,
        out_shape=jax.ShapeDtypeStruct((count, rows, 2 * width), left.dtype),
        grid=(count, rows // tile),
        in_specs=[spec, spec, in_place],
        out_specs=pl.BlockSpec((None, tile, 2 * width), lambda i, j: (i, j, 0)),
        cost_estimate=pl.CostEstimate(flops=0, bytes_accessed=2**10, transcendentals=0),
    )(left, right, wait)


def rows_at(index, count):
    return pl.ds(pl.multiple_of(index * count, count), count)


def cut_call(kernel, info, operands, outs, waits=()):
    return pl.pallas_call(
        lambda info, *refs: kernel(info[0], info[1], *refs[: len(operands)], *refs[len(operands) + len(waits) :]),
        out_shape=outs,
        grid_spec=pltpu.PrefetchScalarGridSpec(
            num_scalar_prefetch=1,
            grid=(1,),
            in_specs=[whole_spec(x.shape) for x in operands] + [in_place] * len(waits),
            out_specs=[whole_spec(x.shape) for x in outs],
        ),
        compiler_params=pltpu.CompilerParams(vmem_limit_bytes=vmem_limit),
        cost_estimate=pl.CostEstimate(flops=0, bytes_accessed=2**10, transcendentals=0),
    )(info, *operands, *waits)


def join_weight(blocks, first, cols, shares):
    rows, width = blocks.shape[0] // (cols * shares), blocks.shape[1] - first

    def kernel(ref, out_ref):
        for k in range(cols):
            for t in range(shares):
                at = (k * shares + t) * rows
                out_ref[t * rows : (t + 1) * rows, k * width : (k + 1) * width] = ref[at : at + rows, first:]

    return pl.pallas_call(
        kernel,
        out_shape=jax.ShapeDtypeStruct((shares * rows, cols * width), blocks.dtype),
        compiler_params=pltpu.CompilerParams(vmem_limit_bytes=vmem_limit),
        cost_estimate=pl.CostEstimate(flops=0, bytes_accessed=2**10, transcendentals=0),
    )(blocks)


def each_index(index, count, work):
    for j in range(count):
        pl.when(index == j)(functools.partial(work, j))


def lanes_at(index, width, first, count):
    return pl.ds(pl.multiple_of(index * width + first, 128), count)


def cut_shared(info, gate, up, down, cols, shares, wait):
    rows, width, features = gate.shape[0] // shares, gate.shape[1] // cols, down.shape[1]
    both, down_rows = 2 * width, gate.shape[1] // cols // shares

    def kernel(e, c, gate_ref, up_ref, down_ref, out):
        for k in range(cols):
            at = rows_at(e, rows)
            out[c ^ k, :rows, :width] = gate_ref[at, k * width : (k + 1) * width]
            out[c ^ k, :rows, width:] = up_ref[at, k * width : (k + 1) * width]

        def cut_down(j):
            for k in range(cols):
                piece = down_ref[k * width + j * down_rows : k * width + (j + 1) * down_rows, :]
                out[c ^ k, rows : rows + down_rows, :] = piece[:, :both]
                out[c ^ k, rows + down_rows :, : features - both] = piece[:, both:]

        each_index(e, shares, cut_down)

    outs = (jax.ShapeDtypeStruct((cols, rows + 2 * down_rows, both), bf16),)
    return cut_call(kernel, info, (gate, up, down), outs, (wait,))[0]


def join_shared(info, parts, rows, features, padded):
    cols, all_rows, both = parts[0].shape
    width, shares, down_rows = both // 2, len(parts), (all_rows - rows) // 2

    def kernel(e, c, *refs):
        in_out, down_out = refs[-2:]
        in_out[...] = jnp.zeros_like(in_out)
        down_out[...] = jnp.zeros_like(down_out)
        for s in range(cols):
            for t, ref in enumerate(refs[:-2]):
                at = rows_at((c ^ s) * shares + (e ^ t), rows)
                in_out[at, :width] = ref[s, :rows, :width]
                in_out[at, padded : padded + width] = ref[s, :rows, width:]

        def join_down(j):
            for s in range(cols):
                for t, ref in enumerate(refs[:-2]):
                    at = slice((j ^ t) * down_rows, ((j ^ t) + 1) * down_rows)
                    down_out[at, lanes_at(c ^ s, features, 0, both)] = ref[s, rows : rows + down_rows, :]
                    down_out[at, lanes_at(c ^ s, features, both, features - both)] = ref[
                        s, rows + down_rows :, : features - both
                    ]

        each_index(e, shares, join_down)

    outs = (
        jax.ShapeDtypeStruct((cols * shares * rows, 2 * padded), bf16),
        jax.ShapeDtypeStruct((padded, cols * features), bf16),
    )
    return cut_call(kernel, info, parts, outs)


def cut_shared_grads(info, grad_in, grad_down, cols, shares, width):
    rows, padded = grad_in.shape[0] // (cols * shares), grad_in.shape[1] // 2
    both, down_rows, features = 2 * width, width // shares, grad_down.shape[1] // cols

    def kernel(e, c, in_ref, down_ref, *outs):
        for s in range(cols):
            for t, out in enumerate(outs):
                at = rows_at((c ^ s) * shares + (e ^ t), rows)
                out[s, :rows, :width] = in_ref[at, :width]
                out[s, :rows, width:] = in_ref[at, padded : padded + width]

        def cut_down(j):
            for s in range(cols):
                for t, out in enumerate(outs):
                    at = slice((j ^ t) * down_rows, ((j ^ t) + 1) * down_rows)
                    out[s, rows : rows + down_rows, :] = down_ref[at, lanes_at(c ^ s, features, 0, both)]
                    out[s, rows + down_rows :, : features - both] = down_ref[
                        at, lanes_at(c ^ s, features, both, features - both)
                    ]

        each_index(e, shares, cut_down)

    outs = (jax.ShapeDtypeStruct((cols, rows + 2 * down_rows, both), bf16),) * shares
    return cut_call(kernel, info, (grad_in, grad_down), outs)


def join_shared_grads(info, parts, rows, features):
    cols, all_rows, both = parts[0].shape
    width, shares, down_rows = both // 2, len(parts), (all_rows - rows) // 2

    def kernel(e, c, *refs):
        gate_out, up_out, down_out = refs[-3:]
        for k in range(cols):
            for t, ref in enumerate(refs[:-3]):
                at, part = rows_at(e ^ t, rows), ref[c ^ k, :rows, :].astype(f32)
                gate_out[at, k * width : (k + 1) * width] = part[:, :width]
                up_out[at, k * width : (k + 1) * width] = part[:, width:]

        def join_down(j):
            for k in range(cols):
                for t, ref in enumerate(refs[:-3]):
                    at = k * width + (j ^ t) * down_rows
                    at = slice(at, at + down_rows)
                    down_out[at, :both] = ref[c ^ k, rows : rows + down_rows, :].astype(f32)
                    down_out[at, both:] = ref[c ^ k, rows + down_rows :, : features - both].astype(f32)

        each_index(e, shares, join_down)

    outs = (
        *[jax.ShapeDtypeStruct((shares * rows, cols * width), f32)] * 2,
        jax.ShapeDtypeStruct((cols * width, features), f32),
    )
    return cut_call(kernel, info, parts, outs)


def attention_call(kernel, place, operands, outs, scratch, work, waits):
    return pl.pallas_call(
        lambda place, *refs: kernel(place, *refs[: len(operands)], *refs[len(operands) + len(waits) :]),
        out_shape=outs,
        grid_spec=pltpu.PrefetchScalarGridSpec(
            num_scalar_prefetch=1,
            grid=(1,),
            in_specs=[whole_spec(x.shape) for x in operands] + [in_place] * len(waits),
            out_specs=[whole_spec(x.shape) for x in outs],
            scratch_shapes=scratch,
        ),
        compiler_params=pltpu.CompilerParams(vmem_limit_bytes=vmem_limit),
        cost_estimate=pl.CostEstimate(
            flops=work, bytes_accessed=2**10, transcendentals=0
        ),
    )(place, *operands, *waits)


def attention_forward(place, queries, kv_parts, chunk, waits):
    rows, total_width = queries.shape
    width = kv_parts[0].shape[1] // 2
    heads, blocks, keys = total_width // width, rows // chunk, rows * len(kv_parts)
    return attention_call(
        functools.partial(attention_kernel, chunk),
        place,
        (queries, *kv_parts),
        (
            jax.ShapeDtypeStruct((rows, total_width), bf16),
            jax.ShapeDtypeStruct((blocks, width, heads * chunk), f32),
            jax.ShapeDtypeStruct((blocks, 1, heads * chunk), f32),
        ),
        [pltpu.VMEM((keys, width), bf16)] * 2,
        4 * rows * heads * keys * width,
        waits,
    )


def attention_backward(place, queries, grads, out, lse, kv_parts, chunk, waits):
    rows, total_width = queries.shape
    width = kv_parts[0].shape[1] // 2
    keys = rows * len(kv_parts)
    return attention_call(
        functools.partial(attention_back_kernel, chunk),
        place,
        (queries, grads, out, lse, *kv_parts),
        (
            jax.ShapeDtypeStruct((rows, total_width), f32),
            jax.ShapeDtypeStruct((len(kv_parts), rows, 2 * width), bf16),
        ),
        [pltpu.VMEM((keys, width), bf16)] * 2 + [pltpu.VMEM((keys, width), f32)] * 2,
        10 * rows * total_width * keys,
        waits,
    )


def silu_back(gate_pre, up_pre, grad_hidden):
    sigmoid_vals = jax.nn.sigmoid(gate_pre)
    silu = gate_pre * sigmoid_vals
    grad_gate = grad_hidden * up_pre * sigmoid_vals * (1.0 + gate_pre * (1.0 - sigmoid_vals))
    return silu * up_pre, grad_gate.astype(bf16), (grad_hidden * silu).astype(bf16)


def experts_kernel(counts, unused, local, tiles, chunks, info, *refs):
    groups = len(counts)
    x_refs, refs = refs[: sum(counts)], refs[sum(counts) :]
    mix_refs, refs = refs[: sum(counts)], refs[sum(counts) :]
    g_refs, refs = refs[:groups], refs[groups:]
    refs = refs[:6] + refs[6 + unused :]
    (
        slot_ref, slot_t_ref, w_in, w_down, s_in, s_down,
        xs_ref, gs_ref, hidden_ref, pre_ref, own_x_ref, own_g_ref, s_hidden_ref, s_pre_ref,
    ), refs = refs[:14], refs[14:]
    out_refs, refs = refs[:groups], refs[groups:]
    norm_refs, refs = refs[:groups], refs[groups:]
    pick, put, acc_in, acc_down, s_acc_in, s_acc_down, term_buf = refs
    step = pl.program_id(0)
    capacity, tokens = pick.shape[1], pick.shape[2]
    width, s_width = w_down.shape[1], s_down.shape[0]

    @pl.when(step == 0)
    def _():
        for at in range(groups * local):
            slots = lax.broadcasted_iota(jnp.int32, (capacity, tokens), 0)
            pick[at] = jnp.where(slots == slot_ref[at : at + 1, :], 1.0, 0.0).astype(bf16)
            slots = lax.broadcasted_iota(jnp.int32, (tokens, capacity), 1)
            put[at // local, :, (at % local) * capacity : (at % local + 1) * capacity] = jnp.where(
                slots == slot_t_ref[:, at : at + 1], 1.0, 0.0
            ).astype(bf16)
        acc_in[...] = jnp.zeros_like(acc_in)
        acc_down[...] = jnp.zeros_like(acc_down)
        s_acc_in[...] = jnp.zeros_like(s_acc_in)
        s_acc_down[...] = jnp.zeros_like(s_acc_down)

    @pl.when(step < tiles)
    def _():
        for t in range(groups):
            parts = slice(sum(counts[:t]), sum(counts[: t + 1]))
            x = jnp.concatenate([ref[...] for ref in x_refs[parts]], axis=0)
            chunk = tokens // chunks
            g = jnp.concatenate(
                [
                    g_refs[t][pl.ds(pl.multiple_of(info[groups + k] * chunk, chunk), chunk), :]
                    for k in range(chunks)
                ],
                axis=0,
            )
            for l in range(local):
                rows = slice(t * capacity, (t + 1) * capacity)
                xs_ref[l, rows, :] = dot(pick[t * local + l], x).astype(bf16)
                gs_ref[l, rows, :] = dot(pick[t * local + l], g).astype(bf16)
            if t == 0:
                own_x_ref[...] = x
                own_g_ref[...] = g
                s_acc_in[...] += dot(x, s_in[...])
                s_acc_down[...] += dot(g, s_down[...], (1, 1))
        for l in range(local):
            acc_in[l] += dot(xs_ref[l], w_in[l])
            acc_down[l] += dot(gs_ref[l], w_down[l], (1, 1))

    @pl.when(step == tiles - 1)
    def _():
        mixes = [
            jnp.concatenate([ref[...] for ref in mix_refs[sum(counts[:t]) : sum(counts[: t + 1])]], axis=0)
            for t in range(groups)
        ]
        lanes = mixes[0].shape[1]
        lane = lax.broadcasted_iota(jnp.int32, (1, lanes), 1)
        spread = []
        for l in range(local):
            expert = info[groups + chunks] + l
            weights = jnp.concatenate([dot(pick[t * local + l], mixes[t]) for t in range(groups)], axis=0)
            weights = jnp.sum(
                jnp.where(lane % (lanes // 2) == expert, weights, 0.0), axis=1, keepdims=True
            )
            grad = acc_down[l]
            hidden, d_gate, d_up = silu_back(acc_in[l, :, :width], acc_in[l, :, width:], grad * weights)
            terms = jnp.sum(hidden * grad, axis=1, keepdims=True)
            hidden_ref[l] = (hidden * weights).astype(bf16)
            pre_ref[l, :, :width] = d_gate
            pre_ref[l, :, width:] = d_up
            spread.append(jnp.where(lane == expert, terms, 0.0).astype(bf16))
        for t in range(groups):
            rows = slice(t * capacity, (t + 1) * capacity)
            term_buf[t] = dot(
                put[t], jnp.concatenate([terms[rows] for terms in spread], axis=0)
            ).astype(bf16)
        hidden, d_gate, d_up = silu_back(s_acc_in[:, :s_width], s_acc_in[:, s_width:], s_acc_down[...])
        s_hidden_ref[...] = hidden.astype(bf16)
        s_pre_ref[:, :s_width] = d_gate
        s_pre_ref[:, s_width:] = d_up

    @pl.when((step >= tiles) & (step < 2 * tiles))
    def _():
        pieces = [dot(hidden_ref[l], w_down[l]).astype(bf16) for l in range(local)]
        d_pieces = [dot(pre_ref[l], w_in[l], (1, 1)).astype(bf16) for l in range(local)]
        for t in range(groups):
            rows = slice(t * capacity, (t + 1) * capacity)
            out = dot(put[t], jnp.concatenate([piece[rows] for piece in pieces], axis=0))
            norm = dot(put[t], jnp.concatenate([piece[rows] for piece in d_pieces], axis=0))
            if t == 0:
                out = out + dot(s_hidden_ref[...], s_down[...])
                norm = norm + dot(s_pre_ref[...], s_in[...], (1, 1))
            out_refs[t][...] = out.astype(bf16)
            norm_refs[t][...] = norm.astype(bf16)

    @pl.when(step == 2 * tiles)
    def _():
        for t in range(groups):
            norm_refs[t][:, : term_buf.shape[2]] = term_buf[t]


def experts_call(at, blocks, held, x_parts, g_all, info, slots, w_in, w_down, s_in, s_down, capacity, waits):
    counts = [len(parts) for parts in x_parts]
    x_parts = [x for parts in x_parts for x in parts]
    groups, local = len(counts), w_in.shape[0]
    chunks = info.shape[0] - groups - 2
    model, whole_width = g_all.shape[1], x_parts[0].shape[1]
    lanes = whole_width - model
    tokens = sum(x.shape[0] for x in x_parts[: counts[0]])
    tile = 512 if groups <= 2 else 256
    tiles = model // tile
    width, s_width = w_down.shape[1], s_down.shape[0]
    rows = groups * capacity

    def tokens_in(i, info):
        return (0, jnp.minimum(i, tiles - 1))

    def grads_in(t):
        return pl.BlockSpec((tokens, tile), lambda i, info: (info[t], jnp.minimum(i, tiles - 1)))

    def picked(i, info):
        return (0, at, jnp.minimum(i, tiles - 1))

    def own(i, info):
        return (at, jnp.minimum(i, tiles - 1))

    def summed(i, info):
        return (info[groups + chunks + 1], jnp.clip(i - tiles, 0, tiles - 1))

    def summed_norm(i, info):
        return (0, jnp.maximum(i - tiles, 0))

    in_specs = [
        *(pl.BlockSpec((x.shape[0], tile), tokens_in) for x in x_parts),
        *(pl.BlockSpec((x.shape[0], lanes), lambda i, info: (0, model // lanes)) for x in x_parts),
        *(grads_in(t) for t in range(groups)),
        whole_spec(slots.shape),
        whole_spec(slots.shape[::-1]),
        pl.BlockSpec((local, tile, 2 * width), lambda i, info: (0, i % tiles, 0)),
        pl.BlockSpec((local, width, tile), lambda i, info: (0, 0, i % tiles)),
        pl.BlockSpec((tile, 2 * s_width), lambda i, info: (i % tiles, 0)),
        pl.BlockSpec((s_width, tile), lambda i, info: (0, i % tiles)),
        *[in_place] * (len(held) + len(waits)),
    ]
    kept = (
        jax.ShapeDtypeStruct((local, blocks * rows, model), bf16),
        jax.ShapeDtypeStruct((local, blocks * rows, model), bf16),
        jax.ShapeDtypeStruct((local, blocks * rows, width), bf16),
        jax.ShapeDtypeStruct((local, blocks * rows, 2 * width), bf16),
        jax.ShapeDtypeStruct((blocks * tokens, model), bf16),
        jax.ShapeDtypeStruct((blocks * tokens, model), bf16),
        jax.ShapeDtypeStruct((blocks * tokens, s_width), bf16),
        jax.ShapeDtypeStruct((blocks * tokens, 2 * s_width), bf16),
        *[jax.ShapeDtypeStruct((blocks * tokens, model), bf16)] * groups,
    )
    norms = (jax.ShapeDtypeStruct((tokens, whole_width), bf16),) * groups
    out_specs = [
        pl.BlockSpec((local, rows, tile), picked),
        pl.BlockSpec((local, rows, tile), picked),
        pl.BlockSpec((local, rows, width), lambda i, info: (0, at, 0)),
        pl.BlockSpec((local, rows, 2 * width), lambda i, info: (0, at, 0)),
        pl.BlockSpec((tokens, tile), own),
        pl.BlockSpec((tokens, tile), own),
        pl.BlockSpec((tokens, s_width), lambda i, info: (at, 0)),
        pl.BlockSpec((tokens, 2 * s_width), lambda i, info: (at, 0)),
        *[pl.BlockSpec((tokens, tile), summed)] * groups,
        *[pl.BlockSpec((tokens, tile), summed_norm)] * groups,
    ]
    work = 2 * model * (
        4 * groups * local * capacity * tokens + 6 * local * rows * width + 6 * tokens * s_width
    )
    first = 1 + len(in_specs) - len(held) - len(waits)
    results = pl.pallas_call(
        functools.partial(experts_kernel, counts, len(held) + len(waits), local, tiles, chunks),
        out_shape=(*kept, *norms),
        grid_spec=pltpu.PrefetchScalarGridSpec(
            num_scalar_prefetch=1,
            grid=(2 * tiles + 1,),
            in_specs=in_specs,
            out_specs=out_specs,
            scratch_shapes=[
                pltpu.VMEM((groups * local, capacity, tokens), bf16),
                pltpu.VMEM((groups, tokens, local * capacity), bf16),
                pltpu.VMEM((local, rows, 2 * width), f32),
                pltpu.VMEM((local, rows, width), f32),
                pltpu.VMEM((tokens, 2 * s_width), f32),
                pltpu.VMEM((tokens, s_width), f32),
                pltpu.VMEM((groups, tokens, lanes), bf16),
            ],
        ),
        input_output_aliases={first + i: i for i in range(len(held))},
        compiler_params=pltpu.CompilerParams(vmem_limit_bytes=vmem_limit),
        cost_estimate=pl.CostEstimate(flops=work, bytes_accessed=2**10, transcendentals=0),
    )(info, *x_parts, *x_parts, *[g_all] * groups, slots, slots.T, w_in, w_down, s_in, s_down, *held, *waits)
    return list(results[: len(kept)]), list(results[len(kept) :])


def shards(
    inputs,
    routes,
    w_query,
    w_key,
    w_value,
    w_output,
    gain_attn,
    gain_moe,
    w_router,
    shared_gate,
    shared_up,
    shared_down,
    expert_gate,
    expert_up,
    expert_down,
    out_grad,
):
    e, r, c = lax.axis_index("exp"), lax.axis_index("row"), lax.axis_index("col")
    E, R, C = lax.axis_size("exp"), lax.axis_size("row"), lax.axis_size("col")
    local_count, model_width, _ = expert_gate.shape
    n_experts = local_count * E * R
    block_rows, top_count = routes.shape
    capacity = 4 * block_rows * top_count // (3 * n_experts)
    home_rows = block_rows // C
    head_width = HEAD_DIM
    query_width, key_width = w_query.shape[1], w_key.shape[1]
    group_heads = query_width // key_width
    attn_scale = head_width ** (-0.5)
    sources = ring_sources("col")

    x = tokens_home(inputs, 0).astype(f32)
    small = jnp.concatenate([w_router.T, gain_attn[None], gain_moe[None]], axis=0)
    small_all = jnp.zeros((small.shape[0], model_width), f32)
    for s, part in enumerate(exchange(small, "col")):
        small_all = lax.dynamic_update_slice(small_all, part, (0, (c ^ s) * small.shape[1]))
    router_t, gain_one, gain_two = (
        small_all[:n_experts],
        small_all[n_experts],
        small_all[n_experts + 1],
    )
    inv_one = rms_inverse(x)
    norm_one = (x * inv_one * gain_one[None, :]).astype(bf16)
    norm_one_parts = row_gather(norm_one)
    norm_one_all = jnp.concatenate(norm_one_parts, axis=0)

    own_weights = own_share(jnp.concatenate([w_key, w_value, w_query, w_output], axis=1))
    weights = lax.all_gather(own_weights, ("col", "exp"), tiled=True)
    weight_in = weights[:, : query_width + 2 * key_width]
    g = tokens_home(out_grad, zero_of(*norm_one_parts[1:3]))
    g_all = lax.all_gather(g, ("exp", "row", "col"), tiled=True)
    raw = dot(norm_one_all, weight_in)
    wait = zero_of(raw)
    here = jnp.stack([e, c]).astype(jnp.int32)
    weight_out = join_weight(weights, query_width + 2 * key_width, C, E)

    s_width = shared_gate.shape[1] // C
    s_padded = -(-s_width // 128) * 128

    def col_swap(parts):
        return jnp.stack([swap(parts[s], "col", s) if s else parts[0] for s in range(C)])

    shared_cut = cut_shared(here, shared_gate, shared_up, shared_down, C, E, raw)
    in_rows, feature_width = shared_gate.shape[0] // E, shared_down.shape[1]
    sh_in, sh_down = join_shared(
        here, exchange(col_swap(shared_cut), "exp"), in_rows, feature_width, s_padded
    )
    expert_in = side_by_side(expert_gate, expert_up, raw)

    own_routes = lax.dynamic_slice_in_dim(routes, c * home_rows, home_rows, 0)
    routes_here = routes.reshape(C, home_rows, top_count)[sources].reshape(block_rows, top_count)
    expert_ids = jnp.arange(n_experts)
    first_expert = (e * R + r) * local_count
    own_ids = first_expert + jnp.arange(local_count)
    earlier = (jnp.arange(block_rows)[:, None] < jnp.arange(block_rows)[None, :]).astype(bf16)
    routes_t = routes_here.T
    routes_t = routes_t + wait
    named = jnp.stack(
        [
            (block[None] == own_ids[:, None, None]).any(axis=1)
            for of_row in exchange(routes_t, "row")
            for block in exchange(of_row, "exp")
        ]
    ).reshape(R, E * local_count, block_rows)
    rank = dot(named.reshape(-1, block_rows).astype(bf16), earlier).astype(jnp.int32)
    slots = jnp.where(named, rank.reshape(named.shape), -1)

    positions = (
        ((r ^ jnp.arange(R)) * block_rows + c * home_rows)[:, None]
        + jnp.arange(home_rows)[None, :]
    ).reshape(-1)
    cosines, sines = rope_tables(positions, head_width)
    own_rows = R * home_rows
    keys = rotate(raw[:, :key_width].reshape(own_rows, 1, head_width), cosines, sines)
    kv = jnp.concatenate([keys.reshape(own_rows, key_width), raw[:, key_width : 2 * key_width]], axis=1)
    kv_parts = exchange(kv.astype(bf16), "col")
    queries = rotate(
        raw[:, 2 * key_width :].reshape(own_rows, group_heads, head_width), cosines, sines
    )
    queries = (queries * attn_scale).astype(bf16).reshape(own_rows, query_width)
    place = jnp.concatenate([jnp.stack([r, c]), c ^ jnp.arange(C)]).astype(jnp.int32)
    attended, att_total, lse = attention_forward(place, queries, kv_parts, home_rows, (expert_in, shared_cut))
    attn_part = dot(attended, weight_out).astype(bf16)
    hidden_state = x + row_reduce(jnp.split(attn_part, R, axis=0))[0]
    inv_two = rms_inverse(hidden_state) + zero_of(sh_in, sh_down).astype(f32)
    norm_two = (hidden_state * inv_two * gain_two[None, :]).astype(bf16)

    norm_float = norm_two.astype(f32)
    logits = lax.dot_general(
        norm_float, router_t, (((1,), (1,)), ((), ())), precision=highest
    )
    router_probs = jax.nn.softmax(logits, axis=-1)
    routed = (own_routes[:, :, None] == expert_ids[None, None, :]).any(axis=1)
    chosen = jnp.where(routed, router_probs, 0.0)
    chosen_sum = jnp.sum(chosen, axis=1, keepdims=True)
    mix = chosen / chosen_sum

    mix_lanes = -(-n_experts // 64) * 64
    mix_first = lax.reduce_precision(mix, 8, 7)
    mix_pad = ((0, 0), (0, mix_lanes - n_experts))
    payload = jnp.concatenate(
        [
            norm_two,
            jnp.pad(mix_first.astype(bf16), mix_pad),
            jnp.pad((mix - mix_first).astype(bf16), mix_pad),
        ],
        axis=1,
    )
    payload = jnp.concatenate(ring_gather(payload, "col"), axis=0)
    payload_rows = row_gather(payload)
    if R == 4:
        payload_rows = [[x] for x in payload_rows[:3]] + [payload_rows[3:]]
    else:
        payload_rows = [[x] for x in payload_rows]
    kept, norms, moved = [], [], []
    for s in range(R):
        x_block = payload_rows[s]
        if E > 2 and kept:
            x_block = [after(x, kept[-1]) for x in x_block]
        info = jnp.concatenate(
            [(e ^ jnp.arange(E)) * R + (r ^ s), sources, jnp.stack([first_expert, r ^ s])]
        ).astype(jnp.int32)
        kept, norm = experts_call(
            s, R, kept, list(zip(*(exchange(x, "exp") for x in x_block))), g_all, info,
            slots[s], expert_in, expert_down, sh_in, sh_down, capacity, norms[-1:],
        )
        seen = moved if s == R - 1 else [x for later in ((1, 2), (3,))[s] for x in payload_rows[later]] if s < 2 else []
        if seen:
            norm = [norm[0], *(after(x, *seen) for x in norm[1:])]
        norms.append(reduce_parts(norm, "exp").astype(bf16))
        if s:
            moved.append(swap(norms[s], "row", s))
    kept, outs = kept[:8], kept[8:]
    rows_x, rows_g, hidden, pre, own_x, own_g, s_hidden, s_pre = kept

    s_pre, s_hidden = after(s_pre, norms[-1]), after(s_hidden, norms[-1])
    d_in = dot(own_x, s_pre, (0, 0)).astype(bf16)
    d_down = dot(s_hidden, own_g, (0, 0)).astype(bf16)
    shared_grads = cut_shared_grads(here, d_in, d_down, C, E, s_width)
    shared_sums = reduce_parts(shared_grads, "exp").astype(bf16)

    norm_block = norms[0].astype(f32)
    for x_sum in moved:
        norm_block = norm_block + x_sum.astype(f32)
    chunks = jnp.split(norm_block.astype(bf16), C, axis=0)
    home = ring_reduce(chunks, "col")
    d_norm, gate_terms = home[:, :model_width], home[:, model_width : model_width + n_experts]
    outs = [outs[0], *(after(x, norms[-1]) for x in outs[1:])]

    out_sum = after(reduce_parts(outs, "exp").astype(bf16), moved[-1], shared_grads[0])
    out_rows = lax.psum_scatter(out_sum, "row", scatter_dimension=0, tiled=True)

    expert_width = expert_gate.shape[2]
    pre = after(pre, moved[-1])
    grad_expert_gate = batch_dot("lrd,lrf->ldf", rows_x, pre[:, :, :expert_width])
    grad_expert_up = batch_dot("lrd,lrf->ldf", rows_x, pre[:, :, expert_width:])
    grad_expert_down = batch_dot("lrf,lrd->lfd", after(hidden, moved[-1]), rows_g)
    inner = jnp.sum(mix * gate_terms, axis=1, keepdims=True)
    d_probs = jnp.where(routed, (gate_terms - inner) / chosen_sum, 0.0)
    d_logits = router_probs * (
        d_probs - jnp.sum(router_probs * d_probs, axis=1, keepdims=True)
    )
    d_norm = d_norm + jnp.dot(d_logits, router_t, precision=highest)
    d_norm = d_norm + zero_of(grad_expert_gate, grad_expert_up, grad_expert_down).astype(f32)
    router_part = lax.dot_general(
        d_logits, norm_float, (((0,), (0,)), ((), ())), precision=highest
    )
    d_v, gain_two_part = rms_backward(hidden_state, inv_two, gain_two, d_norm)
    d_hidden = g.astype(f32) + d_v
    d_attn = d_hidden.astype(bf16)
    d_attn_all = jnp.concatenate(row_gather(d_attn), axis=0)

    out_grads = batch_dot("sf,scd->cfd", attended, d_attn_all.reshape(own_rows, C, -1))
    out_grads = out_grads.astype(bf16).reshape(C * query_width, -1)

    d_attended = dot(d_attn_all, weight_out, (1, 1)).astype(bf16)
    out_chunks = jnp.split(after(out_rows, d_attended), C, axis=0)
    moe_out = out_chunks[0].astype(f32)
    soon = [ring_send(out_chunks[k], "col", k) for k in range(1, C) if 2 * k != C]
    d_queries, d_kv_parts = attention_backward(
        place, queries, d_attended, att_total, lse, kv_parts, home_rows,
        (out_grads,),
    )
    shared_back = col_swap(after(shared_sums, d_attn))
    d_kv_parts = after(d_kv_parts, *soon, shared_back)
    d_kv = reduce_parts([d_kv_parts[k] for k in range(C)], "col")
    soon.append(ring_send(after(out_chunks[C // 2], d_kv), "col", C // 2))
    for part in soon:
        moe_out = moe_out + part.astype(f32)
    d_query_raw = rotate(
        d_queries.reshape(own_rows, group_heads, head_width), cosines, -sines
    ) * attn_scale
    d_key_raw = rotate(d_kv[:, :key_width].reshape(own_rows, 1, head_width), cosines, -sines)
    d_raw = jnp.concatenate(
        [
            d_key_raw.reshape(own_rows, key_width),
            d_kv[:, key_width:],
            d_query_raw.reshape(own_rows, query_width),
        ],
        axis=1,
    ).astype(bf16)
    norm_one_part = dot(d_raw, weight_in, (1, 1)).astype(bf16)
    d_norm_one, halfway = row_reduce(jnp.split(norm_one_part, R, axis=0))
    d_x, gain_one_part = rms_backward(x, inv_one, gain_one, d_norm_one)
    grad_inputs = tokens_back((d_hidden + d_x).astype(bf16))

    output = tokens_back((hidden_state + moe_out).astype(bf16))
    grad_output = reduce_weight(after(out_grads, d_kv), d_norm_one)
    grad_in_all = reduce_weight(
        dot(after(norm_one_all, *halfway), d_raw, (0, 0)).astype(bf16), d_norm_one
    )

    small_part = jnp.concatenate([router_part, gain_one_part[None], gain_two_part[None]], axis=0)
    width = small.shape[1]
    mine = [
        lax.dynamic_slice_in_dim(small_part, (c ^ s) * width, width, 1) for s in range(C)
    ]
    small_sum = all_sum(all_sum(reduce_parts(mine, "col"), "row"), "exp")

    grad_shared_gate, grad_shared_up, grad_shared_down = join_shared_grads(
        here, exchange(after(shared_back, d_norm_one), "exp"), in_rows, feature_width
    )
    return (
        output,
        grad_inputs,
        grad_in_all[:, 2 * key_width :],
        grad_in_all[:, :key_width],
        grad_in_all[:, key_width : 2 * key_width],
        grad_output,
        small_sum[n_experts],
        small_sum[n_experts + 1],
        small_sum[:n_experts].T,
        grad_shared_gate,
        grad_shared_up,
        grad_shared_down,
        grad_expert_gate,
        grad_expert_up,
        grad_expert_down,
    )


def solution(mesh):
    tokens, weight, experts = P(("exp", "row"), "col"), P("col", "row"), P(("exp", "row"), None, "col")
    expert_down, feature = P(("exp", "row"), "col", None), P("col")
    placed = (
        tokens,
        P(("exp", "row"), None),
        weight,
        weight,
        weight,
        P("row", "col"),
        feature,
        feature,
        P("col", None),
        weight,
        weight,
        P("row", "col"),
        experts,
        experts,
        expert_down,
        tokens,
    )
    return jax.shard_map(
        shards,
        mesh=mesh,
        in_specs=placed,
        out_specs=(
            tokens,
            tokens,
            weight,
            weight,
            weight,
            P("row", "col"),
            feature,
            feature,
            P("col", None),
            weight,
            weight,
            P("row", "col"),
            experts,
            experts,
            expert_down,
        ),
        check_vma=False,
    )
```

```python
import functools

import jax
import jax.numpy as jnp
from jax import lax
from jax.experimental import pallas as pl
from jax.experimental.pallas import tpu as pltpu
from jax.sharding import PartitionSpec as P

HEAD_DIM = 128

eps = 1e-05
theta = 500000.0
highest = lax.Precision.HIGHEST
masked_value = -1e30
f32 = jnp.float32
bf16 = jnp.bfloat16
vmem_limit = 56 * 2**20


def swap(x, axis, step):
    return lax.ppermute(x, axis, [(i, i ^ step) for i in range(lax.axis_size(axis))])


def exchange(x, axis):
    return [x] + [swap(x, axis, step) for step in range(1, lax.axis_size(axis))]


def reduce_parts(parts, axis):
    total = parts[0].astype(f32)
    for step in range(1, len(parts)):
        total = total + swap(parts[step], axis, step).astype(f32)
    return total


def all_sum(x, axis):
    step = 1
    while step < lax.axis_size(axis):
        x = x + swap(x, axis, step)
        step *= 2
    return x


def zero_of(*arrays):
    found = jnp.int32(0)
    for x in arrays:
        first = x[(slice(0, 1),) * x.ndim].reshape(())
        found = found + (first != first).astype(jnp.int32)
    return found


def after(x, *earlier):
    place = pl.BlockSpec(memory_space=pl.ANY)
    return pl.pallas_call(
        lambda *refs: None,
        out_shape=jax.ShapeDtypeStruct(x.shape, x.dtype),
        in_specs=[place] * (1 + len(earlier)),
        out_specs=place,
        input_output_aliases={0: 0},
    )(x, *earlier)


def ring_order(n):
    return [0] + list(range(1, n, 2)) + [i for i in range(n - 1, 0, -1) if i % 2 == 0]


def ring_pairs(n, back=False):
    order = ring_order(n)
    pairs = [(order[i], order[(i + 1) % n]) for i in range(n)]
    return [(b, a) for a, b in pairs] if back else pairs


def ring_sources(axis):
    n = lax.axis_size(axis)
    order = ring_order(n)
    place = jnp.array([order.index(i) for i in range(n)])[lax.axis_index(axis)]
    return jnp.array(order)[(place - jnp.arange(n)) % n]


def ring_gather(x, axis):
    parts, n = [x], lax.axis_size(axis)
    for _ in range(n - 1):
        parts.append(lax.ppermute(parts[-1], axis, ring_pairs(n)))
    return parts


def ring_send(x, axis, k):
    order = ring_order(lax.axis_size(axis))
    n = len(order)
    return lax.ppermute(x, axis, [(order[i], order[(i - k) % n]) for i in range(n)])


def ring_reduce(parts, axis):
    total = parts[0].astype(f32)
    for k in range(1, len(parts)):
        total = total + ring_send(parts[k], axis, k).astype(f32)
    return total


def row_gather(x):
    if lax.axis_size("row") != 4:
        return exchange(x, "row")
    x_near, y_near = swap(x, "row", 1), swap(x, "row", 2)
    middle = x.shape[0] // 2
    return [x, x_near, y_near, swap(y_near[:middle], "row", 1), swap(x_near[middle:], "row", 2)]


def add(left, right):
    return left.astype(f32) + right.astype(f32)


def row_reduce(blocks):
    if len(blocks) != 4:
        return reduce_parts(blocks, "row"), blocks[:1]
    own, x_near, y_near, far = blocks
    middle = own.shape[0] // 2
    far_x, far_y = swap(far[:middle], "row", 1), swap(far[middle:], "row", 2)
    y_first = add(y_near[:middle], far_x).astype(bf16)
    x_second = add(x_near[middle:], far_y).astype(bf16)
    y_sum = swap(jnp.concatenate([y_first, y_near[middle:]], axis=0), "row", 2)
    x_sum = swap(jnp.concatenate([x_near[:middle], x_second], axis=0), "row", 1)
    return add(own, x_sum) + y_sum.astype(f32), [far_x, far_y]


def tokens_home(x, wait):
    c, n = lax.axis_index("col"), lax.axis_size("col")
    rows, width = x.shape[0] // n, x.shape[1]
    whole = jnp.zeros((rows, n * width), x.dtype)
    for s in range(n):
        piece = lax.dynamic_slice_in_dim(x, (c ^ s) * rows + wait, rows, 0)
        piece = swap(piece, "col", s) if s else piece
        whole = lax.dynamic_update_slice(whole, piece, (0, (c ^ s) * width))
    return whole


def tokens_back(x):
    c, n = lax.axis_index("col"), lax.axis_size("col")
    rows, width = x.shape[0], x.shape[1] // n
    whole = jnp.zeros((n * rows, width), x.dtype)
    for s in range(n):
        piece = lax.dynamic_slice_in_dim(x, (c ^ s) * width, width, 1)
        piece = swap(piece, "col", s) if s else piece
        whole = lax.dynamic_update_slice(whole, piece, ((c ^ s) * rows, 0))
    return whole


def own_share(weight, wait=0):
    share = weight.shape[0] // lax.axis_size("exp")
    return lax.dynamic_slice_in_dim(weight, lax.axis_index("exp") * share + wait, share, 0)


def all_shares(total):
    e = lax.axis_index("exp")
    shares = lax.axis_size("exp")
    whole = jnp.zeros((shares,) + total.shape, total.dtype)
    for t, piece in enumerate(exchange(total, "exp")):
        whole = lax.dynamic_update_index_in_dim(whole, piece, e ^ t, 0)
    return whole.reshape((shares * total.shape[0],) + total.shape[1:])


def reduce_weight(grad):
    return lax.psum_scatter(grad, ("col", "exp"), scatter_dimension=0, tiled=True)


def rope_tables(positions, head_width):
    half_width = head_width // 2
    frequency = theta ** (-2.0 * jnp.arange(half_width, dtype=f32) / head_width)
    angles = positions.astype(f32)[:, None] * frequency[None, :]
    return (jnp.cos(angles), jnp.sin(angles))


def rotate(source, cosines, sines):
    half_width = source.shape[-1] // 2
    first, second = source[..., :half_width], source[..., half_width:]
    cos_view, sin_view = cosines[:, None, :], sines[:, None, :]
    return jnp.concatenate(
        [first * cos_view - second * sin_view, first * sin_view + second * cos_view], axis=-1
    )


def dot(left, right, contract=(1, 0)):
    return lax.dot_general(
        left, right, (((contract[0],), (contract[1],)), ((), ())), preferred_element_type=f32
    )


def batch_dot(spec, left, right):
    return jnp.einsum(spec, left, right, preferred_element_type=f32)


def rms_inverse(values):
    return lax.rsqrt(jnp.mean(values * values, axis=1, keepdims=True) + eps)


def rms_backward(values, inv_rms, gain, grad_norm):
    scaled_grad = grad_norm * gain[None, :]
    inner = jnp.mean(scaled_grad * values, axis=1, keepdims=True)
    grad_values = inv_rms * (scaled_grad - values * (inv_rms * inv_rms * inner))
    return grad_values, jnp.sum(grad_norm * values * inv_rms, axis=0)


def place_keys(place, kv_refs, key_buf, value_buf, chunk):
    row, blocks, width = place[0], kv_refs[0].shape[0] // chunk, key_buf.shape[1]
    for k, ref in enumerate(kv_refs):
        for s in range(blocks):
            at = pl.multiple_of(((row ^ s) * len(kv_refs) + place[2 + k]) * chunk, chunk)
            key_buf[pl.ds(at, chunk), :] = ref[s * chunk : (s + 1) * chunk, :width]
            value_buf[pl.ds(at, chunk), :] = ref[s * chunk : (s + 1) * chunk, width:]


def head_rows(ref, rows, width):
    block = ref[rows, :]
    return jnp.concatenate(
        [block[:, h * width : (h + 1) * width] for h in range(block.shape[1] // width)], axis=0
    )


def scores_tile(place, key_tile, queries, block, tile, chunk):
    scores = dot(key_tile, queries, (1, 1))
    key_at = tile * key_tile.shape[0] + lax.broadcasted_iota(jnp.int32, scores.shape, 0)
    lane = lax.broadcasted_iota(jnp.int32, scores.shape, 1)
    query_at = block * key_tile.shape[0] + place[1] * chunk + lane % chunk
    return jnp.where(key_at <= query_at, scores, masked_value)


def attention_kernel(chunk, place, q_ref, *refs):
    kv_refs, (out_ref, total_ref, lse_ref, key_buf, value_buf) = refs[:-5], refs[-5:]
    width = key_buf.shape[1]
    blocks = q_ref.shape[0] // chunk
    tile_rows = key_buf.shape[0] // blocks
    place_keys(place, kv_refs, key_buf, value_buf, chunk)

    @pl.loop(0, blocks)
    def _(block):
        rows = pl.ds(pl.multiple_of((place[0] ^ block) * chunk, chunk), chunk)
        queries = head_rows(q_ref, rows, width)
        count = queries.shape[0]

        def step(tile, carry):
            peak, total, out = carry
            at = pl.ds(pl.multiple_of(tile * tile_rows, tile_rows), tile_rows)
            scores = scores_tile(place, key_buf[at, :], queries, block, tile, chunk)
            new_peak = jnp.maximum(peak, jnp.max(scores, axis=0, keepdims=True))
            weights = jnp.exp(scores - new_peak)
            shrink = jnp.exp(peak - new_peak)
            total = total * shrink + jnp.sum(weights, axis=0, keepdims=True)
            part = dot(value_buf[at, :], weights.astype(bf16), (0, 0))
            return new_peak, total, out * shrink + part

        start = (
            jnp.full((1, count), masked_value, f32),
            jnp.zeros((1, count), f32),
            jnp.zeros((width, count), f32),
        )
        peak, total, out = lax.fori_loop(0, block + 1, step, start)
        out = out / total
        total_ref[pl.ds(block, 1)] = out[None]
        lse_ref[pl.ds(block, 1)] = (peak + jnp.log(total))[None]
        for h in range(count // chunk):
            head = out[:, h * chunk : (h + 1) * chunk]
            out_ref[rows, h * width : (h + 1) * width] = head.T.astype(bf16)


def attention_back_kernel(chunk, place, q_ref, grad_ref, total_ref, lse_ref, *refs):
    kv_refs = refs[:-6]
    dq_ref, dkv_ref, key_buf, value_buf, dk_buf, dv_buf = refs[-6:]
    width = key_buf.shape[1]
    blocks = q_ref.shape[0] // chunk
    tile_rows = key_buf.shape[0] // blocks
    place_keys(place, kv_refs, key_buf, value_buf, chunk)
    dk_buf[...] = jnp.zeros_like(dk_buf)
    dv_buf[...] = jnp.zeros_like(dv_buf)

    @pl.loop(0, blocks)
    def _(block):
        rows = pl.ds(pl.multiple_of((place[0] ^ block) * chunk, chunk), chunk)
        queries = head_rows(q_ref, rows, width)
        grads = head_rows(grad_ref, rows, width)
        count = queries.shape[0]
        out = total_ref[pl.ds(block, 1)][0]
        lse = lse_ref[pl.ds(block, 1)][0]
        grads_t = jnp.concatenate(
            [grads[h * chunk : (h + 1) * chunk].astype(f32).T for h in range(count // chunk)], axis=1
        )
        inner = jnp.sum(out * grads_t, axis=0, keepdims=True)

        def step(tile, d_queries):
            at = pl.ds(pl.multiple_of(tile * tile_rows, tile_rows), tile_rows)
            keys = key_buf[at, :]
            scores = scores_tile(place, keys, queries, block, tile, chunk)
            probs = jnp.exp(scores - lse)
            d_probs = dot(value_buf[at, :], grads, (1, 1))
            d_scores = (probs * (d_probs - inner)).astype(bf16)
            dk_buf[at, :] += dot(d_scores, queries)
            dv_buf[at, :] += dot(probs.astype(bf16), grads)
            return d_queries + dot(keys, d_scores, (0, 0))

        d_queries = lax.fori_loop(0, block + 1, step, jnp.zeros((width, count), f32))
        for h in range(count // chunk):
            head = d_queries[:, h * chunk : (h + 1) * chunk]
            dq_ref[rows, h * width : (h + 1) * width] = head.T

    for k in range(len(kv_refs)):
        for s in range(blocks):
            at = pl.ds(pl.multiple_of(((place[0] ^ s) * len(kv_refs) + place[2 + k]) * chunk, chunk), chunk)
            dkv_ref[k, s * chunk : (s + 1) * chunk, :width] = dk_buf[at, :].astype(bf16)
            dkv_ref[k, s * chunk : (s + 1) * chunk, width:] = dv_buf[at, :].astype(bf16)


in_place = pl.BlockSpec(memory_space=pl.ANY)


def whole_spec(shape):
    return pl.BlockSpec(shape, lambda *_: (0,) * len(shape))


def side_by_side(left, right, wait):
    count, rows, width = left.shape
    tile = 512

    def kernel(left_ref, right_ref, _, both_ref):
        both_ref[:, :width] = left_ref[...]
        both_ref[:, width:] = right_ref[...]

    spec = pl.BlockSpec((None, tile, width), lambda i, j: (i, j, 0))
    return pl.pallas_call(
        kernel,
        out_shape=jax.ShapeDtypeStruct((count, rows, 2 * width), left.dtype),
        grid=(count, rows // tile),
        in_specs=[spec, spec, in_place],
        out_specs=pl.BlockSpec((None, tile, 2 * width), lambda i, j: (i, j, 0)),
        cost_estimate=pl.CostEstimate(flops=0, bytes_accessed=2**10, transcendentals=0),
    )(left, right, wait)


def rows_at(index, count):
    return pl.ds(pl.multiple_of(index * count, count), count)


def cut_call(kernel, info, operands, outs, waits=()):
    return pl.pallas_call(
        lambda info, *refs: kernel(info[0], info[1], *refs[: len(operands)], *refs[len(operands) + len(waits) :]),
        out_shape=outs,
        grid_spec=pltpu.PrefetchScalarGridSpec(
            num_scalar_prefetch=1,
            grid=(1,),
            in_specs=[whole_spec(x.shape) for x in operands] + [in_place] * len(waits),
            out_specs=[whole_spec(x.shape) for x in outs],
        ),
        compiler_params=pltpu.CompilerParams(vmem_limit_bytes=vmem_limit),
        cost_estimate=pl.CostEstimate(flops=0, bytes_accessed=2**10, transcendentals=0),
    )(info, *operands, *waits)


def join_weight(blocks, first, cols, shares):
    rows, width = blocks.shape[0] // (cols * shares), blocks.shape[1] - first

    def kernel(ref, out_ref):
        for k in range(cols):
            for t in range(shares):
                at = (k * shares + t) * rows
                out_ref[t * rows : (t + 1) * rows, k * width : (k + 1) * width] = ref[at : at + rows, first:]

    return pl.pallas_call(
        kernel,
        out_shape=jax.ShapeDtypeStruct((shares * rows, cols * width), blocks.dtype),
        compiler_params=pltpu.CompilerParams(vmem_limit_bytes=vmem_limit),
        cost_estimate=pl.CostEstimate(flops=0, bytes_accessed=2**10, transcendentals=0),
    )(blocks)


def each_index(index, count, work):
    for j in range(count):
        pl.when(index == j)(functools.partial(work, j))


def lanes_at(index, width, first, count):
    return pl.ds(pl.multiple_of(index * width + first, 128), count)


def cut_shared(info, gate, up, down, cols, shares, wait):
    rows, width, features = gate.shape[0] // shares, gate.shape[1] // cols, down.shape[1]
    both, down_rows = 2 * width, gate.shape[1] // cols // shares

    def kernel(e, c, gate_ref, up_ref, down_ref, out):
        for k in range(cols):
            at = rows_at(e, rows)
            out[c ^ k, :rows, :width] = gate_ref[at, k * width : (k + 1) * width]
            out[c ^ k, :rows, width:] = up_ref[at, k * width : (k + 1) * width]

        def cut_down(j):
            for k in range(cols):
                piece = down_ref[k * width + j * down_rows : k * width + (j + 1) * down_rows, :]
                out[c ^ k, rows : rows + down_rows, :] = piece[:, :both]
                out[c ^ k, rows + down_rows :, : features - both] = piece[:, both:]

        each_index(e, shares, cut_down)

    outs = (jax.ShapeDtypeStruct((cols, rows + 2 * down_rows, both), bf16),)
    return cut_call(kernel, info, (gate, up, down), outs, (wait,))[0]


def join_shared(info, parts, rows, features, padded):
    cols, all_rows, both = parts[0].shape
    width, shares, down_rows = both // 2, len(parts), (all_rows - rows) // 2

    def kernel(e, c, *refs):
        in_out, down_out = refs[-2:]
        in_out[...] = jnp.zeros_like(in_out)
        down_out[...] = jnp.zeros_like(down_out)
        for s in range(cols):
            for t, ref in enumerate(refs[:-2]):
                at = rows_at((c ^ s) * shares + (e ^ t), rows)
                in_out[at, :width] = ref[s, :rows, :width]
                in_out[at, padded : padded + width] = ref[s, :rows, width:]

        def join_down(j):
            for s in range(cols):
                for t, ref in enumerate(refs[:-2]):
                    at = slice((j ^ t) * down_rows, ((j ^ t) + 1) * down_rows)
                    down_out[at, lanes_at(c ^ s, features, 0, both)] = ref[s, rows : rows + down_rows, :]
                    down_out[at, lanes_at(c ^ s, features, both, features - both)] = ref[
                        s, rows + down_rows :, : features - both
                    ]

        each_index(e, shares, join_down)

    outs = (
        jax.ShapeDtypeStruct((cols * shares * rows, 2 * padded), bf16),
        jax.ShapeDtypeStruct((padded, cols * features), bf16),
    )
    return cut_call(kernel, info, parts, outs)


def cut_shared_grads(info, grad_in, grad_down, cols, shares, width):
    rows, padded = grad_in.shape[0] // (cols * shares), grad_in.shape[1] // 2
    both, down_rows, features = 2 * width, width // shares, grad_down.shape[1] // cols

    def kernel(e, c, in_ref, down_ref, *outs):
        for s in range(cols):
            for t, out in enumerate(outs):
                at = rows_at((c ^ s) * shares + (e ^ t), rows)
                out[s, :rows, :width] = in_ref[at, :width]
                out[s, :rows, width:] = in_ref[at, padded : padded + width]

        def cut_down(j):
            for s in range(cols):
                for t, out in enumerate(outs):
                    at = slice((j ^ t) * down_rows, ((j ^ t) + 1) * down_rows)
                    out[s, rows : rows + down_rows, :] = down_ref[at, lanes_at(c ^ s, features, 0, both)]
                    out[s, rows + down_rows :, : features - both] = down_ref[
                        at, lanes_at(c ^ s, features, both, features - both)
                    ]

        each_index(e, shares, cut_down)

    outs = (jax.ShapeDtypeStruct((cols, rows + 2 * down_rows, both), bf16),) * shares
    return cut_call(kernel, info, (grad_in, grad_down), outs)


def join_shared_grads(info, parts, rows, features):
    cols, all_rows, both = parts[0].shape
    width, shares, down_rows = both // 2, len(parts), (all_rows - rows) // 2

    def kernel(e, c, *refs):
        gate_out, up_out, down_out = refs[-3:]
        for k in range(cols):
            for t, ref in enumerate(refs[:-3]):
                at, part = rows_at(e ^ t, rows), ref[c ^ k, :rows, :].astype(f32)
                gate_out[at, k * width : (k + 1) * width] = part[:, :width]
                up_out[at, k * width : (k + 1) * width] = part[:, width:]

        def join_down(j):
            for k in range(cols):
                for t, ref in enumerate(refs[:-3]):
                    at = k * width + (j ^ t) * down_rows
                    at = slice(at, at + down_rows)
                    down_out[at, :both] = ref[c ^ k, rows : rows + down_rows, :].astype(f32)
                    down_out[at, both:] = ref[c ^ k, rows + down_rows :, : features - both].astype(f32)

        each_index(e, shares, join_down)

    outs = (
        *[jax.ShapeDtypeStruct((shares * rows, cols * width), f32)] * 2,
        jax.ShapeDtypeStruct((cols * width, features), f32),
    )
    return cut_call(kernel, info, parts, outs)


def attention_call(kernel, place, operands, outs, scratch, work, waits):
    return pl.pallas_call(
        lambda place, *refs: kernel(place, *refs[: len(operands)], *refs[len(operands) + len(waits) :]),
        out_shape=outs,
        grid_spec=pltpu.PrefetchScalarGridSpec(
            num_scalar_prefetch=1,
            grid=(1,),
            in_specs=[whole_spec(x.shape) for x in operands] + [in_place] * len(waits),
            out_specs=[whole_spec(x.shape) for x in outs],
            scratch_shapes=scratch,
        ),
        compiler_params=pltpu.CompilerParams(vmem_limit_bytes=vmem_limit),
        cost_estimate=pl.CostEstimate(
            flops=work, bytes_accessed=2**10, transcendentals=0
        ),
    )(place, *operands, *waits)


def attention_forward(place, queries, kv_parts, chunk, waits):
    rows, total_width = queries.shape
    width = kv_parts[0].shape[1] // 2
    heads, blocks, keys = total_width // width, rows // chunk, rows * len(kv_parts)
    return attention_call(
        functools.partial(attention_kernel, chunk),
        place,
        (queries, *kv_parts),
        (
            jax.ShapeDtypeStruct((rows, total_width), bf16),
            jax.ShapeDtypeStruct((blocks, width, heads * chunk), f32),
            jax.ShapeDtypeStruct((blocks, 1, heads * chunk), f32),
        ),
        [pltpu.VMEM((keys, width), bf16)] * 2,
        4 * rows * heads * keys * width,
        waits,
    )


def attention_backward(place, queries, grads, out, lse, kv_parts, chunk, waits):
    rows, total_width = queries.shape
    width = kv_parts[0].shape[1] // 2
    keys = rows * len(kv_parts)
    return attention_call(
        functools.partial(attention_back_kernel, chunk),
        place,
        (queries, grads, out, lse, *kv_parts),
        (
            jax.ShapeDtypeStruct((rows, total_width), f32),
            jax.ShapeDtypeStruct((len(kv_parts), rows, 2 * width), bf16),
        ),
        [pltpu.VMEM((keys, width), bf16)] * 2 + [pltpu.VMEM((keys, width), f32)] * 2,
        10 * rows * total_width * keys,
        waits,
    )


def silu_back(gate_pre, up_pre, grad_hidden):
    sigmoid_vals = jax.nn.sigmoid(gate_pre)
    silu = gate_pre * sigmoid_vals
    grad_gate = grad_hidden * up_pre * sigmoid_vals * (1.0 + gate_pre * (1.0 - sigmoid_vals))
    return silu * up_pre, grad_gate.astype(bf16), (grad_hidden * silu).astype(bf16)


def experts_kernel(counts, unused, local, tiles, chunks, info, *refs):
    groups = len(counts)
    x_refs, refs = refs[: sum(counts)], refs[sum(counts) :]
    mix_refs, refs = refs[: sum(counts)], refs[sum(counts) :]
    g_refs, refs = refs[:groups], refs[groups:]
    refs = refs[:6] + refs[6 + unused :]
    (
        slot_ref, slot_t_ref, w_in, w_down, s_in, s_down,
        xs_ref, gs_ref, hidden_ref, pre_ref, own_x_ref, own_g_ref, s_hidden_ref, s_pre_ref,
    ), refs = refs[:14], refs[14:]
    out_refs, refs = refs[:groups], refs[groups:]
    norm_refs, refs = refs[:groups], refs[groups:]
    pick, put, acc_in, acc_down, s_acc_in, s_acc_down, term_buf = refs
    step = pl.program_id(0)
    capacity, tokens = pick.shape[1], pick.shape[2]
    width, s_width = w_down.shape[1], s_down.shape[0]

    @pl.when(step == 0)
    def _():
        for at in range(groups * local):
            slots = lax.broadcasted_iota(jnp.int32, (capacity, tokens), 0)
            pick[at] = jnp.where(slots == slot_ref[at : at + 1, :], 1.0, 0.0).astype(bf16)
            slots = lax.broadcasted_iota(jnp.int32, (tokens, capacity), 1)
            put[at // local, :, (at % local) * capacity : (at % local + 1) * capacity] = jnp.where(
                slots == slot_t_ref[:, at : at + 1], 1.0, 0.0
            ).astype(bf16)
        acc_in[...] = jnp.zeros_like(acc_in)
        acc_down[...] = jnp.zeros_like(acc_down)
        s_acc_in[...] = jnp.zeros_like(s_acc_in)
        s_acc_down[...] = jnp.zeros_like(s_acc_down)

    @pl.when(step < tiles)
    def _():
        for t in range(groups):
            parts = slice(sum(counts[:t]), sum(counts[: t + 1]))
            x = jnp.concatenate([ref[...] for ref in x_refs[parts]], axis=0)
            chunk = tokens // chunks
            g = jnp.concatenate(
                [
                    g_refs[t][pl.ds(pl.multiple_of(info[groups + k] * chunk, chunk), chunk), :]
                    for k in range(chunks)
                ],
                axis=0,
            )
            for l in range(local):
                rows = slice(t * capacity, (t + 1) * capacity)
                xs_ref[l, rows, :] = dot(pick[t * local + l], x).astype(bf16)
                gs_ref[l, rows, :] = dot(pick[t * local + l], g).astype(bf16)
            if t == 0:
                own_x_ref[...] = x
                own_g_ref[...] = g
                s_acc_in[...] += dot(x, s_in[...])
                s_acc_down[...] += dot(g, s_down[...], (1, 1))
        for l in range(local):
            acc_in[l] += dot(xs_ref[l], w_in[l])
            acc_down[l] += dot(gs_ref[l], w_down[l], (1, 1))

    @pl.when(step == tiles - 1)
    def _():
        mixes = [
            jnp.concatenate([ref[...] for ref in mix_refs[sum(counts[:t]) : sum(counts[: t + 1])]], axis=0)
            for t in range(groups)
        ]
        lanes = mixes[0].shape[1]
        lane = lax.broadcasted_iota(jnp.int32, (1, lanes), 1)
        spread = []
        for l in range(local):
            expert = info[groups + chunks] + l
            weights = jnp.concatenate([dot(pick[t * local + l], mixes[t]) for t in range(groups)], axis=0)
            weights = jnp.sum(
                jnp.where(lane % (lanes // 2) == expert, weights, 0.0), axis=1, keepdims=True
            )
            grad = acc_down[l]
            hidden, d_gate, d_up = silu_back(acc_in[l, :, :width], acc_in[l, :, width:], grad * weights)
            terms = jnp.sum(hidden * grad, axis=1, keepdims=True)
            hidden_ref[l] = (hidden * weights).astype(bf16)
            pre_ref[l, :, :width] = d_gate
            pre_ref[l, :, width:] = d_up
            spread.append(jnp.where(lane == expert, terms, 0.0).astype(bf16))
        for t in range(groups):
            rows = slice(t * capacity, (t + 1) * capacity)
            term_buf[t] = dot(
                put[t], jnp.concatenate([terms[rows] for terms in spread], axis=0)
            ).astype(bf16)
        hidden, d_gate, d_up = silu_back(s_acc_in[:, :s_width], s_acc_in[:, s_width:], s_acc_down[...])
        s_hidden_ref[...] = hidden.astype(bf16)
        s_pre_ref[:, :s_width] = d_gate
        s_pre_ref[:, s_width:] = d_up

    @pl.when((step >= tiles) & (step < 2 * tiles))
    def _():
        pieces = [dot(hidden_ref[l], w_down[l]).astype(bf16) for l in range(local)]
        d_pieces = [dot(pre_ref[l], w_in[l], (1, 1)).astype(bf16) for l in range(local)]
        for t in range(groups):
            rows = slice(t * capacity, (t + 1) * capacity)
            out = dot(put[t], jnp.concatenate([piece[rows] for piece in pieces], axis=0))
            norm = dot(put[t], jnp.concatenate([piece[rows] for piece in d_pieces], axis=0))
            if t == 0:
                out = out + dot(s_hidden_ref[...], s_down[...])
                norm = norm + dot(s_pre_ref[...], s_in[...], (1, 1))
            out_refs[t][...] = out.astype(bf16)
            norm_refs[t][...] = norm.astype(bf16)

    @pl.when(step == 2 * tiles)
    def _():
        for t in range(groups):
            norm_refs[t][:, : term_buf.shape[2]] = term_buf[t]


def experts_call(at, blocks, held, x_parts, g_all, info, slots, w_in, w_down, s_in, s_down, capacity, waits):
    counts = [len(parts) for parts in x_parts]
    x_parts = [x for parts in x_parts for x in parts]
    groups, local = len(counts), w_in.shape[0]
    chunks = info.shape[0] - groups - 2
    model, whole_width = g_all.shape[1], x_parts[0].shape[1]
    lanes = whole_width - model
    tokens = sum(x.shape[0] for x in x_parts[: counts[0]])
    tile = 512 if groups <= 2 else 256
    tiles = model // tile
    width, s_width = w_down.shape[1], s_down.shape[0]
    rows = groups * capacity

    def tokens_in(i, info):
        return (0, jnp.minimum(i, tiles - 1))

    def grads_in(t):
        return pl.BlockSpec((tokens, tile), lambda i, info: (info[t], jnp.minimum(i, tiles - 1)))

    def picked(i, info):
        return (0, at, jnp.minimum(i, tiles - 1))

    def own(i, info):
        return (at, jnp.minimum(i, tiles - 1))

    def summed(i, info):
        return (info[groups + chunks + 1], jnp.clip(i - tiles, 0, tiles - 1))

    def summed_norm(i, info):
        return (0, jnp.maximum(i - tiles, 0))

    in_specs = [
        *(pl.BlockSpec((x.shape[0], tile), tokens_in) for x in x_parts),
        *(pl.BlockSpec((x.shape[0], lanes), lambda i, info: (0, model // lanes)) for x in x_parts),
        *(grads_in(t) for t in range(groups)),
        whole_spec(slots.shape),
        whole_spec(slots.shape[::-1]),
        pl.BlockSpec((local, tile, 2 * width), lambda i, info: (0, i % tiles, 0)),
        pl.BlockSpec((local, width, tile), lambda i, info: (0, 0, i % tiles)),
        pl.BlockSpec((tile, 2 * s_width), lambda i, info: (i % tiles, 0)),
        pl.BlockSpec((s_width, tile), lambda i, info: (0, i % tiles)),
        *[in_place] * (len(held) + len(waits)),
    ]
    kept = (
        jax.ShapeDtypeStruct((local, blocks * rows, model), bf16),
        jax.ShapeDtypeStruct((local, blocks * rows, model), bf16),
        jax.ShapeDtypeStruct((local, blocks * rows, width), bf16),
        jax.ShapeDtypeStruct((local, blocks * rows, 2 * width), bf16),
        jax.ShapeDtypeStruct((blocks * tokens, model), bf16),
        jax.ShapeDtypeStruct((blocks * tokens, model), bf16),
        jax.ShapeDtypeStruct((blocks * tokens, s_width), bf16),
        jax.ShapeDtypeStruct((blocks * tokens, 2 * s_width), bf16),
        *[jax.ShapeDtypeStruct((blocks * tokens, model), bf16)] * groups,
    )
    norms = (jax.ShapeDtypeStruct((tokens, whole_width), bf16),) * groups
    out_specs = [
        pl.BlockSpec((local, rows, tile), picked),
        pl.BlockSpec((local, rows, tile), picked),
        pl.BlockSpec((local, rows, width), lambda i, info: (0, at, 0)),
        pl.BlockSpec((local, rows, 2 * width), lambda i, info: (0, at, 0)),
        pl.BlockSpec((tokens, tile), own),
        pl.BlockSpec((tokens, tile), own),
        pl.BlockSpec((tokens, s_width), lambda i, info: (at, 0)),
        pl.BlockSpec((tokens, 2 * s_width), lambda i, info: (at, 0)),
        *[pl.BlockSpec((tokens, tile), summed)] * groups,
        *[pl.BlockSpec((tokens, tile), summed_norm)] * groups,
    ]
    work = 2 * model * (
        4 * groups * local * capacity * tokens + 6 * local * rows * width + 6 * tokens * s_width
    )
    first = 1 + len(in_specs) - len(held) - len(waits)
    results = pl.pallas_call(
        functools.partial(experts_kernel, counts, len(held) + len(waits), local, tiles, chunks),
        out_shape=(*kept, *norms),
        grid_spec=pltpu.PrefetchScalarGridSpec(
            num_scalar_prefetch=1,
            grid=(2 * tiles + 1,),
            in_specs=in_specs,
            out_specs=out_specs,
            scratch_shapes=[
                pltpu.VMEM((groups * local, capacity, tokens), bf16),
                pltpu.VMEM((groups, tokens, local * capacity), bf16),
                pltpu.VMEM((local, rows, 2 * width), f32),
                pltpu.VMEM((local, rows, width), f32),
                pltpu.VMEM((tokens, 2 * s_width), f32),
                pltpu.VMEM((tokens, s_width), f32),
                pltpu.VMEM((groups, tokens, lanes), bf16),
            ],
        ),
        input_output_aliases={first + i: i for i in range(len(held))},
        compiler_params=pltpu.CompilerParams(vmem_limit_bytes=vmem_limit),
        cost_estimate=pl.CostEstimate(flops=work, bytes_accessed=2**10, transcendentals=0),
    )(info, *x_parts, *x_parts, *[g_all] * groups, slots, slots.T, w_in, w_down, s_in, s_down, *held, *waits)
    return list(results[: len(kept)]), list(results[len(kept) :])


def shards(
    inputs,
    routes,
    w_query,
    w_key,
    w_value,
    w_output,
    gain_attn,
    gain_moe,
    w_router,
    shared_gate,
    shared_up,
    shared_down,
    expert_gate,
    expert_up,
    expert_down,
    out_grad,
):
    e, r, c = lax.axis_index("exp"), lax.axis_index("row"), lax.axis_index("col")
    E, R, C = lax.axis_size("exp"), lax.axis_size("row"), lax.axis_size("col")
    local_count, model_width, _ = expert_gate.shape
    n_experts = local_count * E * R
    block_rows, top_count = routes.shape
    capacity = 4 * block_rows * top_count // (3 * n_experts)
    home_rows = block_rows // C
    head_width = HEAD_DIM
    query_width, key_width = w_query.shape[1], w_key.shape[1]
    group_heads = query_width // key_width
    attn_scale = head_width ** (-0.5)
    sources = ring_sources("col")

    x = tokens_home(inputs, 0).astype(f32)
    small = jnp.concatenate([w_router.T, gain_attn[None], gain_moe[None]], axis=0)
    small_all = jnp.zeros((small.shape[0], model_width), f32)
    for s, part in enumerate(exchange(small, "col")):
        small_all = lax.dynamic_update_slice(small_all, part, (0, (c ^ s) * small.shape[1]))
    router_t, gain_one, gain_two = (
        small_all[:n_experts],
        small_all[n_experts],
        small_all[n_experts + 1],
    )
    inv_one = rms_inverse(x)
    norm_one = (x * inv_one * gain_one[None, :]).astype(bf16)
    norm_one_parts = row_gather(norm_one)
    norm_one_all = jnp.concatenate(norm_one_parts, axis=0)

    own_weights = own_share(jnp.concatenate([w_key, w_value, w_query, w_output], axis=1))
    weights = lax.all_gather(own_weights, ("col", "exp"), tiled=True)
    weight_in = weights[:, : query_width + 2 * key_width]
    g_block = lax.all_gather(
        after(out_grad, weights, *norm_one_parts[1:]), "col", axis=1, tiled=True
    )
    g = lax.dynamic_slice_in_dim(g_block, c * home_rows, home_rows, 0)
    raw = dot(norm_one_all, weight_in)
    wait = zero_of(raw)
    here = jnp.stack([e, c]).astype(jnp.int32)
    weight_out = join_weight(weights, query_width + 2 * key_width, C, E)

    s_width = shared_gate.shape[1] // C
    s_padded = -(-s_width // 128) * 128

    def col_swap(parts):
        return jnp.stack([swap(parts[s], "col", s) if s else parts[0] for s in range(C)])

    shared_cut = cut_shared(here, shared_gate, shared_up, shared_down, C, E, raw)
    in_rows, feature_width = shared_gate.shape[0] // E, shared_down.shape[1]
    shared_parts = col_swap(shared_cut)
    sh_in, sh_down = join_shared(
        here, exchange(shared_parts, "exp"), in_rows, feature_width, s_padded
    )
    expert_in = side_by_side(expert_gate, expert_up, raw)

    own_routes = lax.dynamic_slice_in_dim(routes, c * home_rows, home_rows, 0)
    routes_here = routes.reshape(C, home_rows, top_count)[sources].reshape(block_rows, top_count)
    expert_ids = jnp.arange(n_experts)
    first_expert = (e * R + r) * local_count
    own_ids = first_expert + jnp.arange(local_count)
    earlier = (jnp.arange(block_rows)[:, None] < jnp.arange(block_rows)[None, :]).astype(bf16)
    routes_t = routes_here.T
    routes_t = routes_t + wait
    named = jnp.stack(
        [
            (block[None] == own_ids[:, None, None]).any(axis=1)
            for of_row in exchange(routes_t, "row")
            for block in exchange(of_row, "exp")
        ]
    ).reshape(R, E * local_count, block_rows)
    rank = dot(named.reshape(-1, block_rows).astype(bf16), earlier).astype(jnp.int32)
    slots = jnp.where(named, rank.reshape(named.shape), -1)

    positions = (
        ((r ^ jnp.arange(R)) * block_rows + c * home_rows)[:, None]
        + jnp.arange(home_rows)[None, :]
    ).reshape(-1)
    cosines, sines = rope_tables(positions, head_width)
    own_rows = R * home_rows
    keys = rotate(raw[:, :key_width].reshape(own_rows, 1, head_width), cosines, sines)
    kv = jnp.concatenate([keys.reshape(own_rows, key_width), raw[:, key_width : 2 * key_width]], axis=1)
    kv_parts = exchange(kv.astype(bf16), "col")
    queries = rotate(
        raw[:, 2 * key_width :].reshape(own_rows, group_heads, head_width), cosines, sines
    )
    queries = (queries * attn_scale).astype(bf16).reshape(own_rows, query_width)
    place = jnp.concatenate([jnp.stack([r, c]), c ^ jnp.arange(C)]).astype(jnp.int32)
    attended, att_total, lse = attention_forward(place, queries, kv_parts, home_rows, (expert_in, shared_cut))
    attn_part = dot(attended, weight_out).astype(bf16)
    g_all = lax.all_gather(after(g_block, attn_part), ("exp", "row"), tiled=True)
    hidden_state = x + row_reduce(jnp.split(attn_part, R, axis=0))[0]
    inv_two = rms_inverse(hidden_state) + zero_of(*(shared_parts[s] for s in range(1, C))).astype(f32)
    norm_two = (hidden_state * inv_two * gain_two[None, :]).astype(bf16)

    norm_float = norm_two.astype(f32)
    logits = lax.dot_general(
        norm_float, router_t, (((1,), (1,)), ((), ())), precision=highest
    )
    router_probs = jax.nn.softmax(logits, axis=-1)
    routed = (own_routes[:, :, None] == expert_ids[None, None, :]).any(axis=1)
    chosen = jnp.where(routed, router_probs, 0.0)
    chosen_sum = jnp.sum(chosen, axis=1, keepdims=True)
    mix = chosen / chosen_sum

    mix_lanes = -(-n_experts // 64) * 64
    mix_first = lax.reduce_precision(mix, 8, 7)
    mix_pad = ((0, 0), (0, mix_lanes - n_experts))
    payload = jnp.concatenate(
        [
            norm_two,
            jnp.pad(mix_first.astype(bf16), mix_pad),
            jnp.pad((mix - mix_first).astype(bf16), mix_pad),
        ],
        axis=1,
    )
    payload = jnp.concatenate(ring_gather(payload, "col"), axis=0)
    payload_rows = row_gather(payload)
    if R == 4:
        payload_rows = [[x] for x in payload_rows[:3]] + [payload_rows[3:]]
    else:
        payload_rows = [[x] for x in payload_rows]
    kept, norms, moved = [], [], []
    for s in range(R):
        x_block = payload_rows[s]
        if E > 2 and kept:
            x_block = [after(x, kept[-1]) for x in x_block]
        info = jnp.concatenate(
            [(e ^ jnp.arange(E)) * R + (r ^ s), sources, jnp.stack([first_expert, r ^ s])]
        ).astype(jnp.int32)
        kept, norm = experts_call(
            s, R, kept, list(zip(*(exchange(x, "exp") for x in x_block))), g_all, info,
            slots[s], expert_in, expert_down, sh_in, sh_down, capacity, norms[-1:],
        )
        seen = moved if s == R - 1 else [x for later in ((1, 2), (3,))[s] for x in payload_rows[later]] if s < 2 else []
        if seen:
            norm = [norm[0], *(after(x, *seen) for x in norm[1:])]
        norms.append(reduce_parts(norm, "exp").astype(bf16))
        if s:
            moved.append(swap(norms[s], "row", s))
    kept, outs = kept[:8], kept[8:]
    rows_x, rows_g, hidden, pre, own_x, own_g, s_hidden, s_pre = kept

    s_pre, s_hidden = after(s_pre, norms[-1]), after(s_hidden, norms[-1])
    d_in = dot(own_x, s_pre, (0, 0)).astype(bf16)
    d_down = dot(s_hidden, own_g, (0, 0)).astype(bf16)
    shared_grads = cut_shared_grads(here, d_in, d_down, C, E, s_width)
    shared_sums = reduce_parts(shared_grads, "exp").astype(bf16)

    norm_block = norms[0].astype(f32)
    for x_sum in moved:
        norm_block = norm_block + x_sum.astype(f32)
    chunks = jnp.split(norm_block.astype(bf16), C, axis=0)
    home = ring_reduce(chunks, "col")
    d_norm, gate_terms = home[:, :model_width], home[:, model_width : model_width + n_experts]
    outs = [outs[0], *(after(x, norms[-1]) for x in outs[1:])]

    out_sum = after(reduce_parts(outs, "exp").astype(bf16), moved[-1], shared_grads[0])
    out_rows = lax.psum_scatter(out_sum, "row", scatter_dimension=0, tiled=True)

    expert_width = expert_gate.shape[2]
    pre = after(pre, moved[-1])
    grad_expert_gate = batch_dot("lrd,lrf->ldf", rows_x, pre[:, :, :expert_width])
    grad_expert_up = batch_dot("lrd,lrf->ldf", rows_x, pre[:, :, expert_width:])
    grad_expert_down = batch_dot("lrf,lrd->lfd", after(hidden, moved[-1]), rows_g)
    inner = jnp.sum(mix * gate_terms, axis=1, keepdims=True)
    d_probs = jnp.where(routed, (gate_terms - inner) / chosen_sum, 0.0)
    d_logits = router_probs * (
        d_probs - jnp.sum(router_probs * d_probs, axis=1, keepdims=True)
    )
    d_norm = d_norm + jnp.dot(d_logits, router_t, precision=highest)
    d_norm = d_norm + zero_of(grad_expert_gate, grad_expert_up, grad_expert_down).astype(f32)
    router_part = lax.dot_general(
        d_logits, norm_float, (((0,), (0,)), ((), ())), precision=highest
    )
    d_v, gain_two_part = rms_backward(hidden_state, inv_two, gain_two, d_norm)
    d_hidden = g.astype(f32) + d_v
    d_attn = d_hidden.astype(bf16)
    d_attn_parts = row_gather(d_attn)
    d_attn_all = jnp.concatenate(d_attn_parts, axis=0)

    out_grads = batch_dot("sf,scd->cfd", attended, d_attn_all.reshape(own_rows, C, -1))
    out_grads = out_grads.astype(bf16).reshape(C * query_width, -1)

    d_attended = dot(d_attn_all, weight_out, (1, 1)).astype(bf16)
    out_chunks = jnp.split(after(out_rows, d_attended), C, axis=0)
    moe_out = out_chunks[0].astype(f32)
    soon = [ring_send(out_chunks[k], "col", k) for k in range(1, C) if 2 * k != C]
    d_queries, d_kv_parts = attention_backward(
        place, queries, d_attended, att_total, lse, kv_parts, home_rows,
        (out_grads,),
    )
    shared_back = col_swap(after(shared_sums, *d_attn_parts[1:3]))
    d_kv_parts = after(d_kv_parts, *soon, shared_back)
    d_kv = reduce_parts([d_kv_parts[k] for k in range(C)], "col")
    soon.append(ring_send(after(out_chunks[C // 2], d_kv), "col", C // 2))
    for part in soon:
        moe_out = moe_out + part.astype(f32)
    d_query_raw = rotate(
        d_queries.reshape(own_rows, group_heads, head_width), cosines, -sines
    ) * attn_scale
    d_query_raw = d_query_raw.reshape(own_rows, query_width).astype(bf16)
    norm_one_late = after(norm_one_all, d_kv_parts)
    query_grads = dot(norm_one_late, d_query_raw, (0, 0)).astype(bf16)
    d_key_raw = rotate(d_kv[:, :key_width].reshape(own_rows, 1, head_width), cosines, -sines)
    d_kv_raw = jnp.concatenate(
        [d_key_raw.reshape(own_rows, key_width), d_kv[:, key_width:]], axis=1
    ).astype(bf16)
    norm_one_part = dot(jnp.concatenate([d_kv_raw, d_query_raw], axis=1), weight_in, (1, 1)).astype(bf16)
    d_norm_one, halfway = row_reduce(jnp.split(norm_one_part, R, axis=0))
    d_x, gain_one_part = rms_backward(x, inv_one, gain_one, d_norm_one)
    grad_inputs = tokens_back((d_hidden + d_x).astype(bf16))

    output = tokens_back((hidden_state + moe_out).astype(bf16))
    out_total, query_total = reduce_weight(out_grads), reduce_weight(query_grads)
    kv_grads = dot(after(norm_one_late, *halfway), d_kv_raw, (0, 0)).astype(bf16)
    kv_total = reduce_weight(after(kv_grads, query_total, d_norm_one))
    grad_output = all_shares(after(out_total, d_norm_one)).astype(f32)
    grad_query = all_shares(after(query_total, d_norm_one)).astype(f32)
    grad_kv = all_shares(kv_total).astype(f32)
    small_part = jnp.concatenate([router_part, gain_one_part[None], gain_two_part[None]], axis=0)
    width = small.shape[1]
    mine = [
        lax.dynamic_slice_in_dim(small_part, (c ^ s) * width, width, 1) for s in range(C)
    ]
    small_sum = all_sum(all_sum(reduce_parts(mine, "col"), "row"), "exp")

    grad_shared_gate, grad_shared_up, grad_shared_down = join_shared_grads(
        here, exchange(after(shared_back, d_norm_one), "exp"), in_rows, feature_width
    )
    return (
        output,
        grad_inputs,
        grad_query,
        grad_kv[:, :key_width],
        grad_kv[:, key_width:],
        grad_output,
        small_sum[n_experts],
        small_sum[n_experts + 1],
        small_sum[:n_experts].T,
        grad_shared_gate,
        grad_shared_up,
        grad_shared_down,
        grad_expert_gate,
        grad_expert_up,
        grad_expert_down,
    )


def solution(mesh):
    tokens, weight, experts = P(("exp", "row"), "col"), P("col", "row"), P(("exp", "row"), None, "col")
    expert_down, feature = P(("exp", "row"), "col", None), P("col")
    placed = (
        tokens,
        P(("exp", "row"), None),
        weight,
        weight,
        weight,
        P("row", "col"),
        feature,
        feature,
        P("col", None),
        weight,
        weight,
        P("row", "col"),
        experts,
        experts,
        expert_down,
        tokens,
    )
    return jax.shard_map(
        shards,
        mesh=mesh,
        in_specs=placed,
        out_specs=(
            tokens,
            tokens,
            weight,
            weight,
            weight,
            P("row", "col"),
            feature,
            feature,
            P("col", None),
            weight,
            weight,
            P("row", "col"),
            experts,
            experts,
            expert_down,
        ),
        check_vma=False,
    )
```

```python
import functools

import jax
import jax.numpy as jnp
from jax import lax
from jax.experimental import pallas as pl
from jax.experimental.pallas import tpu as pltpu
from jax.sharding import PartitionSpec as P

HEAD_DIM = 128

eps = 1e-05
theta = 500000.0
highest = lax.Precision.HIGHEST
masked_value = -1e30
f32 = jnp.float32
bf16 = jnp.bfloat16
vmem_limit = 56 * 2**20


def swap(x, axis, step):
    return lax.ppermute(x, axis, [(i, i ^ step) for i in range(lax.axis_size(axis))])


def exchange(x, axis):
    return [x] + [swap(x, axis, step) for step in range(1, lax.axis_size(axis))]


def reduce_parts(parts, axis):
    total = parts[0].astype(f32)
    for step in range(1, len(parts)):
        total = total + swap(parts[step], axis, step).astype(f32)
    return total


def all_sum(x, axis):
    step = 1
    while step < lax.axis_size(axis):
        x = x + swap(x, axis, step)
        step *= 2
    return x


def zero_of(*arrays):
    found = jnp.int32(0)
    for x in arrays:
        first = x[(slice(0, 1),) * x.ndim].reshape(())
        found = found + (first != first).astype(jnp.int32)
    return found


def after(x, *earlier):
    place = pl.BlockSpec(memory_space=pl.ANY)
    return pl.pallas_call(
        lambda *refs: None,
        out_shape=jax.ShapeDtypeStruct(x.shape, x.dtype),
        in_specs=[place] * (1 + len(earlier)),
        out_specs=place,
        input_output_aliases={0: 0},
    )(x, *earlier)


def ring_order(n):
    return [0] + list(range(1, n, 2)) + [i for i in range(n - 1, 0, -1) if i % 2 == 0]


def ring_pairs(n, back=False):
    order = ring_order(n)
    pairs = [(order[i], order[(i + 1) % n]) for i in range(n)]
    return [(b, a) for a, b in pairs] if back else pairs


def ring_sources(axis):
    n = lax.axis_size(axis)
    order = ring_order(n)
    place = jnp.array([order.index(i) for i in range(n)])[lax.axis_index(axis)]
    return jnp.array(order)[(place - jnp.arange(n)) % n]


def ring_gather(x, axis):
    parts, n = [x], lax.axis_size(axis)
    for _ in range(n - 1):
        parts.append(lax.ppermute(parts[-1], axis, ring_pairs(n)))
    return parts


def ring_send(x, axis, k):
    order = ring_order(lax.axis_size(axis))
    n = len(order)
    return lax.ppermute(x, axis, [(order[i], order[(i - k) % n]) for i in range(n)])


def ring_reduce(parts, axis):
    total = parts[0].astype(f32)
    for k in range(1, len(parts)):
        total = total + ring_send(parts[k], axis, k).astype(f32)
    return total


def row_gather(x):
    if lax.axis_size("row") != 4:
        return exchange(x, "row")
    x_near, y_near = swap(x, "row", 1), swap(x, "row", 2)
    middle = x.shape[0] // 2
    return [x, x_near, y_near, swap(y_near[:middle], "row", 1), swap(x_near[middle:], "row", 2)]


def add(left, right):
    return left.astype(f32) + right.astype(f32)


def row_reduce(blocks):
    if len(blocks) != 4:
        return reduce_parts(blocks, "row"), blocks[:1]
    own, x_near, y_near, far = blocks
    middle = own.shape[0] // 2
    far_x, far_y = swap(far[:middle], "row", 1), swap(far[middle:], "row", 2)
    y_first = add(y_near[:middle], far_x).astype(bf16)
    x_second = add(x_near[middle:], far_y).astype(bf16)
    y_sum = swap(jnp.concatenate([y_first, y_near[middle:]], axis=0), "row", 2)
    x_sum = swap(jnp.concatenate([x_near[:middle], x_second], axis=0), "row", 1)
    return add(own, x_sum) + y_sum.astype(f32), [far_x, far_y]


def tokens_home(x, wait):
    c, n = lax.axis_index("col"), lax.axis_size("col")
    rows, width = x.shape[0] // n, x.shape[1]
    whole = jnp.zeros((rows, n * width), x.dtype)
    for s in range(n):
        piece = lax.dynamic_slice_in_dim(x, (c ^ s) * rows + wait, rows, 0)
        piece = swap(piece, "col", s) if s else piece
        whole = lax.dynamic_update_slice(whole, piece, (0, (c ^ s) * width))
    return whole


def tokens_back(x):
    c, n = lax.axis_index("col"), lax.axis_size("col")
    rows, width = x.shape[0], x.shape[1] // n
    whole = jnp.zeros((n * rows, width), x.dtype)
    for s in range(n):
        piece = lax.dynamic_slice_in_dim(x, (c ^ s) * width, width, 1)
        piece = swap(piece, "col", s) if s else piece
        whole = lax.dynamic_update_slice(whole, piece, ((c ^ s) * rows, 0))
    return whole


def own_share(weight, wait=0):
    share = weight.shape[0] // lax.axis_size("exp")
    return lax.dynamic_slice_in_dim(weight, lax.axis_index("exp") * share + wait, share, 0)


def all_shares(total):
    e = lax.axis_index("exp")
    shares = lax.axis_size("exp")
    whole = jnp.zeros((shares,) + total.shape, total.dtype)
    for t, piece in enumerate(exchange(total, "exp")):
        whole = lax.dynamic_update_index_in_dim(whole, piece, e ^ t, 0)
    return whole.reshape((shares * total.shape[0],) + total.shape[1:])


def reduce_weight(grad):
    return lax.psum_scatter(grad, ("col", "exp"), scatter_dimension=0, tiled=True)


def rope_tables(positions, head_width):
    half_width = head_width // 2
    frequency = theta ** (-2.0 * jnp.arange(half_width, dtype=f32) / head_width)
    angles = positions.astype(f32)[:, None] * frequency[None, :]
    return (jnp.cos(angles), jnp.sin(angles))


def rotate(source, cosines, sines):
    half_width = source.shape[-1] // 2
    first, second = source[..., :half_width], source[..., half_width:]
    cos_view, sin_view = cosines[:, None, :], sines[:, None, :]
    return jnp.concatenate(
        [first * cos_view - second * sin_view, first * sin_view + second * cos_view], axis=-1
    )


def dot(left, right, contract=(1, 0)):
    return lax.dot_general(
        left, right, (((contract[0],), (contract[1],)), ((), ())), preferred_element_type=f32
    )


def batch_dot(spec, left, right):
    return jnp.einsum(spec, left, right, preferred_element_type=f32)


def rms_inverse(values):
    return lax.rsqrt(jnp.mean(values * values, axis=1, keepdims=True) + eps)


def rms_backward(values, inv_rms, gain, grad_norm):
    scaled_grad = grad_norm * gain[None, :]
    inner = jnp.mean(scaled_grad * values, axis=1, keepdims=True)
    grad_values = inv_rms * (scaled_grad - values * (inv_rms * inv_rms * inner))
    return grad_values, jnp.sum(grad_norm * values * inv_rms, axis=0)


def place_keys(place, kv_refs, key_buf, value_buf, chunk):
    row, blocks, width = place[0], kv_refs[0].shape[0] // chunk, key_buf.shape[1]
    for k, ref in enumerate(kv_refs):
        for s in range(blocks):
            at = pl.multiple_of(((row ^ s) * len(kv_refs) + place[2 + k]) * chunk, chunk)
            key_buf[pl.ds(at, chunk), :] = ref[s * chunk : (s + 1) * chunk, :width]
            value_buf[pl.ds(at, chunk), :] = ref[s * chunk : (s + 1) * chunk, width:]


def head_rows(ref, rows, width):
    block = ref[rows, :]
    return jnp.concatenate(
        [block[:, h * width : (h + 1) * width] for h in range(block.shape[1] // width)], axis=0
    )


def scores_tile(place, key_tile, queries, block, tile, chunk):
    scores = dot(key_tile, queries, (1, 1))
    key_at = tile * key_tile.shape[0] + lax.broadcasted_iota(jnp.int32, scores.shape, 0)
    lane = lax.broadcasted_iota(jnp.int32, scores.shape, 1)
    query_at = block * key_tile.shape[0] + place[1] * chunk + lane % chunk
    return jnp.where(key_at <= query_at, scores, masked_value)


def attention_kernel(chunk, place, q_ref, *refs):
    kv_refs, (out_ref, total_ref, lse_ref, key_buf, value_buf) = refs[:-5], refs[-5:]
    width = key_buf.shape[1]
    blocks = q_ref.shape[0] // chunk
    tile_rows = key_buf.shape[0] // blocks
    place_keys(place, kv_refs, key_buf, value_buf, chunk)

    @pl.loop(0, blocks)
    def _(block):
        rows = pl.ds(pl.multiple_of((place[0] ^ block) * chunk, chunk), chunk)
        queries = head_rows(q_ref, rows, width)
        count = queries.shape[0]

        def step(tile, carry):
            peak, total, out = carry
            at = pl.ds(pl.multiple_of(tile * tile_rows, tile_rows), tile_rows)
            scores = scores_tile(place, key_buf[at, :], queries, block, tile, chunk)
            new_peak = jnp.maximum(peak, jnp.max(scores, axis=0, keepdims=True))
            weights = jnp.exp(scores - new_peak)
            shrink = jnp.exp(peak - new_peak)
            total = total * shrink + jnp.sum(weights, axis=0, keepdims=True)
            part = dot(value_buf[at, :], weights.astype(bf16), (0, 0))
            return new_peak, total, out * shrink + part

        start = (
            jnp.full((1, count), masked_value, f32),
            jnp.zeros((1, count), f32),
            jnp.zeros((width, count), f32),
        )
        peak, total, out = lax.fori_loop(0, block + 1, step, start)
        out = out / total
        total_ref[pl.ds(block, 1)] = out[None]
        lse_ref[pl.ds(block, 1)] = (peak + jnp.log(total))[None]
        for h in range(count // chunk):
            head = out[:, h * chunk : (h + 1) * chunk]
            out_ref[rows, h * width : (h + 1) * width] = head.T.astype(bf16)


def attention_back_kernel(chunk, place, q_ref, grad_ref, total_ref, lse_ref, *refs):
    kv_refs = refs[:-6]
    dq_ref, dkv_ref, key_buf, value_buf, dk_buf, dv_buf = refs[-6:]
    width = key_buf.shape[1]
    blocks = q_ref.shape[0] // chunk
    tile_rows = key_buf.shape[0] // blocks
    place_keys(place, kv_refs, key_buf, value_buf, chunk)
    dk_buf[...] = jnp.zeros_like(dk_buf)
    dv_buf[...] = jnp.zeros_like(dv_buf)

    @pl.loop(0, blocks)
    def _(block):
        rows = pl.ds(pl.multiple_of((place[0] ^ block) * chunk, chunk), chunk)
        queries = head_rows(q_ref, rows, width)
        grads = head_rows(grad_ref, rows, width)
        count = queries.shape[0]
        out = total_ref[pl.ds(block, 1)][0]
        lse = lse_ref[pl.ds(block, 1)][0]
        grads_t = jnp.concatenate(
            [grads[h * chunk : (h + 1) * chunk].astype(f32).T for h in range(count // chunk)], axis=1
        )
        inner = jnp.sum(out * grads_t, axis=0, keepdims=True)

        def step(tile, d_queries):
            at = pl.ds(pl.multiple_of(tile * tile_rows, tile_rows), tile_rows)
            keys = key_buf[at, :]
            scores = scores_tile(place, keys, queries, block, tile, chunk)
            probs = jnp.exp(scores - lse)
            d_probs = dot(value_buf[at, :], grads, (1, 1))
            d_scores = (probs * (d_probs - inner)).astype(bf16)
            dk_buf[at, :] += dot(d_scores, queries)
            dv_buf[at, :] += dot(probs.astype(bf16), grads)
            return d_queries + dot(keys, d_scores, (0, 0))

        d_queries = lax.fori_loop(0, block + 1, step, jnp.zeros((width, count), f32))
        for h in range(count // chunk):
            head = d_queries[:, h * chunk : (h + 1) * chunk]
            dq_ref[rows, h * width : (h + 1) * width] = head.T

    for k in range(len(kv_refs)):
        for s in range(blocks):
            at = pl.ds(pl.multiple_of(((place[0] ^ s) * len(kv_refs) + place[2 + k]) * chunk, chunk), chunk)
            dkv_ref[k, s * chunk : (s + 1) * chunk, :width] = dk_buf[at, :].astype(bf16)
            dkv_ref[k, s * chunk : (s + 1) * chunk, width:] = dv_buf[at, :].astype(bf16)


in_place = pl.BlockSpec(memory_space=pl.ANY)


def whole_spec(shape):
    return pl.BlockSpec(shape, lambda *_: (0,) * len(shape))


def side_by_side(left, right, wait):
    count, rows, width = left.shape
    tile = 512

    def kernel(left_ref, right_ref, _, both_ref):
        both_ref[:, :width] = left_ref[...]
        both_ref[:, width:] = right_ref[...]

    spec = pl.BlockSpec((None, tile, width), lambda i, j: (i, j, 0))
    return pl.pallas_call(
        kernel,
        out_shape=jax.ShapeDtypeStruct((count, rows, 2 * width), left.dtype),
        grid=(count, rows // tile),
        in_specs=[spec, spec, in_place],
        out_specs=pl.BlockSpec((None, tile, 2 * width), lambda i, j: (i, j, 0)),
        cost_estimate=pl.CostEstimate(flops=0, bytes_accessed=2**10, transcendentals=0),
    )(left, right, wait)


def rows_at(index, count):
    return pl.ds(pl.multiple_of(index * count, count), count)


def cut_call(kernel, info, operands, outs, waits=()):
    return pl.pallas_call(
        lambda info, *refs: kernel(info[0], info[1], *refs[: len(operands)], *refs[len(operands) + len(waits) :]),
        out_shape=outs,
        grid_spec=pltpu.PrefetchScalarGridSpec(
            num_scalar_prefetch=1,
            grid=(1,),
            in_specs=[whole_spec(x.shape) for x in operands] + [in_place] * len(waits),
            out_specs=[whole_spec(x.shape) for x in outs],
        ),
        compiler_params=pltpu.CompilerParams(vmem_limit_bytes=vmem_limit),
        cost_estimate=pl.CostEstimate(flops=0, bytes_accessed=2**10, transcendentals=0),
    )(info, *operands, *waits)


def join_weight(info, parts):
    cols, rows, width = parts[0].shape

    def kernel(e, c, *refs):
        for s in range(cols):
            for t, ref in enumerate(refs[:-1]):
                refs[-1][rows_at(e ^ t, rows), rows_at(c ^ s, width)] = ref[s]

    outs = (jax.ShapeDtypeStruct((len(parts) * rows, cols * width), parts[0].dtype),)
    return cut_call(kernel, info, parts, outs)[0]


def each_index(index, count, work):
    for j in range(count):
        pl.when(index == j)(functools.partial(work, j))


def lanes_at(index, width, first, count):
    return pl.ds(pl.multiple_of(index * width + first, 128), count)


def cut_shared(info, gate, up, down, cols, shares, wait):
    rows, width, features = gate.shape[0] // shares, gate.shape[1] // cols, down.shape[1]
    both, down_rows = 2 * width, gate.shape[1] // cols // shares

    def kernel(e, c, gate_ref, up_ref, down_ref, out):
        for k in range(cols):
            at = rows_at(e, rows)
            out[c ^ k, :rows, :width] = gate_ref[at, k * width : (k + 1) * width]
            out[c ^ k, :rows, width:] = up_ref[at, k * width : (k + 1) * width]

        def cut_down(j):
            for k in range(cols):
                piece = down_ref[k * width + j * down_rows : k * width + (j + 1) * down_rows, :]
                out[c ^ k, rows : rows + down_rows, :] = piece[:, :both]
                out[c ^ k, rows + down_rows :, : features - both] = piece[:, both:]

        each_index(e, shares, cut_down)

    outs = (jax.ShapeDtypeStruct((cols, rows + 2 * down_rows, both), bf16),)
    return cut_call(kernel, info, (gate, up, down), outs, (wait,))[0]


def join_shared(info, parts, rows, features, padded):
    cols, all_rows, both = parts[0].shape
    width, shares, down_rows = both // 2, len(parts), (all_rows - rows) // 2

    def kernel(e, c, *refs):
        in_out, down_out = refs[-2:]
        in_out[...] = jnp.zeros_like(in_out)
        down_out[...] = jnp.zeros_like(down_out)
        for s in range(cols):
            for t, ref in enumerate(refs[:-2]):
                at = rows_at((c ^ s) * shares + (e ^ t), rows)
                in_out[at, :width] = ref[s, :rows, :width]
                in_out[at, padded : padded + width] = ref[s, :rows, width:]

        def join_down(j):
            for s in range(cols):
                for t, ref in enumerate(refs[:-2]):
                    at = slice((j ^ t) * down_rows, ((j ^ t) + 1) * down_rows)
                    down_out[at, lanes_at(c ^ s, features, 0, both)] = ref[s, rows : rows + down_rows, :]
                    down_out[at, lanes_at(c ^ s, features, both, features - both)] = ref[
                        s, rows + down_rows :, : features - both
                    ]

        each_index(e, shares, join_down)

    outs = (
        jax.ShapeDtypeStruct((cols * shares * rows, 2 * padded), bf16),
        jax.ShapeDtypeStruct((padded, cols * features), bf16),
    )
    return cut_call(kernel, info, parts, outs)


def cut_shared_grads(info, grad_in, grad_down, cols, shares, width):
    rows, padded = grad_in.shape[0] // (cols * shares), grad_in.shape[1] // 2
    both, down_rows, features = 2 * width, width // shares, grad_down.shape[1] // cols

    def kernel(e, c, in_ref, down_ref, *outs):
        for s in range(cols):
            for t, out in enumerate(outs):
                at = rows_at((c ^ s) * shares + (e ^ t), rows)
                out[s, :rows, :width] = in_ref[at, :width]
                out[s, :rows, width:] = in_ref[at, padded : padded + width]

        def cut_down(j):
            for s in range(cols):
                for t, out in enumerate(outs):
                    at = slice((j ^ t) * down_rows, ((j ^ t) + 1) * down_rows)
                    out[s, rows : rows + down_rows, :] = down_ref[at, lanes_at(c ^ s, features, 0, both)]
                    out[s, rows + down_rows :, : features - both] = down_ref[
                        at, lanes_at(c ^ s, features, both, features - both)
                    ]

        each_index(e, shares, cut_down)

    outs = (jax.ShapeDtypeStruct((cols, rows + 2 * down_rows, both), bf16),) * shares
    return cut_call(kernel, info, (grad_in, grad_down), outs)


def join_shared_grads(info, parts, rows, features):
    cols, all_rows, both = parts[0].shape
    width, shares, down_rows = both // 2, len(parts), (all_rows - rows) // 2

    def kernel(e, c, *refs):
        gate_out, up_out, down_out = refs[-3:]
        for k in range(cols):
            for t, ref in enumerate(refs[:-3]):
                at, part = rows_at(e ^ t, rows), ref[c ^ k, :rows, :].astype(f32)
                gate_out[at, k * width : (k + 1) * width] = part[:, :width]
                up_out[at, k * width : (k + 1) * width] = part[:, width:]

        def join_down(j):
            for k in range(cols):
                for t, ref in enumerate(refs[:-3]):
                    at = k * width + (j ^ t) * down_rows
                    at = slice(at, at + down_rows)
                    down_out[at, :both] = ref[c ^ k, rows : rows + down_rows, :].astype(f32)
                    down_out[at, both:] = ref[c ^ k, rows + down_rows :, : features - both].astype(f32)

        each_index(e, shares, join_down)

    outs = (
        *[jax.ShapeDtypeStruct((shares * rows, cols * width), f32)] * 2,
        jax.ShapeDtypeStruct((cols * width, features), f32),
    )
    return cut_call(kernel, info, parts, outs)


def attention_call(kernel, place, operands, outs, scratch, work, waits):
    return pl.pallas_call(
        lambda place, *refs: kernel(place, *refs[: len(operands)], *refs[len(operands) + len(waits) :]),
        out_shape=outs,
        grid_spec=pltpu.PrefetchScalarGridSpec(
            num_scalar_prefetch=1,
            grid=(1,),
            in_specs=[whole_spec(x.shape) for x in operands] + [in_place] * len(waits),
            out_specs=[whole_spec(x.shape) for x in outs],
            scratch_shapes=scratch,
        ),
        compiler_params=pltpu.CompilerParams(vmem_limit_bytes=vmem_limit),
        cost_estimate=pl.CostEstimate(
            flops=work, bytes_accessed=2**10, transcendentals=0
        ),
    )(place, *operands, *waits)


def attention_forward(place, queries, kv_parts, chunk, waits):
    rows, total_width = queries.shape
    width = kv_parts[0].shape[1] // 2
    heads, blocks, keys = total_width // width, rows // chunk, rows * len(kv_parts)
    return attention_call(
        functools.partial(attention_kernel, chunk),
        place,
        (queries, *kv_parts),
        (
            jax.ShapeDtypeStruct((rows, total_width), bf16),
            jax.ShapeDtypeStruct((blocks, width, heads * chunk), f32),
            jax.ShapeDtypeStruct((blocks, 1, heads * chunk), f32),
        ),
        [pltpu.VMEM((keys, width), bf16)] * 2,
        4 * rows * heads * keys * width,
        waits,
    )


def attention_backward(place, queries, grads, out, lse, kv_parts, chunk, waits):
    rows, total_width = queries.shape
    width = kv_parts[0].shape[1] // 2
    keys = rows * len(kv_parts)
    return attention_call(
        functools.partial(attention_back_kernel, chunk),
        place,
        (queries, grads, out, lse, *kv_parts),
        (
            jax.ShapeDtypeStruct((rows, total_width), f32),
            jax.ShapeDtypeStruct((len(kv_parts), rows, 2 * width), bf16),
        ),
        [pltpu.VMEM((keys, width), bf16)] * 2 + [pltpu.VMEM((keys, width), f32)] * 2,
        10 * rows * total_width * keys,
        waits,
    )


def silu_back(gate_pre, up_pre, grad_hidden):
    sigmoid_vals = jax.nn.sigmoid(gate_pre)
    silu = gate_pre * sigmoid_vals
    grad_gate = grad_hidden * up_pre * sigmoid_vals * (1.0 + gate_pre * (1.0 - sigmoid_vals))
    return silu * up_pre, grad_gate.astype(bf16), (grad_hidden * silu).astype(bf16)


def experts_kernel(counts, unused, local, tiles, chunks, info, *refs):
    groups = len(counts)
    x_refs, refs = refs[: sum(counts)], refs[sum(counts) :]
    mix_refs, refs = refs[: sum(counts)], refs[sum(counts) :]
    g_refs, refs = refs[:groups], refs[groups:]
    refs = refs[:6] + refs[6 + unused :]
    (
        slot_ref, slot_t_ref, w_in, w_down, s_in, s_down,
        xs_ref, gs_ref, hidden_ref, pre_ref, own_x_ref, own_g_ref, s_hidden_ref, s_pre_ref,
    ), refs = refs[:14], refs[14:]
    out_refs, refs = refs[:groups], refs[groups:]
    norm_refs, refs = refs[:groups], refs[groups:]
    pick, put, acc_in, acc_down, s_acc_in, s_acc_down, term_buf = refs
    step = pl.program_id(0)
    capacity, tokens = pick.shape[1], pick.shape[2]
    width, s_width = w_down.shape[1], s_down.shape[0]

    @pl.when(step == 0)
    def _():
        for at in range(groups * local):
            slots = lax.broadcasted_iota(jnp.int32, (capacity, tokens), 0)
            pick[at] = jnp.where(slots == slot_ref[at : at + 1, :], 1.0, 0.0).astype(bf16)
            slots = lax.broadcasted_iota(jnp.int32, (tokens, capacity), 1)
            put[at // local, :, (at % local) * capacity : (at % local + 1) * capacity] = jnp.where(
                slots == slot_t_ref[:, at : at + 1], 1.0, 0.0
            ).astype(bf16)
        acc_in[...] = jnp.zeros_like(acc_in)
        acc_down[...] = jnp.zeros_like(acc_down)
        s_acc_in[...] = jnp.zeros_like(s_acc_in)
        s_acc_down[...] = jnp.zeros_like(s_acc_down)

    @pl.when(step < tiles)
    def _():
        for t in range(groups):
            parts = slice(sum(counts[:t]), sum(counts[: t + 1]))
            x = jnp.concatenate([ref[...] for ref in x_refs[parts]], axis=0)
            chunk = tokens // chunks
            g = jnp.concatenate(
                [
                    g_refs[t][pl.ds(pl.multiple_of(info[groups + k] * chunk, chunk), chunk), :]
                    for k in range(chunks)
                ],
                axis=0,
            )
            for l in range(local):
                rows = slice(t * capacity, (t + 1) * capacity)
                xs_ref[l, rows, :] = dot(pick[t * local + l], x).astype(bf16)
                gs_ref[l, rows, :] = dot(pick[t * local + l], g).astype(bf16)
            if t == 0:
                own_x_ref[...] = x
                own_g_ref[...] = g
                s_acc_in[...] += dot(x, s_in[...])
                s_acc_down[...] += dot(g, s_down[...], (1, 1))
        for l in range(local):
            acc_in[l] += dot(xs_ref[l], w_in[l])
            acc_down[l] += dot(gs_ref[l], w_down[l], (1, 1))

    @pl.when(step == tiles - 1)
    def _():
        mixes = [
            jnp.concatenate([ref[...] for ref in mix_refs[sum(counts[:t]) : sum(counts[: t + 1])]], axis=0)
            for t in range(groups)
        ]
        lanes = mixes[0].shape[1]
        lane = lax.broadcasted_iota(jnp.int32, (1, lanes), 1)
        spread = []
        for l in range(local):
            expert = info[groups + chunks] + l
            weights = jnp.concatenate([dot(pick[t * local + l], mixes[t]) for t in range(groups)], axis=0)
            weights = jnp.sum(
                jnp.where(lane % (lanes // 2) == expert, weights, 0.0), axis=1, keepdims=True
            )
            grad = acc_down[l]
            hidden, d_gate, d_up = silu_back(acc_in[l, :, :width], acc_in[l, :, width:], grad * weights)
            terms = jnp.sum(hidden * grad, axis=1, keepdims=True)
            hidden_ref[l] = (hidden * weights).astype(bf16)
            pre_ref[l, :, :width] = d_gate
            pre_ref[l, :, width:] = d_up
            spread.append(jnp.where(lane == expert, terms, 0.0).astype(bf16))
        for t in range(groups):
            rows = slice(t * capacity, (t + 1) * capacity)
            term_buf[t] = dot(
                put[t], jnp.concatenate([terms[rows] for terms in spread], axis=0)
            ).astype(bf16)
        hidden, d_gate, d_up = silu_back(s_acc_in[:, :s_width], s_acc_in[:, s_width:], s_acc_down[...])
        s_hidden_ref[...] = hidden.astype(bf16)
        s_pre_ref[:, :s_width] = d_gate
        s_pre_ref[:, s_width:] = d_up

    @pl.when((step >= tiles) & (step < 2 * tiles))
    def _():
        pieces = [dot(hidden_ref[l], w_down[l]).astype(bf16) for l in range(local)]
        d_pieces = [dot(pre_ref[l], w_in[l], (1, 1)).astype(bf16) for l in range(local)]
        for t in range(groups):
            rows = slice(t * capacity, (t + 1) * capacity)
            out = dot(put[t], jnp.concatenate([piece[rows] for piece in pieces], axis=0))
            norm = dot(put[t], jnp.concatenate([piece[rows] for piece in d_pieces], axis=0))
            if t == 0:
                out = out + dot(s_hidden_ref[...], s_down[...])
                norm = norm + dot(s_pre_ref[...], s_in[...], (1, 1))
            out_refs[t][...] = out.astype(bf16)
            norm_refs[t][...] = norm.astype(bf16)

    @pl.when(step == 2 * tiles)
    def _():
        for t in range(groups):
            norm_refs[t][:, : term_buf.shape[2]] = term_buf[t]


def experts_call(at, blocks, held, x_parts, g_all, info, slots, w_in, w_down, s_in, s_down, capacity, waits):
    counts = [len(parts) for parts in x_parts]
    x_parts = [x for parts in x_parts for x in parts]
    groups, local = len(counts), w_in.shape[0]
    chunks = info.shape[0] - groups - 2
    model, whole_width = g_all.shape[1], x_parts[0].shape[1]
    lanes = whole_width - model
    tokens = sum(x.shape[0] for x in x_parts[: counts[0]])
    tile = 512 if groups <= 2 else 256
    tiles = model // tile
    width, s_width = w_down.shape[1], s_down.shape[0]
    rows = groups * capacity

    def tokens_in(i, info):
        return (0, jnp.minimum(i, tiles - 1))

    def grads_in(t):
        return pl.BlockSpec((tokens, tile), lambda i, info: (info[t], jnp.minimum(i, tiles - 1)))

    def picked(i, info):
        return (0, at, jnp.minimum(i, tiles - 1))

    def own(i, info):
        return (at, jnp.minimum(i, tiles - 1))

    def summed(i, info):
        return (info[groups + chunks + 1], jnp.clip(i - tiles, 0, tiles - 1))

    def summed_norm(i, info):
        return (0, jnp.maximum(i - tiles, 0))

    in_specs = [
        *(pl.BlockSpec((x.shape[0], tile), tokens_in) for x in x_parts),
        *(pl.BlockSpec((x.shape[0], lanes), lambda i, info: (0, model // lanes)) for x in x_parts),
        *(grads_in(t) for t in range(groups)),
        whole_spec(slots.shape),
        whole_spec(slots.shape[::-1]),
        pl.BlockSpec((local, tile, 2 * width), lambda i, info: (0, i % tiles, 0)),
        pl.BlockSpec((local, width, tile), lambda i, info: (0, 0, i % tiles)),
        pl.BlockSpec((tile, 2 * s_width), lambda i, info: (i % tiles, 0)),
        pl.BlockSpec((s_width, tile), lambda i, info: (0, i % tiles)),
        *[in_place] * (len(held) + len(waits)),
    ]
    kept = (
        jax.ShapeDtypeStruct((local, blocks * rows, model), bf16),
        jax.ShapeDtypeStruct((local, blocks * rows, model), bf16),
        jax.ShapeDtypeStruct((local, blocks * rows, width), bf16),
        jax.ShapeDtypeStruct((local, blocks * rows, 2 * width), bf16),
        jax.ShapeDtypeStruct((blocks * tokens, model), bf16),
        jax.ShapeDtypeStruct((blocks * tokens, model), bf16),
        jax.ShapeDtypeStruct((blocks * tokens, s_width), bf16),
        jax.ShapeDtypeStruct((blocks * tokens, 2 * s_width), bf16),
        *[jax.ShapeDtypeStruct((blocks * tokens, model), bf16)] * groups,
    )
    norms = (jax.ShapeDtypeStruct((tokens, whole_width), bf16),) * groups
    out_specs = [
        pl.BlockSpec((local, rows, tile), picked),
        pl.BlockSpec((local, rows, tile), picked),
        pl.BlockSpec((local, rows, width), lambda i, info: (0, at, 0)),
        pl.BlockSpec((local, rows, 2 * width), lambda i, info: (0, at, 0)),
        pl.BlockSpec((tokens, tile), own),
        pl.BlockSpec((tokens, tile), own),
        pl.BlockSpec((tokens, s_width), lambda i, info: (at, 0)),
        pl.BlockSpec((tokens, 2 * s_width), lambda i, info: (at, 0)),
        *[pl.BlockSpec((tokens, tile), summed)] * groups,
        *[pl.BlockSpec((tokens, tile), summed_norm)] * groups,
    ]
    work = 2 * model * (
        4 * groups * local * capacity * tokens + 6 * local * rows * width + 6 * tokens * s_width
    )
    first = 1 + len(in_specs) - len(held) - len(waits)
    results = pl.pallas_call(
        functools.partial(experts_kernel, counts, len(held) + len(waits), local, tiles, chunks),
        out_shape=(*kept, *norms),
        grid_spec=pltpu.PrefetchScalarGridSpec(
            num_scalar_prefetch=1,
            grid=(2 * tiles + 1,),
            in_specs=in_specs,
            out_specs=out_specs,
            scratch_shapes=[
                pltpu.VMEM((groups * local, capacity, tokens), bf16),
                pltpu.VMEM((groups, tokens, local * capacity), bf16),
                pltpu.VMEM((local, rows, 2 * width), f32),
                pltpu.VMEM((local, rows, width), f32),
                pltpu.VMEM((tokens, 2 * s_width), f32),
                pltpu.VMEM((tokens, s_width), f32),
                pltpu.VMEM((groups, tokens, lanes), bf16),
            ],
        ),
        input_output_aliases={first + i: i for i in range(len(held))},
        compiler_params=pltpu.CompilerParams(vmem_limit_bytes=vmem_limit),
        cost_estimate=pl.CostEstimate(flops=work, bytes_accessed=2**10, transcendentals=0),
    )(info, *x_parts, *x_parts, *[g_all] * groups, slots, slots.T, w_in, w_down, s_in, s_down, *held, *waits)
    return list(results[: len(kept)]), list(results[len(kept) :])


def shards(
    inputs,
    routes,
    w_query,
    w_key,
    w_value,
    w_output,
    gain_attn,
    gain_moe,
    w_router,
    shared_gate,
    shared_up,
    shared_down,
    expert_gate,
    expert_up,
    expert_down,
    out_grad,
):
    e, r, c = lax.axis_index("exp"), lax.axis_index("row"), lax.axis_index("col")
    E, R, C = lax.axis_size("exp"), lax.axis_size("row"), lax.axis_size("col")
    local_count, model_width, _ = expert_gate.shape
    n_experts = local_count * E * R
    block_rows, top_count = routes.shape
    capacity = 4 * block_rows * top_count // (3 * n_experts)
    home_rows = block_rows // C
    head_width = HEAD_DIM
    query_width, key_width = w_query.shape[1], w_key.shape[1]
    group_heads = query_width // key_width
    attn_scale = head_width ** (-0.5)
    sources = ring_sources("col")

    x = tokens_home(inputs, 0).astype(f32)
    small = jnp.concatenate([w_router.T, gain_attn[None], gain_moe[None]], axis=0)
    small_all = jnp.zeros((small.shape[0], model_width), f32)
    for s, part in enumerate(exchange(small, "col")):
        small_all = lax.dynamic_update_slice(small_all, part, (0, (c ^ s) * small.shape[1]))
    router_t, gain_one, gain_two = (
        small_all[:n_experts],
        small_all[n_experts],
        small_all[n_experts + 1],
    )
    inv_one = rms_inverse(x)
    norm_one = (x * inv_one * gain_one[None, :]).astype(bf16)
    norm_one_parts = row_gather(norm_one)
    norm_one_all = jnp.concatenate(norm_one_parts, axis=0)

    own_in = own_share(jnp.concatenate([w_key, w_value, w_query], axis=1))
    weight_in = lax.all_gather(own_in, ("col", "exp"), tiled=True)
    g_block = lax.all_gather(
        after(out_grad, weight_in, *norm_one_parts[1:]), "col", axis=1, tiled=True
    )
    g = lax.dynamic_slice_in_dim(g_block, c * home_rows, home_rows, 0)
    raw = dot(norm_one_all, weight_in)
    wait = zero_of(raw)
    here = jnp.stack([e, c]).astype(jnp.int32)
    out_parts = exchange(own_share(w_output, wait), "col")
    weight_out = join_weight(here, exchange(jnp.stack(out_parts), "exp"))

    s_width = shared_gate.shape[1] // C
    s_padded = -(-s_width // 128) * 128

    def col_swap(parts):
        return jnp.stack([swap(parts[s], "col", s) if s else parts[0] for s in range(C)])

    shared_cut = cut_shared(here, shared_gate, shared_up, shared_down, C, E, raw)
    in_rows, feature_width = shared_gate.shape[0] // E, shared_down.shape[1]
    shared_parts = col_swap(shared_cut)
    sh_in, sh_down = join_shared(
        here, exchange(shared_parts, "exp"), in_rows, feature_width, s_padded
    )
    expert_in = side_by_side(expert_gate, expert_up, raw)

    own_routes = lax.dynamic_slice_in_dim(routes, c * home_rows, home_rows, 0)
    routes_here = routes.reshape(C, home_rows, top_count)[sources].reshape(block_rows, top_count)
    expert_ids = jnp.arange(n_experts)
    first_expert = (e * R + r) * local_count
    own_ids = first_expert + jnp.arange(local_count)
    earlier = (jnp.arange(block_rows)[:, None] < jnp.arange(block_rows)[None, :]).astype(bf16)
    routes_t = routes_here.T
    routes_t = routes_t + wait
    named = jnp.stack(
        [
            (block[None] == own_ids[:, None, None]).any(axis=1)
            for of_row in exchange(routes_t, "row")
            for block in exchange(of_row, "exp")
        ]
    ).reshape(R, E * local_count, block_rows)
    rank = dot(named.reshape(-1, block_rows).astype(bf16), earlier).astype(jnp.int32)
    slots = jnp.where(named, rank.reshape(named.shape), -1)

    positions = (
        ((r ^ jnp.arange(R)) * block_rows + c * home_rows)[:, None]
        + jnp.arange(home_rows)[None, :]
    ).reshape(-1)
    cosines, sines = rope_tables(positions, head_width)
    own_rows = R * home_rows
    keys = rotate(raw[:, :key_width].reshape(own_rows, 1, head_width), cosines, sines)
    kv = jnp.concatenate([keys.reshape(own_rows, key_width), raw[:, key_width : 2 * key_width]], axis=1)
    kv_parts = exchange(kv.astype(bf16), "col")
    queries = rotate(
        raw[:, 2 * key_width :].reshape(own_rows, group_heads, head_width), cosines, sines
    )
    queries = (queries * attn_scale).astype(bf16).reshape(own_rows, query_width)
    place = jnp.concatenate([jnp.stack([r, c]), c ^ jnp.arange(C)]).astype(jnp.int32)
    attended, att_total, lse = attention_forward(place, queries, kv_parts, home_rows, (expert_in, shared_cut))
    attn_part = dot(attended, weight_out).astype(bf16)
    g_all = lax.all_gather(after(g_block, attended), ("exp", "row"), tiled=True)
    hidden_state = x + row_reduce(jnp.split(attn_part, R, axis=0))[0]
    inv_two = rms_inverse(hidden_state) + zero_of(*(shared_parts[s] for s in range(1, C))).astype(f32)
    norm_two = (hidden_state * inv_two * gain_two[None, :]).astype(bf16)

    norm_float = norm_two.astype(f32)
    logits = lax.dot_general(
        norm_float, router_t, (((1,), (1,)), ((), ())), precision=highest
    )
    router_probs = jax.nn.softmax(logits, axis=-1)
    routed = (own_routes[:, :, None] == expert_ids[None, None, :]).any(axis=1)
    chosen = jnp.where(routed, router_probs, 0.0)
    chosen_sum = jnp.sum(chosen, axis=1, keepdims=True)
    mix = chosen / chosen_sum

    mix_lanes = -(-n_experts // 64) * 64
    mix_first = lax.reduce_precision(mix, 8, 7)
    mix_pad = ((0, 0), (0, mix_lanes - n_experts))
    payload = jnp.concatenate(
        [
            norm_two,
            jnp.pad(mix_first.astype(bf16), mix_pad),
            jnp.pad((mix - mix_first).astype(bf16), mix_pad),
        ],
        axis=1,
    )
    payload = jnp.concatenate(ring_gather(payload, "col"), axis=0)
    payload_rows = row_gather(payload)
    if R == 4:
        payload_rows = [[x] for x in payload_rows[:3]] + [payload_rows[3:]]
    else:
        payload_rows = [[x] for x in payload_rows]

    def shared_gradients(kept):
        own_x, own_g, s_hidden, s_pre = kept[4:8]
        d_in = dot(own_x, s_pre, (0, 0)).astype(bf16)
        d_down = dot(s_hidden, own_g, (0, 0)).astype(bf16)
        return cut_shared_grads(here, d_in, d_down, C, E, s_width)

    kept, norms, moved = [], [], []
    for s in range(R):
        x_block = payload_rows[s]
        if E > 2 and kept:
            x_block = [after(x, kept[-1]) for x in x_block]
        info = jnp.concatenate(
            [(e ^ jnp.arange(E)) * R + (r ^ s), sources, jnp.stack([first_expert, r ^ s])]
        ).astype(jnp.int32)
        kept, norm = experts_call(
            s, R, kept, list(zip(*(exchange(x, "exp") for x in x_block))), g_all, info,
            slots[s], expert_in, expert_down, sh_in, sh_down, capacity, norms[-1:],
        )
        if s == R - 1:
            shared_grads = shared_gradients(kept)
        seen = [*moved, shared_grads[0]] if s == R - 1 else [x for later in ((1, 2), (3,))[s] for x in payload_rows[later]] if s < 2 else []
        if seen:
            norm = [norm[0], *(after(x, *seen) for x in norm[1:])]
        norms.append(reduce_parts(norm, "exp").astype(bf16))
        if s:
            moved.append(swap(norms[s], "row", s))
    kept, outs = kept[:8], kept[8:]
    rows_x, rows_g, hidden, pre = kept[:4]

    shared_back = col_swap(reduce_parts(shared_grads, "exp").astype(bf16))
    norm_block = norms[0].astype(f32)
    for x_sum in moved:
        norm_block = norm_block + x_sum.astype(f32)
    chunks = jnp.split(norm_block.astype(bf16), C, axis=0)
    home = ring_reduce(chunks, "col")
    d_norm, gate_terms = home[:, :model_width], home[:, model_width : model_width + n_experts]
    outs = [outs[0], *(after(x, norms[-1]) for x in outs[1:])]

    out_sum = after(reduce_parts(outs, "exp").astype(bf16), moved[-1], shared_back)
    out_rows = lax.psum_scatter(out_sum, "row", scatter_dimension=0, tiled=True)

    expert_width = expert_gate.shape[2]
    pre = after(pre, moved[-1])
    grad_expert_gate = batch_dot("lrd,lrf->ldf", rows_x, pre[:, :, :expert_width])
    grad_expert_up = batch_dot("lrd,lrf->ldf", rows_x, pre[:, :, expert_width:])
    grad_expert_down = batch_dot("lrf,lrd->lfd", after(hidden, moved[-1]), rows_g)
    inner = jnp.sum(mix * gate_terms, axis=1, keepdims=True)
    d_probs = jnp.where(routed, (gate_terms - inner) / chosen_sum, 0.0)
    d_logits = router_probs * (
        d_probs - jnp.sum(router_probs * d_probs, axis=1, keepdims=True)
    )
    d_norm = d_norm + jnp.dot(d_logits, router_t, precision=highest)
    d_norm = d_norm + zero_of(grad_expert_gate, grad_expert_up, grad_expert_down).astype(f32)
    router_part = lax.dot_general(
        d_logits, norm_float, (((0,), (0,)), ((), ())), precision=highest
    )
    d_v, gain_two_part = rms_backward(hidden_state, inv_two, gain_two, d_norm)
    d_hidden = g.astype(f32) + d_v
    d_attn = d_hidden.astype(bf16)
    d_attn_parts = row_gather(d_attn)
    d_attn_all = jnp.concatenate(d_attn_parts, axis=0)

    out_grads = batch_dot("sf,scd->cfd", attended, d_attn_all.reshape(own_rows, C, -1))
    out_grads = out_grads.astype(bf16).reshape(C * query_width, -1)

    d_attended = dot(d_attn_all, weight_out, (1, 1)).astype(bf16)
    out_chunks = jnp.split(after(out_rows, d_attended), C, axis=0)
    moe_out = ring_send(out_chunks[C - 1], "col", 1)
    d_queries, d_kv_parts = attention_backward(
        place, queries, d_attended, att_total, lse, kv_parts, home_rows,
        (out_grads,),
    )
    d_kv_parts = after(d_kv_parts, moe_out)
    d_kv = reduce_parts([d_kv_parts[k] for k in range(C)], "col")
    moe_out = after(moe_out, d_kv)
    for k in range(C - 2, 0, -1):
        moe_out = ring_send(add(out_chunks[k], moe_out).astype(bf16), "col", 1)
    moe_out = add(out_chunks[0], moe_out)
    d_query_raw = rotate(
        d_queries.reshape(own_rows, group_heads, head_width), cosines, -sines
    ) * attn_scale
    d_query_raw = d_query_raw.reshape(own_rows, query_width).astype(bf16)
    norm_one_late = after(norm_one_all, d_kv_parts)
    query_grads = dot(norm_one_late, d_query_raw, (0, 0)).astype(bf16)
    d_key_raw = rotate(d_kv[:, :key_width].reshape(own_rows, 1, head_width), cosines, -sines)
    d_kv_raw = jnp.concatenate(
        [d_key_raw.reshape(own_rows, key_width), d_kv[:, key_width:]], axis=1
    ).astype(bf16)
    norm_one_part = dot(jnp.concatenate([d_kv_raw, d_query_raw], axis=1), weight_in, (1, 1)).astype(bf16)
    d_norm_one, halfway = row_reduce(jnp.split(norm_one_part, R, axis=0))
    d_x, gain_one_part = rms_backward(x, inv_one, gain_one, d_norm_one)
    grad_inputs = tokens_back((d_hidden + d_x).astype(bf16))

    output = tokens_back((hidden_state + moe_out).astype(bf16))
    out_total, query_total = reduce_weight(out_grads), reduce_weight(query_grads)
    kv_grads = dot(after(norm_one_late, *halfway), d_kv_raw, (0, 0)).astype(bf16)
    kv_total = reduce_weight(after(kv_grads, query_total, d_norm_one))
    grad_output = all_shares(after(out_total, d_norm_one)).astype(f32)
    grad_query = all_shares(after(query_total, d_norm_one)).astype(f32)
    grad_kv = all_shares(kv_total).astype(f32)
    small_part = jnp.concatenate([router_part, gain_one_part[None], gain_two_part[None]], axis=0)
    width = small.shape[1]
    mine = [
        lax.dynamic_slice_in_dim(small_part, (c ^ s) * width, width, 1) for s in range(C)
    ]
    small_sum = all_sum(all_sum(reduce_parts(mine, "col"), "row"), "exp")

    grad_shared_gate, grad_shared_up, grad_shared_down = join_shared_grads(
        here, exchange(after(shared_back, d_norm_one), "exp"), in_rows, feature_width
    )
    return (
        output,
        grad_inputs,
        grad_query,
        grad_kv[:, :key_width],
        grad_kv[:, key_width:],
        grad_output,
        small_sum[n_experts],
        small_sum[n_experts + 1],
        small_sum[:n_experts].T,
        grad_shared_gate,
        grad_shared_up,
        grad_shared_down,
        grad_expert_gate,
        grad_expert_up,
        grad_expert_down,
    )


def solution(mesh):
    tokens, weight, experts = P(("exp", "row"), "col"), P("col", "row"), P(("exp", "row"), None, "col")
    expert_down, feature = P(("exp", "row"), "col", None), P("col")
    placed = (
        tokens,
        P(("exp", "row"), None),
        weight,
        weight,
        weight,
        P("row", "col"),
        feature,
        feature,
        P("col", None),
        weight,
        weight,
        P("row", "col"),
        experts,
        experts,
        expert_down,
        tokens,
    )
    return jax.shard_map(
        shards,
        mesh=mesh,
        in_specs=placed,
        out_specs=(
            tokens,
            tokens,
            weight,
            weight,
            weight,
            P("row", "col"),
            feature,
            feature,
            P("col", None),
            weight,
            weight,
            P("row", "col"),
            experts,
            experts,
            expert_down,
        ),
        check_vma=False,
    )
```

```python
import functools

import jax
import jax.numpy as jnp
from jax import lax
from jax.experimental import pallas as pl
from jax.experimental.pallas import tpu as pltpu
from jax.sharding import PartitionSpec as P

HEAD_DIM = 128

eps = 1e-05
theta = 500000.0
highest = lax.Precision.HIGHEST
masked_value = -1e30
f32 = jnp.float32
bf16 = jnp.bfloat16
vmem_limit = 56 * 2**20


def swap(x, axis, step):
    return lax.ppermute(x, axis, [(i, i ^ step) for i in range(lax.axis_size(axis))])


def exchange(x, axis):
    return [x] + [swap(x, axis, step) for step in range(1, lax.axis_size(axis))]


def reduce_parts(parts, axis):
    total = parts[0].astype(f32)
    for step in range(1, len(parts)):
        total = total + swap(parts[step], axis, step).astype(f32)
    return total


def all_sum(x, axis):
    step = 1
    while step < lax.axis_size(axis):
        x = x + swap(x, axis, step)
        step *= 2
    return x


def zero_of(*arrays):
    found = jnp.int32(0)
    for x in arrays:
        first = x[(slice(0, 1),) * x.ndim].reshape(())
        found = found + (first != first).astype(jnp.int32)
    return found


def after(x, *earlier):
    place = pl.BlockSpec(memory_space=pl.ANY)
    return pl.pallas_call(
        lambda *refs: None,
        out_shape=jax.ShapeDtypeStruct(x.shape, x.dtype),
        in_specs=[place] * (1 + len(earlier)),
        out_specs=place,
        input_output_aliases={0: 0},
    )(x, *earlier)


def ring_order(n):
    return [0] + list(range(1, n, 2)) + [i for i in range(n - 1, 0, -1) if i % 2 == 0]


def ring_pairs(n, back=False):
    order = ring_order(n)
    pairs = [(order[i], order[(i + 1) % n]) for i in range(n)]
    return [(b, a) for a, b in pairs] if back else pairs


def ring_sources(axis):
    n = lax.axis_size(axis)
    order = ring_order(n)
    place = jnp.array([order.index(i) for i in range(n)])[lax.axis_index(axis)]
    return jnp.array(order)[(place - jnp.arange(n)) % n]


def ring_gather(x, axis):
    parts, n = [x], lax.axis_size(axis)
    for _ in range(n - 1):
        parts.append(lax.ppermute(parts[-1], axis, ring_pairs(n)))
    return parts


def ring_send(x, axis, k):
    order = ring_order(lax.axis_size(axis))
    n = len(order)
    return lax.ppermute(x, axis, [(order[i], order[(i - k) % n]) for i in range(n)])


def ring_reduce(parts, axis):
    total = parts[0].astype(f32)
    for k in range(1, len(parts)):
        total = total + ring_send(parts[k], axis, k).astype(f32)
    return total


def row_gather(x):
    if lax.axis_size("row") != 4:
        return exchange(x, "row")
    x_near, y_near = swap(x, "row", 1), swap(x, "row", 2)
    middle = x.shape[0] // 2
    return [x, x_near, y_near, swap(y_near[:middle], "row", 1), swap(x_near[middle:], "row", 2)]


def add(left, right):
    return left.astype(f32) + right.astype(f32)


def row_reduce(blocks):
    if len(blocks) != 4:
        return reduce_parts(blocks, "row"), blocks[:1]
    own, x_near, y_near, far = blocks
    middle = own.shape[0] // 2
    far_x, far_y = swap(far[:middle], "row", 1), swap(far[middle:], "row", 2)
    y_first = add(y_near[:middle], far_x).astype(bf16)
    x_second = add(x_near[middle:], far_y).astype(bf16)
    y_sum = swap(jnp.concatenate([y_first, y_near[middle:]], axis=0), "row", 2)
    x_sum = swap(jnp.concatenate([x_near[:middle], x_second], axis=0), "row", 1)
    return add(own, x_sum) + y_sum.astype(f32), [far_x, far_y]


def tokens_home(x, wait):
    c, n = lax.axis_index("col"), lax.axis_size("col")
    rows, width = x.shape[0] // n, x.shape[1]
    whole = jnp.zeros((rows, n * width), x.dtype)
    for s in range(n):
        piece = lax.dynamic_slice_in_dim(x, (c ^ s) * rows + wait, rows, 0)
        piece = swap(piece, "col", s) if s else piece
        whole = lax.dynamic_update_slice(whole, piece, (0, (c ^ s) * width))
    return whole


def tokens_back(x):
    c, n = lax.axis_index("col"), lax.axis_size("col")
    rows, width = x.shape[0], x.shape[1] // n
    whole, moved = jnp.zeros((n * rows, width), x.dtype), []
    for s in range(n):
        piece = lax.dynamic_slice_in_dim(x, (c ^ s) * width, width, 1)
        if s:
            piece = swap(piece, "col", s)
            moved.append(piece)
        whole = lax.dynamic_update_slice(whole, piece, ((c ^ s) * rows, 0))
    return whole, moved


def own_share(weight, wait=0):
    share = weight.shape[0] // lax.axis_size("exp")
    return lax.dynamic_slice_in_dim(weight, lax.axis_index("exp") * share + wait, share, 0)


def all_shares(total):
    e = lax.axis_index("exp")
    shares = lax.axis_size("exp")
    whole = jnp.zeros((shares,) + total.shape, total.dtype)
    for t, piece in enumerate(exchange(total, "exp")):
        whole = lax.dynamic_update_index_in_dim(whole, piece, e ^ t, 0)
    return whole.reshape((shares * total.shape[0],) + total.shape[1:])


def reduce_weight(grad):
    return lax.psum_scatter(grad, ("col", "exp"), scatter_dimension=0, tiled=True)


def rope_tables(positions, head_width):
    half_width = head_width // 2
    frequency = theta ** (-2.0 * jnp.arange(half_width, dtype=f32) / head_width)
    angles = positions.astype(f32)[:, None] * frequency[None, :]
    return (jnp.cos(angles), jnp.sin(angles))


def rotate(source, cosines, sines):
    half_width = source.shape[-1] // 2
    first, second = source[..., :half_width], source[..., half_width:]
    cos_view, sin_view = cosines[:, None, :], sines[:, None, :]
    return jnp.concatenate(
        [first * cos_view - second * sin_view, first * sin_view + second * cos_view], axis=-1
    )


def dot(left, right, contract=(1, 0)):
    return lax.dot_general(
        left, right, (((contract[0],), (contract[1],)), ((), ())), preferred_element_type=f32
    )


def batch_dot(spec, left, right):
    return jnp.einsum(spec, left, right, preferred_element_type=f32)


def rms_inverse(values):
    return lax.rsqrt(jnp.mean(values * values, axis=1, keepdims=True) + eps)


def rms_backward(values, inv_rms, gain, grad_norm):
    scaled_grad = grad_norm * gain[None, :]
    inner = jnp.mean(scaled_grad * values, axis=1, keepdims=True)
    grad_values = inv_rms * (scaled_grad - values * (inv_rms * inv_rms * inner))
    return grad_values, jnp.sum(grad_norm * values * inv_rms, axis=0)


def place_keys(place, kv_refs, key_buf, value_buf, chunk):
    row, blocks, width = place[0], kv_refs[0].shape[0] // chunk, key_buf.shape[1]
    for k, ref in enumerate(kv_refs):
        for s in range(blocks):
            at = pl.multiple_of(((row ^ s) * len(kv_refs) + place[2 + k]) * chunk, chunk)
            key_buf[pl.ds(at, chunk), :] = ref[s * chunk : (s + 1) * chunk, :width]
            value_buf[pl.ds(at, chunk), :] = ref[s * chunk : (s + 1) * chunk, width:]


def head_rows(ref, rows, width):
    block = ref[rows, :]
    return jnp.concatenate(
        [block[:, h * width : (h + 1) * width] for h in range(block.shape[1] // width)], axis=0
    )


def scores_tile(place, key_tile, queries, block, tile, chunk):
    scores = dot(key_tile, queries, (1, 1))
    key_at = tile * key_tile.shape[0] + lax.broadcasted_iota(jnp.int32, scores.shape, 0)
    lane = lax.broadcasted_iota(jnp.int32, scores.shape, 1)
    query_at = block * key_tile.shape[0] + place[1] * chunk + lane % chunk
    return jnp.where(key_at <= query_at, scores, masked_value)


def attention_kernel(chunk, place, q_ref, *refs):
    kv_refs, (out_ref, total_ref, lse_ref, key_buf, value_buf) = refs[:-5], refs[-5:]
    width = key_buf.shape[1]
    blocks = q_ref.shape[0] // chunk
    tile_rows = key_buf.shape[0] // blocks
    place_keys(place, kv_refs, key_buf, value_buf, chunk)

    @pl.loop(0, blocks)
    def _(block):
        rows = pl.ds(pl.multiple_of((place[0] ^ block) * chunk, chunk), chunk)
        queries = head_rows(q_ref, rows, width)
        count = queries.shape[0]

        def step(tile, carry):
            peak, total, out = carry
            at = pl.ds(pl.multiple_of(tile * tile_rows, tile_rows), tile_rows)
            scores = scores_tile(place, key_buf[at, :], queries, block, tile, chunk)
            new_peak = jnp.maximum(peak, jnp.max(scores, axis=0, keepdims=True))
            weights = jnp.exp(scores - new_peak)
            shrink = jnp.exp(peak - new_peak)
            total = total * shrink + jnp.sum(weights, axis=0, keepdims=True)
            part = dot(value_buf[at, :], weights.astype(bf16), (0, 0))
            return new_peak, total, out * shrink + part

        start = (
            jnp.full((1, count), masked_value, f32),
            jnp.zeros((1, count), f32),
            jnp.zeros((width, count), f32),
        )
        peak, total, out = lax.fori_loop(0, block + 1, step, start)
        out = out / total
        total_ref[pl.ds(block, 1)] = out[None]
        lse_ref[pl.ds(block, 1)] = (peak + jnp.log(total))[None]
        for h in range(count // chunk):
            head = out[:, h * chunk : (h + 1) * chunk]
            out_ref[rows, h * width : (h + 1) * width] = head.T.astype(bf16)


def attention_back_kernel(chunk, place, q_ref, grad_ref, total_ref, lse_ref, *refs):
    kv_refs = refs[:-6]
    dq_ref, dkv_ref, key_buf, value_buf, dk_buf, dv_buf = refs[-6:]
    width = key_buf.shape[1]
    blocks = q_ref.shape[0] // chunk
    tile_rows = key_buf.shape[0] // blocks
    place_keys(place, kv_refs, key_buf, value_buf, chunk)
    dk_buf[...] = jnp.zeros_like(dk_buf)
    dv_buf[...] = jnp.zeros_like(dv_buf)

    @pl.loop(0, blocks)
    def _(block):
        rows = pl.ds(pl.multiple_of((place[0] ^ block) * chunk, chunk), chunk)
        queries = head_rows(q_ref, rows, width)
        grads = head_rows(grad_ref, rows, width)
        count = queries.shape[0]
        out = total_ref[pl.ds(block, 1)][0]
        lse = lse_ref[pl.ds(block, 1)][0]
        grads_t = jnp.concatenate(
            [grads[h * chunk : (h + 1) * chunk].astype(f32).T for h in range(count // chunk)], axis=1
        )
        inner = jnp.sum(out * grads_t, axis=0, keepdims=True)

        def step(tile, d_queries):
            at = pl.ds(pl.multiple_of(tile * tile_rows, tile_rows), tile_rows)
            keys = key_buf[at, :]
            scores = scores_tile(place, keys, queries, block, tile, chunk)
            probs = jnp.exp(scores - lse)
            d_probs = dot(value_buf[at, :], grads, (1, 1))
            d_scores = (probs * (d_probs - inner)).astype(bf16)
            dk_buf[at, :] += dot(d_scores, queries)
            dv_buf[at, :] += dot(probs.astype(bf16), grads)
            return d_queries + dot(keys, d_scores, (0, 0))

        d_queries = lax.fori_loop(0, block + 1, step, jnp.zeros((width, count), f32))
        for h in range(count // chunk):
            head = d_queries[:, h * chunk : (h + 1) * chunk]
            dq_ref[rows, h * width : (h + 1) * width] = head.T

    for k in range(len(kv_refs)):
        for s in range(blocks):
            at = pl.ds(pl.multiple_of(((place[0] ^ s) * len(kv_refs) + place[2 + k]) * chunk, chunk), chunk)
            dkv_ref[k, s * chunk : (s + 1) * chunk, :width] = dk_buf[at, :].astype(bf16)
            dkv_ref[k, s * chunk : (s + 1) * chunk, width:] = dv_buf[at, :].astype(bf16)


in_place = pl.BlockSpec(memory_space=pl.ANY)


def whole_spec(shape):
    return pl.BlockSpec(shape, lambda *_: (0,) * len(shape))


def side_by_side(left, right, wait):
    count, rows, width = left.shape
    tile = 512

    def kernel(left_ref, right_ref, _, both_ref):
        both_ref[:, :width] = left_ref[...]
        both_ref[:, width:] = right_ref[...]

    spec = pl.BlockSpec((None, tile, width), lambda i, j: (i, j, 0))
    return pl.pallas_call(
        kernel,
        out_shape=jax.ShapeDtypeStruct((count, rows, 2 * width), left.dtype),
        grid=(count, rows // tile),
        in_specs=[spec, spec, in_place],
        out_specs=pl.BlockSpec((None, tile, 2 * width), lambda i, j: (i, j, 0)),
        cost_estimate=pl.CostEstimate(flops=0, bytes_accessed=2**10, transcendentals=0),
    )(left, right, wait)


def rows_at(index, count):
    return pl.ds(pl.multiple_of(index * count, count), count)


def cut_call(kernel, info, operands, outs, waits=()):
    return pl.pallas_call(
        lambda info, *refs: kernel(info[0], info[1], *refs[: len(operands)], *refs[len(operands) + len(waits) :]),
        out_shape=outs,
        grid_spec=pltpu.PrefetchScalarGridSpec(
            num_scalar_prefetch=1,
            grid=(1,),
            in_specs=[whole_spec(x.shape) for x in operands] + [in_place] * len(waits),
            out_specs=[whole_spec(x.shape) for x in outs],
        ),
        compiler_params=pltpu.CompilerParams(vmem_limit_bytes=vmem_limit),
        cost_estimate=pl.CostEstimate(flops=0, bytes_accessed=2**10, transcendentals=0),
    )(info, *operands, *waits)


def join_weight(info, parts):
    cols, rows, width = parts[0].shape

    def kernel(e, c, *refs):
        for s in range(cols):
            for t, ref in enumerate(refs[:-1]):
                refs[-1][rows_at(e ^ t, rows), rows_at(c ^ s, width)] = ref[s]

    outs = (jax.ShapeDtypeStruct((len(parts) * rows, cols * width), parts[0].dtype),)
    return cut_call(kernel, info, parts, outs)[0]


def each_index(index, count, work):
    for j in range(count):
        pl.when(index == j)(functools.partial(work, j))


def lanes_at(index, width, first, count):
    return pl.ds(pl.multiple_of(index * width + first, 128), count)


def cut_shared(info, gate, up, down, cols, shares, wait):
    rows, width, features = gate.shape[0] // shares, gate.shape[1] // cols, down.shape[1]
    both, down_rows = 2 * width, gate.shape[1] // cols // shares

    def kernel(e, c, gate_ref, up_ref, down_ref, out):
        for k in range(cols):
            at = rows_at(e, rows)
            out[c ^ k, :rows, :width] = gate_ref[at, k * width : (k + 1) * width]
            out[c ^ k, :rows, width:] = up_ref[at, k * width : (k + 1) * width]

        def cut_down(j):
            for k in range(cols):
                piece = down_ref[k * width + j * down_rows : k * width + (j + 1) * down_rows, :]
                out[c ^ k, rows : rows + down_rows, :] = piece[:, :both]
                out[c ^ k, rows + down_rows :, : features - both] = piece[:, both:]

        each_index(e, shares, cut_down)

    outs = (jax.ShapeDtypeStruct((cols, rows + 2 * down_rows, both), bf16),)
    return cut_call(kernel, info, (gate, up, down), outs, (wait,))[0]


def join_shared(info, parts, rows, features, padded):
    cols, all_rows, both = parts[0].shape
    width, shares, down_rows = both // 2, len(parts), (all_rows - rows) // 2

    def kernel(e, c, *refs):
        in_out, down_out = refs[-2:]
        in_out[...] = jnp.zeros_like(in_out)
        down_out[...] = jnp.zeros_like(down_out)
        for s in range(cols):
            for t, ref in enumerate(refs[:-2]):
                at = rows_at((c ^ s) * shares + (e ^ t), rows)
                in_out[at, :width] = ref[s, :rows, :width]
                in_out[at, padded : padded + width] = ref[s, :rows, width:]

        def join_down(j):
            for s in range(cols):
                for t, ref in enumerate(refs[:-2]):
                    at = slice((j ^ t) * down_rows, ((j ^ t) + 1) * down_rows)
                    down_out[at, lanes_at(c ^ s, features, 0, both)] = ref[s, rows : rows + down_rows, :]
                    down_out[at, lanes_at(c ^ s, features, both, features - both)] = ref[
                        s, rows + down_rows :, : features - both
                    ]

        each_index(e, shares, join_down)

    outs = (
        jax.ShapeDtypeStruct((cols * shares * rows, 2 * padded), bf16),
        jax.ShapeDtypeStruct((padded, cols * features), bf16),
    )
    return cut_call(kernel, info, parts, outs)


def cut_shared_grads(info, grad_in, grad_down, cols, shares, width):
    rows, padded = grad_in.shape[0] // (cols * shares), grad_in.shape[1] // 2
    both, down_rows, features = 2 * width, width // shares, grad_down.shape[1] // cols

    def kernel(e, c, in_ref, down_ref, *outs):
        for s in range(cols):
            for t, out in enumerate(outs):
                at = rows_at((c ^ s) * shares + (e ^ t), rows)
                out[s, :rows, :width] = in_ref[at, :width]
                out[s, :rows, width:] = in_ref[at, padded : padded + width]

        def cut_down(j):
            for s in range(cols):
                for t, out in enumerate(outs):
                    at = slice((j ^ t) * down_rows, ((j ^ t) + 1) * down_rows)
                    out[s, rows : rows + down_rows, :] = down_ref[at, lanes_at(c ^ s, features, 0, both)]
                    out[s, rows + down_rows :, : features - both] = down_ref[
                        at, lanes_at(c ^ s, features, both, features - both)
                    ]

        each_index(e, shares, cut_down)

    outs = (jax.ShapeDtypeStruct((cols, rows + 2 * down_rows, both), bf16),) * shares
    return cut_call(kernel, info, (grad_in, grad_down), outs)


def join_shared_grads(info, parts, rows, features):
    cols, all_rows, both = parts[0].shape
    width, shares, down_rows = both // 2, len(parts), (all_rows - rows) // 2

    def kernel(e, c, *refs):
        gate_out, up_out, down_out = refs[-3:]
        for k in range(cols):
            for t, ref in enumerate(refs[:-3]):
                at, part = rows_at(e ^ t, rows), ref[c ^ k, :rows, :].astype(f32)
                gate_out[at, k * width : (k + 1) * width] = part[:, :width]
                up_out[at, k * width : (k + 1) * width] = part[:, width:]

        def join_down(j):
            for k in range(cols):
                for t, ref in enumerate(refs[:-3]):
                    at = k * width + (j ^ t) * down_rows
                    at = slice(at, at + down_rows)
                    down_out[at, :both] = ref[c ^ k, rows : rows + down_rows, :].astype(f32)
                    down_out[at, both:] = ref[c ^ k, rows + down_rows :, : features - both].astype(f32)

        each_index(e, shares, join_down)

    outs = (
        *[jax.ShapeDtypeStruct((shares * rows, cols * width), f32)] * 2,
        jax.ShapeDtypeStruct((cols * width, features), f32),
    )
    return cut_call(kernel, info, parts, outs)


def attention_call(kernel, place, operands, outs, scratch, work, waits):
    return pl.pallas_call(
        lambda place, *refs: kernel(place, *refs[: len(operands)], *refs[len(operands) + len(waits) :]),
        out_shape=outs,
        grid_spec=pltpu.PrefetchScalarGridSpec(
            num_scalar_prefetch=1,
            grid=(1,),
            in_specs=[whole_spec(x.shape) for x in operands] + [in_place] * len(waits),
            out_specs=[whole_spec(x.shape) for x in outs],
            scratch_shapes=scratch,
        ),
        compiler_params=pltpu.CompilerParams(vmem_limit_bytes=vmem_limit),
        cost_estimate=pl.CostEstimate(
            flops=work, bytes_accessed=2**10, transcendentals=0
        ),
    )(place, *operands, *waits)


def attention_forward(place, queries, kv_parts, chunk, waits):
    rows, total_width = queries.shape
    width = kv_parts[0].shape[1] // 2
    heads, blocks, keys = total_width // width, rows // chunk, rows * len(kv_parts)
    return attention_call(
        functools.partial(attention_kernel, chunk),
        place,
        (queries, *kv_parts),
        (
            jax.ShapeDtypeStruct((rows, total_width), bf16),
            jax.ShapeDtypeStruct((blocks, width, heads * chunk), f32),
            jax.ShapeDtypeStruct((blocks, 1, heads * chunk), f32),
        ),
        [pltpu.VMEM((keys, width), bf16)] * 2,
        4 * rows * heads * keys * width,
        waits,
    )


def attention_backward(place, queries, grads, out, lse, kv_parts, chunk, waits):
    rows, total_width = queries.shape
    width = kv_parts[0].shape[1] // 2
    keys = rows * len(kv_parts)
    return attention_call(
        functools.partial(attention_back_kernel, chunk),
        place,
        (queries, grads, out, lse, *kv_parts),
        (
            jax.ShapeDtypeStruct((rows, total_width), f32),
            jax.ShapeDtypeStruct((len(kv_parts), rows, 2 * width), bf16),
        ),
        [pltpu.VMEM((keys, width), bf16)] * 2 + [pltpu.VMEM((keys, width), f32)] * 2,
        10 * rows * total_width * keys,
        waits,
    )


def silu_back(gate_pre, up_pre, grad_hidden):
    sigmoid_vals = jax.nn.sigmoid(gate_pre)
    silu = gate_pre * sigmoid_vals
    grad_gate = grad_hidden * up_pre * sigmoid_vals * (1.0 + gate_pre * (1.0 - sigmoid_vals))
    return silu * up_pre, grad_gate.astype(bf16), (grad_hidden * silu).astype(bf16)


def experts_kernel(counts, unused, local, tiles, chunks, info, *refs):
    groups = len(counts)
    x_refs, refs = refs[: sum(counts)], refs[sum(counts) :]
    mix_refs, refs = refs[: sum(counts)], refs[sum(counts) :]
    g_refs, refs = refs[:groups], refs[groups:]
    refs = refs[:6] + refs[6 + unused :]
    (
        slot_ref, slot_t_ref, w_in, w_down, s_in, s_down,
        xs_ref, gs_ref, hidden_ref, pre_ref, own_x_ref, own_g_ref, s_hidden_ref, s_pre_ref,
    ), refs = refs[:14], refs[14:]
    out_refs, refs = refs[:groups], refs[groups:]
    norm_refs, refs = refs[:groups], refs[groups:]
    pick, put, acc_in, acc_down, s_acc_in, s_acc_down, term_buf = refs
    step = pl.program_id(0)
    capacity, tokens = pick.shape[1], pick.shape[2]
    width, s_width = w_down.shape[1], s_down.shape[0]

    @pl.when(step == 0)
    def _():
        for at in range(groups * local):
            slots = lax.broadcasted_iota(jnp.int32, (capacity, tokens), 0)
            pick[at] = jnp.where(slots == slot_ref[at : at + 1, :], 1.0, 0.0).astype(bf16)
            slots = lax.broadcasted_iota(jnp.int32, (tokens, capacity), 1)
            put[at // local, :, (at % local) * capacity : (at % local + 1) * capacity] = jnp.where(
                slots == slot_t_ref[:, at : at + 1], 1.0, 0.0
            ).astype(bf16)
        acc_in[...] = jnp.zeros_like(acc_in)
        acc_down[...] = jnp.zeros_like(acc_down)
        s_acc_in[...] = jnp.zeros_like(s_acc_in)
        s_acc_down[...] = jnp.zeros_like(s_acc_down)

    @pl.when(step < tiles)
    def _():
        for t in range(groups):
            parts = slice(sum(counts[:t]), sum(counts[: t + 1]))
            x = jnp.concatenate([ref[...] for ref in x_refs[parts]], axis=0)
            chunk = tokens // chunks
            g = jnp.concatenate(
                [
                    g_refs[t][pl.ds(pl.multiple_of(info[groups + k] * chunk, chunk), chunk), :]
                    for k in range(chunks)
                ],
                axis=0,
            )
            for l in range(local):
                rows = slice(t * capacity, (t + 1) * capacity)
                xs_ref[l, rows, :] = dot(pick[t * local + l], x).astype(bf16)
                gs_ref[l, rows, :] = dot(pick[t * local + l], g).astype(bf16)
            if t == 0:
                own_x_ref[...] = x
                own_g_ref[...] = g
                s_acc_in[...] += dot(x, s_in[...])
                s_acc_down[...] += dot(g, s_down[...], (1, 1))
        for l in range(local):
            acc_in[l] += dot(xs_ref[l], w_in[l])
            acc_down[l] += dot(gs_ref[l], w_down[l], (1, 1))

    @pl.when(step == tiles - 1)
    def _():
        mixes = [
            jnp.concatenate([ref[...] for ref in mix_refs[sum(counts[:t]) : sum(counts[: t + 1])]], axis=0)
            for t in range(groups)
        ]
        lanes = mixes[0].shape[1]
        lane = lax.broadcasted_iota(jnp.int32, (1, lanes), 1)
        spread = []
        for l in range(local):
            expert = info[groups + chunks] + l
            weights = jnp.concatenate([dot(pick[t * local + l], mixes[t]) for t in range(groups)], axis=0)
            weights = jnp.sum(
                jnp.where(lane % (lanes // 2) == expert, weights, 0.0), axis=1, keepdims=True
            )
            grad = acc_down[l]
            hidden, d_gate, d_up = silu_back(acc_in[l, :, :width], acc_in[l, :, width:], grad * weights)
            terms = jnp.sum(hidden * grad, axis=1, keepdims=True)
            hidden_ref[l] = (hidden * weights).astype(bf16)
            pre_ref[l, :, :width] = d_gate
            pre_ref[l, :, width:] = d_up
            spread.append(jnp.where(lane == expert, terms, 0.0).astype(bf16))
        for t in range(groups):
            rows = slice(t * capacity, (t + 1) * capacity)
            term_buf[t] = dot(
                put[t], jnp.concatenate([terms[rows] for terms in spread], axis=0)
            ).astype(bf16)
        hidden, d_gate, d_up = silu_back(s_acc_in[:, :s_width], s_acc_in[:, s_width:], s_acc_down[...])
        s_hidden_ref[...] = hidden.astype(bf16)
        s_pre_ref[:, :s_width] = d_gate
        s_pre_ref[:, s_width:] = d_up

    @pl.when((step >= tiles) & (step < 2 * tiles))
    def _():
        pieces = [dot(hidden_ref[l], w_down[l]).astype(bf16) for l in range(local)]
        d_pieces = [dot(pre_ref[l], w_in[l], (1, 1)).astype(bf16) for l in range(local)]
        for t in range(groups):
            rows = slice(t * capacity, (t + 1) * capacity)
            out = dot(put[t], jnp.concatenate([piece[rows] for piece in pieces], axis=0))
            norm = dot(put[t], jnp.concatenate([piece[rows] for piece in d_pieces], axis=0))
            if t == 0:
                out = out + dot(s_hidden_ref[...], s_down[...])
                norm = norm + dot(s_pre_ref[...], s_in[...], (1, 1))
            out_refs[t][...] = out.astype(bf16)
            norm_refs[t][...] = norm.astype(bf16)

    @pl.when(step == 2 * tiles)
    def _():
        for t in range(groups):
            norm_refs[t][:, : term_buf.shape[2]] = term_buf[t]


def experts_call(at, blocks, held, x_parts, g_all, info, slots, w_in, w_down, s_in, s_down, capacity, waits):
    counts = [len(parts) for parts in x_parts]
    x_parts = [x for parts in x_parts for x in parts]
    groups, local = len(counts), w_in.shape[0]
    chunks = info.shape[0] - groups - 2
    model, whole_width = g_all.shape[1], x_parts[0].shape[1]
    lanes = whole_width - model
    tokens = sum(x.shape[0] for x in x_parts[: counts[0]])
    tile = 512 if groups <= 2 else 256
    tiles = model // tile
    width, s_width = w_down.shape[1], s_down.shape[0]
    rows = groups * capacity

    def tokens_in(i, info):
        return (0, jnp.minimum(i, tiles - 1))

    def grads_in(t):
        return pl.BlockSpec((tokens, tile), lambda i, info: (info[t], jnp.minimum(i, tiles - 1)))

    def picked(i, info):
        return (0, at, jnp.minimum(i, tiles - 1))

    def own(i, info):
        return (at, jnp.minimum(i, tiles - 1))

    def summed(i, info):
        return (info[groups + chunks + 1], jnp.clip(i - tiles, 0, tiles - 1))

    def summed_norm(i, info):
        return (0, jnp.maximum(i - tiles, 0))

    in_specs = [
        *(pl.BlockSpec((x.shape[0], tile), tokens_in) for x in x_parts),
        *(pl.BlockSpec((x.shape[0], lanes), lambda i, info: (0, model // lanes)) for x in x_parts),
        *(grads_in(t) for t in range(groups)),
        whole_spec(slots.shape),
        whole_spec(slots.shape[::-1]),
        pl.BlockSpec((local, tile, 2 * width), lambda i, info: (0, i % tiles, 0)),
        pl.BlockSpec((local, width, tile), lambda i, info: (0, 0, i % tiles)),
        pl.BlockSpec((tile, 2 * s_width), lambda i, info: (i % tiles, 0)),
        pl.BlockSpec((s_width, tile), lambda i, info: (0, i % tiles)),
        *[in_place] * (len(held) + len(waits)),
    ]
    kept = (
        jax.ShapeDtypeStruct((local, blocks * rows, model), bf16),
        jax.ShapeDtypeStruct((local, blocks * rows, model), bf16),
        jax.ShapeDtypeStruct((local, blocks * rows, width), bf16),
        jax.ShapeDtypeStruct((local, blocks * rows, 2 * width), bf16),
        jax.ShapeDtypeStruct((blocks * tokens, model), bf16),
        jax.ShapeDtypeStruct((blocks * tokens, model), bf16),
        jax.ShapeDtypeStruct((blocks * tokens, s_width), bf16),
        jax.ShapeDtypeStruct((blocks * tokens, 2 * s_width), bf16),
        *[jax.ShapeDtypeStruct((blocks * tokens, model), bf16)] * groups,
    )
    norms = (jax.ShapeDtypeStruct((tokens, whole_width), bf16),) * groups
    out_specs = [
        pl.BlockSpec((local, rows, tile), picked),
        pl.BlockSpec((local, rows, tile), picked),
        pl.BlockSpec((local, rows, width), lambda i, info: (0, at, 0)),
        pl.BlockSpec((local, rows, 2 * width), lambda i, info: (0, at, 0)),
        pl.BlockSpec((tokens, tile), own),
        pl.BlockSpec((tokens, tile), own),
        pl.BlockSpec((tokens, s_width), lambda i, info: (at, 0)),
        pl.BlockSpec((tokens, 2 * s_width), lambda i, info: (at, 0)),
        *[pl.BlockSpec((tokens, tile), summed)] * groups,
        *[pl.BlockSpec((tokens, tile), summed_norm)] * groups,
    ]
    work = 2 * model * (
        4 * groups * local * capacity * tokens + 6 * local * rows * width + 6 * tokens * s_width
    )
    first = 1 + len(in_specs) - len(held) - len(waits)
    results = pl.pallas_call(
        functools.partial(experts_kernel, counts, len(held) + len(waits), local, tiles, chunks),
        out_shape=(*kept, *norms),
        grid_spec=pltpu.PrefetchScalarGridSpec(
            num_scalar_prefetch=1,
            grid=(2 * tiles + 1,),
            in_specs=in_specs,
            out_specs=out_specs,
            scratch_shapes=[
                pltpu.VMEM((groups * local, capacity, tokens), bf16),
                pltpu.VMEM((groups, tokens, local * capacity), bf16),
                pltpu.VMEM((local, rows, 2 * width), f32),
                pltpu.VMEM((local, rows, width), f32),
                pltpu.VMEM((tokens, 2 * s_width), f32),
                pltpu.VMEM((tokens, s_width), f32),
                pltpu.VMEM((groups, tokens, lanes), bf16),
            ],
        ),
        input_output_aliases={first + i: i for i in range(len(held))},
        compiler_params=pltpu.CompilerParams(vmem_limit_bytes=vmem_limit),
        cost_estimate=pl.CostEstimate(flops=work, bytes_accessed=2**10, transcendentals=0),
    )(info, *x_parts, *x_parts, *[g_all] * groups, slots, slots.T, w_in, w_down, s_in, s_down, *held, *waits)
    return list(results[: len(kept)]), list(results[len(kept) :])


def shards(
    inputs,
    routes,
    w_query,
    w_key,
    w_value,
    w_output,
    gain_attn,
    gain_moe,
    w_router,
    shared_gate,
    shared_up,
    shared_down,
    expert_gate,
    expert_up,
    expert_down,
    out_grad,
):
    e, r, c = lax.axis_index("exp"), lax.axis_index("row"), lax.axis_index("col")
    E, R, C = lax.axis_size("exp"), lax.axis_size("row"), lax.axis_size("col")
    local_count, model_width, _ = expert_gate.shape
    n_experts = local_count * E * R
    block_rows, top_count = routes.shape
    capacity = 4 * block_rows * top_count // (3 * n_experts)
    home_rows = block_rows // C
    head_width = HEAD_DIM
    query_width, key_width = w_query.shape[1], w_key.shape[1]
    group_heads = query_width // key_width
    attn_scale = head_width ** (-0.5)
    sources = ring_sources("col")

    x = tokens_home(inputs, 0).astype(f32)
    small = jnp.concatenate([w_router.T, gain_attn[None], gain_moe[None]], axis=0)
    small_all = jnp.zeros((small.shape[0], model_width), f32)
    for s, part in enumerate(exchange(small, "col")):
        small_all = lax.dynamic_update_slice(small_all, part, (0, (c ^ s) * small.shape[1]))
    router_t, gain_one, gain_two = (
        small_all[:n_experts],
        small_all[n_experts],
        small_all[n_experts + 1],
    )
    inv_one = rms_inverse(x)
    norm_one = (x * inv_one * gain_one[None, :]).astype(bf16)
    norm_one_parts = row_gather(norm_one)
    norm_one_all = jnp.concatenate(norm_one_parts, axis=0)

    own_in = own_share(jnp.concatenate([w_key, w_value, w_query], axis=1))
    weight_in = lax.all_gather(own_in, ("col", "exp"), tiled=True)
    g_block = lax.all_gather(
        after(out_grad, weight_in, *norm_one_parts[1:]), "col", axis=1, tiled=True
    )
    g = lax.dynamic_slice_in_dim(g_block, c * home_rows, home_rows, 0)
    raw = dot(norm_one_all, weight_in)
    wait = zero_of(raw)
    here = jnp.stack([e, c]).astype(jnp.int32)
    out_parts = exchange(own_share(w_output, wait), "col")
    weight_out = join_weight(here, exchange(jnp.stack(out_parts), "exp"))

    s_width = shared_gate.shape[1] // C
    s_padded = -(-s_width // 128) * 128

    def col_swap(parts):
        return [swap(parts[s], "col", s) if s else parts[0] for s in range(C)]

    shared_cut = cut_shared(here, shared_gate, shared_up, shared_down, C, E, raw)
    in_rows, feature_width = shared_gate.shape[0] // E, shared_down.shape[1]
    shared_parts = col_swap(shared_cut)
    shared_moved = shared_parts[1:]
    sh_in, sh_down = join_shared(
        here, exchange(jnp.stack(shared_parts), "exp"), in_rows, feature_width, s_padded
    )
    expert_in = side_by_side(expert_gate, expert_up, raw)

    own_routes = lax.dynamic_slice_in_dim(routes, c * home_rows, home_rows, 0)
    routes_here = routes.reshape(C, home_rows, top_count)[sources].reshape(block_rows, top_count)
    expert_ids = jnp.arange(n_experts)
    first_expert = (e * R + r) * local_count
    own_ids = first_expert + jnp.arange(local_count)
    earlier = (jnp.arange(block_rows)[:, None] < jnp.arange(block_rows)[None, :]).astype(bf16)
    routes_t = routes_here.T
    routes_t = routes_t + wait
    named = jnp.stack(
        [
            (block[None] == own_ids[:, None, None]).any(axis=1)
            for of_row in exchange(routes_t, "row")
            for block in exchange(of_row, "exp")
        ]
    ).reshape(R, E * local_count, block_rows)
    rank = dot(named.reshape(-1, block_rows).astype(bf16), earlier).astype(jnp.int32)
    slots = jnp.where(named, rank.reshape(named.shape), -1)

    positions = (
        ((r ^ jnp.arange(R)) * block_rows + c * home_rows)[:, None]
        + jnp.arange(home_rows)[None, :]
    ).reshape(-1)
    cosines, sines = rope_tables(positions, head_width)
    own_rows = R * home_rows
    keys = rotate(raw[:, :key_width].reshape(own_rows, 1, head_width), cosines, sines)
    kv = jnp.concatenate([keys.reshape(own_rows, key_width), raw[:, key_width : 2 * key_width]], axis=1)
    kv_parts = exchange(kv.astype(bf16), "col")
    queries = rotate(
        raw[:, 2 * key_width :].reshape(own_rows, group_heads, head_width), cosines, sines
    )
    queries = (queries * attn_scale).astype(bf16).reshape(own_rows, query_width)
    place = jnp.concatenate([jnp.stack([r, c]), c ^ jnp.arange(C)]).astype(jnp.int32)
    attended, att_total, lse = attention_forward(place, queries, kv_parts, home_rows, (expert_in, shared_cut, *out_parts[1:]))
    attn_part = dot(after(attended, *shared_moved), weight_out).astype(bf16)
    g_all = lax.all_gather(after(g_block, attended), ("exp", "row"), tiled=True)
    hidden_state = x + row_reduce(jnp.split(attn_part, R, axis=0))[0]
    inv_two = rms_inverse(hidden_state)
    norm_two = (hidden_state * inv_two * gain_two[None, :]).astype(bf16)

    norm_float = norm_two.astype(f32)
    logits = lax.dot_general(
        norm_float, router_t, (((1,), (1,)), ((), ())), precision=highest
    )
    router_probs = jax.nn.softmax(logits, axis=-1)
    routed = (own_routes[:, :, None] == expert_ids[None, None, :]).any(axis=1)
    chosen = jnp.where(routed, router_probs, 0.0)
    chosen_sum = jnp.sum(chosen, axis=1, keepdims=True)
    mix = chosen / chosen_sum

    mix_lanes = -(-n_experts // 64) * 64
    mix_first = lax.reduce_precision(mix, 8, 7)
    mix_pad = ((0, 0), (0, mix_lanes - n_experts))
    payload = jnp.concatenate(
        [
            norm_two,
            jnp.pad(mix_first.astype(bf16), mix_pad),
            jnp.pad((mix - mix_first).astype(bf16), mix_pad),
        ],
        axis=1,
    )
    payload = jnp.concatenate(ring_gather(payload, "col"), axis=0)
    payload_rows = row_gather(payload)
    if R == 4:
        payload_rows = [[x] for x in payload_rows[:3]] + [payload_rows[3:]]
    else:
        payload_rows = [[x] for x in payload_rows]

    def shared_gradients(kept):
        own_x, own_g, s_hidden, s_pre = kept[4:8]
        d_in = dot(own_x, s_pre, (0, 0)).astype(bf16)
        d_down = dot(s_hidden, own_g, (0, 0)).astype(bf16)
        return cut_shared_grads(here, d_in, d_down, C, E, s_width)

    kept, norms, moved = [], [], []
    for s in range(R):
        x_block = payload_rows[s]
        if E > 2 and kept:
            x_block = [after(x, kept[-1]) for x in x_block]
        info = jnp.concatenate(
            [(e ^ jnp.arange(E)) * R + (r ^ s), sources, jnp.stack([first_expert, r ^ s])]
        ).astype(jnp.int32)
        kept, norm = experts_call(
            s, R, kept, list(zip(*(exchange(x, "exp") for x in x_block))), g_all, info,
            slots[s], expert_in, expert_down, sh_in, sh_down, capacity, norms[-1:],
        )
        if s == R - 1:
            shared_grads = shared_gradients(kept)
        seen = [*moved, shared_grads[0]] if s == R - 1 else [x for later in ((1, 2), (3,))[s] for x in payload_rows[later]] if s < 2 else []
        if seen:
            norm = [norm[0], *(after(x, *seen) for x in norm[1:])]
        norms.append(reduce_parts(norm, "exp").astype(bf16))
        if s:
            moved.append(swap(norms[s], "row", s))
    kept, outs = kept[:8], kept[8:]
    rows_x, rows_g, hidden, pre = kept[:4]

    shared_sum = reduce_parts(shared_grads, "exp").astype(bf16)
    outs_moved = [swap(after(outs[t], norms[-1], shared_sum), "exp", t) for t in range(1, E)]
    shared_back = jnp.stack(col_swap(shared_sum))
    norm_block = norms[0].astype(f32)
    for x_sum in moved:
        norm_block = norm_block + x_sum.astype(f32)
    chunks = jnp.split(norm_block.astype(bf16), C, axis=0)
    home = ring_reduce(chunks, "col")
    d_norm, gate_terms = home[:, :model_width], home[:, model_width : model_width + n_experts]
    out_sum = outs[0].astype(f32)
    for part in outs_moved:
        out_sum = add(out_sum, part)
    out_sum = after(out_sum.astype(bf16), moved[-1], shared_back)
    out_rows = lax.psum_scatter(out_sum, "row", scatter_dimension=0, tiled=True)

    expert_width = expert_gate.shape[2]
    pre = after(pre, moved[-1])
    grad_expert_gate = batch_dot("lrd,lrf->ldf", rows_x, pre[:, :, :expert_width])
    grad_expert_up = batch_dot("lrd,lrf->ldf", rows_x, pre[:, :, expert_width:])
    grad_expert_down = batch_dot("lrf,lrd->lfd", after(hidden, moved[-1]), rows_g)
    inner = jnp.sum(mix * gate_terms, axis=1, keepdims=True)
    d_probs = jnp.where(routed, (gate_terms - inner) / chosen_sum, 0.0)
    d_logits = router_probs * (
        d_probs - jnp.sum(router_probs * d_probs, axis=1, keepdims=True)
    )
    d_norm = d_norm + jnp.dot(d_logits, router_t, precision=highest)
    d_norm = d_norm + zero_of(grad_expert_gate, grad_expert_up, grad_expert_down).astype(f32)
    router_part = lax.dot_general(
        d_logits, norm_float, (((0,), (0,)), ((), ())), precision=highest
    )
    d_v, gain_two_part = rms_backward(hidden_state, inv_two, gain_two, d_norm)
    d_hidden = g.astype(f32) + d_v
    d_attn = d_hidden.astype(bf16)
    d_attn_parts = row_gather(d_attn)
    d_attn_all = jnp.concatenate(d_attn_parts, axis=0)

    out_grads = batch_dot("sf,scd->cfd", attended, d_attn_all.reshape(own_rows, C, -1))
    out_grads = out_grads.astype(bf16).reshape(C * query_width, -1)

    d_attended = dot(d_attn_all, weight_out, (1, 1)).astype(bf16)
    out_chunks = jnp.split(after(out_rows, d_attended), C, axis=0)
    moe_out = ring_send(out_chunks[C - 1], "col", 1)
    d_queries, d_kv_parts = attention_backward(
        place, queries, d_attended, att_total, lse, kv_parts, home_rows,
        (out_grads,),
    )
    d_kv_parts = after(d_kv_parts, moe_out)
    d_kv = reduce_parts([d_kv_parts[k] for k in range(C)], "col")
    for k in range(C - 2, 0, -1):
        moe_out = ring_send(add(out_chunks[k], moe_out).astype(bf16), "col", 1)
    moe_out = add(out_chunks[0], moe_out)
    d_query_raw = rotate(
        d_queries.reshape(own_rows, group_heads, head_width), cosines, -sines
    ) * attn_scale
    d_query_raw = d_query_raw.reshape(own_rows, query_width).astype(bf16)
    norm_one_late = after(norm_one_all, d_kv_parts)
    query_grads = dot(norm_one_late, d_query_raw, (0, 0)).astype(bf16)
    d_key_raw = rotate(d_kv[:, :key_width].reshape(own_rows, 1, head_width), cosines, -sines)
    d_kv_raw = jnp.concatenate(
        [d_key_raw.reshape(own_rows, key_width), d_kv[:, key_width:]], axis=1
    ).astype(bf16)
    norm_one_part = dot(jnp.concatenate([d_kv_raw, d_query_raw], axis=1), weight_in, (1, 1)).astype(bf16)
    d_norm_one, halfway = row_reduce(jnp.split(norm_one_part, R, axis=0))
    d_x, gain_one_part = rms_backward(
        x, inv_one, gain_one + zero_of(moe_out).astype(f32), d_norm_one
    )
    grad_inputs, back = tokens_back((d_hidden + d_x).astype(bf16))

    output = tokens_back((hidden_state + moe_out).astype(bf16))[0]
    out_total, query_total = reduce_weight(out_grads), reduce_weight(query_grads)
    kv_grads = dot(after(norm_one_late, *halfway), d_kv_raw, (0, 0)).astype(bf16)
    kv_total = reduce_weight(after(kv_grads, query_total, d_norm_one))
    grad_output = all_shares(after(out_total, d_norm_one)).astype(f32)
    grad_query = all_shares(after(query_total, d_norm_one)).astype(f32)
    grad_kv = all_shares(kv_total).astype(f32)
    small_part = jnp.concatenate([router_part, gain_one_part[None], gain_two_part[None]], axis=0)
    small_part = small_part + zero_of(*back).astype(f32)
    width = small.shape[1]
    mine = [
        lax.dynamic_slice_in_dim(small_part, (c ^ s) * width, width, 1) for s in range(C)
    ]
    small_sum = all_sum(all_sum(reduce_parts(mine, "col"), "row"), "exp")

    grad_shared_gate, grad_shared_up, grad_shared_down = join_shared_grads(
        here, exchange(after(shared_back, d_norm_one), "exp"), in_rows, feature_width
    )
    return (
        output,
        grad_inputs,
        grad_query,
        grad_kv[:, :key_width],
        grad_kv[:, key_width:],
        grad_output,
        small_sum[n_experts],
        small_sum[n_experts + 1],
        small_sum[:n_experts].T,
        grad_shared_gate,
        grad_shared_up,
        grad_shared_down,
        grad_expert_gate,
        grad_expert_up,
        grad_expert_down,
    )


def solution(mesh):
    tokens, weight, experts = P(("exp", "row"), "col"), P("col", "row"), P(("exp", "row"), None, "col")
    expert_down, feature = P(("exp", "row"), "col", None), P("col")
    placed = (
        tokens,
        P(("exp", "row"), None),
        weight,
        weight,
        weight,
        P("row", "col"),
        feature,
        feature,
        P("col", None),
        weight,
        weight,
        P("row", "col"),
        experts,
        experts,
        expert_down,
        tokens,
    )
    return jax.shard_map(
        shards,
        mesh=mesh,
        in_specs=placed,
        out_specs=(
            tokens,
            tokens,
            weight,
            weight,
            weight,
            P("row", "col"),
            feature,
            feature,
            P("col", None),
            weight,
            weight,
            P("row", "col"),
            experts,
            experts,
            expert_down,
        ),
        check_vma=False,
    )
```

```python
import functools

import jax
import jax.numpy as jnp
from jax import lax
from jax.experimental import pallas as pl
from jax.experimental.pallas import tpu as pltpu
from jax.sharding import PartitionSpec as P

HEAD_DIM = 128

eps = 1e-05
theta = 500000.0
highest = lax.Precision.HIGHEST
masked_value = -1e30
f32 = jnp.float32
bf16 = jnp.bfloat16
vmem_limit = 56 * 2**20


def swap(x, axis, step):
    return lax.ppermute(x, axis, [(i, i ^ step) for i in range(lax.axis_size(axis))])


def exchange(x, axis):
    return [x] + [swap(x, axis, step) for step in range(1, lax.axis_size(axis))]


def reduce_parts(parts, axis):
    total = parts[0].astype(f32)
    for step in range(1, len(parts)):
        total = total + swap(parts[step], axis, step).astype(f32)
    return total


def all_sum(x, axis):
    step = 1
    while step < lax.axis_size(axis):
        x = x + swap(x, axis, step)
        step *= 2
    return x


def zero_of(*arrays):
    found = jnp.int32(0)
    for x in arrays:
        first = x[(slice(0, 1),) * x.ndim].reshape(())
        found = found + (first != first).astype(jnp.int32)
    return found


def after(x, *earlier):
    place = pl.BlockSpec(memory_space=pl.ANY)
    return pl.pallas_call(
        lambda *refs: None,
        out_shape=jax.ShapeDtypeStruct(x.shape, x.dtype),
        in_specs=[place] * (1 + len(earlier)),
        out_specs=place,
        input_output_aliases={0: 0},
    )(x, *earlier)


def ring_order(n):
    return [0] + list(range(1, n, 2)) + [i for i in range(n - 1, 0, -1) if i % 2 == 0]


def ring_pairs(n, back=False):
    order = ring_order(n)
    pairs = [(order[i], order[(i + 1) % n]) for i in range(n)]
    return [(b, a) for a, b in pairs] if back else pairs


def ring_sources(axis):
    n = lax.axis_size(axis)
    order = ring_order(n)
    place = jnp.array([order.index(i) for i in range(n)])[lax.axis_index(axis)]
    return jnp.array(order)[(place - jnp.arange(n)) % n]


def ring_gather(x, axis):
    parts, n = [x], lax.axis_size(axis)
    for _ in range(n - 1):
        parts.append(lax.ppermute(parts[-1], axis, ring_pairs(n)))
    return parts


def ring_send(x, axis, k):
    order = ring_order(lax.axis_size(axis))
    n = len(order)
    return lax.ppermute(x, axis, [(order[i], order[(i - k) % n]) for i in range(n)])


def ring_reduce(parts, axis):
    total = parts[0].astype(f32)
    for k in range(1, len(parts)):
        total = total + ring_send(parts[k], axis, k).astype(f32)
    return total


def row_gather(x):
    if lax.axis_size("row") != 4:
        return exchange(x, "row")
    x_near, y_near = swap(x, "row", 1), swap(x, "row", 2)
    middle = x.shape[0] // 2
    return [x, x_near, y_near, swap(y_near[:middle], "row", 1), swap(x_near[middle:], "row", 2)]


def add(left, right):
    return left.astype(f32) + right.astype(f32)


def row_reduce(blocks):
    if len(blocks) != 4:
        return reduce_parts(blocks, "row"), blocks[:1]
    own, x_near, y_near, far = blocks
    middle = own.shape[0] // 2
    far_x, far_y = swap(far[:middle], "row", 1), swap(far[middle:], "row", 2)
    y_first = add(y_near[:middle], far_x).astype(bf16)
    x_second = add(x_near[middle:], far_y).astype(bf16)
    y_sum = swap(jnp.concatenate([y_first, y_near[middle:]], axis=0), "row", 2)
    x_sum = swap(jnp.concatenate([x_near[:middle], x_second], axis=0), "row", 1)
    return add(own, x_sum) + y_sum.astype(f32), [far_x, far_y]


def tokens_home(x, wait):
    c, n = lax.axis_index("col"), lax.axis_size("col")
    rows, width = x.shape[0] // n, x.shape[1]
    whole = jnp.zeros((rows, n * width), x.dtype)
    for s in range(n):
        piece = lax.dynamic_slice_in_dim(x, (c ^ s) * rows + wait, rows, 0)
        piece = swap(piece, "col", s) if s else piece
        whole = lax.dynamic_update_slice(whole, piece, (0, (c ^ s) * width))
    return whole


def tokens_back(x):
    c, n = lax.axis_index("col"), lax.axis_size("col")
    rows, width = x.shape[0], x.shape[1] // n
    whole, moved = jnp.zeros((n * rows, width), x.dtype), []
    for s in range(n):
        piece = lax.dynamic_slice_in_dim(x, (c ^ s) * width, width, 1)
        if s:
            piece = swap(piece, "col", s)
            moved.append(piece)
        whole = lax.dynamic_update_slice(whole, piece, ((c ^ s) * rows, 0))
    return whole, moved


def own_share(weight, wait=0):
    share = weight.shape[0] // lax.axis_size("exp")
    return lax.dynamic_slice_in_dim(weight, lax.axis_index("exp") * share + wait, share, 0)


def all_shares(total):
    e = lax.axis_index("exp")
    shares = lax.axis_size("exp")
    whole = jnp.zeros((shares,) + total.shape, total.dtype)
    for t, piece in enumerate(exchange(total, "exp")):
        whole = lax.dynamic_update_index_in_dim(whole, piece, e ^ t, 0)
    return whole.reshape((shares * total.shape[0],) + total.shape[1:])


def reduce_weight(grad):
    return lax.psum_scatter(grad, ("col", "exp"), scatter_dimension=0, tiled=True)


def rope_tables(positions, head_width):
    half_width = head_width // 2
    frequency = theta ** (-2.0 * jnp.arange(half_width, dtype=f32) / head_width)
    angles = positions.astype(f32)[:, None] * frequency[None, :]
    return (jnp.cos(angles), jnp.sin(angles))


def rotate(source, cosines, sines):
    half_width = source.shape[-1] // 2
    first, second = source[..., :half_width], source[..., half_width:]
    cos_view, sin_view = cosines[:, None, :], sines[:, None, :]
    return jnp.concatenate(
        [first * cos_view - second * sin_view, first * sin_view + second * cos_view], axis=-1
    )


def dot(left, right, contract=(1, 0)):
    return lax.dot_general(
        left, right, (((contract[0],), (contract[1],)), ((), ())), preferred_element_type=f32
    )


def batch_dot(spec, left, right):
    return jnp.einsum(spec, left, right, preferred_element_type=f32)


def rms_inverse(values):
    return lax.rsqrt(jnp.mean(values * values, axis=1, keepdims=True) + eps)


def rms_backward(values, inv_rms, gain, grad_norm):
    scaled_grad = grad_norm * gain[None, :]
    inner = jnp.mean(scaled_grad * values, axis=1, keepdims=True)
    grad_values = inv_rms * (scaled_grad - values * (inv_rms * inv_rms * inner))
    return grad_values, jnp.sum(grad_norm * values * inv_rms, axis=0)


def place_keys(place, kv_refs, key_buf, value_buf, chunk):
    row, blocks, width = place[0], kv_refs[0].shape[0] // chunk, key_buf.shape[1]
    for k, ref in enumerate(kv_refs):
        for s in range(blocks):
            at = pl.multiple_of(((row ^ s) * len(kv_refs) + place[2 + k]) * chunk, chunk)
            key_buf[pl.ds(at, chunk), :] = ref[s * chunk : (s + 1) * chunk, :width]
            value_buf[pl.ds(at, chunk), :] = ref[s * chunk : (s + 1) * chunk, width:]


def head_rows(ref, rows, width):
    block = ref[rows, :]
    return jnp.concatenate(
        [block[:, h * width : (h + 1) * width] for h in range(block.shape[1] // width)], axis=0
    )


def scores_tile(place, key_tile, queries, block, tile, chunk):
    scores = dot(key_tile, queries, (1, 1))
    key_at = tile * key_tile.shape[0] + lax.broadcasted_iota(jnp.int32, scores.shape, 0)
    lane = lax.broadcasted_iota(jnp.int32, scores.shape, 1)
    query_at = block * key_tile.shape[0] + place[1] * chunk + lane % chunk
    return jnp.where(key_at <= query_at, scores, masked_value)


def attention_kernel(chunk, place, q_ref, *refs):
    kv_refs, (out_ref, total_ref, lse_ref, key_buf, value_buf) = refs[:-5], refs[-5:]
    width = key_buf.shape[1]
    blocks = q_ref.shape[0] // chunk
    tile_rows = key_buf.shape[0] // blocks
    place_keys(place, kv_refs, key_buf, value_buf, chunk)

    @pl.loop(0, blocks)
    def _(block):
        rows = pl.ds(pl.multiple_of((place[0] ^ block) * chunk, chunk), chunk)
        queries = head_rows(q_ref, rows, width)
        count = queries.shape[0]

        def step(tile, carry):
            peak, total, out = carry
            at = pl.ds(pl.multiple_of(tile * tile_rows, tile_rows), tile_rows)
            scores = scores_tile(place, key_buf[at, :], queries, block, tile, chunk)
            new_peak = jnp.maximum(peak, jnp.max(scores, axis=0, keepdims=True))
            weights = jnp.exp(scores - new_peak)
            shrink = jnp.exp(peak - new_peak)
            total = total * shrink + jnp.sum(weights, axis=0, keepdims=True)
            part = dot(value_buf[at, :], weights.astype(bf16), (0, 0))
            return new_peak, total, out * shrink + part

        start = (
            jnp.full((1, count), masked_value, f32),
            jnp.zeros((1, count), f32),
            jnp.zeros((width, count), f32),
        )
        peak, total, out = lax.fori_loop(0, block + 1, step, start)
        out = out / total
        total_ref[pl.ds(block, 1)] = out[None]
        lse_ref[pl.ds(block, 1)] = (peak + jnp.log(total))[None]
        for h in range(count // chunk):
            head = out[:, h * chunk : (h + 1) * chunk]
            out_ref[rows, h * width : (h + 1) * width] = head.T.astype(bf16)


def attention_back_kernel(chunk, place, q_ref, grad_ref, total_ref, lse_ref, *refs):
    kv_refs = refs[:-6]
    dq_ref, dkv_ref, key_buf, value_buf, dk_buf, dv_buf = refs[-6:]
    width = key_buf.shape[1]
    blocks = q_ref.shape[0] // chunk
    tile_rows = key_buf.shape[0] // blocks
    place_keys(place, kv_refs, key_buf, value_buf, chunk)
    dk_buf[...] = jnp.zeros_like(dk_buf)
    dv_buf[...] = jnp.zeros_like(dv_buf)

    @pl.loop(0, blocks)
    def _(block):
        rows = pl.ds(pl.multiple_of((place[0] ^ block) * chunk, chunk), chunk)
        queries = head_rows(q_ref, rows, width)
        grads = head_rows(grad_ref, rows, width)
        count = queries.shape[0]
        out = total_ref[pl.ds(block, 1)][0]
        lse = lse_ref[pl.ds(block, 1)][0]
        grads_t = jnp.concatenate(
            [grads[h * chunk : (h + 1) * chunk].astype(f32).T for h in range(count // chunk)], axis=1
        )
        inner = jnp.sum(out * grads_t, axis=0, keepdims=True)

        def step(tile, d_queries):
            at = pl.ds(pl.multiple_of(tile * tile_rows, tile_rows), tile_rows)
            keys = key_buf[at, :]
            scores = scores_tile(place, keys, queries, block, tile, chunk)
            probs = jnp.exp(scores - lse)
            d_probs = dot(value_buf[at, :], grads, (1, 1))
            d_scores = (probs * (d_probs - inner)).astype(bf16)
            dk_buf[at, :] += dot(d_scores, queries)
            dv_buf[at, :] += dot(probs.astype(bf16), grads)
            return d_queries + dot(keys, d_scores, (0, 0))

        d_queries = lax.fori_loop(0, block + 1, step, jnp.zeros((width, count), f32))
        for h in range(count // chunk):
            head = d_queries[:, h * chunk : (h + 1) * chunk]
            dq_ref[rows, h * width : (h + 1) * width] = head.T

    for k in range(len(kv_refs)):
        for s in range(blocks):
            at = pl.ds(pl.multiple_of(((place[0] ^ s) * len(kv_refs) + place[2 + k]) * chunk, chunk), chunk)
            dkv_ref[k, s * chunk : (s + 1) * chunk, :width] = dk_buf[at, :].astype(bf16)
            dkv_ref[k, s * chunk : (s + 1) * chunk, width:] = dv_buf[at, :].astype(bf16)


in_place = pl.BlockSpec(memory_space=pl.ANY)


def whole_spec(shape):
    return pl.BlockSpec(shape, lambda *_: (0,) * len(shape))


def side_by_side(left, right, wait):
    count, rows, width = left.shape
    tile = 512

    def kernel(left_ref, right_ref, _, both_ref):
        both_ref[:, :width] = left_ref[...]
        both_ref[:, width:] = right_ref[...]

    spec = pl.BlockSpec((None, tile, width), lambda i, j: (i, j, 0))
    return pl.pallas_call(
        kernel,
        out_shape=jax.ShapeDtypeStruct((count, rows, 2 * width), left.dtype),
        grid=(count, rows // tile),
        in_specs=[spec, spec, in_place],
        out_specs=pl.BlockSpec((None, tile, 2 * width), lambda i, j: (i, j, 0)),
        cost_estimate=pl.CostEstimate(flops=0, bytes_accessed=2**10, transcendentals=0),
    )(left, right, wait)


def rows_at(index, count):
    return pl.ds(pl.multiple_of(index * count, count), count)


def cut_call(kernel, info, operands, outs, waits=()):
    return pl.pallas_call(
        lambda info, *refs: kernel(info[0], info[1], *refs[: len(operands)], *refs[len(operands) + len(waits) :]),
        out_shape=outs,
        grid_spec=pltpu.PrefetchScalarGridSpec(
            num_scalar_prefetch=1,
            grid=(1,),
            in_specs=[whole_spec(x.shape) for x in operands] + [in_place] * len(waits),
            out_specs=[whole_spec(x.shape) for x in outs],
        ),
        compiler_params=pltpu.CompilerParams(vmem_limit_bytes=vmem_limit),
        cost_estimate=pl.CostEstimate(flops=0, bytes_accessed=2**10, transcendentals=0),
    )(info, *operands, *waits)


def join_weight(blocks, first, cols, shares):
    rows, width = blocks.shape[0] // (cols * shares), blocks.shape[1] - first

    def kernel(ref, out_ref):
        for k in range(cols):
            for t in range(shares):
                at = (k * shares + t) * rows
                out_ref[t * rows : (t + 1) * rows, k * width : (k + 1) * width] = ref[at : at + rows, first:]

    return pl.pallas_call(
        kernel,
        out_shape=jax.ShapeDtypeStruct((shares * rows, cols * width), blocks.dtype),
        compiler_params=pltpu.CompilerParams(vmem_limit_bytes=vmem_limit),
        cost_estimate=pl.CostEstimate(flops=0, bytes_accessed=2**10, transcendentals=0),
    )(blocks)


def each_index(index, count, work):
    for j in range(count):
        pl.when(index == j)(functools.partial(work, j))


def lanes_at(index, width, first, count):
    return pl.ds(pl.multiple_of(index * width + first, 128), count)


def cut_shared(info, gate, up, down, cols, shares, wait):
    rows, width, features = gate.shape[0] // shares, gate.shape[1] // cols, down.shape[1]
    both, down_rows = 2 * width, gate.shape[1] // cols // shares

    def kernel(e, c, gate_ref, up_ref, down_ref, out):
        for k in range(cols):
            at = rows_at(e, rows)
            out[c ^ k, :rows, :width] = gate_ref[at, k * width : (k + 1) * width]
            out[c ^ k, :rows, width:] = up_ref[at, k * width : (k + 1) * width]

        def cut_down(j):
            for k in range(cols):
                piece = down_ref[k * width + j * down_rows : k * width + (j + 1) * down_rows, :]
                out[c ^ k, rows : rows + down_rows, :] = piece[:, :both]
                out[c ^ k, rows + down_rows :, : features - both] = piece[:, both:]

        each_index(e, shares, cut_down)

    outs = (jax.ShapeDtypeStruct((cols, rows + 2 * down_rows, both), bf16),)
    return cut_call(kernel, info, (gate, up, down), outs, (wait,))[0]


def join_shared(info, parts, rows, features, padded):
    cols, all_rows, both = parts[0].shape
    width, shares, down_rows = both // 2, len(parts), (all_rows - rows) // 2

    def kernel(e, c, *refs):
        in_out, down_out = refs[-2:]
        in_out[...] = jnp.zeros_like(in_out)
        down_out[...] = jnp.zeros_like(down_out)
        for s in range(cols):
            for t, ref in enumerate(refs[:-2]):
                at = rows_at((c ^ s) * shares + (e ^ t), rows)
                in_out[at, :width] = ref[s, :rows, :width]
                in_out[at, padded : padded + width] = ref[s, :rows, width:]

        def join_down(j):
            for s in range(cols):
                for t, ref in enumerate(refs[:-2]):
                    at = slice((j ^ t) * down_rows, ((j ^ t) + 1) * down_rows)
                    down_out[at, lanes_at(c ^ s, features, 0, both)] = ref[s, rows : rows + down_rows, :]
                    down_out[at, lanes_at(c ^ s, features, both, features - both)] = ref[
                        s, rows + down_rows :, : features - both
                    ]

        each_index(e, shares, join_down)

    outs = (
        jax.ShapeDtypeStruct((cols * shares * rows, 2 * padded), bf16),
        jax.ShapeDtypeStruct((padded, cols * features), bf16),
    )
    return cut_call(kernel, info, parts, outs)


def cut_shared_grads(info, grad_in, grad_down, cols, shares, width):
    rows, padded = grad_in.shape[0] // (cols * shares), grad_in.shape[1] // 2
    both, down_rows, features = 2 * width, width // shares, grad_down.shape[1] // cols

    def kernel(e, c, in_ref, down_ref, *outs):
        for s in range(cols):
            for t, out in enumerate(outs):
                at = rows_at((c ^ s) * shares + (e ^ t), rows)
                out[s, :rows, :width] = in_ref[at, :width]
                out[s, :rows, width:] = in_ref[at, padded : padded + width]

        def cut_down(j):
            for s in range(cols):
                for t, out in enumerate(outs):
                    at = slice((j ^ t) * down_rows, ((j ^ t) + 1) * down_rows)
                    out[s, rows : rows + down_rows, :] = down_ref[at, lanes_at(c ^ s, features, 0, both)]
                    out[s, rows + down_rows :, : features - both] = down_ref[
                        at, lanes_at(c ^ s, features, both, features - both)
                    ]

        each_index(e, shares, cut_down)

    outs = (jax.ShapeDtypeStruct((cols, rows + 2 * down_rows, both), bf16),) * shares
    return cut_call(kernel, info, (grad_in, grad_down), outs)


def join_shared_grads(info, parts, rows, features):
    cols, all_rows, both = parts[0].shape
    width, shares, down_rows = both // 2, len(parts), (all_rows - rows) // 2

    def kernel(e, c, *refs):
        gate_out, up_out, down_out = refs[-3:]
        for k in range(cols):
            for t, ref in enumerate(refs[:-3]):
                at, part = rows_at(e ^ t, rows), ref[c ^ k, :rows, :].astype(f32)
                gate_out[at, k * width : (k + 1) * width] = part[:, :width]
                up_out[at, k * width : (k + 1) * width] = part[:, width:]

        def join_down(j):
            for k in range(cols):
                for t, ref in enumerate(refs[:-3]):
                    at = k * width + (j ^ t) * down_rows
                    at = slice(at, at + down_rows)
                    down_out[at, :both] = ref[c ^ k, rows : rows + down_rows, :].astype(f32)
                    down_out[at, both:] = ref[c ^ k, rows + down_rows :, : features - both].astype(f32)

        each_index(e, shares, join_down)

    outs = (
        *[jax.ShapeDtypeStruct((shares * rows, cols * width), f32)] * 2,
        jax.ShapeDtypeStruct((cols * width, features), f32),
    )
    return cut_call(kernel, info, parts, outs)


def attention_call(kernel, place, operands, outs, scratch, work, waits):
    return pl.pallas_call(
        lambda place, *refs: kernel(place, *refs[: len(operands)], *refs[len(operands) + len(waits) :]),
        out_shape=outs,
        grid_spec=pltpu.PrefetchScalarGridSpec(
            num_scalar_prefetch=1,
            grid=(1,),
            in_specs=[whole_spec(x.shape) for x in operands] + [in_place] * len(waits),
            out_specs=[whole_spec(x.shape) for x in outs],
            scratch_shapes=scratch,
        ),
        compiler_params=pltpu.CompilerParams(vmem_limit_bytes=vmem_limit),
        cost_estimate=pl.CostEstimate(
            flops=work, bytes_accessed=2**10, transcendentals=0
        ),
    )(place, *operands, *waits)


def attention_forward(place, queries, kv_parts, chunk, waits):
    rows, total_width = queries.shape
    width = kv_parts[0].shape[1] // 2
    heads, blocks, keys = total_width // width, rows // chunk, rows * len(kv_parts)
    return attention_call(
        functools.partial(attention_kernel, chunk),
        place,
        (queries, *kv_parts),
        (
            jax.ShapeDtypeStruct((rows, total_width), bf16),
            jax.ShapeDtypeStruct((blocks, width, heads * chunk), f32),
            jax.ShapeDtypeStruct((blocks, 1, heads * chunk), f32),
        ),
        [pltpu.VMEM((keys, width), bf16)] * 2,
        4 * rows * heads * keys * width,
        waits,
    )


def attention_backward(place, queries, grads, out, lse, kv_parts, chunk, waits):
    rows, total_width = queries.shape
    width = kv_parts[0].shape[1] // 2
    keys = rows * len(kv_parts)
    return attention_call(
        functools.partial(attention_back_kernel, chunk),
        place,
        (queries, grads, out, lse, *kv_parts),
        (
            jax.ShapeDtypeStruct((rows, total_width), f32),
            jax.ShapeDtypeStruct((len(kv_parts), rows, 2 * width), bf16),
        ),
        [pltpu.VMEM((keys, width), bf16)] * 2 + [pltpu.VMEM((keys, width), f32)] * 2,
        10 * rows * total_width * keys,
        waits,
    )


def silu_back(gate_pre, up_pre, grad_hidden):
    sigmoid_vals = jax.nn.sigmoid(gate_pre)
    silu = gate_pre * sigmoid_vals
    grad_gate = grad_hidden * up_pre * sigmoid_vals * (1.0 + gate_pre * (1.0 - sigmoid_vals))
    return silu * up_pre, grad_gate.astype(bf16), (grad_hidden * silu).astype(bf16)


def experts_kernel(counts, unused, local, tiles, chunks, info, *refs):
    groups = len(counts)
    x_refs, refs = refs[: sum(counts)], refs[sum(counts) :]
    mix_refs, refs = refs[: sum(counts)], refs[sum(counts) :]
    g_refs, refs = refs[:groups], refs[groups:]
    refs = refs[:6] + refs[6 + unused :]
    (
        slot_ref, slot_t_ref, w_in, w_down, s_in, s_down,
        xs_ref, gs_ref, hidden_ref, pre_ref, own_x_ref, own_g_ref, s_hidden_ref, s_pre_ref,
    ), refs = refs[:14], refs[14:]
    out_refs, refs = refs[:groups], refs[groups:]
    norm_refs, refs = refs[:groups], refs[groups:]
    pick, put, acc_in, acc_down, s_acc_in, s_acc_down, term_buf = refs
    step = pl.program_id(0)
    capacity, tokens = pick.shape[1], pick.shape[2]
    width, s_width = w_down.shape[1], s_down.shape[0]

    @pl.when(step == 0)
    def _():
        for at in range(groups * local):
            slots = lax.broadcasted_iota(jnp.int32, (capacity, tokens), 0)
            pick[at] = jnp.where(slots == slot_ref[at : at + 1, :], 1.0, 0.0).astype(bf16)
            slots = lax.broadcasted_iota(jnp.int32, (tokens, capacity), 1)
            put[at // local, :, (at % local) * capacity : (at % local + 1) * capacity] = jnp.where(
                slots == slot_t_ref[:, at : at + 1], 1.0, 0.0
            ).astype(bf16)
        acc_in[...] = jnp.zeros_like(acc_in)
        acc_down[...] = jnp.zeros_like(acc_down)
        s_acc_in[...] = jnp.zeros_like(s_acc_in)
        s_acc_down[...] = jnp.zeros_like(s_acc_down)

    @pl.when(step < tiles)
    def _():
        for t in range(groups):
            parts = slice(sum(counts[:t]), sum(counts[: t + 1]))
            x = jnp.concatenate([ref[...] for ref in x_refs[parts]], axis=0)
            chunk = tokens // chunks
            g = jnp.concatenate(
                [
                    g_refs[t][pl.ds(pl.multiple_of(info[k] * chunk, chunk), chunk), :]
                    for k in range(chunks)
                ],
                axis=0,
            )
            for l in range(local):
                rows = slice(t * capacity, (t + 1) * capacity)
                xs_ref[l, rows, :] = dot(pick[t * local + l], x).astype(bf16)
                gs_ref[l, rows, :] = dot(pick[t * local + l], g).astype(bf16)
            if t == 0:
                own_x_ref[...] = x
                own_g_ref[...] = g
                s_acc_in[...] += dot(x, s_in[...])
                s_acc_down[...] += dot(g, s_down[...], (1, 1))
        for l in range(local):
            acc_in[l] += dot(xs_ref[l], w_in[l])
            acc_down[l] += dot(gs_ref[l], w_down[l], (1, 1))

    @pl.when(step == tiles - 1)
    def _():
        mixes = [
            jnp.concatenate([ref[...] for ref in mix_refs[sum(counts[:t]) : sum(counts[: t + 1])]], axis=0)
            for t in range(groups)
        ]
        lanes = mixes[0].shape[1]
        lane = lax.broadcasted_iota(jnp.int32, (1, lanes), 1)
        spread = []
        for l in range(local):
            expert = info[chunks] + l
            weights = jnp.concatenate([dot(pick[t * local + l], mixes[t]) for t in range(groups)], axis=0)
            weights = jnp.sum(
                jnp.where(lane % (lanes // 2) == expert, weights, 0.0), axis=1, keepdims=True
            )
            grad = acc_down[l]
            hidden, d_gate, d_up = silu_back(acc_in[l, :, :width], acc_in[l, :, width:], grad * weights)
            terms = jnp.sum(hidden * grad, axis=1, keepdims=True)
            hidden_ref[l] = (hidden * weights).astype(bf16)
            pre_ref[l, :, :width] = d_gate
            pre_ref[l, :, width:] = d_up
            spread.append(jnp.where(lane == expert, terms, 0.0).astype(bf16))
        for t in range(groups):
            rows = slice(t * capacity, (t + 1) * capacity)
            term_buf[t] = dot(
                put[t], jnp.concatenate([terms[rows] for terms in spread], axis=0)
            ).astype(bf16)
        hidden, d_gate, d_up = silu_back(s_acc_in[:, :s_width], s_acc_in[:, s_width:], s_acc_down[...])
        s_hidden_ref[...] = hidden.astype(bf16)
        s_pre_ref[:, :s_width] = d_gate
        s_pre_ref[:, s_width:] = d_up

    @pl.when((step >= tiles) & (step < 2 * tiles))
    def _():
        pieces = [dot(hidden_ref[l], w_down[l]).astype(bf16) for l in range(local)]
        d_pieces = [dot(pre_ref[l], w_in[l], (1, 1)).astype(bf16) for l in range(local)]
        for t in range(groups):
            rows = slice(t * capacity, (t + 1) * capacity)
            out = dot(put[t], jnp.concatenate([piece[rows] for piece in pieces], axis=0))
            norm = dot(put[t], jnp.concatenate([piece[rows] for piece in d_pieces], axis=0))
            if t == 0:
                out = out + dot(s_hidden_ref[...], s_down[...])
                norm = norm + dot(s_pre_ref[...], s_in[...], (1, 1))
            out_refs[t][...] = out.astype(bf16)
            norm_refs[t][...] = norm.astype(bf16)

    @pl.when(step == 2 * tiles)
    def _():
        for t in range(groups):
            norm_refs[t][:, : term_buf.shape[2]] = term_buf[t]


def experts_call(at, blocks, held, x_parts, g_parts, info, slots, w_in, w_down, s_in, s_down, capacity, waits):
    counts = [len(parts) for parts in x_parts]
    x_parts = [x for parts in x_parts for x in parts]
    groups, local = len(counts), w_in.shape[0]
    chunks = info.shape[0] - 2
    model, whole_width = g_parts[0].shape[1], x_parts[0].shape[1]
    lanes = whole_width - model
    tokens = sum(x.shape[0] for x in x_parts[: counts[0]])
    tile = 512 if groups <= 2 else 256
    tiles = model // tile
    width, s_width = w_down.shape[1], s_down.shape[0]
    rows = groups * capacity

    def tokens_in(i, info):
        return (0, jnp.minimum(i, tiles - 1))

    def picked(i, info):
        return (0, at, jnp.minimum(i, tiles - 1))

    def own(i, info):
        return (at, jnp.minimum(i, tiles - 1))

    def summed(i, info):
        return (info[chunks + 1], jnp.clip(i - tiles, 0, tiles - 1))

    def summed_norm(i, info):
        return (0, jnp.maximum(i - tiles, 0))

    in_specs = [
        *(pl.BlockSpec((x.shape[0], tile), tokens_in) for x in x_parts),
        *(pl.BlockSpec((x.shape[0], lanes), lambda i, info: (0, model // lanes)) for x in x_parts),
        *[pl.BlockSpec((tokens, tile), tokens_in)] * groups,
        whole_spec(slots.shape),
        whole_spec(slots.shape[::-1]),
        pl.BlockSpec((local, tile, 2 * width), lambda i, info: (0, i % tiles, 0)),
        pl.BlockSpec((local, width, tile), lambda i, info: (0, 0, i % tiles)),
        pl.BlockSpec((tile, 2 * s_width), lambda i, info: (i % tiles, 0)),
        pl.BlockSpec((s_width, tile), lambda i, info: (0, i % tiles)),
        *[in_place] * (len(held) + len(waits)),
    ]
    kept = (
        jax.ShapeDtypeStruct((local, blocks * rows, model), bf16),
        jax.ShapeDtypeStruct((local, blocks * rows, model), bf16),
        jax.ShapeDtypeStruct((local, blocks * rows, width), bf16),
        jax.ShapeDtypeStruct((local, blocks * rows, 2 * width), bf16),
        jax.ShapeDtypeStruct((blocks * tokens, model), bf16),
        jax.ShapeDtypeStruct((blocks * tokens, model), bf16),
        jax.ShapeDtypeStruct((blocks * tokens, s_width), bf16),
        jax.ShapeDtypeStruct((blocks * tokens, 2 * s_width), bf16),
        *[jax.ShapeDtypeStruct((blocks * tokens, model), bf16)] * groups,
    )
    norms = (jax.ShapeDtypeStruct((tokens, whole_width), bf16),) * groups
    out_specs = [
        pl.BlockSpec((local, rows, tile), picked),
        pl.BlockSpec((local, rows, tile), picked),
        pl.BlockSpec((local, rows, width), lambda i, info: (0, at, 0)),
        pl.BlockSpec((local, rows, 2 * width), lambda i, info: (0, at, 0)),
        pl.BlockSpec((tokens, tile), own),
        pl.BlockSpec((tokens, tile), own),
        pl.BlockSpec((tokens, s_width), lambda i, info: (at, 0)),
        pl.BlockSpec((tokens, 2 * s_width), lambda i, info: (at, 0)),
        *[pl.BlockSpec((tokens, tile), summed)] * groups,
        *[pl.BlockSpec((tokens, tile), summed_norm)] * groups,
    ]
    work = 2 * model * (
        4 * groups * local * capacity * tokens + 6 * local * rows * width + 6 * tokens * s_width
    )
    first = 1 + len(in_specs) - len(held) - len(waits)
    results = pl.pallas_call(
        functools.partial(experts_kernel, counts, len(held) + len(waits), local, tiles, chunks),
        out_shape=(*kept, *norms),
        grid_spec=pltpu.PrefetchScalarGridSpec(
            num_scalar_prefetch=1,
            grid=(2 * tiles + 1,),
            in_specs=in_specs,
            out_specs=out_specs,
            scratch_shapes=[
                pltpu.VMEM((groups * local, capacity, tokens), bf16),
                pltpu.VMEM((groups, tokens, local * capacity), bf16),
                pltpu.VMEM((local, rows, 2 * width), f32),
                pltpu.VMEM((local, rows, width), f32),
                pltpu.VMEM((tokens, 2 * s_width), f32),
                pltpu.VMEM((tokens, s_width), f32),
                pltpu.VMEM((groups, tokens, lanes), bf16),
            ],
        ),
        input_output_aliases={first + i: i for i in range(len(held))},
        compiler_params=pltpu.CompilerParams(vmem_limit_bytes=vmem_limit),
        cost_estimate=pl.CostEstimate(flops=work, bytes_accessed=2**10, transcendentals=0),
    )(info, *x_parts, *x_parts, *g_parts, slots, slots.T, w_in, w_down, s_in, s_down, *held, *waits)
    return list(results[: len(kept)]), list(results[len(kept) :])


def shards(
    inputs,
    routes,
    w_query,
    w_key,
    w_value,
    w_output,
    gain_attn,
    gain_moe,
    w_router,
    shared_gate,
    shared_up,
    shared_down,
    expert_gate,
    expert_up,
    expert_down,
    out_grad,
):
    e, r, c = lax.axis_index("exp"), lax.axis_index("row"), lax.axis_index("col")
    E, R, C = lax.axis_size("exp"), lax.axis_size("row"), lax.axis_size("col")
    local_count, model_width, _ = expert_gate.shape
    n_experts = local_count * E * R
    block_rows, top_count = routes.shape
    capacity = 4 * block_rows * top_count // (3 * n_experts)
    home_rows = block_rows // C
    head_width = HEAD_DIM
    query_width, key_width = w_query.shape[1], w_key.shape[1]
    group_heads = query_width // key_width
    attn_scale = head_width ** (-0.5)
    sources = ring_sources("col")

    x = tokens_home(inputs, 0).astype(f32)
    small = jnp.concatenate([w_router.T, gain_attn[None], gain_moe[None]], axis=0)
    small_all = jnp.zeros((small.shape[0], model_width), f32)
    for s, part in enumerate(exchange(small, "col")):
        small_all = lax.dynamic_update_slice(small_all, part, (0, (c ^ s) * small.shape[1]))
    router_t, gain_one, gain_two = (
        small_all[:n_experts],
        small_all[n_experts],
        small_all[n_experts + 1],
    )
    inv_one = rms_inverse(x)
    norm_one = (x * inv_one * gain_one[None, :]).astype(bf16)
    norm_one_parts = row_gather(norm_one)
    norm_one_all = jnp.concatenate(norm_one_parts, axis=0)

    own_weights = own_share(jnp.concatenate([w_key, w_value, w_query, w_output], axis=1))
    weights = lax.all_gather(own_weights, ("col", "exp"), tiled=True)
    weight_in = weights[:, : query_width + 2 * key_width]
    raw = dot(norm_one_all, weight_in)
    wait = zero_of(raw)
    here = jnp.stack([e, c]).astype(jnp.int32)
    weight_out = join_weight(weights, query_width + 2 * key_width, C, E)

    s_width = shared_gate.shape[1] // C
    s_padded = -(-s_width // 128) * 128

    def col_swap(parts):
        return [swap(parts[s], "col", s) if s else parts[0] for s in range(C)]

    shared_cut = cut_shared(here, shared_gate, shared_up, shared_down, C, E, raw)
    in_rows, feature_width = shared_gate.shape[0] // E, shared_down.shape[1]
    expert_in = side_by_side(expert_gate, expert_up, raw)

    own_routes = lax.dynamic_slice_in_dim(routes, c * home_rows, home_rows, 0)
    routes_here = routes.reshape(C, home_rows, top_count)[sources].reshape(block_rows, top_count)
    expert_ids = jnp.arange(n_experts)
    first_expert = (e * R + r) * local_count
    own_ids = first_expert + jnp.arange(local_count)
    earlier = (jnp.arange(block_rows)[:, None] < jnp.arange(block_rows)[None, :]).astype(bf16)
    routes_t = routes_here.T
    routes_t = routes_t + wait
    named = jnp.stack(
        [
            (block[None] == own_ids[:, None, None]).any(axis=1)
            for of_row in exchange(routes_t, "row")
            for block in exchange(of_row, "exp")
        ]
    ).reshape(R, E * local_count, block_rows)
    rank = dot(named.reshape(-1, block_rows).astype(bf16), earlier).astype(jnp.int32)
    slots = jnp.where(named, rank.reshape(named.shape), -1)

    positions = (
        ((r ^ jnp.arange(R)) * block_rows + c * home_rows)[:, None]
        + jnp.arange(home_rows)[None, :]
    ).reshape(-1)
    cosines, sines = rope_tables(positions, head_width)
    own_rows = R * home_rows
    keys = rotate(raw[:, :key_width].reshape(own_rows, 1, head_width), cosines, sines)
    kv = jnp.concatenate([keys.reshape(own_rows, key_width), raw[:, key_width : 2 * key_width]], axis=1)
    kv_parts = exchange(kv.astype(bf16), "col")
    g_block = lax.all_gather(after(out_grad, *kv_parts[1:]), "col", axis=1, tiled=True)
    g = lax.dynamic_slice_in_dim(g_block, c * home_rows, home_rows, 0)
    queries = rotate(
        raw[:, 2 * key_width :].reshape(own_rows, group_heads, head_width), cosines, sines
    )
    queries = (queries * attn_scale).astype(bf16).reshape(own_rows, query_width)
    place = jnp.concatenate([jnp.stack([r, c]), c ^ jnp.arange(C)]).astype(jnp.int32)
    attended, att_total, lse = attention_forward(place, queries, kv_parts, home_rows, (expert_in, shared_cut))
    attn_part = dot(attended, weight_out).astype(bf16)
    shared_parts = col_swap(after(shared_cut, attended))
    sh_in, sh_down = join_shared(
        here, exchange(jnp.stack(shared_parts), "exp"), in_rows, feature_width, s_padded
    )
    hidden_state = x + row_reduce(jnp.split(attn_part, R, axis=0))[0]
    inv_two = rms_inverse(hidden_state) + zero_of(g_block, *shared_parts[1:]).astype(f32)
    norm_two = (hidden_state * inv_two * gain_two[None, :]).astype(bf16)

    norm_float = norm_two.astype(f32)
    logits = lax.dot_general(
        norm_float, router_t, (((1,), (1,)), ((), ())), precision=highest
    )
    router_probs = jax.nn.softmax(logits, axis=-1)
    routed = (own_routes[:, :, None] == expert_ids[None, None, :]).any(axis=1)
    chosen = jnp.where(routed, router_probs, 0.0)
    chosen_sum = jnp.sum(chosen, axis=1, keepdims=True)
    mix = chosen / chosen_sum

    mix_lanes = -(-n_experts // 64) * 64
    mix_first = lax.reduce_precision(mix, 8, 7)
    mix_pad = ((0, 0), (0, mix_lanes - n_experts))
    payload = jnp.concatenate(
        [
            norm_two,
            jnp.pad(mix_first.astype(bf16), mix_pad),
            jnp.pad((mix - mix_first).astype(bf16), mix_pad),
        ],
        axis=1,
    )
    payload = jnp.concatenate(ring_gather(payload, "col"), axis=0)
    grad_rows = row_gather(g_block)
    payload = after(payload, *grad_rows[1:3])
    payload_rows = row_gather(payload)
    if R == 4:
        grad_rows = grad_rows[:3] + [jnp.concatenate(grad_rows[3:], axis=0)]
        payload_rows = [[x] for x in payload_rows[:3]] + [payload_rows[3:]]
    else:
        payload_rows = [[x] for x in payload_rows]

    def shared_gradients(kept):
        own_x, own_g, s_hidden, s_pre = kept[4:8]
        d_in = dot(own_x, s_pre, (0, 0)).astype(bf16)
        d_down = dot(s_hidden, own_g, (0, 0)).astype(bf16)
        return cut_shared_grads(here, d_in, d_down, C, E, s_width)

    kept, norms, moved = [], [], []
    for s in range(R):
        x_block = payload_rows[s]
        if E > 2 and kept:
            x_block = [after(x, kept[-1]) for x in x_block]
            grad_rows[s] = after(grad_rows[s], kept[-1])
        info = jnp.concatenate(
            [sources, jnp.stack([first_expert, r ^ s])]
        ).astype(jnp.int32)
        kept, norm = experts_call(
            s, R, kept, list(zip(*(exchange(x, "exp") for x in x_block))),
            exchange(grad_rows[s], "exp"), info,
            slots[s], expert_in, expert_down, sh_in, sh_down, capacity, norms[-1:],
        )
        if s == R - 1:
            shared_grads = shared_gradients(kept)
        seen = [*moved, shared_grads[0]] if s == R - 1 else [x for later in ((1, 2), (3,))[s] for x in payload_rows[later]] if s < 2 else []
        if seen:
            norm = [norm[0], *(after(x, *seen) for x in norm[1:])]
        norms.append(reduce_parts(norm, "exp").astype(bf16))
        if s:
            moved.append(swap(norms[s], "row", s))
    kept, outs = kept[:8], kept[8:]
    rows_x, rows_g, hidden, pre = kept[:4]

    shared_sum = reduce_parts(shared_grads, "exp").astype(bf16)
    outs_moved = [swap(after(outs[t], norms[-1], shared_sum), "exp", t) for t in range(1, E)]
    shared_back = jnp.stack(col_swap(shared_sum))
    norm_block = norms[0].astype(f32)
    for x_sum in moved:
        norm_block = norm_block + x_sum.astype(f32)
    chunks = jnp.split(norm_block.astype(bf16), C, axis=0)
    home = ring_reduce(chunks, "col")
    d_norm, gate_terms = home[:, :model_width], home[:, model_width : model_width + n_experts]
    out_sum = outs[0].astype(f32)
    for part in outs_moved:
        out_sum = add(out_sum, part)
    out_sum = after(out_sum.astype(bf16), moved[-1], shared_back)
    out_rows = lax.psum_scatter(out_sum, "row", scatter_dimension=0, tiled=True)

    expert_width = expert_gate.shape[2]
    pre = after(pre, moved[-1])
    grad_expert_gate = batch_dot("lrd,lrf->ldf", rows_x, pre[:, :, :expert_width])
    grad_expert_up = batch_dot("lrd,lrf->ldf", rows_x, pre[:, :, expert_width:])
    grad_expert_down = batch_dot("lrf,lrd->lfd", after(hidden, moved[-1]), rows_g)
    inner = jnp.sum(mix * gate_terms, axis=1, keepdims=True)
    d_probs = jnp.where(routed, (gate_terms - inner) / chosen_sum, 0.0)
    d_logits = router_probs * (
        d_probs - jnp.sum(router_probs * d_probs, axis=1, keepdims=True)
    )
    d_norm = d_norm + jnp.dot(d_logits, router_t, precision=highest)
    d_norm = d_norm + zero_of(grad_expert_gate, grad_expert_up, grad_expert_down).astype(f32)
    router_part = lax.dot_general(
        d_logits, norm_float, (((0,), (0,)), ((), ())), precision=highest
    )
    d_v, gain_two_part = rms_backward(hidden_state, inv_two, gain_two, d_norm)
    d_hidden = g.astype(f32) + d_v
    d_attn = d_hidden.astype(bf16)
    d_attn_parts = row_gather(d_attn)
    d_attn_all = jnp.concatenate(d_attn_parts, axis=0)

    out_grads = batch_dot("sf,scd->cfd", attended, d_attn_all.reshape(own_rows, C, -1))
    out_grads = out_grads.astype(bf16).reshape(C * query_width, -1)

    d_attended = dot(d_attn_all, weight_out, (1, 1)).astype(bf16)
    out_chunks = jnp.split(after(out_rows, d_attended), C, axis=0)
    moe_out = ring_send(out_chunks[C - 1], "col", 1)
    d_queries, d_kv_parts = attention_backward(
        place, queries, d_attended, att_total, lse, kv_parts, home_rows,
        (out_grads,),
    )
    d_kv_parts = after(d_kv_parts, moe_out)
    d_kv = reduce_parts([d_kv_parts[k] for k in range(C)], "col")
    for k in range(C - 2, 0, -1):
        moe_out = ring_send(add(out_chunks[k], moe_out).astype(bf16), "col", 1)
    moe_out = add(out_chunks[0], moe_out)
    d_query_raw = rotate(
        d_queries.reshape(own_rows, group_heads, head_width), cosines, -sines
    ) * attn_scale
    d_query_raw = d_query_raw.reshape(own_rows, query_width).astype(bf16)
    norm_one_late = after(norm_one_all, d_kv_parts)
    query_grads = dot(norm_one_late, d_query_raw, (0, 0)).astype(bf16)
    d_key_raw = rotate(d_kv[:, :key_width].reshape(own_rows, 1, head_width), cosines, -sines)
    d_kv_raw = jnp.concatenate(
        [d_key_raw.reshape(own_rows, key_width), d_kv[:, key_width:]], axis=1
    ).astype(bf16)
    norm_one_part = dot(jnp.concatenate([d_kv_raw, d_query_raw], axis=1), weight_in, (1, 1)).astype(bf16)
    d_norm_one, halfway = row_reduce(jnp.split(norm_one_part, R, axis=0))
    d_x, gain_one_part = rms_backward(
        x, inv_one, gain_one + zero_of(moe_out).astype(f32), d_norm_one
    )
    grad_inputs, back = tokens_back((d_hidden + d_x).astype(bf16))

    output = tokens_back((hidden_state + moe_out).astype(bf16))[0]
    out_total, query_total = reduce_weight(out_grads), reduce_weight(query_grads)
    kv_grads = dot(after(norm_one_late, *halfway), d_kv_raw, (0, 0)).astype(bf16)
    kv_total = reduce_weight(after(kv_grads, query_total, d_norm_one))
    grad_output = all_shares(after(out_total, d_norm_one)).astype(f32)
    grad_query = all_shares(after(query_total, d_norm_one)).astype(f32)
    grad_kv = all_shares(kv_total).astype(f32)
    small_part = jnp.concatenate([router_part, gain_one_part[None], gain_two_part[None]], axis=0)
    small_part = small_part + zero_of(*back).astype(f32)
    width = small.shape[1]
    mine = [
        lax.dynamic_slice_in_dim(small_part, (c ^ s) * width, width, 1) for s in range(C)
    ]
    small_sum = all_sum(all_sum(reduce_parts(mine, "col"), "row"), "exp")

    grad_shared_gate, grad_shared_up, grad_shared_down = join_shared_grads(
        here, exchange(after(shared_back, d_norm_one), "exp"), in_rows, feature_width
    )
    return (
        output,
        grad_inputs,
        grad_query,
        grad_kv[:, :key_width],
        grad_kv[:, key_width:],
        grad_output,
        small_sum[n_experts],
        small_sum[n_experts + 1],
        small_sum[:n_experts].T,
        grad_shared_gate,
        grad_shared_up,
        grad_shared_down,
        grad_expert_gate,
        grad_expert_up,
        grad_expert_down,
    )


def solution(mesh):
    tokens, weight, experts = P(("exp", "row"), "col"), P("col", "row"), P(("exp", "row"), None, "col")
    expert_down, feature = P(("exp", "row"), "col", None), P("col")
    placed = (
        tokens,
        P(("exp", "row"), None),
        weight,
        weight,
        weight,
        P("row", "col"),
        feature,
        feature,
        P("col", None),
        weight,
        weight,
        P("row", "col"),
        experts,
        experts,
        expert_down,
        tokens,
    )
    return jax.shard_map(
        shards,
        mesh=mesh,
        in_specs=placed,
        out_specs=(
            tokens,
            tokens,
            weight,
            weight,
            weight,
            P("row", "col"),
            feature,
            feature,
            P("col", None),
            weight,
            weight,
            P("row", "col"),
            experts,
            experts,
            expert_down,
        ),
        check_vma=False,
    )
```

```python
import functools

import jax
import jax.numpy as jnp
from jax import lax
from jax.experimental import pallas as pl
from jax.experimental.pallas import tpu as pltpu
from jax.sharding import PartitionSpec as P

HEAD_DIM = 128

eps = 1e-05
theta = 500000.0
highest = lax.Precision.HIGHEST
masked_value = -1e30
f32 = jnp.float32
bf16 = jnp.bfloat16
vmem_limit = 56 * 2**20


def swap(x, axis, step):
    return lax.ppermute(x, axis, [(i, i ^ step) for i in range(lax.axis_size(axis))])


def exchange(x, axis):
    return [x] + [swap(x, axis, step) for step in range(1, lax.axis_size(axis))]


def reduce_parts(parts, axis):
    total = parts[0].astype(f32)
    for step in range(1, len(parts)):
        total = total + swap(parts[step], axis, step).astype(f32)
    return total


def all_sum(x, axis):
    step = 1
    if lax.axis_size(axis) == 4:
        own, near, other, far = exchange(x, axis)
        return (own + near) + (other + far)
    while step < lax.axis_size(axis):
        x = x + swap(x, axis, step)
        step *= 2
    return x


def zero_of(*arrays):
    found = jnp.int32(0)
    for x in arrays:
        first = x[(slice(0, 1),) * x.ndim].reshape(())
        found = found + (first != first).astype(jnp.int32)
    return found


def after(x, *earlier):
    place = pl.BlockSpec(memory_space=pl.ANY)
    return pl.pallas_call(
        lambda *refs: None,
        out_shape=jax.ShapeDtypeStruct(x.shape, x.dtype),
        in_specs=[place] * (1 + len(earlier)),
        out_specs=place,
        input_output_aliases={0: 0},
    )(x, *earlier)


def ring_order(n):
    return [0] + list(range(1, n, 2)) + [i for i in range(n - 1, 0, -1) if i % 2 == 0]


def ring_pairs(n, back=False):
    order = ring_order(n)
    pairs = [(order[i], order[(i + 1) % n]) for i in range(n)]
    return [(b, a) for a, b in pairs] if back else pairs


def ring_sources(axis):
    n = lax.axis_size(axis)
    order = ring_order(n)
    place = jnp.array([order.index(i) for i in range(n)])[lax.axis_index(axis)]
    return jnp.array(order)[(place - jnp.arange(n)) % n]


def ring_gather(x, axis):
    parts, n = [x], lax.axis_size(axis)
    for _ in range(n - 1):
        parts.append(lax.ppermute(parts[-1], axis, ring_pairs(n)))
    return parts


def ring_send(x, axis, k):
    order = ring_order(lax.axis_size(axis))
    n = len(order)
    return lax.ppermute(x, axis, [(order[i], order[(i - k) % n]) for i in range(n)])


def ring_reduce(parts, axis):
    total = parts[0].astype(f32)
    for k in range(1, len(parts)):
        total = total + ring_send(parts[k], axis, k).astype(f32)
    return total


def row_gather(x):
    if lax.axis_size("row") != 4:
        return exchange(x, "row")
    x_near, y_near = swap(x, "row", 1), swap(x, "row", 2)
    middle = x.shape[0] // 2
    return [x, x_near, y_near, swap(y_near[:middle], "row", 1), swap(x_near[middle:], "row", 2)]


def add(left, right):
    return left.astype(f32) + right.astype(f32)


def row_reduce(blocks):
    if len(blocks) != 4:
        return reduce_parts(blocks, "row"), blocks[:1]
    own, x_near, y_near, far = blocks
    middle = own.shape[0] // 2
    far_x, far_y = swap(far[:middle], "row", 1), swap(far[middle:], "row", 2)
    y_first = add(y_near[:middle], far_x).astype(bf16)
    x_second = add(x_near[middle:], far_y).astype(bf16)
    y_sum = swap(jnp.concatenate([y_first, y_near[middle:]], axis=0), "row", 2)
    x_sum = swap(jnp.concatenate([x_near[:middle], x_second], axis=0), "row", 1)
    return add(own, x_sum) + y_sum.astype(f32), [far_x, far_y]


def tokens_home(x, wait):
    c, n = lax.axis_index("col"), lax.axis_size("col")
    rows, width = x.shape[0] // n, x.shape[1]
    whole = jnp.zeros((rows, n * width), x.dtype)
    for s in range(n):
        piece = lax.dynamic_slice_in_dim(x, (c ^ s) * rows + wait, rows, 0)
        piece = swap(piece, "col", s) if s else piece
        whole = lax.dynamic_update_slice(whole, piece, (0, (c ^ s) * width))
    return whole


def tokens_back(x):
    c, n = lax.axis_index("col"), lax.axis_size("col")
    rows, width = x.shape[0], x.shape[1] // n
    whole, moved = jnp.zeros((n * rows, width), x.dtype), []
    for s in range(n):
        piece = lax.dynamic_slice_in_dim(x, (c ^ s) * width, width, 1)
        if s:
            piece = swap(piece, "col", s)
            moved.append(piece)
        whole = lax.dynamic_update_slice(whole, piece, ((c ^ s) * rows, 0))
    return whole, moved


def own_share(weight, wait=0):
    share = weight.shape[0] // lax.axis_size("exp")
    return lax.dynamic_slice_in_dim(weight, lax.axis_index("exp") * share + wait, share, 0)


def all_shares(total):
    e = lax.axis_index("exp")
    shares = lax.axis_size("exp")
    whole = jnp.zeros((shares,) + total.shape, total.dtype)
    for t, piece in enumerate(exchange(total, "exp")):
        whole = lax.dynamic_update_index_in_dim(whole, piece, e ^ t, 0)
    return whole.reshape((shares * total.shape[0],) + total.shape[1:])


def reduce_weight(grad):
    return lax.psum_scatter(grad, ("col", "exp"), scatter_dimension=0, tiled=True)


def rope_tables(positions, head_width):
    half_width = head_width // 2
    frequency = theta ** (-2.0 * jnp.arange(half_width, dtype=f32) / head_width)
    angles = positions.astype(f32)[:, None] * frequency[None, :]
    return (jnp.cos(angles), jnp.sin(angles))


def rotate(source, cosines, sines):
    half_width = source.shape[-1] // 2
    first, second = source[..., :half_width], source[..., half_width:]
    cos_view, sin_view = cosines[:, None, :], sines[:, None, :]
    return jnp.concatenate(
        [first * cos_view - second * sin_view, first * sin_view + second * cos_view], axis=-1
    )


def dot(left, right, contract=(1, 0)):
    return lax.dot_general(
        left, right, (((contract[0],), (contract[1],)), ((), ())), preferred_element_type=f32
    )


def batch_dot(spec, left, right):
    return jnp.einsum(spec, left, right, preferred_element_type=f32)


def rms_inverse(values):
    return lax.rsqrt(jnp.mean(values * values, axis=1, keepdims=True) + eps)


def rms_backward(values, inv_rms, gain, grad_norm):
    scaled_grad = grad_norm * gain[None, :]
    inner = jnp.mean(scaled_grad * values, axis=1, keepdims=True)
    grad_values = inv_rms * (scaled_grad - values * (inv_rms * inv_rms * inner))
    return grad_values, jnp.sum(grad_norm * values * inv_rms, axis=0)


def place_keys(place, kv_refs, key_buf, value_buf, chunk):
    row, blocks, width = place[0], kv_refs[0].shape[0] // chunk, key_buf.shape[1]
    for k, ref in enumerate(kv_refs):
        for s in range(blocks):
            at = pl.multiple_of(((row ^ s) * len(kv_refs) + place[2 + k]) * chunk, chunk)
            key_buf[pl.ds(at, chunk), :] = ref[s * chunk : (s + 1) * chunk, :width]
            value_buf[pl.ds(at, chunk), :] = ref[s * chunk : (s + 1) * chunk, width:]


def head_rows(ref, rows, width):
    block = ref[rows, :]
    return jnp.concatenate(
        [block[:, h * width : (h + 1) * width] for h in range(block.shape[1] // width)], axis=0
    )


def scores_tile(place, key_tile, queries, block, tile, chunk):
    scores = dot(key_tile, queries, (1, 1))
    key_at = tile * key_tile.shape[0] + lax.broadcasted_iota(jnp.int32, scores.shape, 0)
    lane = lax.broadcasted_iota(jnp.int32, scores.shape, 1)
    query_at = block * key_tile.shape[0] + place[1] * chunk + lane % chunk
    return jnp.where(key_at <= query_at, scores, masked_value)


def attention_kernel(chunk, place, q_ref, *refs):
    kv_refs, (out_ref, total_ref, lse_ref, key_buf, value_buf) = refs[:-5], refs[-5:]
    width = key_buf.shape[1]
    blocks = q_ref.shape[0] // chunk
    tile_rows = key_buf.shape[0] // blocks
    place_keys(place, kv_refs, key_buf, value_buf, chunk)

    @pl.loop(0, blocks)
    def _(block):
        rows = pl.ds(pl.multiple_of((place[0] ^ block) * chunk, chunk), chunk)
        queries = head_rows(q_ref, rows, width)
        count = queries.shape[0]

        def step(tile, carry):
            peak, total, out = carry
            at = pl.ds(pl.multiple_of(tile * tile_rows, tile_rows), tile_rows)
            scores = scores_tile(place, key_buf[at, :], queries, block, tile, chunk)
            new_peak = jnp.maximum(peak, jnp.max(scores, axis=0, keepdims=True))
            weights = jnp.exp(scores - new_peak)
            shrink = jnp.exp(peak - new_peak)
            total = total * shrink + jnp.sum(weights, axis=0, keepdims=True)
            part = dot(value_buf[at, :], weights.astype(bf16), (0, 0))
            return new_peak, total, out * shrink + part

        start = (
            jnp.full((1, count), masked_value, f32),
            jnp.zeros((1, count), f32),
            jnp.zeros((width, count), f32),
        )
        peak, total, out = lax.fori_loop(0, block + 1, step, start)
        out = out / total
        total_ref[pl.ds(block, 1)] = out[None]
        lse_ref[pl.ds(block, 1)] = (peak + jnp.log(total))[None]
        for h in range(count // chunk):
            head = out[:, h * chunk : (h + 1) * chunk]
            out_ref[rows, h * width : (h + 1) * width] = head.T.astype(bf16)


def attention_back_kernel(chunk, place, q_ref, grad_ref, total_ref, lse_ref, *refs):
    kv_refs = refs[:-6]
    dq_ref, dkv_ref, key_buf, value_buf, dk_buf, dv_buf = refs[-6:]
    width = key_buf.shape[1]
    blocks = q_ref.shape[0] // chunk
    tile_rows = key_buf.shape[0] // blocks
    place_keys(place, kv_refs, key_buf, value_buf, chunk)
    dk_buf[...] = jnp.zeros_like(dk_buf)
    dv_buf[...] = jnp.zeros_like(dv_buf)

    @pl.loop(0, blocks)
    def _(block):
        rows = pl.ds(pl.multiple_of((place[0] ^ block) * chunk, chunk), chunk)
        queries = head_rows(q_ref, rows, width)
        grads = head_rows(grad_ref, rows, width)
        count = queries.shape[0]
        out = total_ref[pl.ds(block, 1)][0]
        lse = lse_ref[pl.ds(block, 1)][0]
        grads_t = jnp.concatenate(
            [grads[h * chunk : (h + 1) * chunk].astype(f32).T for h in range(count // chunk)], axis=1
        )
        inner = jnp.sum(out * grads_t, axis=0, keepdims=True)

        def step(tile, d_queries):
            at = pl.ds(pl.multiple_of(tile * tile_rows, tile_rows), tile_rows)
            keys = key_buf[at, :]
            scores = scores_tile(place, keys, queries, block, tile, chunk)
            probs = jnp.exp(scores - lse)
            d_probs = dot(value_buf[at, :], grads, (1, 1))
            d_scores = (probs * (d_probs - inner)).astype(bf16)
            dk_buf[at, :] += dot(d_scores, queries)
            dv_buf[at, :] += dot(probs.astype(bf16), grads)
            return d_queries + dot(keys, d_scores, (0, 0))

        d_queries = lax.fori_loop(0, block + 1, step, jnp.zeros((width, count), f32))
        for h in range(count // chunk):
            head = d_queries[:, h * chunk : (h + 1) * chunk]
            dq_ref[rows, h * width : (h + 1) * width] = head.T

    for k in range(len(kv_refs)):
        for s in range(blocks):
            at = pl.ds(pl.multiple_of(((place[0] ^ s) * len(kv_refs) + place[2 + k]) * chunk, chunk), chunk)
            dkv_ref[k, s * chunk : (s + 1) * chunk, :width] = dk_buf[at, :].astype(bf16)
            dkv_ref[k, s * chunk : (s + 1) * chunk, width:] = dv_buf[at, :].astype(bf16)


in_place = pl.BlockSpec(memory_space=pl.ANY)


def whole_spec(shape):
    return pl.BlockSpec(shape, lambda *_: (0,) * len(shape))


def side_by_side(left, right, wait):
    count, rows, width = left.shape
    tile = 512

    def kernel(left_ref, right_ref, _, both_ref):
        both_ref[:, :width] = left_ref[...]
        both_ref[:, width:] = right_ref[...]

    spec = pl.BlockSpec((None, tile, width), lambda i, j: (i, j, 0))
    return pl.pallas_call(
        kernel,
        out_shape=jax.ShapeDtypeStruct((count, rows, 2 * width), left.dtype),
        grid=(count, rows // tile),
        in_specs=[spec, spec, in_place],
        out_specs=pl.BlockSpec((None, tile, 2 * width), lambda i, j: (i, j, 0)),
        cost_estimate=pl.CostEstimate(flops=0, bytes_accessed=2**10, transcendentals=0),
    )(left, right, wait)


def rows_at(index, count):
    return pl.ds(pl.multiple_of(index * count, count), count)


def cut_call(kernel, info, operands, outs, waits=()):
    return pl.pallas_call(
        lambda info, *refs: kernel(info[0], info[1], *refs[: len(operands)], *refs[len(operands) + len(waits) :]),
        out_shape=outs,
        grid_spec=pltpu.PrefetchScalarGridSpec(
            num_scalar_prefetch=1,
            grid=(1,),
            in_specs=[whole_spec(x.shape) for x in operands] + [in_place] * len(waits),
            out_specs=[whole_spec(x.shape) for x in outs],
        ),
        compiler_params=pltpu.CompilerParams(vmem_limit_bytes=vmem_limit),
        cost_estimate=pl.CostEstimate(flops=0, bytes_accessed=2**10, transcendentals=0),
    )(info, *operands, *waits)


def join_weight(blocks, first, cols, shares):
    rows, width = blocks.shape[0] // (cols * shares), blocks.shape[1] - first

    def kernel(ref, out_ref):
        for k in range(cols):
            for t in range(shares):
                at = (k * shares + t) * rows
                out_ref[t * rows : (t + 1) * rows, k * width : (k + 1) * width] = ref[at : at + rows, first:]

    return pl.pallas_call(
        kernel,
        out_shape=jax.ShapeDtypeStruct((shares * rows, cols * width), blocks.dtype),
        compiler_params=pltpu.CompilerParams(vmem_limit_bytes=vmem_limit),
        cost_estimate=pl.CostEstimate(flops=0, bytes_accessed=2**10, transcendentals=0),
    )(blocks)


def each_index(index, count, work):
    for j in range(count):
        pl.when(index == j)(functools.partial(work, j))


def lanes_at(index, width, first, count):
    return pl.ds(pl.multiple_of(index * width + first, 128), count)


def cut_shared(info, gate, up, down, cols, shares, wait):
    rows, width, features = gate.shape[0] // shares, gate.shape[1] // cols, down.shape[1]
    both, down_rows = 2 * width, gate.shape[1] // cols // shares

    def kernel(e, c, gate_ref, up_ref, down_ref, out):
        for k in range(cols):
            at = rows_at(e, rows)
            out[c ^ k, :rows, :width] = gate_ref[at, k * width : (k + 1) * width]
            out[c ^ k, :rows, width:] = up_ref[at, k * width : (k + 1) * width]

        def cut_down(j):
            for k in range(cols):
                piece = down_ref[k * width + j * down_rows : k * width + (j + 1) * down_rows, :]
                out[c ^ k, rows : rows + down_rows, :] = piece[:, :both]
                out[c ^ k, rows + down_rows :, : features - both] = piece[:, both:]

        each_index(e, shares, cut_down)

    outs = (jax.ShapeDtypeStruct((cols, rows + 2 * down_rows, both), bf16),)
    return cut_call(kernel, info, (gate, up, down), outs, (wait,))[0]


def join_shared(info, parts, rows, features, padded):
    cols, all_rows, both = parts[0].shape
    width, shares, down_rows = both // 2, len(parts), (all_rows - rows) // 2

    def kernel(e, c, *refs):
        in_out, down_out = refs[-2:]
        in_out[...] = jnp.zeros_like(in_out)
        down_out[...] = jnp.zeros_like(down_out)
        for s in range(cols):
            for t, ref in enumerate(refs[:-2]):
                at = rows_at((c ^ s) * shares + (e ^ t), rows)
                in_out[at, :width] = ref[s, :rows, :width]
                in_out[at, padded : padded + width] = ref[s, :rows, width:]

        def join_down(j):
            for s in range(cols):
                for t, ref in enumerate(refs[:-2]):
                    at = slice((j ^ t) * down_rows, ((j ^ t) + 1) * down_rows)
                    down_out[at, lanes_at(c ^ s, features, 0, both)] = ref[s, rows : rows + down_rows, :]
                    down_out[at, lanes_at(c ^ s, features, both, features - both)] = ref[
                        s, rows + down_rows :, : features - both
                    ]

        each_index(e, shares, join_down)

    outs = (
        jax.ShapeDtypeStruct((cols * shares * rows, 2 * padded), bf16),
        jax.ShapeDtypeStruct((padded, cols * features), bf16),
    )
    return cut_call(kernel, info, parts, outs)


def cut_shared_grads(info, grad_in, grad_down, cols, shares, width):
    rows, padded = grad_in.shape[0] // (cols * shares), grad_in.shape[1] // 2
    both, down_rows, features = 2 * width, width // shares, grad_down.shape[1] // cols

    def kernel(e, c, in_ref, down_ref, *outs):
        for s in range(cols):
            for t, out in enumerate(outs):
                at = rows_at((c ^ s) * shares + (e ^ t), rows)
                out[s, :rows, :width] = in_ref[at, :width]
                out[s, :rows, width:] = in_ref[at, padded : padded + width]

        def cut_down(j):
            for s in range(cols):
                for t, out in enumerate(outs):
                    at = slice((j ^ t) * down_rows, ((j ^ t) + 1) * down_rows)
                    out[s, rows : rows + down_rows, :] = down_ref[at, lanes_at(c ^ s, features, 0, both)]
                    out[s, rows + down_rows :, : features - both] = down_ref[
                        at, lanes_at(c ^ s, features, both, features - both)
                    ]

        each_index(e, shares, cut_down)

    outs = (jax.ShapeDtypeStruct((cols, rows + 2 * down_rows, both), bf16),) * shares
    return cut_call(kernel, info, (grad_in, grad_down), outs)


def join_shared_grads(info, parts, rows, features):
    cols, all_rows, both = parts[0].shape
    width, shares, down_rows = both // 2, len(parts), (all_rows - rows) // 2

    def kernel(e, c, *refs):
        gate_out, up_out, down_out = refs[-3:]
        for k in range(cols):
            for t, ref in enumerate(refs[:-3]):
                at, part = rows_at(e ^ t, rows), ref[c ^ k, :rows, :].astype(f32)
                gate_out[at, k * width : (k + 1) * width] = part[:, :width]
                up_out[at, k * width : (k + 1) * width] = part[:, width:]

        def join_down(j):
            for k in range(cols):
                for t, ref in enumerate(refs[:-3]):
                    at = k * width + (j ^ t) * down_rows
                    at = slice(at, at + down_rows)
                    down_out[at, :both] = ref[c ^ k, rows : rows + down_rows, :].astype(f32)
                    down_out[at, both:] = ref[c ^ k, rows + down_rows :, : features - both].astype(f32)

        each_index(e, shares, join_down)

    outs = (
        *[jax.ShapeDtypeStruct((shares * rows, cols * width), f32)] * 2,
        jax.ShapeDtypeStruct((cols * width, features), f32),
    )
    return cut_call(kernel, info, parts, outs)


def attention_call(kernel, place, operands, outs, scratch, work, waits):
    return pl.pallas_call(
        lambda place, *refs: kernel(place, *refs[: len(operands)], *refs[len(operands) + len(waits) :]),
        out_shape=outs,
        grid_spec=pltpu.PrefetchScalarGridSpec(
            num_scalar_prefetch=1,
            grid=(1,),
            in_specs=[whole_spec(x.shape) for x in operands] + [in_place] * len(waits),
            out_specs=[whole_spec(x.shape) for x in outs],
            scratch_shapes=scratch,
        ),
        compiler_params=pltpu.CompilerParams(vmem_limit_bytes=vmem_limit),
        cost_estimate=pl.CostEstimate(
            flops=work, bytes_accessed=2**10, transcendentals=0
        ),
    )(place, *operands, *waits)


def attention_forward(place, queries, kv_parts, chunk, waits):
    rows, total_width = queries.shape
    width = kv_parts[0].shape[1] // 2
    heads, blocks, keys = total_width // width, rows // chunk, rows * len(kv_parts)
    return attention_call(
        functools.partial(attention_kernel, chunk),
        place,
        (queries, *kv_parts),
        (
            jax.ShapeDtypeStruct((rows, total_width), bf16),
            jax.ShapeDtypeStruct((blocks, width, heads * chunk), f32),
            jax.ShapeDtypeStruct((blocks, 1, heads * chunk), f32),
        ),
        [pltpu.VMEM((keys, width), bf16)] * 2,
        4 * rows * heads * keys * width,
        waits,
    )


def attention_backward(place, queries, grads, out, lse, kv_parts, chunk, waits):
    rows, total_width = queries.shape
    width = kv_parts[0].shape[1] // 2
    keys = rows * len(kv_parts)
    return attention_call(
        functools.partial(attention_back_kernel, chunk),
        place,
        (queries, grads, out, lse, *kv_parts),
        (
            jax.ShapeDtypeStruct((rows, total_width), f32),
            jax.ShapeDtypeStruct((len(kv_parts), rows, 2 * width), bf16),
        ),
        [pltpu.VMEM((keys, width), bf16)] * 2 + [pltpu.VMEM((keys, width), f32)] * 2,
        10 * rows * total_width * keys,
        waits,
    )


def silu_back(gate_pre, up_pre, grad_hidden):
    sigmoid_vals = jax.nn.sigmoid(gate_pre)
    silu = gate_pre * sigmoid_vals
    grad_gate = grad_hidden * up_pre * sigmoid_vals * (1.0 + gate_pre * (1.0 - sigmoid_vals))
    return silu * up_pre, grad_gate.astype(bf16), (grad_hidden * silu).astype(bf16)


def experts_kernel(counts, unused, local, tiles, chunks, info, *refs):
    groups = len(counts)
    x_refs, refs = refs[: sum(counts)], refs[sum(counts) :]
    mix_refs, refs = refs[: sum(counts)], refs[sum(counts) :]
    g_refs, refs = refs[:groups], refs[groups:]
    refs = refs[:6] + refs[6 + unused :]
    (
        slot_ref, slot_t_ref, w_in, w_down, s_in, s_down,
        xs_ref, gs_ref, hidden_ref, pre_ref, own_x_ref, own_g_ref, s_hidden_ref, s_pre_ref,
    ), refs = refs[:14], refs[14:]
    out_refs, refs = refs[:groups], refs[groups:]
    norm_refs, refs = refs[:groups], refs[groups:]
    pick, put, acc_in, acc_down, s_acc_in, s_acc_down, term_buf = refs
    step = pl.program_id(0)
    capacity, tokens = pick.shape[1], pick.shape[2]
    width, s_width = w_down.shape[1], s_down.shape[0]

    @pl.when(step == 0)
    def _():
        for at in range(groups * local):
            slots = lax.broadcasted_iota(jnp.int32, (capacity, tokens), 0)
            pick[at] = jnp.where(slots == slot_ref[at : at + 1, :], 1.0, 0.0).astype(bf16)
            slots = lax.broadcasted_iota(jnp.int32, (tokens, capacity), 1)
            put[at // local, :, (at % local) * capacity : (at % local + 1) * capacity] = jnp.where(
                slots == slot_t_ref[:, at : at + 1], 1.0, 0.0
            ).astype(bf16)
        acc_in[...] = jnp.zeros_like(acc_in)
        acc_down[...] = jnp.zeros_like(acc_down)
        s_acc_in[...] = jnp.zeros_like(s_acc_in)
        s_acc_down[...] = jnp.zeros_like(s_acc_down)

    @pl.when(step < tiles)
    def _():
        for t in range(groups):
            parts = slice(sum(counts[:t]), sum(counts[: t + 1]))
            x = jnp.concatenate([ref[...] for ref in x_refs[parts]], axis=0)
            chunk = tokens // chunks
            g = jnp.concatenate(
                [
                    g_refs[t][pl.ds(pl.multiple_of(info[k] * chunk, chunk), chunk), :]
                    for k in range(chunks)
                ],
                axis=0,
            )
            for l in range(local):
                rows = slice(t * capacity, (t + 1) * capacity)
                xs_ref[l, rows, :] = dot(pick[t * local + l], x).astype(bf16)
                gs_ref[l, rows, :] = dot(pick[t * local + l], g).astype(bf16)
            if t == 0:
                own_x_ref[...] = x
                own_g_ref[...] = g
                s_acc_in[...] += dot(x, s_in[...])
                s_acc_down[...] += dot(g, s_down[...], (1, 1))
        for l in range(local):
            acc_in[l] += dot(xs_ref[l], w_in[l])
            acc_down[l] += dot(gs_ref[l], w_down[l], (1, 1))

    @pl.when(step == tiles - 1)
    def _():
        mixes = [
            jnp.concatenate([ref[...] for ref in mix_refs[sum(counts[:t]) : sum(counts[: t + 1])]], axis=0)
            for t in range(groups)
        ]
        lanes = mixes[0].shape[1]
        lane = lax.broadcasted_iota(jnp.int32, (1, lanes), 1)
        spread = []
        for l in range(local):
            expert = info[chunks] + l
            weights = jnp.concatenate([dot(pick[t * local + l], mixes[t]) for t in range(groups)], axis=0)
            weights = jnp.sum(
                jnp.where(lane % (lanes // 2) == expert, weights, 0.0), axis=1, keepdims=True
            )
            grad = acc_down[l]
            hidden, d_gate, d_up = silu_back(acc_in[l, :, :width], acc_in[l, :, width:], grad * weights)
            terms = jnp.sum(hidden * grad, axis=1, keepdims=True)
            hidden_ref[l] = (hidden * weights).astype(bf16)
            pre_ref[l, :, :width] = d_gate
            pre_ref[l, :, width:] = d_up
            spread.append(jnp.where(lane == expert, terms, 0.0).astype(bf16))
        for t in range(groups):
            rows = slice(t * capacity, (t + 1) * capacity)
            term_buf[t] = dot(
                put[t], jnp.concatenate([terms[rows] for terms in spread], axis=0)
            ).astype(bf16)
        hidden, d_gate, d_up = silu_back(s_acc_in[:, :s_width], s_acc_in[:, s_width:], s_acc_down[...])
        s_hidden_ref[...] = hidden.astype(bf16)
        s_pre_ref[:, :s_width] = d_gate
        s_pre_ref[:, s_width:] = d_up

    @pl.when((step >= tiles) & (step < 2 * tiles))
    def _():
        pieces = [dot(hidden_ref[l], w_down[l]).astype(bf16) for l in range(local)]
        d_pieces = [dot(pre_ref[l], w_in[l], (1, 1)).astype(bf16) for l in range(local)]
        for t in range(groups):
            rows = slice(t * capacity, (t + 1) * capacity)
            out = dot(put[t], jnp.concatenate([piece[rows] for piece in pieces], axis=0))
            norm = dot(put[t], jnp.concatenate([piece[rows] for piece in d_pieces], axis=0))
            if t == 0:
                out = out + dot(s_hidden_ref[...], s_down[...])
                norm = norm + dot(s_pre_ref[...], s_in[...], (1, 1))
            out_refs[t][...] = out.astype(bf16)
            norm_refs[t][...] = norm.astype(bf16)

    @pl.when(step == 2 * tiles)
    def _():
        for t in range(groups):
            norm_refs[t][:, : term_buf.shape[2]] = term_buf[t]


def experts_call(at, blocks, held, x_parts, g_parts, info, slots, w_in, w_down, s_in, s_down, capacity, waits):
    counts = [len(parts) for parts in x_parts]
    x_parts = [x for parts in x_parts for x in parts]
    groups, local = len(counts), w_in.shape[0]
    chunks = info.shape[0] - 2
    model, whole_width = g_parts[0].shape[1], x_parts[0].shape[1]
    lanes = whole_width - model
    tokens = sum(x.shape[0] for x in x_parts[: counts[0]])
    tile = 512 if groups <= 2 else 256
    tiles = model // tile
    width, s_width = w_down.shape[1], s_down.shape[0]
    rows = groups * capacity

    def tokens_in(i, info):
        return (0, jnp.minimum(i, tiles - 1))

    def picked(i, info):
        return (0, at, jnp.minimum(i, tiles - 1))

    def own(i, info):
        return (at, jnp.minimum(i, tiles - 1))

    def summed(i, info):
        return (info[chunks + 1], jnp.clip(i - tiles, 0, tiles - 1))

    def summed_norm(i, info):
        return (0, jnp.maximum(i - tiles, 0))

    in_specs = [
        *(pl.BlockSpec((x.shape[0], tile), tokens_in) for x in x_parts),
        *(pl.BlockSpec((x.shape[0], lanes), lambda i, info: (0, model // lanes)) for x in x_parts),
        *[pl.BlockSpec((tokens, tile), tokens_in)] * groups,
        whole_spec(slots.shape),
        whole_spec(slots.shape[::-1]),
        pl.BlockSpec((local, tile, 2 * width), lambda i, info: (0, i % tiles, 0)),
        pl.BlockSpec((local, width, tile), lambda i, info: (0, 0, i % tiles)),
        pl.BlockSpec((tile, 2 * s_width), lambda i, info: (i % tiles, 0)),
        pl.BlockSpec((s_width, tile), lambda i, info: (0, i % tiles)),
        *[in_place] * (len(held) + len(waits)),
    ]
    kept = (
        jax.ShapeDtypeStruct((local, blocks * rows, model), bf16),
        jax.ShapeDtypeStruct((local, blocks * rows, model), bf16),
        jax.ShapeDtypeStruct((local, blocks * rows, width), bf16),
        jax.ShapeDtypeStruct((local, blocks * rows, 2 * width), bf16),
        jax.ShapeDtypeStruct((blocks * tokens, model), bf16),
        jax.ShapeDtypeStruct((blocks * tokens, model), bf16),
        jax.ShapeDtypeStruct((blocks * tokens, s_width), bf16),
        jax.ShapeDtypeStruct((blocks * tokens, 2 * s_width), bf16),
        *[jax.ShapeDtypeStruct((blocks * tokens, model), bf16)] * groups,
    )
    norms = (jax.ShapeDtypeStruct((tokens, whole_width), bf16),) * groups
    out_specs = [
        pl.BlockSpec((local, rows, tile), picked),
        pl.BlockSpec((local, rows, tile), picked),
        pl.BlockSpec((local, rows, width), lambda i, info: (0, at, 0)),
        pl.BlockSpec((local, rows, 2 * width), lambda i, info: (0, at, 0)),
        pl.BlockSpec((tokens, tile), own),
        pl.BlockSpec((tokens, tile), own),
        pl.BlockSpec((tokens, s_width), lambda i, info: (at, 0)),
        pl.BlockSpec((tokens, 2 * s_width), lambda i, info: (at, 0)),
        *[pl.BlockSpec((tokens, tile), summed)] * groups,
        *[pl.BlockSpec((tokens, tile), summed_norm)] * groups,
    ]
    work = 2 * model * (
        4 * groups * local * capacity * tokens + 6 * local * rows * width + 6 * tokens * s_width
    )
    first = 1 + len(in_specs) - len(held) - len(waits)
    results = pl.pallas_call(
        functools.partial(experts_kernel, counts, len(held) + len(waits), local, tiles, chunks),
        out_shape=(*kept, *norms),
        grid_spec=pltpu.PrefetchScalarGridSpec(
            num_scalar_prefetch=1,
            grid=(2 * tiles + 1,),
            in_specs=in_specs,
            out_specs=out_specs,
            scratch_shapes=[
                pltpu.VMEM((groups * local, capacity, tokens), bf16),
                pltpu.VMEM((groups, tokens, local * capacity), bf16),
                pltpu.VMEM((local, rows, 2 * width), f32),
                pltpu.VMEM((local, rows, width), f32),
                pltpu.VMEM((tokens, 2 * s_width), f32),
                pltpu.VMEM((tokens, s_width), f32),
                pltpu.VMEM((groups, tokens, lanes), bf16),
            ],
        ),
        input_output_aliases={first + i: i for i in range(len(held))},
        compiler_params=pltpu.CompilerParams(vmem_limit_bytes=vmem_limit),
        cost_estimate=pl.CostEstimate(flops=work, bytes_accessed=2**10, transcendentals=0),
    )(info, *x_parts, *x_parts, *g_parts, slots, slots.T, w_in, w_down, s_in, s_down, *held, *waits)
    return list(results[: len(kept)]), list(results[len(kept) :])


def shards(
    inputs,
    routes,
    w_query,
    w_key,
    w_value,
    w_output,
    gain_attn,
    gain_moe,
    w_router,
    shared_gate,
    shared_up,
    shared_down,
    expert_gate,
    expert_up,
    expert_down,
    out_grad,
):
    e, r, c = lax.axis_index("exp"), lax.axis_index("row"), lax.axis_index("col")
    E, R, C = lax.axis_size("exp"), lax.axis_size("row"), lax.axis_size("col")
    local_count, model_width, _ = expert_gate.shape
    n_experts = local_count * E * R
    block_rows, top_count = routes.shape
    capacity = 4 * block_rows * top_count // (3 * n_experts)
    home_rows = block_rows // C
    head_width = HEAD_DIM
    query_width, key_width = w_query.shape[1], w_key.shape[1]
    group_heads = query_width // key_width
    attn_scale = head_width ** (-0.5)
    sources = ring_sources("col")

    x = tokens_home(inputs, 0).astype(f32)
    small = jnp.concatenate([w_router.T, gain_attn[None], gain_moe[None]], axis=0)
    small_all = jnp.zeros((small.shape[0], model_width), f32)
    for s, part in enumerate(exchange(small, "col")):
        small_all = lax.dynamic_update_slice(small_all, part, (0, (c ^ s) * small.shape[1]))
    router_t, gain_one, gain_two = (
        small_all[:n_experts],
        small_all[n_experts],
        small_all[n_experts + 1],
    )
    inv_one = rms_inverse(x)
    norm_one = (x * inv_one * gain_one[None, :]).astype(bf16)
    norm_one_parts = row_gather(norm_one)
    norm_one_all = jnp.concatenate(norm_one_parts, axis=0)

    own_weights = own_share(jnp.concatenate([w_key, w_value, w_query, w_output], axis=1))
    weights = lax.all_gather(own_weights, ("col", "exp"), tiled=True)
    weight_in = weights[:, : query_width + 2 * key_width]
    raw = dot(norm_one_all, weight_in)
    wait = zero_of(raw)
    here = jnp.stack([e, c]).astype(jnp.int32)
    weight_out = join_weight(weights, query_width + 2 * key_width, C, E)

    s_width = shared_gate.shape[1] // C
    s_padded = -(-s_width // 128) * 128

    def col_swap(parts):
        return [swap(parts[s], "col", s) if s else parts[0] for s in range(C)]

    shared_cut = cut_shared(here, shared_gate, shared_up, shared_down, C, E, raw)
    in_rows, feature_width = shared_gate.shape[0] // E, shared_down.shape[1]
    expert_in = side_by_side(expert_gate, expert_up, raw)

    own_routes = lax.dynamic_slice_in_dim(routes, c * home_rows, home_rows, 0)
    routes_here = routes.reshape(C, home_rows, top_count)[sources].reshape(block_rows, top_count)
    expert_ids = jnp.arange(n_experts)
    first_expert = (e * R + r) * local_count
    own_ids = first_expert + jnp.arange(local_count)
    earlier = (jnp.arange(block_rows)[:, None] < jnp.arange(block_rows)[None, :]).astype(bf16)
    routes_t = routes_here.T
    routes_t = routes_t + wait
    named = jnp.stack(
        [
            (block[None] == own_ids[:, None, None]).any(axis=1)
            for of_row in exchange(routes_t, "row")
            for block in exchange(of_row, "exp")
        ]
    ).reshape(R, E * local_count, block_rows)
    rank = dot(named.reshape(-1, block_rows).astype(bf16), earlier).astype(jnp.int32)
    slots = jnp.where(named, rank.reshape(named.shape), -1)

    positions = (
        ((r ^ jnp.arange(R)) * block_rows + c * home_rows)[:, None]
        + jnp.arange(home_rows)[None, :]
    ).reshape(-1)
    cosines, sines = rope_tables(positions, head_width)
    own_rows = R * home_rows
    keys = rotate(raw[:, :key_width].reshape(own_rows, 1, head_width), cosines, sines)
    kv = jnp.concatenate([keys.reshape(own_rows, key_width), raw[:, key_width : 2 * key_width]], axis=1)
    kv_parts = exchange(kv.astype(bf16), "col")
    g_block = lax.all_gather(after(out_grad, *kv_parts[1:]), "col", axis=1, tiled=True)
    g = lax.dynamic_slice_in_dim(g_block, c * home_rows, home_rows, 0)
    queries = rotate(
        raw[:, 2 * key_width :].reshape(own_rows, group_heads, head_width), cosines, sines
    )
    queries = (queries * attn_scale).astype(bf16).reshape(own_rows, query_width)
    place = jnp.concatenate([jnp.stack([r, c]), c ^ jnp.arange(C)]).astype(jnp.int32)
    attended, att_total, lse = attention_forward(place, queries, kv_parts, home_rows, (expert_in, shared_cut))
    attn_part = dot(attended, weight_out).astype(bf16)
    shared_parts = col_swap(after(shared_cut, attended))
    sh_in, sh_down = join_shared(
        here, exchange(jnp.stack(shared_parts), "exp"), in_rows, feature_width, s_padded
    )
    hidden_state = x + row_reduce(jnp.split(attn_part, R, axis=0))[0]
    inv_two = rms_inverse(hidden_state) + zero_of(g_block, *shared_parts[1:]).astype(f32)
    norm_two = (hidden_state * inv_two * gain_two[None, :]).astype(bf16)

    norm_float = norm_two.astype(f32)
    logits = lax.dot_general(
        norm_float, router_t, (((1,), (1,)), ((), ())), precision=highest
    )
    router_probs = jax.nn.softmax(logits, axis=-1)
    routed = (own_routes[:, :, None] == expert_ids[None, None, :]).any(axis=1)
    chosen = jnp.where(routed, router_probs, 0.0)
    chosen_sum = jnp.sum(chosen, axis=1, keepdims=True)
    mix = chosen / chosen_sum

    mix_lanes = -(-n_experts // 64) * 64
    mix_first = lax.reduce_precision(mix, 8, 7)
    mix_pad = ((0, 0), (0, mix_lanes - n_experts))
    payload = jnp.concatenate(
        [
            norm_two,
            jnp.pad(mix_first.astype(bf16), mix_pad),
            jnp.pad((mix - mix_first).astype(bf16), mix_pad),
        ],
        axis=1,
    )
    payload = jnp.concatenate(ring_gather(payload, "col"), axis=0)
    grad_rows = row_gather(g_block)
    grad_own = exchange(g_block, "exp")
    payload = after(payload, *grad_rows[1:3], *grad_own[1:], sh_in)
    payload_rows = row_gather(payload)
    if R == 4:
        grad_rows = grad_rows[:3] + [jnp.concatenate(grad_rows[3:], axis=0)]
        payload_rows = [[x] for x in payload_rows[:3]] + [payload_rows[3:]]
    else:
        payload_rows = [[x] for x in payload_rows]

    def shared_gradients(kept):
        own_x, own_g, s_hidden, s_pre = kept[4:8]
        d_in = dot(own_x, s_pre, (0, 0)).astype(bf16)
        d_down = dot(s_hidden, own_g, (0, 0)).astype(bf16)
        return cut_shared_grads(here, d_in, d_down, C, E, s_width)

    kept, norms, moved = [], [], []
    for s in range(R):
        x_block = payload_rows[s]
        if E > 2 and kept:
            x_block = [after(x, kept[-1]) for x in x_block]
            grad_rows[s] = after(grad_rows[s], kept[-1])
        info = jnp.concatenate(
            [sources, jnp.stack([first_expert, r ^ s])]
        ).astype(jnp.int32)
        kept, norm = experts_call(
            s, R, kept, list(zip(*(exchange(x, "exp") for x in x_block))),
            exchange(grad_rows[s], "exp") if s else grad_own, info,
            slots[s], expert_in, expert_down, sh_in, sh_down, capacity, norms[-1:],
        )
        if s == R - 1:
            shared_grads = shared_gradients(kept)
        seen = [*moved, shared_grads[0]] if s == R - 1 else [x for later in ((1, 2), (3,))[s] for x in payload_rows[later]] if s < 2 else []
        if seen:
            norm = [norm[0], *(after(x, *seen) for x in norm[1:])]
        norms.append(reduce_parts(norm, "exp").astype(bf16))
        if s:
            moved.append(swap(norms[s], "row", s))
    kept, outs = kept[:8], kept[8:]
    rows_x, rows_g, hidden, pre = kept[:4]

    shared_sum = reduce_parts(shared_grads, "exp").astype(bf16)
    outs_moved = [swap(after(outs[t], norms[-1], shared_sum), "exp", t) for t in range(1, E)]
    shared_back = jnp.stack(col_swap(shared_sum))
    norm_block = norms[0].astype(f32)
    for x_sum in moved:
        norm_block = norm_block + x_sum.astype(f32)
    chunks = jnp.split(norm_block.astype(bf16), C, axis=0)
    home = ring_reduce(chunks, "col")
    d_norm, gate_terms = home[:, :model_width], home[:, model_width : model_width + n_experts]
    out_sum = outs[0].astype(f32)
    for part in outs_moved:
        out_sum = add(out_sum, part)
    out_sum = after(out_sum.astype(bf16), moved[-1], shared_back)
    out_rows = lax.psum_scatter(out_sum, "row", scatter_dimension=0, tiled=True)

    expert_width = expert_gate.shape[2]
    pre = after(pre, moved[-1])
    grad_expert_gate = batch_dot("lrd,lrf->ldf", rows_x, pre[:, :, :expert_width])
    grad_expert_up = batch_dot("lrd,lrf->ldf", rows_x, pre[:, :, expert_width:])
    grad_expert_down = batch_dot("lrf,lrd->lfd", after(hidden, moved[-1]), rows_g)
    inner = jnp.sum(mix * gate_terms, axis=1, keepdims=True)
    d_probs = jnp.where(routed, (gate_terms - inner) / chosen_sum, 0.0)
    d_logits = router_probs * (
        d_probs - jnp.sum(router_probs * d_probs, axis=1, keepdims=True)
    )
    d_norm = d_norm + jnp.dot(d_logits, router_t, precision=highest)
    d_norm = d_norm + zero_of(grad_expert_gate, grad_expert_up, grad_expert_down).astype(f32)
    router_part = lax.dot_general(
        d_logits, norm_float, (((0,), (0,)), ((), ())), precision=highest
    )
    d_v, gain_two_part = rms_backward(hidden_state, inv_two, gain_two, d_norm)
    d_hidden = g.astype(f32) + d_v
    d_attn = d_hidden.astype(bf16)
    d_attn_parts = row_gather(d_attn)
    d_attn_all = jnp.concatenate(d_attn_parts, axis=0)

    out_grads = batch_dot("sf,scd->cfd", attended, d_attn_all.reshape(own_rows, C, -1))
    out_grads = out_grads.astype(bf16).reshape(C * query_width, -1)

    d_attended = dot(d_attn_all, weight_out, (1, 1)).astype(bf16)
    out_chunks = jnp.split(after(out_rows, d_attended), C, axis=0)
    moe_out = ring_send(out_chunks[C - 1], "col", 1)
    d_queries, d_kv_parts = attention_backward(
        place, queries, d_attended, att_total, lse, kv_parts, home_rows,
        (out_grads,),
    )
    d_kv_parts = after(d_kv_parts, moe_out)
    d_kv = reduce_parts([d_kv_parts[k] for k in range(C)], "col")
    moe_out = ring_send(add(out_chunks[C - 2], moe_out).astype(bf16), "col", 1)
    ring_here = zero_of(moe_out)
    for k in range(C - 3, 0, -1):
        moe_out = ring_send(add(out_chunks[k], moe_out).astype(bf16), "col", 1)
    moe_out = add(out_chunks[0], moe_out)
    d_query_raw = rotate(
        d_queries.reshape(own_rows, group_heads, head_width), cosines, -sines
    ) * (attn_scale + ring_here.astype(f32))
    d_query_raw = d_query_raw.reshape(own_rows, query_width).astype(bf16)
    norm_one_late = after(norm_one_all, d_kv_parts)
    query_grads = dot(norm_one_late, d_query_raw, (0, 0)).astype(bf16)
    d_key_raw = rotate(d_kv[:, :key_width].reshape(own_rows, 1, head_width), cosines, -sines)
    d_kv_raw = jnp.concatenate(
        [d_key_raw.reshape(own_rows, key_width), d_kv[:, key_width:]], axis=1
    ).astype(bf16)
    norm_one_part = dot(jnp.concatenate([d_kv_raw, d_query_raw], axis=1), weight_in, (1, 1)).astype(bf16)
    d_norm_one, halfway = row_reduce(jnp.split(norm_one_part, R, axis=0))
    grad_shared_gate, grad_shared_up, grad_shared_down = join_shared_grads(
        here, exchange(after(shared_back, d_kv), "exp"), in_rows, feature_width
    )
    late = zero_of(moe_out, grad_shared_gate).astype(f32)
    d_x, gain_one_part = rms_backward(x, inv_one, gain_one + late, d_norm_one)
    grad_inputs, back = tokens_back((d_hidden + d_x).astype(bf16))

    output = tokens_back((hidden_state + moe_out).astype(bf16))[0]
    out_total, query_total = reduce_weight(out_grads), reduce_weight(query_grads)
    kv_grads = dot(after(norm_one_late, *halfway), d_kv_raw, (0, 0)).astype(bf16)
    kv_total = reduce_weight(after(kv_grads, query_total, moe_out))
    grad_output = all_shares(after(out_total, d_norm_one)).astype(f32)
    grad_query = all_shares(after(query_total, d_norm_one)).astype(f32)
    grad_kv = all_shares(kv_total).astype(f32)
    small_part = jnp.concatenate([router_part, gain_one_part[None], gain_two_part[None]], axis=0)
    small_part = small_part + zero_of(*back).astype(f32)
    width = small.shape[1]
    mine = [
        lax.dynamic_slice_in_dim(small_part, (c ^ s) * width, width, 1) for s in range(C)
    ]
    small_sum = all_sum(all_sum(reduce_parts(mine, "col"), "row"), "exp")

    return (
        output,
        grad_inputs,
        grad_query,
        grad_kv[:, :key_width],
        grad_kv[:, key_width:],
        grad_output,
        small_sum[n_experts],
        small_sum[n_experts + 1],
        small_sum[:n_experts].T,
        grad_shared_gate,
        grad_shared_up,
        grad_shared_down,
        grad_expert_gate,
        grad_expert_up,
        grad_expert_down,
    )


def solution(mesh):
    tokens, weight, experts = P(("exp", "row"), "col"), P("col", "row"), P(("exp", "row"), None, "col")
    expert_down, feature = P(("exp", "row"), "col", None), P("col")
    placed = (
        tokens,
        P(("exp", "row"), None),
        weight,
        weight,
        weight,
        P("row", "col"),
        feature,
        feature,
        P("col", None),
        weight,
        weight,
        P("row", "col"),
        experts,
        experts,
        expert_down,
        tokens,
    )
    return jax.shard_map(
        shards,
        mesh=mesh,
        in_specs=placed,
        out_specs=(
            tokens,
            tokens,
            weight,
            weight,
            weight,
            P("row", "col"),
            feature,
            feature,
            P("col", None),
            weight,
            weight,
            P("row", "col"),
            experts,
            experts,
            expert_down,
        ),
        check_vma=False,
    )
```

```python
import functools

import jax
import jax.numpy as jnp
from jax import lax
from jax.experimental import pallas as pl
from jax.experimental.pallas import tpu as pltpu
from jax.sharding import PartitionSpec as P

HEAD_DIM = 128

eps = 1e-05
theta = 500000.0
highest = lax.Precision.HIGHEST
masked_value = -1e30
f32 = jnp.float32
bf16 = jnp.bfloat16
vmem_limit = 56 * 2**20


def swap(x, axis, step):
    return lax.ppermute(x, axis, [(i, i ^ step) for i in range(lax.axis_size(axis))])


def exchange(x, axis):
    return [x] + [swap(x, axis, step) for step in range(1, lax.axis_size(axis))]


def reduce_parts(parts, axis):
    total = parts[0].astype(f32)
    for step in range(1, len(parts)):
        total = total + swap(parts[step], axis, step).astype(f32)
    return total


def all_sum(x, axis):
    step = 1
    if lax.axis_size(axis) == 4:
        own, near, other, far = exchange(x, axis)
        return (own + near) + (other + far)
    while step < lax.axis_size(axis):
        x = x + swap(x, axis, step)
        step *= 2
    return x


def zero_of(*arrays):
    found = jnp.int32(0)
    for x in arrays:
        first = x[(slice(0, 1),) * x.ndim].reshape(())
        found = found + (first != first).astype(jnp.int32)
    return found


def after(x, *earlier):
    place = pl.BlockSpec(memory_space=pl.ANY)
    return pl.pallas_call(
        lambda *refs: None,
        out_shape=jax.ShapeDtypeStruct(x.shape, x.dtype),
        in_specs=[place] * (1 + len(earlier)),
        out_specs=place,
        input_output_aliases={0: 0},
    )(x, *earlier)


def ring_order(n):
    return [0] + list(range(1, n, 2)) + [i for i in range(n - 1, 0, -1) if i % 2 == 0]


def ring_pairs(n, back=False):
    order = ring_order(n)
    pairs = [(order[i], order[(i + 1) % n]) for i in range(n)]
    return [(b, a) for a, b in pairs] if back else pairs


def ring_sources(axis):
    n = lax.axis_size(axis)
    order = ring_order(n)
    place = jnp.array([order.index(i) for i in range(n)])[lax.axis_index(axis)]
    return jnp.array(order)[(place - jnp.arange(n)) % n]


def ring_gather(x, axis):
    parts, n = [x], lax.axis_size(axis)
    for _ in range(n - 1):
        parts.append(lax.ppermute(parts[-1], axis, ring_pairs(n)))
    return parts


def ring_send(x, axis, k):
    order = ring_order(lax.axis_size(axis))
    n = len(order)
    return lax.ppermute(x, axis, [(order[i], order[(i - k) % n]) for i in range(n)])


def ring_reduce(parts, axis):
    total = parts[0].astype(f32)
    for k in range(1, len(parts)):
        total = total + ring_send(parts[k], axis, k).astype(f32)
    return total


def row_gather(x):
    if lax.axis_size("row") != 4:
        return exchange(x, "row")
    x_near, y_near = swap(x, "row", 1), swap(x, "row", 2)
    middle = x.shape[0] // 2
    return [x, x_near, y_near, swap(y_near[:middle], "row", 1), swap(x_near[middle:], "row", 2)]


def add(left, right):
    return left.astype(f32) + right.astype(f32)


def row_reduce(blocks):
    if len(blocks) != 4:
        return reduce_parts(blocks, "row"), blocks[:1]
    own, x_near, y_near, far = blocks
    middle = own.shape[0] // 2
    far_x, far_y = swap(far[:middle], "row", 1), swap(far[middle:], "row", 2)
    y_first = add(y_near[:middle], far_x).astype(bf16)
    x_second = add(x_near[middle:], far_y).astype(bf16)
    y_sum = swap(jnp.concatenate([y_first, y_near[middle:]], axis=0), "row", 2)
    x_sum = swap(jnp.concatenate([x_near[:middle], x_second], axis=0), "row", 1)
    return add(own, x_sum) + y_sum.astype(f32), [far_x, far_y]


def tokens_home(x, wait):
    c, n = lax.axis_index("col"), lax.axis_size("col")
    rows, width = x.shape[0] // n, x.shape[1]
    whole = jnp.zeros((rows, n * width), x.dtype)
    for s in range(n):
        piece = lax.dynamic_slice_in_dim(x, (c ^ s) * rows + wait, rows, 0)
        piece = swap(piece, "col", s) if s else piece
        whole = lax.dynamic_update_slice(whole, piece, (0, (c ^ s) * width))
    return whole


def tokens_back(x):
    c, n = lax.axis_index("col"), lax.axis_size("col")
    rows, width = x.shape[0], x.shape[1] // n
    whole, moved = jnp.zeros((n * rows, width), x.dtype), []
    for s in range(n):
        piece = lax.dynamic_slice_in_dim(x, (c ^ s) * width, width, 1)
        if s:
            piece = swap(piece, "col", s)
            moved.append(piece)
        whole = lax.dynamic_update_slice(whole, piece, ((c ^ s) * rows, 0))
    return whole, moved


def own_share(weight, wait=0):
    share = weight.shape[0] // lax.axis_size("exp")
    return lax.dynamic_slice_in_dim(weight, lax.axis_index("exp") * share + wait, share, 0)


def all_shares(total):
    e = lax.axis_index("exp")
    shares = lax.axis_size("exp")
    whole = jnp.zeros((shares,) + total.shape, total.dtype)
    for t, piece in enumerate(exchange(total, "exp")):
        whole = lax.dynamic_update_index_in_dim(whole, piece, e ^ t, 0)
    return whole.reshape((shares * total.shape[0],) + total.shape[1:])


def reduce_weight(grad):
    return lax.psum_scatter(grad, ("col", "exp"), scatter_dimension=0, tiled=True)


def rope_tables(positions, head_width):
    half_width = head_width // 2
    frequency = theta ** (-2.0 * jnp.arange(half_width, dtype=f32) / head_width)
    angles = positions.astype(f32)[:, None] * frequency[None, :]
    return (jnp.cos(angles), jnp.sin(angles))


def rotate(source, cosines, sines):
    half_width = source.shape[-1] // 2
    first, second = source[..., :half_width], source[..., half_width:]
    cos_view, sin_view = cosines[:, None, :], sines[:, None, :]
    return jnp.concatenate(
        [first * cos_view - second * sin_view, first * sin_view + second * cos_view], axis=-1
    )


def dot(left, right, contract=(1, 0)):
    return lax.dot_general(
        left, right, (((contract[0],), (contract[1],)), ((), ())), preferred_element_type=f32
    )


def batch_dot(spec, left, right):
    return jnp.einsum(spec, left, right, preferred_element_type=f32)


def rms_inverse(values):
    return lax.rsqrt(jnp.mean(values * values, axis=1, keepdims=True) + eps)


def rms_backward(values, inv_rms, gain, grad_norm):
    scaled_grad = grad_norm * gain[None, :]
    inner = jnp.mean(scaled_grad * values, axis=1, keepdims=True)
    grad_values = inv_rms * (scaled_grad - values * (inv_rms * inv_rms * inner))
    return grad_values, jnp.sum(grad_norm * values * inv_rms, axis=0)


def place_keys(place, kv_refs, key_buf, value_buf, chunk):
    row, blocks, width = place[0], kv_refs[0].shape[0] // chunk, key_buf.shape[1]
    for k, ref in enumerate(kv_refs):
        for s in range(blocks):
            at = pl.multiple_of(((row ^ s) * len(kv_refs) + place[2 + k]) * chunk, chunk)
            key_buf[pl.ds(at, chunk), :] = ref[s * chunk : (s + 1) * chunk, :width]
            value_buf[pl.ds(at, chunk), :] = ref[s * chunk : (s + 1) * chunk, width:]


def head_rows(ref, rows, width):
    block = ref[rows, :]
    return jnp.concatenate(
        [block[:, h * width : (h + 1) * width] for h in range(block.shape[1] // width)], axis=0
    )


def scores_tile(place, key_tile, queries, block, tile, chunk):
    scores = dot(key_tile, queries, (1, 1))
    key_at = tile * key_tile.shape[0] + lax.broadcasted_iota(jnp.int32, scores.shape, 0)
    lane = lax.broadcasted_iota(jnp.int32, scores.shape, 1)
    query_at = block * key_tile.shape[0] + place[1] * chunk + lane % chunk
    return jnp.where(key_at <= query_at, scores, masked_value)


def attention_kernel(chunk, place, q_ref, *refs):
    kv_refs, (out_ref, total_ref, lse_ref, key_buf, value_buf) = refs[:-5], refs[-5:]
    width = key_buf.shape[1]
    blocks = q_ref.shape[0] // chunk
    tile_rows = key_buf.shape[0] // blocks
    place_keys(place, kv_refs, key_buf, value_buf, chunk)

    @pl.loop(0, blocks)
    def _(block):
        rows = pl.ds(pl.multiple_of((place[0] ^ block) * chunk, chunk), chunk)
        queries = head_rows(q_ref, rows, width)
        count = queries.shape[0]

        def step(tile, carry):
            peak, total, out = carry
            at = pl.ds(pl.multiple_of(tile * tile_rows, tile_rows), tile_rows)
            scores = scores_tile(place, key_buf[at, :], queries, block, tile, chunk)
            new_peak = jnp.maximum(peak, jnp.max(scores, axis=0, keepdims=True))
            weights = jnp.exp(scores - new_peak)
            shrink = jnp.exp(peak - new_peak)
            total = total * shrink + jnp.sum(weights, axis=0, keepdims=True)
            part = dot(value_buf[at, :], weights.astype(bf16), (0, 0))
            return new_peak, total, out * shrink + part

        start = (
            jnp.full((1, count), masked_value, f32),
            jnp.zeros((1, count), f32),
            jnp.zeros((width, count), f32),
        )
        peak, total, out = lax.fori_loop(0, block + 1, step, start)
        out = out / total
        total_ref[pl.ds(block, 1)] = out[None]
        lse_ref[pl.ds(block, 1)] = (peak + jnp.log(total))[None]
        for h in range(count // chunk):
            head = out[:, h * chunk : (h + 1) * chunk]
            out_ref[rows, h * width : (h + 1) * width] = head.T.astype(bf16)


def attention_back_kernel(chunk, place, q_ref, grad_ref, total_ref, lse_ref, *refs):
    kv_refs = refs[:-6]
    dq_ref, dkv_ref, key_buf, value_buf, dk_buf, dv_buf = refs[-6:]
    width = key_buf.shape[1]
    blocks = q_ref.shape[0] // chunk
    tile_rows = key_buf.shape[0] // blocks
    place_keys(place, kv_refs, key_buf, value_buf, chunk)
    dk_buf[...] = jnp.zeros_like(dk_buf)
    dv_buf[...] = jnp.zeros_like(dv_buf)

    @pl.loop(0, blocks)
    def _(block):
        rows = pl.ds(pl.multiple_of((place[0] ^ block) * chunk, chunk), chunk)
        queries = head_rows(q_ref, rows, width)
        grads = head_rows(grad_ref, rows, width)
        count = queries.shape[0]
        out = total_ref[pl.ds(block, 1)][0]
        lse = lse_ref[pl.ds(block, 1)][0]
        grads_t = jnp.concatenate(
            [grads[h * chunk : (h + 1) * chunk].astype(f32).T for h in range(count // chunk)], axis=1
        )
        inner = jnp.sum(out * grads_t, axis=0, keepdims=True)

        def step(tile, d_queries):
            at = pl.ds(pl.multiple_of(tile * tile_rows, tile_rows), tile_rows)
            keys = key_buf[at, :]
            scores = scores_tile(place, keys, queries, block, tile, chunk)
            probs = jnp.exp(scores - lse)
            d_probs = dot(value_buf[at, :], grads, (1, 1))
            d_scores = (probs * (d_probs - inner)).astype(bf16)
            dk_buf[at, :] += dot(d_scores, queries)
            dv_buf[at, :] += dot(probs.astype(bf16), grads)
            return d_queries + dot(keys, d_scores, (0, 0))

        d_queries = lax.fori_loop(0, block + 1, step, jnp.zeros((width, count), f32))
        for h in range(count // chunk):
            head = d_queries[:, h * chunk : (h + 1) * chunk]
            dq_ref[rows, h * width : (h + 1) * width] = head.T

    for k in range(len(kv_refs)):
        for s in range(blocks):
            at = pl.ds(pl.multiple_of(((place[0] ^ s) * len(kv_refs) + place[2 + k]) * chunk, chunk), chunk)
            dkv_ref[k, s * chunk : (s + 1) * chunk, :width] = dk_buf[at, :].astype(bf16)
            dkv_ref[k, s * chunk : (s + 1) * chunk, width:] = dv_buf[at, :].astype(bf16)


in_place = pl.BlockSpec(memory_space=pl.ANY)


def whole_spec(shape):
    return pl.BlockSpec(shape, lambda *_: (0,) * len(shape))


def side_by_side(left, right, wait):
    count, rows, width = left.shape
    tile = 512

    def kernel(left_ref, right_ref, _, both_ref):
        both_ref[:, :width] = left_ref[...]
        both_ref[:, width:] = right_ref[...]

    spec = pl.BlockSpec((None, tile, width), lambda i, j: (i, j, 0))
    return pl.pallas_call(
        kernel,
        out_shape=jax.ShapeDtypeStruct((count, rows, 2 * width), left.dtype),
        grid=(count, rows // tile),
        in_specs=[spec, spec, in_place],
        out_specs=pl.BlockSpec((None, tile, 2 * width), lambda i, j: (i, j, 0)),
        cost_estimate=pl.CostEstimate(flops=0, bytes_accessed=2**10, transcendentals=0),
    )(left, right, wait)


def rows_at(index, count):
    return pl.ds(pl.multiple_of(index * count, count), count)


def cut_call(kernel, info, operands, outs, waits=()):
    return pl.pallas_call(
        lambda info, *refs: kernel(info[0], info[1], *refs[: len(operands)], *refs[len(operands) + len(waits) :]),
        out_shape=outs,
        grid_spec=pltpu.PrefetchScalarGridSpec(
            num_scalar_prefetch=1,
            grid=(1,),
            in_specs=[whole_spec(x.shape) for x in operands] + [in_place] * len(waits),
            out_specs=[whole_spec(x.shape) for x in outs],
        ),
        compiler_params=pltpu.CompilerParams(vmem_limit_bytes=vmem_limit),
        cost_estimate=pl.CostEstimate(flops=0, bytes_accessed=2**10, transcendentals=0),
    )(info, *operands, *waits)


def join_weight(blocks, first, cols, shares):
    rows, width = blocks.shape[0] // (cols * shares), blocks.shape[1] - first

    def kernel(ref, out_ref):
        for k in range(cols):
            for t in range(shares):
                at = (k * shares + t) * rows
                out_ref[t * rows : (t + 1) * rows, k * width : (k + 1) * width] = ref[at : at + rows, first:]

    return pl.pallas_call(
        kernel,
        out_shape=jax.ShapeDtypeStruct((shares * rows, cols * width), blocks.dtype),
        compiler_params=pltpu.CompilerParams(vmem_limit_bytes=vmem_limit),
        cost_estimate=pl.CostEstimate(flops=0, bytes_accessed=2**10, transcendentals=0),
    )(blocks)


def each_index(index, count, work):
    for j in range(count):
        pl.when(index == j)(functools.partial(work, j))


def lanes_at(index, width, first, count):
    return pl.ds(pl.multiple_of(index * width + first, 128), count)


def cut_shared(info, gate, up, down, cols, shares, wait):
    rows, width, features = gate.shape[0] // shares, gate.shape[1] // cols, down.shape[1]
    both, down_rows = 2 * width, gate.shape[1] // cols // shares

    def kernel(e, c, gate_ref, up_ref, down_ref, out):
        for k in range(cols):
            at = rows_at(e, rows)
            out[c ^ k, :rows, :width] = gate_ref[at, k * width : (k + 1) * width]
            out[c ^ k, :rows, width:] = up_ref[at, k * width : (k + 1) * width]

        def cut_down(j):
            for k in range(cols):
                piece = down_ref[k * width + j * down_rows : k * width + (j + 1) * down_rows, :]
                out[c ^ k, rows : rows + down_rows, :] = piece[:, :both]
                out[c ^ k, rows + down_rows :, : features - both] = piece[:, both:]

        each_index(e, shares, cut_down)

    outs = (jax.ShapeDtypeStruct((cols, rows + 2 * down_rows, both), bf16),)
    return cut_call(kernel, info, (gate, up, down), outs, (wait,))[0]


def join_shared(info, parts, rows, features, padded):
    cols, all_rows, both = parts[0].shape
    width, shares, down_rows = both // 2, len(parts), (all_rows - rows) // 2

    def kernel(e, c, *refs):
        in_out, down_out = refs[-2:]
        in_out[...] = jnp.zeros_like(in_out)
        down_out[...] = jnp.zeros_like(down_out)
        for s in range(cols):
            for t, ref in enumerate(refs[:-2]):
                at = rows_at((c ^ s) * shares + (e ^ t), rows)
                in_out[at, :width] = ref[s, :rows, :width]
                in_out[at, padded : padded + width] = ref[s, :rows, width:]

        def join_down(j):
            for s in range(cols):
                for t, ref in enumerate(refs[:-2]):
                    at = slice((j ^ t) * down_rows, ((j ^ t) + 1) * down_rows)
                    down_out[at, lanes_at(c ^ s, features, 0, both)] = ref[s, rows : rows + down_rows, :]
                    down_out[at, lanes_at(c ^ s, features, both, features - both)] = ref[
                        s, rows + down_rows :, : features - both
                    ]

        each_index(e, shares, join_down)

    outs = (
        jax.ShapeDtypeStruct((cols * shares * rows, 2 * padded), bf16),
        jax.ShapeDtypeStruct((padded, cols * features), bf16),
    )
    return cut_call(kernel, info, parts, outs)


def cut_shared_grads(info, grad_in, grad_down, cols, shares, width):
    rows, padded = grad_in.shape[0] // (cols * shares), grad_in.shape[1] // 2
    both, down_rows, features = 2 * width, width // shares, grad_down.shape[1] // cols

    def kernel(e, c, in_ref, down_ref, *outs):
        for s in range(cols):
            for t, out in enumerate(outs):
                at = rows_at((c ^ s) * shares + (e ^ t), rows)
                out[s, :rows, :width] = in_ref[at, :width]
                out[s, :rows, width:] = in_ref[at, padded : padded + width]

        def cut_down(j):
            for s in range(cols):
                for t, out in enumerate(outs):
                    at = slice((j ^ t) * down_rows, ((j ^ t) + 1) * down_rows)
                    out[s, rows : rows + down_rows, :] = down_ref[at, lanes_at(c ^ s, features, 0, both)]
                    out[s, rows + down_rows :, : features - both] = down_ref[
                        at, lanes_at(c ^ s, features, both, features - both)
                    ]

        each_index(e, shares, cut_down)

    outs = (jax.ShapeDtypeStruct((cols, rows + 2 * down_rows, both), bf16),) * shares
    return cut_call(kernel, info, (grad_in, grad_down), outs)


def join_shared_grads(info, parts, rows, features):
    cols, all_rows, both = parts[0].shape
    width, shares, down_rows = both // 2, len(parts), (all_rows - rows) // 2

    def kernel(e, c, *refs):
        gate_out, up_out, down_out = refs[-3:]
        for k in range(cols):
            for t, ref in enumerate(refs[:-3]):
                at, part = rows_at(e ^ t, rows), ref[c ^ k, :rows, :].astype(f32)
                gate_out[at, k * width : (k + 1) * width] = part[:, :width]
                up_out[at, k * width : (k + 1) * width] = part[:, width:]

        def join_down(j):
            for k in range(cols):
                for t, ref in enumerate(refs[:-3]):
                    at = k * width + (j ^ t) * down_rows
                    at = slice(at, at + down_rows)
                    down_out[at, :both] = ref[c ^ k, rows : rows + down_rows, :].astype(f32)
                    down_out[at, both:] = ref[c ^ k, rows + down_rows :, : features - both].astype(f32)

        each_index(e, shares, join_down)

    outs = (
        *[jax.ShapeDtypeStruct((shares * rows, cols * width), f32)] * 2,
        jax.ShapeDtypeStruct((cols * width, features), f32),
    )
    return cut_call(kernel, info, parts, outs)


def attention_call(kernel, place, operands, outs, scratch, work, waits):
    return pl.pallas_call(
        lambda place, *refs: kernel(place, *refs[: len(operands)], *refs[len(operands) + len(waits) :]),
        out_shape=outs,
        grid_spec=pltpu.PrefetchScalarGridSpec(
            num_scalar_prefetch=1,
            grid=(1,),
            in_specs=[whole_spec(x.shape) for x in operands] + [in_place] * len(waits),
            out_specs=[whole_spec(x.shape) for x in outs],
            scratch_shapes=scratch,
        ),
        compiler_params=pltpu.CompilerParams(vmem_limit_bytes=vmem_limit),
        cost_estimate=pl.CostEstimate(
            flops=work, bytes_accessed=2**10, transcendentals=0
        ),
    )(place, *operands, *waits)


def attention_forward(place, queries, kv_parts, chunk, waits):
    rows, total_width = queries.shape
    width = kv_parts[0].shape[1] // 2
    heads, blocks, keys = total_width // width, rows // chunk, rows * len(kv_parts)
    return attention_call(
        functools.partial(attention_kernel, chunk),
        place,
        (queries, *kv_parts),
        (
            jax.ShapeDtypeStruct((rows, total_width), bf16),
            jax.ShapeDtypeStruct((blocks, width, heads * chunk), f32),
            jax.ShapeDtypeStruct((blocks, 1, heads * chunk), f32),
        ),
        [pltpu.VMEM((keys, width), bf16)] * 2,
        4 * rows * heads * keys * width,
        waits,
    )


def attention_backward(place, queries, grads, out, lse, kv_parts, chunk, waits):
    rows, total_width = queries.shape
    width = kv_parts[0].shape[1] // 2
    keys = rows * len(kv_parts)
    return attention_call(
        functools.partial(attention_back_kernel, chunk),
        place,
        (queries, grads, out, lse, *kv_parts),
        (
            jax.ShapeDtypeStruct((rows, total_width), f32),
            jax.ShapeDtypeStruct((len(kv_parts), rows, 2 * width), bf16),
        ),
        [pltpu.VMEM((keys, width), bf16)] * 2 + [pltpu.VMEM((keys, width), f32)] * 2,
        10 * rows * total_width * keys,
        waits,
    )


def silu_back(gate_pre, up_pre, grad_hidden):
    sigmoid_vals = jax.nn.sigmoid(gate_pre)
    silu = gate_pre * sigmoid_vals
    grad_gate = grad_hidden * up_pre * sigmoid_vals * (1.0 + gate_pre * (1.0 - sigmoid_vals))
    return silu * up_pre, grad_gate.astype(bf16), (grad_hidden * silu).astype(bf16)


def experts_kernel(counts, unused, local, tiles, chunks, info, *refs):
    groups = len(counts)
    x_refs, refs = refs[: sum(counts)], refs[sum(counts) :]
    mix_refs, refs = refs[: sum(counts)], refs[sum(counts) :]
    g_refs, refs = refs[:groups], refs[groups:]
    refs = refs[:6] + refs[6 + unused :]
    (
        slot_ref, slot_t_ref, w_in, w_down, s_in, s_down,
        xs_ref, gs_ref, hidden_ref, pre_ref, own_x_ref, own_g_ref, s_hidden_ref, s_pre_ref,
    ), refs = refs[:14], refs[14:]
    out_refs, refs = refs[:groups], refs[groups:]
    norm_refs, refs = refs[:groups], refs[groups:]
    pick, put, acc_in, acc_down, s_acc_in, s_acc_down, term_buf = refs
    step = pl.program_id(0)
    capacity, tokens = pick.shape[1], pick.shape[2]
    width, s_width = w_down.shape[1], s_down.shape[0]

    @pl.when(step == 0)
    def _():
        for at in range(groups * local):
            slots = lax.broadcasted_iota(jnp.int32, (capacity, tokens), 0)
            pick[at] = jnp.where(slots == slot_ref[at : at + 1, :], 1.0, 0.0).astype(bf16)
            slots = lax.broadcasted_iota(jnp.int32, (tokens, capacity), 1)
            put[at // local, :, (at % local) * capacity : (at % local + 1) * capacity] = jnp.where(
                slots == slot_t_ref[:, at : at + 1], 1.0, 0.0
            ).astype(bf16)
        acc_in[...] = jnp.zeros_like(acc_in)
        acc_down[...] = jnp.zeros_like(acc_down)
        s_acc_in[...] = jnp.zeros_like(s_acc_in)
        s_acc_down[...] = jnp.zeros_like(s_acc_down)

    @pl.when(step < tiles)
    def _():
        for t in range(groups):
            parts = slice(sum(counts[:t]), sum(counts[: t + 1]))
            x = jnp.concatenate([ref[...] for ref in x_refs[parts]], axis=0)
            chunk = tokens // chunks
            g = jnp.concatenate(
                [
                    g_refs[t][pl.ds(pl.multiple_of(info[k] * chunk, chunk), chunk), :]
                    for k in range(chunks)
                ],
                axis=0,
            )
            for l in range(local):
                rows = slice(t * capacity, (t + 1) * capacity)
                xs_ref[l, rows, :] = dot(pick[t * local + l], x).astype(bf16)
                gs_ref[l, rows, :] = dot(pick[t * local + l], g).astype(bf16)
            if t == 0:
                own_x_ref[...] = x
                own_g_ref[...] = g
                s_acc_in[...] += dot(x, s_in[...])
                s_acc_down[...] += dot(g, s_down[...], (1, 1))
        for l in range(local):
            acc_in[l] += dot(xs_ref[l], w_in[l])
            acc_down[l] += dot(gs_ref[l], w_down[l], (1, 1))

    @pl.when(step == tiles - 1)
    def _():
        mixes = [
            jnp.concatenate([ref[...] for ref in mix_refs[sum(counts[:t]) : sum(counts[: t + 1])]], axis=0)
            for t in range(groups)
        ]
        lanes = mixes[0].shape[1]
        lane = lax.broadcasted_iota(jnp.int32, (1, lanes), 1)
        spread = []
        for l in range(local):
            expert = info[chunks] + l
            weights = jnp.concatenate([dot(pick[t * local + l], mixes[t]) for t in range(groups)], axis=0)
            weights = jnp.sum(
                jnp.where(lane % (lanes // 2) == expert, weights, 0.0), axis=1, keepdims=True
            )
            grad = acc_down[l]
            hidden, d_gate, d_up = silu_back(acc_in[l, :, :width], acc_in[l, :, width:], grad * weights)
            terms = jnp.sum(hidden * grad, axis=1, keepdims=True)
            hidden_ref[l] = (hidden * weights).astype(bf16)
            pre_ref[l, :, :width] = d_gate
            pre_ref[l, :, width:] = d_up
            spread.append(jnp.where(lane == expert, terms, 0.0).astype(bf16))
        for t in range(groups):
            rows = slice(t * capacity, (t + 1) * capacity)
            term_buf[t] = dot(
                put[t], jnp.concatenate([terms[rows] for terms in spread], axis=0)
            ).astype(bf16)
        hidden, d_gate, d_up = silu_back(s_acc_in[:, :s_width], s_acc_in[:, s_width:], s_acc_down[...])
        s_hidden_ref[...] = hidden.astype(bf16)
        s_pre_ref[:, :s_width] = d_gate
        s_pre_ref[:, s_width:] = d_up

    @pl.when((step >= tiles) & (step < 2 * tiles))
    def _():
        pieces = [dot(hidden_ref[l], w_down[l]).astype(bf16) for l in range(local)]
        d_pieces = [dot(pre_ref[l], w_in[l], (1, 1)).astype(bf16) for l in range(local)]
        for t in range(groups):
            rows = slice(t * capacity, (t + 1) * capacity)
            out = dot(put[t], jnp.concatenate([piece[rows] for piece in pieces], axis=0))
            norm = dot(put[t], jnp.concatenate([piece[rows] for piece in d_pieces], axis=0))
            if t == 0:
                out = out + dot(s_hidden_ref[...], s_down[...])
                norm = norm + dot(s_pre_ref[...], s_in[...], (1, 1))
            out_refs[t][...] = out.astype(bf16)
            norm_refs[t][...] = norm.astype(bf16)

    @pl.when(step == 2 * tiles)
    def _():
        for t in range(groups):
            norm_refs[t][:, : term_buf.shape[2]] = term_buf[t]


def experts_call(at, blocks, held, x_parts, g_parts, info, slots, w_in, w_down, s_in, s_down, capacity, waits):
    counts = [len(parts) for parts in x_parts]
    x_parts = [x for parts in x_parts for x in parts]
    groups, local = len(counts), w_in.shape[0]
    chunks = info.shape[0] - 2
    model, whole_width = g_parts[0].shape[1], x_parts[0].shape[1]
    lanes = whole_width - model
    tokens = sum(x.shape[0] for x in x_parts[: counts[0]])
    tile = 512 if groups <= 2 else 256
    tiles = model // tile
    width, s_width = w_down.shape[1], s_down.shape[0]
    rows = groups * capacity

    def tokens_in(i, info):
        return (0, jnp.minimum(i, tiles - 1))

    def picked(i, info):
        return (0, at, jnp.minimum(i, tiles - 1))

    def own(i, info):
        return (at, jnp.minimum(i, tiles - 1))

    def summed(i, info):
        return (info[chunks + 1], jnp.clip(i - tiles, 0, tiles - 1))

    def summed_norm(i, info):
        return (0, jnp.maximum(i - tiles, 0))

    in_specs = [
        *(pl.BlockSpec((x.shape[0], tile), tokens_in) for x in x_parts),
        *(pl.BlockSpec((x.shape[0], lanes), lambda i, info: (0, model // lanes)) for x in x_parts),
        *[pl.BlockSpec((tokens, tile), tokens_in)] * groups,
        whole_spec(slots.shape),
        whole_spec(slots.shape[::-1]),
        pl.BlockSpec((local, tile, 2 * width), lambda i, info: (0, i % tiles, 0)),
        pl.BlockSpec((local, width, tile), lambda i, info: (0, 0, i % tiles)),
        pl.BlockSpec((tile, 2 * s_width), lambda i, info: (i % tiles, 0)),
        pl.BlockSpec((s_width, tile), lambda i, info: (0, i % tiles)),
        *[in_place] * (len(held) + len(waits)),
    ]
    kept = (
        jax.ShapeDtypeStruct((local, blocks * rows, model), bf16),
        jax.ShapeDtypeStruct((local, blocks * rows, model), bf16),
        jax.ShapeDtypeStruct((local, blocks * rows, width), bf16),
        jax.ShapeDtypeStruct((local, blocks * rows, 2 * width), bf16),
        jax.ShapeDtypeStruct((blocks * tokens, model), bf16),
        jax.ShapeDtypeStruct((blocks * tokens, model), bf16),
        jax.ShapeDtypeStruct((blocks * tokens, s_width), bf16),
        jax.ShapeDtypeStruct((blocks * tokens, 2 * s_width), bf16),
        *[jax.ShapeDtypeStruct((blocks * tokens, model), bf16)] * groups,
    )
    norms = (jax.ShapeDtypeStruct((tokens, whole_width), bf16),) * groups
    out_specs = [
        pl.BlockSpec((local, rows, tile), picked),
        pl.BlockSpec((local, rows, tile), picked),
        pl.BlockSpec((local, rows, width), lambda i, info: (0, at, 0)),
        pl.BlockSpec((local, rows, 2 * width), lambda i, info: (0, at, 0)),
        pl.BlockSpec((tokens, tile), own),
        pl.BlockSpec((tokens, tile), own),
        pl.BlockSpec((tokens, s_width), lambda i, info: (at, 0)),
        pl.BlockSpec((tokens, 2 * s_width), lambda i, info: (at, 0)),
        *[pl.BlockSpec((tokens, tile), summed)] * groups,
        *[pl.BlockSpec((tokens, tile), summed_norm)] * groups,
    ]
    work = 2 * model * (
        4 * groups * local * capacity * tokens + 6 * local * rows * width + 6 * tokens * s_width
    )
    first = 1 + len(in_specs) - len(held) - len(waits)
    results = pl.pallas_call(
        functools.partial(experts_kernel, counts, len(held) + len(waits), local, tiles, chunks),
        out_shape=(*kept, *norms),
        grid_spec=pltpu.PrefetchScalarGridSpec(
            num_scalar_prefetch=1,
            grid=(2 * tiles + 1,),
            in_specs=in_specs,
            out_specs=out_specs,
            scratch_shapes=[
                pltpu.VMEM((groups * local, capacity, tokens), bf16),
                pltpu.VMEM((groups, tokens, local * capacity), bf16),
                pltpu.VMEM((local, rows, 2 * width), f32),
                pltpu.VMEM((local, rows, width), f32),
                pltpu.VMEM((tokens, 2 * s_width), f32),
                pltpu.VMEM((tokens, s_width), f32),
                pltpu.VMEM((groups, tokens, lanes), bf16),
            ],
        ),
        input_output_aliases={first + i: i for i in range(len(held))},
        compiler_params=pltpu.CompilerParams(vmem_limit_bytes=vmem_limit),
        cost_estimate=pl.CostEstimate(flops=work, bytes_accessed=2**10, transcendentals=0),
    )(info, *x_parts, *x_parts, *g_parts, slots, slots.T, w_in, w_down, s_in, s_down, *held, *waits)
    return list(results[: len(kept)]), list(results[len(kept) :])


def shards(
    inputs,
    routes,
    w_query,
    w_key,
    w_value,
    w_output,
    gain_attn,
    gain_moe,
    w_router,
    shared_gate,
    shared_up,
    shared_down,
    expert_gate,
    expert_up,
    expert_down,
    out_grad,
):
    e, r, c = lax.axis_index("exp"), lax.axis_index("row"), lax.axis_index("col")
    E, R, C = lax.axis_size("exp"), lax.axis_size("row"), lax.axis_size("col")
    local_count, model_width, _ = expert_gate.shape
    n_experts = local_count * E * R
    block_rows, top_count = routes.shape
    capacity = 4 * block_rows * top_count // (3 * n_experts)
    home_rows = block_rows // C
    head_width = HEAD_DIM
    query_width, key_width = w_query.shape[1], w_key.shape[1]
    group_heads = query_width // key_width
    attn_scale = head_width ** (-0.5)
    sources = ring_sources("col")

    x = tokens_home(inputs, 0).astype(f32)
    small = jnp.concatenate([w_router.T, gain_attn[None], gain_moe[None]], axis=0)
    small_all = jnp.zeros((small.shape[0], model_width), f32)
    for s, part in enumerate(exchange(small, "col")):
        small_all = lax.dynamic_update_slice(small_all, part, (0, (c ^ s) * small.shape[1]))
    router_t, gain_one, gain_two = (
        small_all[:n_experts],
        small_all[n_experts],
        small_all[n_experts + 1],
    )
    inv_one = rms_inverse(x)
    norm_one = (x * inv_one * gain_one[None, :]).astype(bf16)
    norm_one_parts = row_gather(norm_one)
    norm_one_all = jnp.concatenate(norm_one_parts, axis=0)

    own_weights = own_share(jnp.concatenate([w_key, w_value, w_query, w_output], axis=1))
    weights = lax.all_gather(own_weights, ("col", "exp"), tiled=True)
    weight_in = weights[:, : query_width + 2 * key_width]
    raw = dot(norm_one_all, weight_in)
    wait = zero_of(raw)
    here = jnp.stack([e, c]).astype(jnp.int32)
    weight_out = join_weight(weights, query_width + 2 * key_width, C, E)

    s_width = shared_gate.shape[1] // C
    s_padded = -(-s_width // 128) * 128

    def col_swap(parts):
        return [swap(parts[s], "col", s) if s else parts[0] for s in range(C)]

    shared_cut = cut_shared(here, shared_gate, shared_up, shared_down, C, E, raw)
    in_rows, feature_width = shared_gate.shape[0] // E, shared_down.shape[1]
    expert_in = side_by_side(expert_gate, expert_up, raw)

    own_routes = lax.dynamic_slice_in_dim(routes, c * home_rows, home_rows, 0)
    routes_here = routes.reshape(C, home_rows, top_count)[sources].reshape(block_rows, top_count)
    expert_ids = jnp.arange(n_experts)
    first_expert = (e * R + r) * local_count
    own_ids = first_expert + jnp.arange(local_count)
    earlier = (jnp.arange(block_rows)[:, None] < jnp.arange(block_rows)[None, :]).astype(bf16)
    routes_t = routes_here.T
    routes_t = routes_t + wait
    named = jnp.stack(
        [
            (block[None] == own_ids[:, None, None]).any(axis=1)
            for of_row in exchange(routes_t, "row")
            for block in exchange(of_row, "exp")
        ]
    ).reshape(R, E * local_count, block_rows)
    rank = dot(named.reshape(-1, block_rows).astype(bf16), earlier).astype(jnp.int32)
    slots = jnp.where(named, rank.reshape(named.shape), -1)

    positions = (
        ((r ^ jnp.arange(R)) * block_rows + c * home_rows)[:, None]
        + jnp.arange(home_rows)[None, :]
    ).reshape(-1)
    cosines, sines = rope_tables(positions, head_width)
    own_rows = R * home_rows
    keys = rotate(raw[:, :key_width].reshape(own_rows, 1, head_width), cosines, sines)
    kv = jnp.concatenate([keys.reshape(own_rows, key_width), raw[:, key_width : 2 * key_width]], axis=1)
    kv_parts = exchange(kv.astype(bf16), "col")
    g_block = lax.all_gather(after(out_grad, *kv_parts[1:]), "col", axis=1, tiled=True)
    g = lax.dynamic_slice_in_dim(g_block, c * home_rows, home_rows, 0)
    queries = rotate(
        raw[:, 2 * key_width :].reshape(own_rows, group_heads, head_width), cosines, sines
    )
    queries = (queries * attn_scale).astype(bf16).reshape(own_rows, query_width)
    place = jnp.concatenate([jnp.stack([r, c]), c ^ jnp.arange(C)]).astype(jnp.int32)
    attended, att_total, lse = attention_forward(place, queries, kv_parts, home_rows, (expert_in, shared_cut))
    attn_part = dot(attended, weight_out).astype(bf16)
    shared_parts = col_swap(after(shared_cut, attended))
    sh_in, sh_down = join_shared(
        here, exchange(jnp.stack(shared_parts), "exp"), in_rows, feature_width, s_padded
    )
    hidden_state = x + row_reduce(jnp.split(attn_part, R, axis=0))[0]
    inv_two = rms_inverse(hidden_state) + zero_of(g_block, *shared_parts[1:]).astype(f32)
    norm_two = (hidden_state * inv_two * gain_two[None, :]).astype(bf16)

    norm_float = norm_two.astype(f32)
    logits = lax.dot_general(
        norm_float, router_t, (((1,), (1,)), ((), ())), precision=highest
    )
    router_probs = jax.nn.softmax(logits, axis=-1)
    routed = (own_routes[:, :, None] == expert_ids[None, None, :]).any(axis=1)
    chosen = jnp.where(routed, router_probs, 0.0)
    chosen_sum = jnp.sum(chosen, axis=1, keepdims=True)
    mix = chosen / chosen_sum

    mix_lanes = -(-n_experts // 64) * 64
    mix_first = lax.reduce_precision(mix, 8, 7)
    mix_pad = ((0, 0), (0, mix_lanes - n_experts))
    payload = jnp.concatenate(
        [
            norm_two,
            jnp.pad(mix_first.astype(bf16), mix_pad),
            jnp.pad((mix - mix_first).astype(bf16), mix_pad),
        ],
        axis=1,
    )
    payload = jnp.concatenate(ring_gather(payload, "col"), axis=0)
    grad_rows = row_gather(g_block)
    grad_own = exchange(g_block, "exp")
    payload = after(payload, *grad_rows[1:3], *grad_own[1:], sh_in)
    payload_rows = row_gather(payload)
    if R == 4:
        grad_rows = grad_rows[:3] + [jnp.concatenate(grad_rows[3:], axis=0)]
        payload_rows = [[x] for x in payload_rows[:3]] + [payload_rows[3:]]
    else:
        payload_rows = [[x] for x in payload_rows]

    def shared_gradients(kept):
        own_x, own_g, s_hidden, s_pre = kept[4:8]
        d_in = dot(own_x, s_pre, (0, 0)).astype(bf16)
        d_down = dot(s_hidden, own_g, (0, 0)).astype(bf16)
        return cut_shared_grads(here, d_in, d_down, C, E, s_width)

    kept, norms, moved = [], [], []
    for s in range(R):
        x_block = payload_rows[s]
        if E > 2 and kept:
            x_block = [after(x, kept[-1]) for x in x_block]
            grad_rows[s] = after(grad_rows[s], kept[-1])
        info = jnp.concatenate(
            [sources, jnp.stack([first_expert, r ^ s])]
        ).astype(jnp.int32)
        kept, norm = experts_call(
            s, R, kept, list(zip(*(exchange(x, "exp") for x in x_block))),
            exchange(grad_rows[s], "exp") if s else grad_own, info,
            slots[s], expert_in, expert_down, sh_in, sh_down, capacity, norms[-1:],
        )
        if s == R - 1:
            shared_grads = shared_gradients(kept)
        seen = [*moved, shared_grads[0]] if s == R - 1 else [x for later in ((1, 2), (3,))[s] for x in payload_rows[later]] if s < 2 else []
        if seen:
            norm = [norm[0], *(after(x, *seen) for x in norm[1:])]
        norms.append(reduce_parts(norm, "exp").astype(bf16))
        if s:
            moved.append(swap(norms[s], "row", s))
    kept, outs = kept[:8], kept[8:]
    rows_x, rows_g, hidden, pre = kept[:4]

    shared_sum = reduce_parts(shared_grads, "exp").astype(bf16)
    outs_moved = [swap(after(outs[t], norms[-1], shared_sum), "exp", t) for t in range(1, E)]
    shared_back = jnp.stack(col_swap(shared_sum))
    norm_block = norms[0].astype(f32)
    for x_sum in moved:
        norm_block = norm_block + x_sum.astype(f32)
    chunks = jnp.split(norm_block.astype(bf16), C, axis=0)
    home = ring_reduce(chunks, "col")
    d_norm, gate_terms = home[:, :model_width], home[:, model_width : model_width + n_experts]
    out_sum = outs[0].astype(f32)
    for part in outs_moved:
        out_sum = add(out_sum, part)
    out_sum = after(out_sum.astype(bf16), moved[-1], shared_back)
    out_rows = lax.psum_scatter(out_sum, "row", scatter_dimension=0, tiled=True)

    expert_width = expert_gate.shape[2]
    pre = after(pre, moved[-1])
    grad_expert_gate = batch_dot("lrd,lrf->ldf", rows_x, pre[:, :, :expert_width])
    grad_expert_up = batch_dot("lrd,lrf->ldf", rows_x, pre[:, :, expert_width:])
    grad_expert_down = batch_dot("lrf,lrd->lfd", after(hidden, moved[-1]), rows_g)
    inner = jnp.sum(mix * gate_terms, axis=1, keepdims=True)
    d_probs = jnp.where(routed, (gate_terms - inner) / chosen_sum, 0.0)
    d_logits = router_probs * (
        d_probs - jnp.sum(router_probs * d_probs, axis=1, keepdims=True)
    )
    d_norm = d_norm + jnp.dot(d_logits, router_t, precision=highest)
    d_norm = d_norm + zero_of(grad_expert_gate, grad_expert_up, grad_expert_down).astype(f32)
    router_part = lax.dot_general(
        d_logits, norm_float, (((0,), (0,)), ((), ())), precision=highest
    )
    d_v, gain_two_part = rms_backward(hidden_state, inv_two, gain_two, d_norm)
    d_hidden = g.astype(f32) + d_v
    d_attn = d_hidden.astype(bf16)
    d_attn_parts = row_gather(d_attn)
    d_attn_all = jnp.concatenate(d_attn_parts, axis=0)

    out_grads = batch_dot("sf,scd->cfd", attended, d_attn_all.reshape(own_rows, C, -1))
    out_grads = out_grads.astype(bf16).reshape(C * query_width, -1)

    d_attended = dot(d_attn_all, weight_out, (1, 1)).astype(bf16)
    out_chunks = jnp.split(after(out_rows, d_attended), C, axis=0)
    moe_out = ring_send(out_chunks[C - 1], "col", 1)
    d_queries, d_kv_parts = attention_backward(
        place, queries, d_attended, att_total, lse, kv_parts, home_rows,
        (out_grads,),
    )
    d_kv_parts = after(d_kv_parts, moe_out)
    d_kv = reduce_parts([d_kv_parts[k] for k in range(C)], "col")
    for k in range(C - 2, 0, -1):
        moe_out = ring_send(add(out_chunks[k], moe_out).astype(bf16), "col", 1)
    d_query_raw = rotate(
        d_queries.reshape(own_rows, group_heads, head_width), cosines, -sines
    ) * attn_scale
    d_query_raw = d_query_raw.reshape(own_rows, query_width).astype(bf16)
    norm_one_late = after(norm_one_all, d_kv_parts)
    query_grads = dot(norm_one_late, d_query_raw, (0, 0)).astype(bf16)
    d_key_raw = rotate(d_kv[:, :key_width].reshape(own_rows, 1, head_width), cosines, -sines)
    d_kv_raw = jnp.concatenate(
        [d_key_raw.reshape(own_rows, key_width), d_kv[:, key_width:]], axis=1
    ).astype(bf16)
    norm_one_part = dot(jnp.concatenate([d_kv_raw, d_query_raw], axis=1), weight_in, (1, 1)).astype(bf16)
    d_norm_one, halfway = row_reduce(jnp.split(norm_one_part, R, axis=0))
    d_x, gain_one_part = rms_backward(x, inv_one, gain_one, d_norm_one)
    grad_inputs, back = tokens_back((d_hidden + d_x).astype(bf16))

    moe_out = add(out_chunks[0], after(moe_out, *back))
    output = tokens_back((hidden_state + moe_out).astype(bf16))[0]
    out_total, query_total = reduce_weight(out_grads), reduce_weight(query_grads)
    kv_grads = dot(after(norm_one_late, *halfway), d_kv_raw, (0, 0)).astype(bf16)
    kv_total = reduce_weight(after(kv_grads, query_total, d_norm_one))
    grad_output = all_shares(after(out_total, d_norm_one)).astype(f32)
    grad_query = all_shares(after(query_total, d_norm_one)).astype(f32)
    grad_kv = all_shares(kv_total).astype(f32)
    small_part = jnp.concatenate([router_part, gain_one_part[None], gain_two_part[None]], axis=0)
    small_part = small_part + zero_of(*back).astype(f32)
    width = small.shape[1]
    mine = [
        lax.dynamic_slice_in_dim(small_part, (c ^ s) * width, width, 1) for s in range(C)
    ]
    small_sum = all_sum(all_sum(reduce_parts(mine, "col"), "row"), "exp")

    grad_shared_gate, grad_shared_up, grad_shared_down = join_shared_grads(
        here, exchange(after(shared_back, d_norm_one), "exp"), in_rows, feature_width
    )
    return (
        output,
        grad_inputs,
        grad_query,
        grad_kv[:, :key_width],
        grad_kv[:, key_width:],
        grad_output,
        small_sum[n_experts],
        small_sum[n_experts + 1],
        small_sum[:n_experts].T,
        grad_shared_gate,
        grad_shared_up,
        grad_shared_down,
        grad_expert_gate,
        grad_expert_up,
        grad_expert_down,
    )


def solution(mesh):
    tokens, weight, experts = P(("exp", "row"), "col"), P("col", "row"), P(("exp", "row"), None, "col")
    expert_down, feature = P(("exp", "row"), "col", None), P("col")
    placed = (
        tokens,
        P(("exp", "row"), None),
        weight,
        weight,
        weight,
        P("row", "col"),
        feature,
        feature,
        P("col", None),
        weight,
        weight,
        P("row", "col"),
        experts,
        experts,
        expert_down,
        tokens,
    )
    return jax.shard_map(
        shards,
        mesh=mesh,
        in_specs=placed,
        out_specs=(
            tokens,
            tokens,
            weight,
            weight,
            weight,
            P("row", "col"),
            feature,
            feature,
            P("col", None),
            weight,
            weight,
            P("row", "col"),
            experts,
            experts,
            expert_down,
        ),
        check_vma=False,
    )
```

```python
import functools

import jax
import jax.numpy as jnp
from jax import lax
from jax.experimental import pallas as pl
from jax.experimental.pallas import tpu as pltpu
from jax.sharding import PartitionSpec as P

HEAD_DIM = 128

eps = 1e-05
theta = 500000.0
highest = lax.Precision.HIGHEST
masked_value = -1e30
f32 = jnp.float32
bf16 = jnp.bfloat16
vmem_limit = 56 * 2**20


def swap(x, axis, step):
    return lax.ppermute(x, axis, [(i, i ^ step) for i in range(lax.axis_size(axis))])


def exchange(x, axis):
    return [x] + [swap(x, axis, step) for step in range(1, lax.axis_size(axis))]


def reduce_parts(parts, axis):
    total = parts[0].astype(f32)
    for step in range(1, len(parts)):
        total = total + swap(parts[step], axis, step).astype(f32)
    return total


def all_sum(x, axis):
    step = 1
    if lax.axis_size(axis) == 4:
        own, near, other, far = exchange(x, axis)
        return (own + near) + (other + far)
    while step < lax.axis_size(axis):
        x = x + swap(x, axis, step)
        step *= 2
    return x


def zero_of(*arrays):
    found = jnp.int32(0)
    for x in arrays:
        first = x[(slice(0, 1),) * x.ndim].reshape(())
        found = found + (first != first).astype(jnp.int32)
    return found


def after(x, *earlier):
    place = pl.BlockSpec(memory_space=pl.ANY)
    return pl.pallas_call(
        lambda *refs: None,
        out_shape=jax.ShapeDtypeStruct(x.shape, x.dtype),
        in_specs=[place] * (1 + len(earlier)),
        out_specs=place,
        input_output_aliases={0: 0},
    )(x, *earlier)


def ring_order(n):
    return [0] + list(range(1, n, 2)) + [i for i in range(n - 1, 0, -1) if i % 2 == 0]


def ring_pairs(n, back=False):
    order = ring_order(n)
    pairs = [(order[i], order[(i + 1) % n]) for i in range(n)]
    return [(b, a) for a, b in pairs] if back else pairs


def ring_sources(axis):
    n = lax.axis_size(axis)
    order = ring_order(n)
    place = jnp.array([order.index(i) for i in range(n)])[lax.axis_index(axis)]
    return jnp.array(order)[(place - jnp.arange(n)) % n]


def ring_gather(x, axis):
    parts, n = [x], lax.axis_size(axis)
    for _ in range(n - 1):
        parts.append(lax.ppermute(parts[-1], axis, ring_pairs(n)))
    return parts


def ring_send(x, axis, k):
    order = ring_order(lax.axis_size(axis))
    n = len(order)
    return lax.ppermute(x, axis, [(order[i], order[(i - k) % n]) for i in range(n)])


def ring_reduce(parts, axis):
    total = parts[0].astype(f32)
    for k in range(1, len(parts)):
        total = total + ring_send(parts[k], axis, k).astype(f32)
    return total


def row_gather(x):
    if lax.axis_size("row") != 4:
        return exchange(x, "row")
    x_near, y_near = swap(x, "row", 1), swap(x, "row", 2)
    middle = x.shape[0] // 2
    return [x, x_near, y_near, swap(y_near[:middle], "row", 1), swap(x_near[middle:], "row", 2)]


def add(left, right):
    return left.astype(f32) + right.astype(f32)


def row_reduce(blocks):
    if len(blocks) != 4:
        return reduce_parts(blocks, "row"), blocks[:1]
    own, x_near, y_near, far = blocks
    middle = own.shape[0] // 2
    far_x, far_y = swap(far[:middle], "row", 1), swap(far[middle:], "row", 2)
    y_first = add(y_near[:middle], far_x).astype(bf16)
    x_second = add(x_near[middle:], far_y).astype(bf16)
    y_sum = swap(jnp.concatenate([y_first, y_near[middle:]], axis=0), "row", 2)
    x_sum = swap(jnp.concatenate([x_near[:middle], x_second], axis=0), "row", 1)
    return add(own, x_sum) + y_sum.astype(f32), [far_x, far_y]


def tokens_home(x, wait):
    c, n = lax.axis_index("col"), lax.axis_size("col")
    rows, width = x.shape[0] // n, x.shape[1]
    whole = jnp.zeros((rows, n * width), x.dtype)
    for s in range(n):
        piece = lax.dynamic_slice_in_dim(x, (c ^ s) * rows + wait, rows, 0)
        piece = swap(piece, "col", s) if s else piece
        whole = lax.dynamic_update_slice(whole, piece, (0, (c ^ s) * width))
    return whole


def tokens_back(x):
    c, n = lax.axis_index("col"), lax.axis_size("col")
    rows, width = x.shape[0], x.shape[1] // n
    whole, moved = jnp.zeros((n * rows, width), x.dtype), []
    for s in range(n):
        piece = lax.dynamic_slice_in_dim(x, (c ^ s) * width, width, 1)
        if s:
            piece = swap(piece, "col", s)
            moved.append(piece)
        whole = lax.dynamic_update_slice(whole, piece, ((c ^ s) * rows, 0))
    return whole, moved


def own_share(weight, wait=0):
    share = weight.shape[0] // lax.axis_size("exp")
    return lax.dynamic_slice_in_dim(weight, lax.axis_index("exp") * share + wait, share, 0)


def all_shares(total):
    e = lax.axis_index("exp")
    shares = lax.axis_size("exp")
    whole = jnp.zeros((shares,) + total.shape, total.dtype)
    for t, piece in enumerate(exchange(total, "exp")):
        whole = lax.dynamic_update_index_in_dim(whole, piece, e ^ t, 0)
    return whole.reshape((shares * total.shape[0],) + total.shape[1:])


def reduce_weight(grad):
    return lax.psum_scatter(grad, ("col", "exp"), scatter_dimension=0, tiled=True)


def rope_tables(positions, head_width):
    half_width = head_width // 2
    frequency = theta ** (-2.0 * jnp.arange(half_width, dtype=f32) / head_width)
    angles = positions.astype(f32)[:, None] * frequency[None, :]
    return (jnp.cos(angles), jnp.sin(angles))


def rotate(source, cosines, sines):
    half_width = source.shape[-1] // 2
    first, second = source[..., :half_width], source[..., half_width:]
    cos_view, sin_view = cosines[:, None, :], sines[:, None, :]
    return jnp.concatenate(
        [first * cos_view - second * sin_view, first * sin_view + second * cos_view], axis=-1
    )


def dot(left, right, contract=(1, 0)):
    return lax.dot_general(
        left, right, (((contract[0],), (contract[1],)), ((), ())), preferred_element_type=f32
    )


def batch_dot(spec, left, right):
    return jnp.einsum(spec, left, right, preferred_element_type=f32)


def rms_inverse(values):
    return lax.rsqrt(jnp.mean(values * values, axis=1, keepdims=True) + eps)


def rms_backward(values, inv_rms, gain, grad_norm):
    scaled_grad = grad_norm * gain[None, :]
    inner = jnp.mean(scaled_grad * values, axis=1, keepdims=True)
    grad_values = inv_rms * (scaled_grad - values * (inv_rms * inv_rms * inner))
    return grad_values, jnp.sum(grad_norm * values * inv_rms, axis=0)


def place_keys(place, kv_refs, key_buf, value_buf, chunk):
    row, blocks, width = place[0], kv_refs[0].shape[0] // chunk, key_buf.shape[1]
    for k, ref in enumerate(kv_refs):
        for s in range(blocks):
            at = pl.multiple_of(((row ^ s) * len(kv_refs) + place[2 + k]) * chunk, chunk)
            key_buf[pl.ds(at, chunk), :] = ref[s * chunk : (s + 1) * chunk, :width]
            value_buf[pl.ds(at, chunk), :] = ref[s * chunk : (s + 1) * chunk, width:]


def head_rows(ref, rows, width):
    block = ref[rows, :]
    return jnp.concatenate(
        [block[:, h * width : (h + 1) * width] for h in range(block.shape[1] // width)], axis=0
    )


def scores_tile(place, key_tile, queries, block, tile, chunk):
    scores = dot(key_tile, queries, (1, 1))
    key_at = tile * key_tile.shape[0] + lax.broadcasted_iota(jnp.int32, scores.shape, 0)
    lane = lax.broadcasted_iota(jnp.int32, scores.shape, 1)
    query_at = block * key_tile.shape[0] + place[1] * chunk + lane % chunk
    return jnp.where(key_at <= query_at, scores, masked_value)


def attention_kernel(chunk, place, q_ref, *refs):
    kv_refs, (out_ref, total_ref, lse_ref, key_buf, value_buf) = refs[:-5], refs[-5:]
    width = key_buf.shape[1]
    blocks = q_ref.shape[0] // chunk
    tile_rows = key_buf.shape[0] // blocks
    place_keys(place, kv_refs, key_buf, value_buf, chunk)

    @pl.loop(0, blocks)
    def _(block):
        rows = pl.ds(pl.multiple_of((place[0] ^ block) * chunk, chunk), chunk)
        queries = head_rows(q_ref, rows, width)
        count = queries.shape[0]

        def step(tile, carry):
            peak, total, out = carry
            at = pl.ds(pl.multiple_of(tile * tile_rows, tile_rows), tile_rows)
            scores = scores_tile(place, key_buf[at, :], queries, block, tile, chunk)
            new_peak = jnp.maximum(peak, jnp.max(scores, axis=0, keepdims=True))
            weights = jnp.exp(scores - new_peak)
            shrink = jnp.exp(peak - new_peak)
            total = total * shrink + jnp.sum(weights, axis=0, keepdims=True)
            part = dot(value_buf[at, :], weights.astype(bf16), (0, 0))
            return new_peak, total, out * shrink + part

        start = (
            jnp.full((1, count), masked_value, f32),
            jnp.zeros((1, count), f32),
            jnp.zeros((width, count), f32),
        )
        peak, total, out = lax.fori_loop(0, block + 1, step, start)
        out = out / total
        total_ref[pl.ds(block, 1)] = out[None]
        lse_ref[pl.ds(block, 1)] = (peak + jnp.log(total))[None]
        for h in range(count // chunk):
            head = out[:, h * chunk : (h + 1) * chunk]
            out_ref[rows, h * width : (h + 1) * width] = head.T.astype(bf16)


def attention_back_kernel(chunk, place, q_ref, grad_ref, total_ref, lse_ref, *refs):
    kv_refs = refs[:-6]
    dq_ref, dkv_ref, key_buf, value_buf, dk_buf, dv_buf = refs[-6:]
    width = key_buf.shape[1]
    blocks = q_ref.shape[0] // chunk
    tile_rows = key_buf.shape[0] // blocks
    place_keys(place, kv_refs, key_buf, value_buf, chunk)
    dk_buf[...] = jnp.zeros_like(dk_buf)
    dv_buf[...] = jnp.zeros_like(dv_buf)

    @pl.loop(0, blocks)
    def _(block):
        rows = pl.ds(pl.multiple_of((place[0] ^ block) * chunk, chunk), chunk)
        queries = head_rows(q_ref, rows, width)
        grads = head_rows(grad_ref, rows, width)
        count = queries.shape[0]
        out = total_ref[pl.ds(block, 1)][0]
        lse = lse_ref[pl.ds(block, 1)][0]
        grads_t = jnp.concatenate(
            [grads[h * chunk : (h + 1) * chunk].astype(f32).T for h in range(count // chunk)], axis=1
        )
        inner = jnp.sum(out * grads_t, axis=0, keepdims=True)

        def step(tile, d_queries):
            at = pl.ds(pl.multiple_of(tile * tile_rows, tile_rows), tile_rows)
            keys = key_buf[at, :]
            scores = scores_tile(place, keys, queries, block, tile, chunk)
            probs = jnp.exp(scores - lse)
            d_probs = dot(value_buf[at, :], grads, (1, 1))
            d_scores = (probs * (d_probs - inner)).astype(bf16)
            dk_buf[at, :] += dot(d_scores, queries)
            dv_buf[at, :] += dot(probs.astype(bf16), grads)
            return d_queries + dot(keys, d_scores, (0, 0))

        d_queries = lax.fori_loop(0, block + 1, step, jnp.zeros((width, count), f32))
        for h in range(count // chunk):
            head = d_queries[:, h * chunk : (h + 1) * chunk]
            dq_ref[rows, h * width : (h + 1) * width] = head.T

    for k in range(len(kv_refs)):
        for s in range(blocks):
            at = pl.ds(pl.multiple_of(((place[0] ^ s) * len(kv_refs) + place[2 + k]) * chunk, chunk), chunk)
            dkv_ref[k, s * chunk : (s + 1) * chunk, :width] = dk_buf[at, :].astype(bf16)
            dkv_ref[k, s * chunk : (s + 1) * chunk, width:] = dv_buf[at, :].astype(bf16)


in_place = pl.BlockSpec(memory_space=pl.ANY)


def whole_spec(shape):
    return pl.BlockSpec(shape, lambda *_: (0,) * len(shape))


def side_by_side(left, right, wait):
    count, rows, width = left.shape
    tile = 512

    def kernel(left_ref, right_ref, _, both_ref):
        both_ref[:, :width] = left_ref[...]
        both_ref[:, width:] = right_ref[...]

    spec = pl.BlockSpec((None, tile, width), lambda i, j: (i, j, 0))
    return pl.pallas_call(
        kernel,
        out_shape=jax.ShapeDtypeStruct((count, rows, 2 * width), left.dtype),
        grid=(count, rows // tile),
        in_specs=[spec, spec, in_place],
        out_specs=pl.BlockSpec((None, tile, 2 * width), lambda i, j: (i, j, 0)),
        cost_estimate=pl.CostEstimate(flops=0, bytes_accessed=2**10, transcendentals=0),
    )(left, right, wait)


def rows_at(index, count):
    return pl.ds(pl.multiple_of(index * count, count), count)


def cut_call(kernel, info, operands, outs, waits=()):
    return pl.pallas_call(
        lambda info, *refs: kernel(info[0], info[1], *refs[: len(operands)], *refs[len(operands) + len(waits) :]),
        out_shape=outs,
        grid_spec=pltpu.PrefetchScalarGridSpec(
            num_scalar_prefetch=1,
            grid=(1,),
            in_specs=[whole_spec(x.shape) for x in operands] + [in_place] * len(waits),
            out_specs=[whole_spec(x.shape) for x in outs],
        ),
        compiler_params=pltpu.CompilerParams(vmem_limit_bytes=vmem_limit),
        cost_estimate=pl.CostEstimate(flops=0, bytes_accessed=2**10, transcendentals=0),
    )(info, *operands, *waits)


def join_weight(blocks, first, cols, shares):
    rows, width = blocks.shape[0] // (cols * shares), blocks.shape[1] - first

    def kernel(ref, out_ref):
        for k in range(cols):
            for t in range(shares):
                at = (k * shares + t) * rows
                out_ref[t * rows : (t + 1) * rows, k * width : (k + 1) * width] = ref[at : at + rows, first:]

    return pl.pallas_call(
        kernel,
        out_shape=jax.ShapeDtypeStruct((shares * rows, cols * width), blocks.dtype),
        compiler_params=pltpu.CompilerParams(vmem_limit_bytes=vmem_limit),
        cost_estimate=pl.CostEstimate(flops=0, bytes_accessed=2**10, transcendentals=0),
    )(blocks)


def each_index(index, count, work):
    for j in range(count):
        pl.when(index == j)(functools.partial(work, j))


def lanes_at(index, width, first, count):
    return pl.ds(pl.multiple_of(index * width + first, 128), count)


def cut_shared(info, gate, up, down, cols, shares, wait):
    rows, width, features = gate.shape[0] // shares, gate.shape[1] // cols, down.shape[1]
    both, down_rows = 2 * width, gate.shape[1] // cols // shares

    def kernel(e, c, gate_ref, up_ref, down_ref, out):
        for k in range(cols):
            at = rows_at(e, rows)
            out[c ^ k, :rows, :width] = gate_ref[at, k * width : (k + 1) * width]
            out[c ^ k, :rows, width:] = up_ref[at, k * width : (k + 1) * width]

        def cut_down(j):
            for k in range(cols):
                piece = down_ref[k * width + j * down_rows : k * width + (j + 1) * down_rows, :]
                out[c ^ k, rows : rows + down_rows, :] = piece[:, :both]
                out[c ^ k, rows + down_rows :, : features - both] = piece[:, both:]

        each_index(e, shares, cut_down)

    outs = (jax.ShapeDtypeStruct((cols, rows + 2 * down_rows, both), bf16),)
    return cut_call(kernel, info, (gate, up, down), outs, (wait,))[0]


def join_shared(info, parts, rows, features, padded):
    cols, all_rows, both = parts[0].shape
    width, shares, down_rows = both // 2, len(parts), (all_rows - rows) // 2

    def kernel(e, c, *refs):
        in_out, down_out = refs[-2:]
        in_out[...] = jnp.zeros_like(in_out)
        down_out[...] = jnp.zeros_like(down_out)
        for s in range(cols):
            for t, ref in enumerate(refs[:-2]):
                at = rows_at((c ^ s) * shares + (e ^ t), rows)
                in_out[at, :width] = ref[s, :rows, :width]
                in_out[at, padded : padded + width] = ref[s, :rows, width:]

        def join_down(j):
            for s in range(cols):
                for t, ref in enumerate(refs[:-2]):
                    at = slice((j ^ t) * down_rows, ((j ^ t) + 1) * down_rows)
                    down_out[at, lanes_at(c ^ s, features, 0, both)] = ref[s, rows : rows + down_rows, :]
                    down_out[at, lanes_at(c ^ s, features, both, features - both)] = ref[
                        s, rows + down_rows :, : features - both
                    ]

        each_index(e, shares, join_down)

    outs = (
        jax.ShapeDtypeStruct((cols * shares * rows, 2 * padded), bf16),
        jax.ShapeDtypeStruct((padded, cols * features), bf16),
    )
    return cut_call(kernel, info, parts, outs)


def cut_shared_grads(info, grad_in, grad_down, cols, shares, width):
    rows, padded = grad_in.shape[0] // (cols * shares), grad_in.shape[1] // 2
    both, down_rows, features = 2 * width, width // shares, grad_down.shape[1] // cols

    def kernel(e, c, in_ref, down_ref, *outs):
        for s in range(cols):
            for t, out in enumerate(outs):
                at = rows_at((c ^ s) * shares + (e ^ t), rows)
                out[s, :rows, :width] = in_ref[at, :width]
                out[s, :rows, width:] = in_ref[at, padded : padded + width]

        def cut_down(j):
            for s in range(cols):
                for t, out in enumerate(outs):
                    at = slice((j ^ t) * down_rows, ((j ^ t) + 1) * down_rows)
                    out[s, rows : rows + down_rows, :] = down_ref[at, lanes_at(c ^ s, features, 0, both)]
                    out[s, rows + down_rows :, : features - both] = down_ref[
                        at, lanes_at(c ^ s, features, both, features - both)
                    ]

        each_index(e, shares, cut_down)

    outs = (jax.ShapeDtypeStruct((cols, rows + 2 * down_rows, both), bf16),) * shares
    return cut_call(kernel, info, (grad_in, grad_down), outs)


def join_shared_grads(info, parts, rows, features):
    cols, all_rows, both = parts[0].shape
    width, shares, down_rows = both // 2, len(parts), (all_rows - rows) // 2

    def kernel(e, c, *refs):
        gate_out, up_out, down_out = refs[-3:]
        for k in range(cols):
            for t, ref in enumerate(refs[:-3]):
                at, part = rows_at(e ^ t, rows), ref[c ^ k, :rows, :].astype(f32)
                gate_out[at, k * width : (k + 1) * width] = part[:, :width]
                up_out[at, k * width : (k + 1) * width] = part[:, width:]

        def join_down(j):
            for k in range(cols):
                for t, ref in enumerate(refs[:-3]):
                    at = k * width + (j ^ t) * down_rows
                    at = slice(at, at + down_rows)
                    down_out[at, :both] = ref[c ^ k, rows : rows + down_rows, :].astype(f32)
                    down_out[at, both:] = ref[c ^ k, rows + down_rows :, : features - both].astype(f32)

        each_index(e, shares, join_down)

    outs = (
        *[jax.ShapeDtypeStruct((shares * rows, cols * width), f32)] * 2,
        jax.ShapeDtypeStruct((cols * width, features), f32),
    )
    return cut_call(kernel, info, parts, outs)


def attention_call(kernel, place, operands, outs, scratch, work, waits):
    return pl.pallas_call(
        lambda place, *refs: kernel(place, *refs[: len(operands)], *refs[len(operands) + len(waits) :]),
        out_shape=outs,
        grid_spec=pltpu.PrefetchScalarGridSpec(
            num_scalar_prefetch=1,
            grid=(1,),
            in_specs=[whole_spec(x.shape) for x in operands] + [in_place] * len(waits),
            out_specs=[whole_spec(x.shape) for x in outs],
            scratch_shapes=scratch,
        ),
        compiler_params=pltpu.CompilerParams(vmem_limit_bytes=vmem_limit),
        cost_estimate=pl.CostEstimate(
            flops=work, bytes_accessed=2**10, transcendentals=0
        ),
    )(place, *operands, *waits)


def attention_forward(place, queries, kv_parts, chunk, waits):
    rows, total_width = queries.shape
    width = kv_parts[0].shape[1] // 2
    heads, blocks, keys = total_width // width, rows // chunk, rows * len(kv_parts)
    return attention_call(
        functools.partial(attention_kernel, chunk),
        place,
        (queries, *kv_parts),
        (
            jax.ShapeDtypeStruct((rows, total_width), bf16),
            jax.ShapeDtypeStruct((blocks, width, heads * chunk), f32),
            jax.ShapeDtypeStruct((blocks, 1, heads * chunk), f32),
        ),
        [pltpu.VMEM((keys, width), bf16)] * 2,
        4 * rows * heads * keys * width,
        waits,
    )


def attention_backward(place, queries, grads, out, lse, kv_parts, chunk, waits):
    rows, total_width = queries.shape
    width = kv_parts[0].shape[1] // 2
    keys = rows * len(kv_parts)
    return attention_call(
        functools.partial(attention_back_kernel, chunk),
        place,
        (queries, grads, out, lse, *kv_parts),
        (
            jax.ShapeDtypeStruct((rows, total_width), f32),
            jax.ShapeDtypeStruct((len(kv_parts), rows, 2 * width), bf16),
        ),
        [pltpu.VMEM((keys, width), bf16)] * 2 + [pltpu.VMEM((keys, width), f32)] * 2,
        10 * rows * total_width * keys,
        waits,
    )


def silu_back(gate_pre, up_pre, grad_hidden):
    sigmoid_vals = jax.nn.sigmoid(gate_pre)
    silu = gate_pre * sigmoid_vals
    grad_gate = grad_hidden * up_pre * sigmoid_vals * (1.0 + gate_pre * (1.0 - sigmoid_vals))
    return silu * up_pre, grad_gate.astype(bf16), (grad_hidden * silu).astype(bf16)


def experts_kernel(counts, unused, local, tiles, chunks, info, *refs):
    groups = len(counts)
    x_refs, refs = refs[: sum(counts)], refs[sum(counts) :]
    mix_refs, refs = refs[: sum(counts)], refs[sum(counts) :]
    g_refs, refs = refs[:groups], refs[groups:]
    refs = refs[:6] + refs[6 + unused :]
    (
        slot_ref, slot_t_ref, w_in, w_down, s_in, s_down,
        xs_ref, gs_ref, hidden_ref, pre_ref, own_x_ref, own_g_ref, s_hidden_ref, s_pre_ref,
    ), refs = refs[:14], refs[14:]
    out_refs, refs = refs[:groups], refs[groups:]
    norm_refs, refs = refs[:groups], refs[groups:]
    pick, put, acc_in, acc_down, s_acc_in, s_acc_down, term_buf = refs
    step = pl.program_id(0)
    capacity, tokens = pick.shape[1], pick.shape[2]
    width, s_width = w_down.shape[1], s_down.shape[0]

    @pl.when(step == 0)
    def _():
        for at in range(groups * local):
            slots = lax.broadcasted_iota(jnp.int32, (capacity, tokens), 0)
            pick[at] = jnp.where(slots == slot_ref[at : at + 1, :], 1.0, 0.0).astype(bf16)
            slots = lax.broadcasted_iota(jnp.int32, (tokens, capacity), 1)
            put[at // local, :, (at % local) * capacity : (at % local + 1) * capacity] = jnp.where(
                slots == slot_t_ref[:, at : at + 1], 1.0, 0.0
            ).astype(bf16)
        acc_in[...] = jnp.zeros_like(acc_in)
        acc_down[...] = jnp.zeros_like(acc_down)
        s_acc_in[...] = jnp.zeros_like(s_acc_in)
        s_acc_down[...] = jnp.zeros_like(s_acc_down)

    @pl.when(step < tiles)
    def _():
        for t in range(groups):
            parts = slice(sum(counts[:t]), sum(counts[: t + 1]))
            x = jnp.concatenate([ref[...] for ref in x_refs[parts]], axis=0)
            chunk = tokens // chunks
            g = jnp.concatenate(
                [
                    g_refs[t][pl.ds(pl.multiple_of(info[k] * chunk, chunk), chunk), :]
                    for k in range(chunks)
                ],
                axis=0,
            )
            for l in range(local):
                rows = slice(t * capacity, (t + 1) * capacity)
                xs_ref[l, rows, :] = dot(pick[t * local + l], x).astype(bf16)
                gs_ref[l, rows, :] = dot(pick[t * local + l], g).astype(bf16)
            if t == 0:
                own_x_ref[...] = x
                own_g_ref[...] = g
                s_acc_in[...] += dot(x, s_in[...])
                s_acc_down[...] += dot(g, s_down[...], (1, 1))
        for l in range(local):
            acc_in[l] += dot(xs_ref[l], w_in[l])
            acc_down[l] += dot(gs_ref[l], w_down[l], (1, 1))

    @pl.when(step == tiles - 1)
    def _():
        mixes = [
            jnp.concatenate([ref[...] for ref in mix_refs[sum(counts[:t]) : sum(counts[: t + 1])]], axis=0)
            for t in range(groups)
        ]
        lanes = mixes[0].shape[1]
        lane = lax.broadcasted_iota(jnp.int32, (1, lanes), 1)
        spread = []
        for l in range(local):
            expert = info[chunks] + l
            weights = jnp.concatenate([dot(pick[t * local + l], mixes[t]) for t in range(groups)], axis=0)
            weights = jnp.sum(
                jnp.where(lane % (lanes // 2) == expert, weights, 0.0), axis=1, keepdims=True
            )
            grad = acc_down[l]
            hidden, d_gate, d_up = silu_back(acc_in[l, :, :width], acc_in[l, :, width:], grad * weights)
            terms = jnp.sum(hidden * grad, axis=1, keepdims=True)
            hidden_ref[l] = (hidden * weights).astype(bf16)
            pre_ref[l, :, :width] = d_gate
            pre_ref[l, :, width:] = d_up
            spread.append(jnp.where(lane == expert, terms, 0.0).astype(bf16))
        for t in range(groups):
            rows = slice(t * capacity, (t + 1) * capacity)
            term_buf[t] = dot(
                put[t], jnp.concatenate([terms[rows] for terms in spread], axis=0)
            ).astype(bf16)
        hidden, d_gate, d_up = silu_back(s_acc_in[:, :s_width], s_acc_in[:, s_width:], s_acc_down[...])
        s_hidden_ref[...] = hidden.astype(bf16)
        s_pre_ref[:, :s_width] = d_gate
        s_pre_ref[:, s_width:] = d_up

    @pl.when((step >= tiles) & (step < 2 * tiles))
    def _():
        pieces = [dot(hidden_ref[l], w_down[l]).astype(bf16) for l in range(local)]
        d_pieces = [dot(pre_ref[l], w_in[l], (1, 1)).astype(bf16) for l in range(local)]
        for t in range(groups):
            rows = slice(t * capacity, (t + 1) * capacity)
            out = dot(put[t], jnp.concatenate([piece[rows] for piece in pieces], axis=0))
            norm = dot(put[t], jnp.concatenate([piece[rows] for piece in d_pieces], axis=0))
            if t == 0:
                out = out + dot(s_hidden_ref[...], s_down[...])
                norm = norm + dot(s_pre_ref[...], s_in[...], (1, 1))
            out_refs[t][...] = out.astype(bf16)
            norm_refs[t][...] = norm.astype(bf16)

    @pl.when(step == 2 * tiles)
    def _():
        for t in range(groups):
            norm_refs[t][:, : term_buf.shape[2]] = term_buf[t]


def experts_call(at, blocks, held, x_parts, g_parts, info, slots, w_in, w_down, s_in, s_down, capacity, waits):
    counts = [len(parts) for parts in x_parts]
    x_parts = [x for parts in x_parts for x in parts]
    groups, local = len(counts), w_in.shape[0]
    chunks = info.shape[0] - 2
    model, whole_width = g_parts[0].shape[1], x_parts[0].shape[1]
    lanes = whole_width - model
    tokens = sum(x.shape[0] for x in x_parts[: counts[0]])
    tile = 512 if groups <= 2 else 256
    tiles = model // tile
    width, s_width = w_down.shape[1], s_down.shape[0]
    rows = groups * capacity

    def tokens_in(i, info):
        return (0, jnp.minimum(i, tiles - 1))

    def picked(i, info):
        return (0, at, jnp.minimum(i, tiles - 1))

    def own(i, info):
        return (at, jnp.minimum(i, tiles - 1))

    def summed(i, info):
        return (info[chunks + 1], jnp.clip(i - tiles, 0, tiles - 1))

    def summed_norm(i, info):
        return (0, jnp.maximum(i - tiles, 0))

    in_specs = [
        *(pl.BlockSpec((x.shape[0], tile), tokens_in) for x in x_parts),
        *(pl.BlockSpec((x.shape[0], lanes), lambda i, info: (0, model // lanes)) for x in x_parts),
        *[pl.BlockSpec((tokens, tile), tokens_in)] * groups,
        whole_spec(slots.shape),
        whole_spec(slots.shape[::-1]),
        pl.BlockSpec((local, tile, 2 * width), lambda i, info: (0, i % tiles, 0)),
        pl.BlockSpec((local, width, tile), lambda i, info: (0, 0, i % tiles)),
        pl.BlockSpec((tile, 2 * s_width), lambda i, info: (i % tiles, 0)),
        pl.BlockSpec((s_width, tile), lambda i, info: (0, i % tiles)),
        *[in_place] * (len(held) + len(waits)),
    ]
    kept = (
        jax.ShapeDtypeStruct((local, blocks * rows, model), bf16),
        jax.ShapeDtypeStruct((local, blocks * rows, model), bf16),
        jax.ShapeDtypeStruct((local, blocks * rows, width), bf16),
        jax.ShapeDtypeStruct((local, blocks * rows, 2 * width), bf16),
        jax.ShapeDtypeStruct((blocks * tokens, model), bf16),
        jax.ShapeDtypeStruct((blocks * tokens, model), bf16),
        jax.ShapeDtypeStruct((blocks * tokens, s_width), bf16),
        jax.ShapeDtypeStruct((blocks * tokens, 2 * s_width), bf16),
        *[jax.ShapeDtypeStruct((blocks * tokens, model), bf16)] * groups,
    )
    norms = (jax.ShapeDtypeStruct((tokens, whole_width), bf16),) * groups
    out_specs = [
        pl.BlockSpec((local, rows, tile), picked),
        pl.BlockSpec((local, rows, tile), picked),
        pl.BlockSpec((local, rows, width), lambda i, info: (0, at, 0)),
        pl.BlockSpec((local, rows, 2 * width), lambda i, info: (0, at, 0)),
        pl.BlockSpec((tokens, tile), own),
        pl.BlockSpec((tokens, tile), own),
        pl.BlockSpec((tokens, s_width), lambda i, info: (at, 0)),
        pl.BlockSpec((tokens, 2 * s_width), lambda i, info: (at, 0)),
        *[pl.BlockSpec((tokens, tile), summed)] * groups,
        *[pl.BlockSpec((tokens, tile), summed_norm)] * groups,
    ]
    work = 2 * model * (
        4 * groups * local * capacity * tokens + 6 * local * rows * width + 6 * tokens * s_width
    )
    first = 1 + len(in_specs) - len(held) - len(waits)
    results = pl.pallas_call(
        functools.partial(experts_kernel, counts, len(held) + len(waits), local, tiles, chunks),
        out_shape=(*kept, *norms),
        grid_spec=pltpu.PrefetchScalarGridSpec(
            num_scalar_prefetch=1,
            grid=(2 * tiles + 1,),
            in_specs=in_specs,
            out_specs=out_specs,
            scratch_shapes=[
                pltpu.VMEM((groups * local, capacity, tokens), bf16),
                pltpu.VMEM((groups, tokens, local * capacity), bf16),
                pltpu.VMEM((local, rows, 2 * width), f32),
                pltpu.VMEM((local, rows, width), f32),
                pltpu.VMEM((tokens, 2 * s_width), f32),
                pltpu.VMEM((tokens, s_width), f32),
                pltpu.VMEM((groups, tokens, lanes), bf16),
            ],
        ),
        input_output_aliases={first + i: i for i in range(len(held))},
        compiler_params=pltpu.CompilerParams(vmem_limit_bytes=vmem_limit),
        cost_estimate=pl.CostEstimate(flops=work, bytes_accessed=2**10, transcendentals=0),
    )(info, *x_parts, *x_parts, *g_parts, slots, slots.T, w_in, w_down, s_in, s_down, *held, *waits)
    return list(results[: len(kept)]), list(results[len(kept) :])


def shards(
    inputs,
    routes,
    w_query,
    w_key,
    w_value,
    w_output,
    gain_attn,
    gain_moe,
    w_router,
    shared_gate,
    shared_up,
    shared_down,
    expert_gate,
    expert_up,
    expert_down,
    out_grad,
):
    e, r, c = lax.axis_index("exp"), lax.axis_index("row"), lax.axis_index("col")
    E, R, C = lax.axis_size("exp"), lax.axis_size("row"), lax.axis_size("col")
    local_count, model_width, _ = expert_gate.shape
    n_experts = local_count * E * R
    block_rows, top_count = routes.shape
    capacity = 4 * block_rows * top_count // (3 * n_experts)
    home_rows = block_rows // C
    head_width = HEAD_DIM
    query_width, key_width = w_query.shape[1], w_key.shape[1]
    group_heads = query_width // key_width
    attn_scale = head_width ** (-0.5)
    sources = ring_sources("col")

    x = tokens_home(inputs, 0).astype(f32)
    small = jnp.concatenate([w_router.T, gain_attn[None], gain_moe[None]], axis=0)
    small_all = jnp.zeros((small.shape[0], model_width), f32)
    for s, part in enumerate(exchange(small, "col")):
        small_all = lax.dynamic_update_slice(small_all, part, (0, (c ^ s) * small.shape[1]))
    router_t, gain_one, gain_two = (
        small_all[:n_experts],
        small_all[n_experts],
        small_all[n_experts + 1],
    )
    inv_one = rms_inverse(x)
    norm_one = (x * inv_one * gain_one[None, :]).astype(bf16)
    norm_one_parts = row_gather(norm_one)
    norm_one_all = jnp.concatenate(norm_one_parts, axis=0)

    own_in = own_share(jnp.concatenate([w_key, w_value, w_query], axis=1))
    weight_in = lax.all_gather(own_in, ("col", "exp"), tiled=True)
    raw = dot(norm_one_all, weight_in)
    wait = zero_of(raw)
    here = jnp.stack([e, c]).astype(jnp.int32)
    weight_out = lax.all_gather(own_share(w_output, wait), ("col", "exp"), tiled=True)
    weight_out = join_weight(weight_out, 0, C, E)

    s_width = shared_gate.shape[1] // C
    s_padded = -(-s_width // 128) * 128

    def col_swap(parts):
        return [swap(parts[s], "col", s) if s else parts[0] for s in range(C)]

    shared_cut = cut_shared(here, shared_gate, shared_up, shared_down, C, E, raw)
    in_rows, feature_width = shared_gate.shape[0] // E, shared_down.shape[1]
    expert_in = side_by_side(expert_gate, expert_up, raw)

    own_routes = lax.dynamic_slice_in_dim(routes, c * home_rows, home_rows, 0)
    routes_here = routes.reshape(C, home_rows, top_count)[sources].reshape(block_rows, top_count)
    expert_ids = jnp.arange(n_experts)
    first_expert = (e * R + r) * local_count
    own_ids = first_expert + jnp.arange(local_count)
    earlier = (jnp.arange(block_rows)[:, None] < jnp.arange(block_rows)[None, :]).astype(bf16)
    routes_t = routes_here.T
    routes_t = routes_t + wait
    named = jnp.stack(
        [
            (block[None] == own_ids[:, None, None]).any(axis=1)
            for of_row in exchange(routes_t, "row")
            for block in exchange(of_row, "exp")
        ]
    ).reshape(R, E * local_count, block_rows)
    rank = dot(named.reshape(-1, block_rows).astype(bf16), earlier).astype(jnp.int32)
    slots = jnp.where(named, rank.reshape(named.shape), -1)

    positions = (
        ((r ^ jnp.arange(R)) * block_rows + c * home_rows)[:, None]
        + jnp.arange(home_rows)[None, :]
    ).reshape(-1)
    cosines, sines = rope_tables(positions, head_width)
    own_rows = R * home_rows
    keys = rotate(raw[:, :key_width].reshape(own_rows, 1, head_width), cosines, sines)
    kv = jnp.concatenate([keys.reshape(own_rows, key_width), raw[:, key_width : 2 * key_width]], axis=1)
    kv_parts = exchange(kv.astype(bf16), "col")
    g_block = lax.all_gather(after(out_grad, *kv_parts[1:], expert_in, shared_cut), "col", axis=1, tiled=True)
    g = lax.dynamic_slice_in_dim(g_block, c * home_rows, home_rows, 0)
    queries = rotate(
        raw[:, 2 * key_width :].reshape(own_rows, group_heads, head_width), cosines, sines
    )
    queries = (queries * attn_scale).astype(bf16).reshape(own_rows, query_width)
    place = jnp.concatenate([jnp.stack([r, c]), c ^ jnp.arange(C)]).astype(jnp.int32)
    attended, att_total, lse = attention_forward(place, queries, kv_parts, home_rows, (expert_in, shared_cut))
    attn_part = dot(attended, weight_out).astype(bf16)
    shared_parts = col_swap(after(shared_cut, attended))
    sh_in, sh_down = join_shared(
        here, exchange(jnp.stack(shared_parts), "exp"), in_rows, feature_width, s_padded
    )
    hidden_state = x + row_reduce(jnp.split(attn_part, R, axis=0))[0]
    inv_two = rms_inverse(hidden_state) + zero_of(g_block, *shared_parts[1:]).astype(f32)
    norm_two = (hidden_state * inv_two * gain_two[None, :]).astype(bf16)

    norm_float = norm_two.astype(f32)
    logits = lax.dot_general(
        norm_float, router_t, (((1,), (1,)), ((), ())), precision=highest
    )
    router_probs = jax.nn.softmax(logits, axis=-1)
    routed = (own_routes[:, :, None] == expert_ids[None, None, :]).any(axis=1)
    chosen = jnp.where(routed, router_probs, 0.0)
    chosen_sum = jnp.sum(chosen, axis=1, keepdims=True)
    mix = chosen / chosen_sum

    mix_lanes = -(-n_experts // 64) * 64
    mix_first = lax.reduce_precision(mix, 8, 7)
    mix_pad = ((0, 0), (0, mix_lanes - n_experts))
    payload = jnp.concatenate(
        [
            norm_two,
            jnp.pad(mix_first.astype(bf16), mix_pad),
            jnp.pad((mix - mix_first).astype(bf16), mix_pad),
        ],
        axis=1,
    )
    payload = jnp.concatenate(ring_gather(payload, "col"), axis=0)
    grad_rows = row_gather(g_block)
    grad_own = exchange(g_block, "exp")
    payload = after(payload, *grad_rows[1:3], *grad_own[1:], sh_in)
    payload_rows = row_gather(payload)
    if R == 4:
        grad_rows = grad_rows[:3] + [jnp.concatenate(grad_rows[3:], axis=0)]
        payload_rows = [[x] for x in payload_rows[:3]] + [payload_rows[3:]]
    else:
        payload_rows = [[x] for x in payload_rows]

    def shared_gradients(kept):
        own_x, own_g, s_hidden, s_pre = kept[4:8]
        d_in = dot(own_x, s_pre, (0, 0)).astype(bf16)
        d_down = dot(s_hidden, own_g, (0, 0)).astype(bf16)
        return cut_shared_grads(here, d_in, d_down, C, E, s_width)

    kept, norms, moved = [], [], []
    for s in range(R):
        x_block = payload_rows[s]
        if E > 2 and kept:
            x_block = [after(x, kept[-1]) for x in x_block]
            grad_rows[s] = after(grad_rows[s], kept[-1])
        info = jnp.concatenate(
            [sources, jnp.stack([first_expert, r ^ s])]
        ).astype(jnp.int32)
        kept, norm = experts_call(
            s, R, kept, list(zip(*(exchange(x, "exp") for x in x_block))),
            exchange(grad_rows[s], "exp") if s else grad_own, info,
            slots[s], expert_in, expert_down, sh_in, sh_down, capacity, norms[-1:],
        )
        if s == R - 1:
            shared_grads = shared_gradients(kept)
        seen = [*moved, shared_grads[0]] if s == R - 1 else [x for later in ((1, 2), (3,))[s] for x in payload_rows[later]] if s < 2 else []
        if seen:
            norm = [norm[0], *(after(x, *seen) for x in norm[1:])]
        norms.append(reduce_parts(norm, "exp").astype(bf16))
        if s:
            moved.append(swap(norms[s], "row", s))
    kept, outs = kept[:8], kept[8:]
    rows_x, rows_g, hidden, pre = kept[:4]

    shared_sum = reduce_parts(shared_grads, "exp").astype(bf16)
    outs_moved = [swap(after(outs[t], norms[-1], shared_sum), "exp", t) for t in range(1, E)]
    shared_back = jnp.stack(col_swap(shared_sum))
    norm_block = norms[0].astype(f32)
    for x_sum in moved:
        norm_block = norm_block + x_sum.astype(f32)
    chunks = jnp.split(norm_block.astype(bf16), C, axis=0)
    home = ring_reduce(chunks, "col")
    d_norm, gate_terms = home[:, :model_width], home[:, model_width : model_width + n_experts]
    out_sum = outs[0].astype(f32)
    for part in outs_moved:
        out_sum = add(out_sum, part)
    out_sum = after(out_sum.astype(bf16), moved[-1], shared_back)
    out_rows = lax.psum_scatter(out_sum, "row", scatter_dimension=0, tiled=True)

    expert_width = expert_gate.shape[2]
    pre = after(pre, moved[-1])
    grad_expert_gate = batch_dot("lrd,lrf->ldf", rows_x, pre[:, :, :expert_width])
    grad_expert_up = batch_dot("lrd,lrf->ldf", rows_x, pre[:, :, expert_width:])
    grad_expert_down = batch_dot("lrf,lrd->lfd", after(hidden, moved[-1]), rows_g)
    inner = jnp.sum(mix * gate_terms, axis=1, keepdims=True)
    d_probs = jnp.where(routed, (gate_terms - inner) / chosen_sum, 0.0)
    d_logits = router_probs * (
        d_probs - jnp.sum(router_probs * d_probs, axis=1, keepdims=True)
    )
    d_norm = d_norm + jnp.dot(d_logits, router_t, precision=highest)
    d_norm = d_norm + zero_of(grad_expert_gate, grad_expert_up, grad_expert_down).astype(f32)
    router_part = lax.dot_general(
        d_logits, norm_float, (((0,), (0,)), ((), ())), precision=highest
    )
    d_v, gain_two_part = rms_backward(hidden_state, inv_two, gain_two, d_norm)
    d_hidden = g.astype(f32) + d_v
    d_attn = d_hidden.astype(bf16)
    d_attn_parts = row_gather(d_attn)
    d_attn_all = jnp.concatenate(d_attn_parts, axis=0)

    out_grads = batch_dot("sf,scd->cfd", attended, d_attn_all.reshape(own_rows, C, -1))
    out_grads = out_grads.astype(bf16).reshape(C * query_width, -1)

    d_attended = dot(d_attn_all, weight_out, (1, 1)).astype(bf16)
    out_chunks = jnp.split(after(out_rows, d_attended), C, axis=0)
    moe_out = ring_send(out_chunks[C - 1], "col", 1)
    d_queries, d_kv_parts = attention_backward(
        place, queries, d_attended, att_total, lse, kv_parts, home_rows,
        (out_grads,),
    )
    d_kv_parts = after(d_kv_parts, moe_out)
    d_kv = reduce_parts([d_kv_parts[k] for k in range(C)], "col")
    for k in range(C - 2, 0, -1):
        moe_out = ring_send(add(out_chunks[k], moe_out).astype(bf16), "col", 1)
    d_query_raw = rotate(
        d_queries.reshape(own_rows, group_heads, head_width), cosines, -sines
    ) * attn_scale
    d_query_raw = d_query_raw.reshape(own_rows, query_width).astype(bf16)
    norm_one_late = after(norm_one_all, d_kv_parts)
    query_grads = dot(norm_one_late, d_query_raw, (0, 0)).astype(bf16)
    d_key_raw = rotate(d_kv[:, :key_width].reshape(own_rows, 1, head_width), cosines, -sines)
    d_kv_raw = jnp.concatenate(
        [d_key_raw.reshape(own_rows, key_width), d_kv[:, key_width:]], axis=1
    ).astype(bf16)
    norm_one_part = dot(jnp.concatenate([d_kv_raw, d_query_raw], axis=1), weight_in, (1, 1)).astype(bf16)
    d_norm_one, halfway = row_reduce(jnp.split(norm_one_part, R, axis=0))
    d_x, gain_one_part = rms_backward(x, inv_one, gain_one, d_norm_one)
    grad_inputs, back = tokens_back((d_hidden + d_x).astype(bf16))

    moe_out = add(out_chunks[0], after(moe_out, *back))
    output = tokens_back((hidden_state + moe_out).astype(bf16))[0]
    out_total, query_total = reduce_weight(out_grads), reduce_weight(query_grads)
    kv_grads = dot(after(norm_one_late, *halfway), d_kv_raw, (0, 0)).astype(bf16)
    kv_total = reduce_weight(after(kv_grads, query_total, d_norm_one))
    grad_output = all_shares(after(out_total, d_norm_one)).astype(f32)
    grad_query = all_shares(after(query_total, d_norm_one)).astype(f32)
    grad_kv = all_shares(kv_total).astype(f32)
    small_part = jnp.concatenate([router_part, gain_one_part[None], gain_two_part[None]], axis=0)
    small_part = small_part + zero_of(*back).astype(f32)
    width = small.shape[1]
    mine = [
        lax.dynamic_slice_in_dim(small_part, (c ^ s) * width, width, 1) for s in range(C)
    ]
    small_sum = all_sum(all_sum(reduce_parts(mine, "col"), "row"), "exp")

    grad_shared_gate, grad_shared_up, grad_shared_down = join_shared_grads(
        here, exchange(after(shared_back, d_norm_one), "exp"), in_rows, feature_width
    )
    return (
        output,
        grad_inputs,
        grad_query,
        grad_kv[:, :key_width],
        grad_kv[:, key_width:],
        grad_output,
        small_sum[n_experts],
        small_sum[n_experts + 1],
        small_sum[:n_experts].T,
        grad_shared_gate,
        grad_shared_up,
        grad_shared_down,
        grad_expert_gate,
        grad_expert_up,
        grad_expert_down,
    )


def solution(mesh):
    tokens, weight, experts = P(("exp", "row"), "col"), P("col", "row"), P(("exp", "row"), None, "col")
    expert_down, feature = P(("exp", "row"), "col", None), P("col")
    placed = (
        tokens,
        P(("exp", "row"), None),
        weight,
        weight,
        weight,
        P("row", "col"),
        feature,
        feature,
        P("col", None),
        weight,
        weight,
        P("row", "col"),
        experts,
        experts,
        expert_down,
        tokens,
    )
    return jax.shard_map(
        shards,
        mesh=mesh,
        in_specs=placed,
        out_specs=(
            tokens,
            tokens,
            weight,
            weight,
            weight,
            P("row", "col"),
            feature,
            feature,
            P("col", None),
            weight,
            weight,
            P("row", "col"),
            experts,
            experts,
            expert_down,
        ),
        check_vma=False,
    )
```
